32 devices in a mesh: section: 2 (over x), dp: 4 (over z), mp: 4 (over y, core).
Axes of the slice: x: 2, y: 2, z: 4, core: 2. Of those that a mesh axis runs over, the one named last changes fastest.
Arguments:
- ends_in: bfloat16 [2, 8192, 768], P('section', 'dp'), may hold values from -6 to 6
- seq_lengths: int32 [8, 8], P('dp'), may hold values from 1 to 512, 1024 in all within a row
- norm_gains: bfloat16 [2, 768, 2], P('section', 'dp'), may hold values from 0.099609375 to 1.8984375
- qk_weight: bfloat16 [2, 768, 2, 768], P('section', 'dp', None, 'mp'), may hold values from -0.21875 to 0.21875
- value_weight: bfloat16 [768, 1152], P('dp'), may hold values from -0.21875 to 0.21875
- out_weight: bfloat16 [2, 768, 768], P('section', 'mp', 'dp'), may hold values from -2.5 to 2.5
- fc_weight: bfloat16 [2, 768, 3072], P('section', 'dp', 'mp'), may hold values from -0.21875 to 0.21875
- proj_weight: bfloat16 [2, 3072, 768], P('section', 'mp', 'dp'), may hold values from -0.109375 to 0.109375
Outputs:
- ends_out: bfloat16 [2, 8192, 768], P('section', 'dp')
- grad_attn_gain: float32 [2, 768], P('section', 'dp')
- grad_mlp_gain: float32 [2, 768], P('section', 'dp')
- grad_qk: float32 [2, 768, 2, 768], P('section', 'dp', None, 'mp')
- grad_value: float32 [768, 1152], P('dp')
- grad_out: float32 [2, 768, 768], P('section', 'mp', 'dp')
- grad_fc: float32 [2, 768, 3072], P('section', 'dp', 'mp')
- grad_proj: float32 [2, 3072, 768], P('section', 'mp', 'dp')
The draws below stay inside these ranges and needn't reach their ends.
Inputs may be any that keep to these rules, and one draw needn't show every extreme that they name: `seq_lengths`: row b holds the lengths of the 8 sequences of micro-batch b; they sum to 1024, the longest is exactly 512.
All inputs are finite; a program needn't handle non-finite values.
Results may differ from the reference program's by a relative error of at most 0.03.
Values may be sent and summed in bfloat16 or wider, within the bound.
A program may use at most 192 MiB of HBM per device.

```python
import math
import jax
import jax.numpy as jnp
import numpy as np
from jax import lax

D = 768
HEADS = 12
FF = 3072
HD = 64
GROUPS = 4
MB_TOK = 1024
MAXLEN = 512
SEQS = 8
MICRO = 2
TOKENS = 8192
N_DP = 4


def level_of(key, extent, cuts, low, high):
    def one(position, shards_of):
        steps = jax.random.uniform(jax.random.fold_in(jax.random.fold_in(key, 6), position), (shards_of,), jnp.float32, low / len(cuts), high / len(cuts))
        return jnp.repeat(jnp.exp(steps), extent[position] // shards_of).reshape((-1,) + (1,) * (len(extent) - position - 1))

    loudness = one(*cuts[0])
    for cut in cuts[1:]:
        loudness = loudness * one(*cut)
    return loudness


def length_profile(amount, total, reach, slope):
    loads = [(1 << 20) // math.isqrt(standing ** slope) + 1 for standing in range(2, amount + 1)]
    rest, counts = total - reach - (amount - 1), [1] * (amount - 1)
    while rest > 0:
        candidates = [i for i in range(amount - 1) if counts[i] < reach]
        mass, left = sum([loads[i] for i in candidates]), rest
        for i in candidates:
            extra = min(reach - counts[i], max(1, left * loads[i] // mass), rest)
            counts[i] = counts[i] + extra
            rest = rest - extra
    return np.array([reach] + counts)


def uneven_parts(own_key, amount, total, limit, skew):
    if amount == 2:
        one = jax.random.randint(own_key, (), max(1, total - limit), min(limit, total - 1) + 1)
        return jnp.stack([one, total - one])
    tallies = jnp.asarray(length_profile(amount, total, limit, skew), jnp.int32)
    couples = (amount - 1) // 2
    donor, receiver = tallies[1:1 + 2 * couples:2], tallies[2:2 + 2 * couples:2]
    room = jnp.minimum(donor - 1, limit - receiver)
    passed = jax.random.randint(jax.random.fold_in(own_key, 1), (couples,), 0, 1 << 20) % (room + 1)
    tallies = tallies.at[1:1 + 2 * couples:2].set(donor - passed).at[2:2 + 2 * couples:2].set(receiver + passed)
    return tallies[jax.random.permutation(jax.random.fold_in(own_key, 2), amount)]


def bell_draw(rng, dims, scale, limit, pieces=(), kind=jnp.bfloat16):
    drawn = scale * jax.random.normal(rng, dims, jnp.float32)
    if pieces:
        drawn = drawn * level_of(rng, dims, pieces, -0.22, 0.18)
    return jnp.clip(drawn, -limit, limit).astype(kind)


def setup_inputs(seed: int = 0) -> dict:
    splits = jax.random.split(jax.random.key(seed), 9)
    ends_in = bell_draw(splits[0], (2, TOKENS, D), 1.0, 6.0, ((0, 2), (1, 4)))
    seq_lengths = jax.vmap(lambda own: uneven_parts(own, SEQS, MB_TOK, MAXLEN, 2))(jax.random.split(splits[1], (N_DP * MICRO))).reshape((N_DP * MICRO, SEQS)).astype(jnp.int32)
    norm_gains = jnp.clip(1.0 + 0.18 * jax.random.normal(splits[2], (2, D, 2), jnp.float32), 0.099609375, 1.8984375).astype(jnp.bfloat16)
    qk_weight = bell_draw(splits[3], (2, D, 2, D), D ** -0.5, 0.21875, ((0, 2), (1, 4), (3, 4)))
    value_weight = bell_draw(splits[4], (D, 3 * D // 2), D ** -0.5, 0.21875, ((0, 4),))
    out_weight = bell_draw(splits[5], (2, D, D), (max(D // 128, 2)) ** -0.5, 2.5, ((0, 2), (1, 4), (2, 4)))
    fc_weight = bell_draw(splits[6], (2, D, FF), D ** -0.5, 0.21875, ((0, 2), (1, 4), (2, 4)))
    proj_weight = bell_draw(splits[7], (2, FF, D), FF ** -0.5, 0.109375, ((0, 2), (1, 4), (2, 4)))
    return dict(ends_in=ends_in, seq_lengths=seq_lengths, norm_gains=norm_gains, qk_weight=qk_weight, value_weight=value_weight, out_weight=out_weight, fc_weight=fc_weight, proj_weight=proj_weight)


EPSILON = 1e-05
HIGHEST = lax.Precision.HIGHEST

@jax.custom_vjp
def low(v):
    return lax.optimization_barrier(v.astype(jnp.bfloat16)).astype(jnp.float32)

@jax.custom_vjp
def low_back(v):
    return v

def low_keep(v):
    return (low(v), None)

def low_pass(kept, grad):
    return (grad,)

def back_keep(v):
    return (v, None)

def back_low(kept, grad):
    return (low(grad),)
low.defvjp(low_keep, low_pass)
low_back.defvjp(back_keep, back_low)

def normalize(in_rows, gain_row):
    row_mean = lax.optimization_barrier(jnp.mean(in_rows, axis=-1, keepdims=True))
    centred = in_rows - row_mean
    row_var = lax.optimization_barrier(jnp.mean(centred * centred, axis=-1, keepdims=True))
    return centred * lax.rsqrt(row_var + EPSILON) * gain_row

def segment_ids(lengths):
    seq_ends = jnp.cumsum(lengths).astype(jnp.int32)
    places = jnp.arange(MB_TOK, dtype=jnp.int32)
    return lax.optimization_barrier(jnp.sum((places[:, None] >= seq_ends[None, :]).astype(jnp.int32), axis=1))

def attend(query_heads, key_heads, value_heads, segment):
    block_rows = min(512, MB_TOK)
    places = jnp.arange(MB_TOK, dtype=jnp.int32)
    scaling = 1.0 / math.sqrt(HD)

    def one_block(block_start):
        query_block = lax.dynamic_slice_in_dim(query_heads, block_start, block_rows, 0)
        seg_block = lax.dynamic_slice_in_dim(segment, block_start, block_rows, 0)
        pos_block = block_start + jnp.arange(block_rows, dtype=jnp.int32)
        scores = low_back(scaling * jnp.einsum('qhd,khd->hqk', query_block, key_heads, precision=HIGHEST))
        allowed = (seg_block[:, None] == segment[None, :]) & (places[None, :] <= pos_block[:, None])
        scores = jnp.where(allowed[None], scores, -1e+30)
        prob_vals = low(jax.nn.softmax(scores, axis=-1))
        return jnp.einsum('hqk,khd->qhd', prob_vals, value_heads, precision=HIGHEST)
    block_starts = jnp.arange(MB_TOK // block_rows, dtype=jnp.int32) * block_rows
    blocks = lax.map(jax.checkpoint(one_block), block_starts)
    return blocks.reshape(MB_TOK, HEADS, HD)

def column_groups(matrix, groups):
    return matrix.reshape(matrix.shape[0], groups, matrix.shape[1] // groups).transpose(1, 0, 2)

def row_groups(matrix):
    return matrix.reshape(GROUPS, matrix.shape[0] // GROUPS, matrix.shape[1])

def project(spread, matrix):
    return jnp.einsum('grd,gdc->grc', spread, matrix, precision=HIGHEST)

def to_heads(grouped):
    return grouped.transpose(1, 0, 2).reshape(MB_TOK, HEADS, HD)

def layer(in_rows, gain_pair, w_query, w_key, w_fresh, reused, w_out, w_up, w_down, segment):
    normed = low(normalize(in_rows, gain_pair[:, 0]))
    spread = low_back(jnp.broadcast_to(normed, (GROUPS,) + normed.shape))
    query_vals = low_back(low(project(spread, column_groups(w_query, GROUPS))))
    key_vals = low_back(low(project(spread, column_groups(w_key, GROUPS))))
    fresh_groups = w_fresh.shape[1] * GROUPS // D
    fresh_vals = low_back(low(project(spread[:fresh_groups], column_groups(w_fresh, fresh_groups))))
    if reused is None:
        value_vals = fresh_vals
    else:
        value_vals = jnp.concatenate([fresh_vals, low_back(reused)], axis=0)
    attn_mixed = attend(to_heads(query_vals), to_heads(key_vals), to_heads(value_vals), segment)
    attn_mixed = low_back(low(attn_mixed.reshape(MB_TOK, GROUPS, D // GROUPS).transpose(1, 0, 2)))
    attn_terms = low_back(low(project(attn_mixed, row_groups(w_out))))
    middle = in_rows + lax.optimization_barrier(jnp.sum(attn_terms, axis=0))
    normed_two = low(normalize(middle, gain_pair[:, 1]))
    spread_two = low_back(jnp.broadcast_to(normed_two, (GROUPS,) + normed_two.shape))
    hidden = low_back(project(spread_two, column_groups(w_up, GROUPS)))
    acted_vals = low(jax.nn.gelu(hidden))
    mlp_terms = low_back(low(project(acted_vals, row_groups(w_down))))
    return (middle + lax.optimization_barrier(jnp.sum(mlp_terms, axis=0)), value_vals)

def forward(params, in_rows, segment):
    gain_all, qk_all, value_all, out_all, up_all, down_all = params
    first_out, first_values = layer(in_rows, gain_all[0], qk_all[0, :, 0], qk_all[0, :, 1], value_all[:, :D], None, out_all[0], up_all[0], down_all[0], segment)
    second_in = low_back(low(first_out))
    second_out, second_values = layer(second_in, gain_all[1], qk_all[1, :, 0], qk_all[1, :, 1], value_all[:, D:], first_values[GROUPS // 2:], out_all[1], up_all[1], down_all[1], segment)
    return second_out

def reference(ends_in, seq_lengths, norm_gains, qk_weight, value_weight, out_weight, fc_weight, proj_weight):
    params = tuple((weight.astype(jnp.float32) for weight in (norm_gains, qk_weight, value_weight, out_weight, fc_weight, proj_weight)))
    batches = N_DP * MICRO
    inputs = ends_in[0].astype(jnp.float32).reshape(batches, MB_TOK, D)
    cotangent = ends_in[1].astype(jnp.float32).reshape(batches, MB_TOK, D)

    def one_batch(totals, batch_data):
        in_rows, grad_out, lengths = batch_data
        segment = segment_ids(lengths)

        def run_layers(weights, rows_in):
            return forward(weights, rows_in, segment)
        output, pullback = jax.vjp(run_layers, params, in_rows)
        grad_terms, grad_rows = pullback(grad_out)
        totals = tuple((total_term + new_term for total_term, new_term in zip(totals, grad_terms)))
        return (totals, (output, grad_rows))
    zero_terms = tuple((jnp.zeros_like(weight) for weight in params))
    totals, (outputs, grads_in) = lax.scan(one_batch, zero_terms, (inputs, cotangent, seq_lengths))
    ends_out = jnp.stack([grads_in.reshape(TOKENS, D), outputs.reshape(TOKENS, D)]).astype(jnp.bfloat16)
    return (ends_out, totals[0][:, :, 0], totals[0][:, :, 1], totals[1], totals[2], totals[3], totals[4], totals[5])
```

```python
import functools
import math

import jax
import jax.numpy as jnp
from jax import lax
from jax.experimental import pallas as pl
from jax.experimental.pallas import tpu as pltpu
from jax.sharding import Mesh, PartitionSpec as P

HEAD = 64
MB_TOK = 1024
PIECE = 256
PIECES = MB_TOK // PIECE
WINDOW = 3
LANES = 128
EPSILON = 1e-05
GELU_K = math.sqrt(2.0 / math.pi)
GELU_C = 0.044715
MESH = pl.DeviceIdType.MESH
F32 = jnp.float32
LOW = jnp.bfloat16


def mm(left, right):
    return lax.dot_general(left, right, (((1,), (0,)), ((), ())), preferred_element_type=F32)


def mm_back(left, right):
    return lax.dot_general(left, right, (((1,), (1,)), ((), ())), preferred_element_type=F32)


def normalize(rows):
    centred = rows - jnp.mean(rows, axis=1, keepdims=True)
    factor = lax.rsqrt(jnp.mean(centred * centred, axis=1, keepdims=True) + EPSILON)
    return centred * factor, factor


def norm_back(grad, plain, factor, gain):
    scaled = grad * gain
    return factor * (
        scaled
        - jnp.mean(scaled, axis=1, keepdims=True)
        - plain * jnp.mean(scaled * plain, axis=1, keepdims=True)
    )


def flip(tile):
    return pltpu.roll(tile, HEAD, 1)


def layers_kernel(
    width, x_ref, start_ref, gain_ref, w_ref,
    out_ref, grad_ref, gain_grad_ref,
    wa, q_s, k_s, v_s, kt_s, vt_s, o_s, lse_s, plain1, plain2, fac1, fac2,
    a_t, m_t, g_t, h_t, e_s, gd_s, dz_s, do_s, dqkv, dk_acc, dv_acc, bias_s,
    there, there_v, here, here_v, swap_out, swap_in,
    sem_xs, sem_xr, sem_vs, sem_vr, sem_cs, sem_cr,
):
    section = lax.axis_index("section")
    core = lax.axis_index("core")
    other_layer = {"section": 1 - section}
    other_core = {"core": 1 - core}
    first = section == 0
    tiles = width // 2 // LANES

    barrier = pltpu.get_barrier_semaphore()
    pl.semaphore_signal(barrier, inc=1, device_id=other_layer, device_id_type=MESH)
    pl.semaphore_signal(barrier, inc=1, device_id=other_core, device_id_type=MESH)
    pl.semaphore_wait(barrier, 2)

    lane = lax.broadcasted_iota(jnp.int32, (1, LANES), 1)
    low_half = lane < HEAD

    def halves(tile):
        return [jnp.where(low_half, tile, jnp.zeros_like(tile)),
                jnp.where(low_half, jnp.zeros_like(tile), tile)]

    def group_tile(group, index):
        return w_ref[group, :, index * LANES:(index + 1) * LANES]

    for kind in range(4):
        for group in range(2):
            spot = (kind * tiles + group) * LANES
            wa[:, spot:spot + LANES] = group_tile(group, kind)
    for pair in range(2):
        one, two = (group_tile(group, 4 + pair).astype(F32) for group in range(2))
        spot = (2 * pair * tiles + 2) * LANES
        wa[:, spot:spot + LANES] = jnp.where(low_half, one, flip(two)).astype(LOW)
        spot = ((2 * pair + 1) * tiles + 2) * LANES
        wa[:, spot:spot + LANES] = jnp.where(low_half, flip(one), two).astype(LOW)

    gain1 = gain_ref[0:1, :]
    gain2 = gain_ref[1:2, :]
    qkv_cols = 3 * tiles * LANES
    hidden = width

    def swap(slot, value):
        swap_out[...] = value
        copy = pltpu.make_async_remote_copy(
            src_ref=swap_out, dst_ref=swap_in.at[slot],
            send_sem=sem_cs.at[slot], recv_sem=sem_cr.at[slot],
            device_id=other_core, device_id_type=MESH,
        )
        copy.start()
        copy.wait()
        return swap_out[...].astype(F32) + swap_in[slot].astype(F32)

    def hand_over(piece):
        return (
            pltpu.make_async_remote_copy(
                src_ref=there.at[piece], dst_ref=here.at[piece],
                send_sem=sem_xs.at[piece], recv_sem=sem_xr.at[piece],
                device_id=other_layer, device_id_type=MESH,
            ),
            pltpu.make_async_remote_copy(
                src_ref=there_v.at[piece], dst_ref=here_v.at[piece],
                send_sem=sem_vs.at[piece], recv_sem=sem_vr.at[piece],
                device_id=other_layer, device_id_type=MESH,
            ),
        )

    def reused(tile_index):
        if tile_index == 0:
            return None
        if tile_index == 1:
            return jnp.logical_and(jnp.logical_not(first), lane >= 0)
        return jnp.logical_and(jnp.logical_not(first), lane >= HEAD)

    def make_bias(piece, count):
        base = piece * PIECE
        query = base + lax.broadcasted_iota(jnp.int32, (1, PIECE), 1)
        begin = start_ref[piece]
        for j in range(count):
            key = base - (count - 1 - j) * PIECE + lax.broadcasted_iota(jnp.int32, (PIECE, 1), 0)
            fine = jnp.logical_and(key >= begin, key <= query)
            bias_s[j] = jnp.where(fine, 0.0, -1e30).astype(F32)

    def attend(piece, count):
        make_bias(piece, count)
        for t in range(tiles):
            parts = []
            for h, query in enumerate(halves(q_s[piece, t])):
                scores = [
                    mm_back(k_s[piece - (count - 1 - j), t], query) + bias_s[j] for j in range(count)
                ]
                top = functools.reduce(
                    jnp.maximum, [jnp.max(s, axis=0, keepdims=True) for s in scores])
                expo = [jnp.exp(s - top) for s in scores]
                total = functools.reduce(
                    jnp.add, [jnp.sum(e, axis=0, keepdims=True) for e in expo])
                mixed = functools.reduce(jnp.add, [
                    mm(vt_s[piece - (count - 1 - j), t, h * HEAD:(h + 1) * HEAD, :], e.astype(LOW))
                    for j, e in enumerate(expo)
                ])
                parts.append(mixed * (1.0 / total))
                lse_s[piece, 2 * t + h] = top + jnp.log(total)
            o_s[piece, t] = jnp.concatenate(parts, axis=0).T.astype(LOW)

    def attend_back(piece, count):
        make_bias(piece, count)
        for t in range(tiles):
            inner = (do_s[t].astype(F32) * o_s[piece, t].astype(F32)).T
            queries = halves(q_s[piece, t])
            grads = halves(do_s[t])
            dq = [0.0, 0.0]
            sums = [jnp.sum(inner[h * HEAD:(h + 1) * HEAD], axis=0, keepdims=True) for h in range(2)]
            for j in range(count):
                at = piece - (count - 1 - j)
                dk_new, dv_new = 0.0, 0.0
                for h in range(2):
                    probs = jnp.exp(
                        mm_back(k_s[at, t], queries[h]) + bias_s[j] - lse_s[piece, 2 * t + h])
                    dprobs = mm_back(v_s[at, t], grads[h])
                    dscores = (probs * (dprobs - sums[h])).astype(LOW)
                    dv_new = dv_new + mm(probs.astype(LOW), grads[h])
                    dk_new = dk_new + mm(dscores, queries[h])
                    dq[h] = dq[h] + mm(kt_s[at, t, h * HEAD:(h + 1) * HEAD, :], dscores)
                dk_acc[at, t] += dk_new
                dv_acc[at, t] += dv_new
            dq_t = jnp.concatenate(dq, axis=0) * 0.125
            dqkv[piece, :, t * LANES:(t + 1) * LANES] = dq_t.T.astype(LOW)

    def by_count(piece, run):
        for count in range(1, WINDOW + 1):
            fits = piece >= WINDOW - 1 if count == WINDOW else piece == count - 1

            @pl.when(fits)
            def _(count=count):
                run(piece, count)

    def forward(piece, carry):
        @pl.when(jnp.logical_not(first))
        def _():
            for copy in hand_over(piece):
                copy.wait_recv()

        rows = jnp.where(first, x_ref[piece], here[piece]).astype(F32)
        plain, factor = normalize(rows)
        plain1[piece] = plain
        fac1[piece] = factor
        normed = plain * gain1
        a_t[piece] = normed.T.astype(LOW)
        qkv = mm(normed.astype(LOW), wa[:, :qkv_cols])
        for t in range(tiles):
            q_s[piece, t] = (qkv[:, t * LANES:(t + 1) * LANES].astype(LOW) * 0.125).astype(LOW)
            key = qkv[:, (tiles + t) * LANES:(tiles + t + 1) * LANES].astype(LOW)
            value = qkv[:, (2 * tiles + t) * LANES:(2 * tiles + t + 1) * LANES].astype(LOW)
            mask = reused(t)
            if mask is not None:
                value = jnp.where(mask, here_v[piece, t - 1], value)
                there_v[piece, t - 1] = value
            k_s[piece, t] = key
            v_s[piece, t] = value
            kt_s[piece, t] = key.astype(F32).T.astype(LOW)
            vt_s[piece, t] = value.astype(F32).T.astype(LOW)
        by_count(piece, attend)
        mixed = jnp.concatenate([o_s[piece, t] for t in range(tiles)], axis=1)
        middle = rows + swap(0, mm_back(mixed, wa[:, qkv_cols:]).astype(LOW))
        plain, factor = normalize(middle)
        plain2[piece] = plain
        fac2[piece] = factor
        normed = plain * gain2
        m_t[piece] = normed.T.astype(LOW)
        normed = normed.astype(LOW)
        total = 0.0
        for group in range(2):
            z = mm(normed, w_ref[group, :, hidden:2 * hidden])
            square = z * z
            bent = jnp.tanh(GELU_K * z * (1.0 + GELU_C * square))
            upper = 0.5 * (1.0 + bent)
            acted = (z * upper).astype(LOW)
            slope = upper + 0.5 * z * (1.0 - bent * bent) * (GELU_K * (1.0 + 3.0 * GELU_C * square))
            gd_s[piece, group] = slope.astype(LOW)
            e_s[piece, group] = acted
            total = total + mm_back(acted, w_ref[group, :, 2 * hidden:])
        result = middle + swap(1, total.astype(LOW))
        there[piece] = result.astype(LOW)

        @pl.when(first)
        def _():
            for copy in hand_over(piece):
                copy.start()

        @pl.when(jnp.logical_not(first))
        def _():
            out_ref[piece] = there[piece]

        return carry

    lax.fori_loop(0, PIECES, forward, 0)

    @pl.when(first)
    def _():
        for piece in range(PIECES):
            for copy in hand_over(piece):
                copy.wait_send()

    gain_grad_ref[...] = jnp.zeros_like(gain_grad_ref)
    dk_acc[...] = jnp.zeros_like(dk_acc)
    dv_acc[...] = jnp.zeros_like(dv_acc)

    def backward(step, carry):
        piece = PIECES - 1 - step

        @pl.when(first)
        def _():
            for copy in hand_over(piece):
                copy.wait_recv()

        grad_low = jnp.where(first, here[piece], x_ref[piece])
        grad = grad_low.astype(F32)
        g_t[piece] = grad.T.astype(LOW)
        total = 0.0
        for group in range(2):
            dz = mm(grad_low, w_ref[group, :, 2 * hidden:]) * gd_s[piece, group].astype(F32)
            dz = dz.astype(LOW)
            dz_s[piece, group] = dz
            total = total + mm_back(dz, w_ref[group, :, hidden:2 * hidden])
        dm = swap(0, total.astype(LOW))
        plain = plain2[piece]
        gain_grad_ref[1:2, :] += jnp.sum(dm * plain, axis=0, keepdims=True)
        middle = grad + norm_back(dm, plain, fac2[piece], gain2)
        h_t[piece] = middle.T.astype(LOW)
        dmixed = mm(middle.astype(LOW), wa[:, qkv_cols:]).astype(LOW)
        for t in range(tiles):
            do_s[t] = dmixed[:, t * LANES:(t + 1) * LANES]
        by_count(piece, attend_back)
        for t in range(tiles):
            dvalue = dv_acc[piece, t]
            mask = reused(t)
            if mask is not None:
                there_v[piece, t - 1] = dvalue.astype(LOW)
                came = jnp.logical_and(first, jnp.logical_or(t == 1, lane >= HEAD))
                dvalue = jnp.where(came, dvalue + here_v[piece, t - 1].astype(F32), dvalue)
                dvalue = jnp.where(mask, 0.0, dvalue)
            spot = (tiles + t) * LANES
            dqkv[piece, :, spot:spot + LANES] = dk_acc[piece, t].astype(LOW)
            spot = (2 * tiles + t) * LANES
            dqkv[piece, :, spot:spot + LANES] = dvalue.astype(LOW)
        da = swap(1, mm_back(dqkv[piece], wa[:, :qkv_cols]).astype(LOW))
        plain = plain1[piece]
        gain_grad_ref[0:1, :] += jnp.sum(da * plain, axis=0, keepdims=True)
        grad_in = middle + norm_back(da, plain, fac1[piece], gain1)
        there[piece] = grad_in.astype(LOW)

        @pl.when(jnp.logical_not(first))
        def _():
            for copy in hand_over(piece):
                copy.start()

        @pl.when(first)
        def _():
            out_ref[piece] = there[piece]

        return carry

    lax.fori_loop(0, PIECES, backward, 0)

    block = 256

    def weight_block(index, carry):
        group, column = index // (hidden // block), index % (hidden // block)
        spot = pl.multiple_of(column * block, block)
        total = 0.0
        other = 0.0
        for piece in range(PIECES):
            total = total + mm(m_t[piece], dz_s[piece, group, :, pl.ds(spot, block)])
            other = other + mm(g_t[piece], e_s[piece, group, :, pl.ds(spot, block)])
        grad_ref[group, :, pl.ds(pl.multiple_of(hidden + spot, block), block)] = total.astype(LOW)
        grad_ref[group, :, pl.ds(pl.multiple_of(2 * hidden + spot, block), block)] = other.astype(LOW)
        return carry

    lax.fori_loop(0, 2 * (hidden // block), weight_block, 0)

    pairs = []
    for kind in range(4):
        total = 0.0
        for piece in range(PIECES):
            if kind < 3:
                width_kind = tiles * LANES
                total = total + mm(a_t[piece], dqkv[piece, :, kind * width_kind:(kind + 1) * width_kind])
            else:
                mixed = jnp.concatenate([o_s[piece, t] for t in range(tiles)], axis=1)
                total = total + mm(h_t[piece], mixed)
        for group in range(2):
            part = total[:, group * LANES:(group + 1) * LANES].astype(LOW)
            grad_ref[group, :, kind * LANES:(kind + 1) * LANES] = part
        pairs.append(total[:, 2 * LANES:])
    for pair in range(2):
        one, two = pairs[2 * pair:2 * pair + 2]
        spot = (4 + pair) * LANES
        grad_ref[0, :, spot:spot + LANES] = jnp.where(low_half, one, flip(two)).astype(LOW)
        grad_ref[1, :, spot:spot + LANES] = jnp.where(low_half, flip(one), two).astype(LOW)

    @pl.when(jnp.logical_not(first))
    def _():
        for piece in range(PIECES):
            for copy in hand_over(piece):
                copy.wait_send()


def run_layers(x_rows, starts, gains, weights):
    width = x_rows.shape[2]
    tiles = width // 2 // LANES
    vmem = pl.BlockSpec(memory_space=pltpu.VMEM)
    per_tile = (PIECES, tiles, PIECE, LANES)
    turned = (PIECES, tiles, LANES, PIECE)
    flat = (PIECES, PIECE, width)
    flat_turned = (PIECES, width, PIECE)
    wide = (PIECES, 2, PIECE, width)
    low = lambda shape: pltpu.VMEM(shape, LOW)
    full = lambda shape: pltpu.VMEM(shape, F32)
    dma = lambda count: pltpu.SemaphoreType.DMA((count,))
    return pl.pallas_call(
        functools.partial(layers_kernel, width),
        out_shape=(
            jax.ShapeDtypeStruct(flat, LOW),
            jax.ShapeDtypeStruct(weights.shape, LOW),
            jax.ShapeDtypeStruct((8, width), F32),
        ),
        in_specs=[vmem] * 4,
        out_specs=(vmem,) * 3,
        scratch_shapes=[
            low((width, 4 * tiles * LANES)),
            low(per_tile), low(per_tile), low(per_tile), low(turned), low(turned), low(per_tile),
            full((PIECES, 2 * tiles, 1, PIECE)),
            full(flat), full(flat), full((PIECES, PIECE, 1)), full((PIECES, PIECE, 1)),
            low(flat_turned), low(flat_turned), low(flat_turned), low(flat_turned),
            low(wide), low(wide), low(wide), low((tiles, PIECE, LANES)),
            low((PIECES, PIECE, 3 * tiles * LANES)), full(per_tile), full(per_tile),
            full((WINDOW, PIECE, PIECE)),
            low(flat), low((PIECES, 2, PIECE, LANES)), low(flat), low((PIECES, 2, PIECE, LANES)),
            low((PIECE, width)), low((2, PIECE, width)),
            dma(PIECES), dma(PIECES), dma(PIECES), dma(PIECES), dma(2), dma(2),
        ],
        compiler_params=pltpu.CompilerParams(
            collective_id=0, has_side_effects=True, vmem_limit_bytes=63 << 20),
        name="layers",
    )(x_rows, starts, gains, weights)


def pack(parts):
    w_qk, w_value, w_out, w_up, w_down = parts
    query, key, out_t = w_qk[:, 0], w_qk[:, 1], w_out.T
    edge = 2 * HEAD
    return jnp.concatenate(
        [query[:, :edge], key[:, :edge], w_value[:, :edge], out_t[:, :edge],
         query[:, edge:], key[:, edge:], w_value[:, edge:], out_t[:, edge:], w_up, w_down.T],
        axis=1)


def unpack(packed):
    edge = 2 * HEAD
    cut = lambda spot, size: packed[:, spot:spot + size]
    query = jnp.concatenate([cut(0, edge), cut(4 * edge, HEAD)], axis=1)
    key = jnp.concatenate([cut(edge, edge), cut(4 * edge + HEAD, HEAD)], axis=1)
    value = jnp.concatenate([cut(2 * edge, edge), cut(5 * edge, HEAD)], axis=1)
    out_t = jnp.concatenate([cut(3 * edge, edge), cut(5 * edge + HEAD, HEAD)], axis=1)
    hidden = packed.shape[1] // 3
    return (
        jnp.stack([query, key], axis=1), value, out_t.T,
        cut(hidden, hidden), cut(2 * hidden, hidden).T)


def shards(
    ends_in, seq_lengths, norm_gains, qk_weight, value_weight, out_weight, fc_weight, proj_weight
):
    section = lax.axis_index("section")
    lane_y = lax.axis_index("y")
    group = 2 * lane_y + lax.axis_index("core")
    first = section == 0
    cols = qk_weight.shape[3]
    width = ends_in.shape[2]
    fresh = (value_weight.shape[1] - width) // cols
    offset = jnp.where(first, group, width // cols + jnp.minimum(group, fresh - 1)) * cols
    w_value = lax.dynamic_slice_in_dim(value_weight, offset, cols, 1)
    packed = pack((qk_weight[0], w_value, out_weight[0], fc_weight[0], proj_weight[0]))
    weights = lax.all_gather(packed, "dp", axis=0, tiled=True)
    weights = lax.all_gather(weights, "y", axis=0)
    gains = lax.all_gather(norm_gains[0], "dp", axis=0, tiled=True).astype(F32).T
    gains = jnp.concatenate([gains, jnp.zeros((6, width), F32)], axis=0)
    x_rows = lax.dynamic_slice_in_dim(ends_in[0], lane_y * MB_TOK, MB_TOK, 0)
    x_rows = x_rows.reshape(PIECES, PIECE, width)
    ends = jnp.cumsum(lax.dynamic_index_in_dim(seq_lengths, lane_y, 0, keepdims=False))
    places = jnp.arange(MB_TOK, dtype=jnp.int32)
    starts = jnp.max(
        jnp.where(ends[None, :] <= places[:, None], ends[None, :], 0), axis=1)
    starts = starts.astype(jnp.int32).reshape(PIECES, 1, PIECE)
    out_rows, grads, gain_grads = run_layers(x_rows, starts, gains, weights)
    both = lax.all_gather(out_rows.reshape(MB_TOK, width), "y", axis=0, tiled=True)
    grads = lax.psum_scatter(grads, "y", scatter_dimension=0, tiled=False)
    grads = lax.psum_scatter(grads, "dp", scatter_dimension=0, tiled=True)
    gain_rows = lax.psum(gain_grads[:2], "y").T
    gain_rows = lax.psum_scatter(gain_rows, "dp", scatter_dimension=0, tiled=True)
    d_qk, d_value, d_out, d_up, d_down = unpack(grads.astype(F32))
    values = lax.all_gather(d_value.astype(LOW), ("section", "y", "core"), axis=0)
    kept = width // cols + fresh
    d_value = jnp.concatenate([values[index] for index in range(kept)], axis=1).astype(F32)
    return (
        both[None], gain_rows[:, 0][None], gain_rows[:, 1][None], d_qk[None], d_value,
        d_out[None], d_up[None], d_down[None])


def solution(mesh):
    sections, depth, split = (mesh.shape[name] for name in ("section", "dp", "mp"))
    grid = Mesh(mesh.devices.reshape(sections, depth, split // 2, 2), ("section", "dp", "y", "core"))
    mp = ("y", "core")
    in_specs = (
        P("section", "dp", None),
        P("dp", None),
        P("section", "dp", None),
        P("section", "dp", None, mp),
        P("dp", None),
        P("section", mp, "dp"),
        P("section", "dp", mp),
        P("section", mp, "dp"),
    )
    out_specs = (
        P("section", "dp", None),
        P("section", "dp"),
        P("section", "dp"),
        P("section", "dp", None, mp),
        P("dp", None),
        P("section", mp, "dp"),
        P("section", "dp", mp),
        P("section", mp, "dp"),
    )
    return jax.shard_map(shards, mesh=grid, in_specs=in_specs, out_specs=out_specs, check_vma=False)
```

```python
import functools
import math

import jax
import jax.numpy as jnp
from jax import lax
from jax.experimental import pallas as pl
from jax.experimental.pallas import tpu as pltpu
from jax.sharding import Mesh, PartitionSpec as P

HEAD = 64
MB_TOK = 1024
PIECE = 256
PIECES = MB_TOK // PIECE
WINDOW = 3
LANES = 128
EPSILON = 1e-05
GELU_K = math.sqrt(2.0 / math.pi)
GELU_C = 0.044715
MESH = pl.DeviceIdType.MESH
F32 = jnp.float32
LOW = jnp.bfloat16


def mm(left, right):
    return lax.dot_general(left, right, (((1,), (0,)), ((), ())), preferred_element_type=F32)


def mm_back(left, right):
    return lax.dot_general(left, right, (((1,), (1,)), ((), ())), preferred_element_type=F32)


def normalize(rows):
    centred = rows - jnp.mean(rows, axis=1, keepdims=True)
    factor = lax.rsqrt(jnp.mean(centred * centred, axis=1, keepdims=True) + EPSILON)
    return centred * factor, factor


def norm_back(grad, plain, factor, gain):
    scaled = grad * gain
    return factor * (
        scaled
        - jnp.mean(scaled, axis=1, keepdims=True)
        - plain * jnp.mean(scaled * plain, axis=1, keepdims=True)
    )


def flip(tile):
    return pltpu.roll(tile, HEAD, 1)


def layers_kernel(width, depth, inside, *refs):
    refs = list(refs)
    take = lambda count: [refs.pop(0) for _ in range(count)]
    x_ref, start_ref, gain_ref, part_ref = take(4)
    out_ref, grad_ref, gain_grad_ref = take(3)
    if inside:
        (value_ref,) = take(1)
    (wa, q_s, k_s, v_s, kt_s, vt_s, o_s, lse_s, plain1, plain2, fac1, fac2,
     a_t, m_t, g_t, h_t, e_s, gd_s, do_s, dqkv, spare, bias_s,
     there, there_v, here, here_v, swap_out, swap_in,
     sem_x, sem_v, sem_f, sem_c, sem_o, sem_l) = take(34)
    if inside:
        (w_ref, gain_all, sums, y_in, z_in, gain_y, gain_z,
         sem_az, sem_ay, sem_gz, sem_ry, sem_rz, sem_gg, sem_va) = take(14)
    else:
        w_ref, sums = part_ref, grad_ref

    section = lax.axis_index("section")
    core = lax.axis_index("core")
    lane_y = lax.axis_index("y")
    deep = lax.axis_index("dp")
    other_layer = {"section": 1 - section}
    other_core = {"core": 1 - core}
    other_y = {"y": 1 - lane_y}
    first = section == 0
    second = jnp.logical_not(first)
    tiles = width // 2 // LANES
    hidden = width
    rows_own = width // depth
    half_cols = width // 2

    def send(src, dst, sems, index, target):
        return pltpu.make_async_remote_copy(
            src_ref=src, dst_ref=dst, send_sem=sems.at[(0,) + index], recv_sem=sems.at[(1,) + index],
            device_id=target, device_id_type=MESH)

    def peer(step):
        return {"dp": lax.rem(deep + step, depth)}

    barrier = pltpu.get_barrier_semaphore()
    friends = [other_layer, other_core, other_y]
    if inside:
        friends = friends + [peer(step) for step in range(1, depth)]
    for friend in friends:
        pl.semaphore_signal(barrier, inc=1, device_id=friend, device_id_type=MESH)
    pl.semaphore_wait(barrier, len(friends))

    lane = lax.broadcasted_iota(jnp.int32, (1, LANES), 1)
    low_half = lane < HEAD

    def rows_at(place):
        return pl.ds(pl.multiple_of(place * rows_own, rows_own), rows_own)

    def cols_at(part):
        return pl.ds(part * hidden, hidden)

    def own_copy(part):
        return pltpu.make_async_copy(
            part_ref.at[:, cols_at(part)], w_ref.at[lane_y, rows_at(deep), cols_at(part)],
            sem_l.at[part])

    def gather_z(part, step):
        return send(part_ref.at[:, cols_at(part)],
                    w_ref.at[lane_y, rows_at(deep), cols_at(part)], sem_az, (part, step), peer(step))

    def gather_y(part, step):
        if step == 0:
            return send(part_ref.at[:, cols_at(part)],
                        w_ref.at[lane_y, rows_at(deep), cols_at(part)], sem_ay, (part, 0), other_y)
        spot = w_ref.at[lane_y, rows_at(lax.rem(deep - step + depth, depth)), cols_at(part)]
        return send(spot, spot, sem_ay, (part, step), other_y)

    def gather_gain(step):
        return send(gain_ref, gain_all.at[deep], sem_gz, (step,), peer(step))

    def gather_start(part):
        own_copy(part).start()
        for step in range(1, depth):
            gather_z(part, step).start()
        gather_y(part, 0).start()

    def gather_pass(part):
        for step in range(1, depth):
            gather_z(part, step).wait_recv()
            gather_y(part, step).start()

    def gather_end(part):
        own_copy(part).wait()
        for step in range(depth):
            gather_y(part, step).wait()
        for step in range(1, depth):
            gather_z(part, step).wait_send()

    block = 2 * LANES

    def block_at(index):
        return pl.ds(index * block, block)

    def reduce_y(index):
        return send(sums.at[1 - lane_y, :, block_at(index)], y_in.at[:, block_at(index)],
                    sem_ry, (index,), other_y)

    def reduce_z(index, step):
        return send(sums.at[lane_y, rows_at(lax.rem(deep + step, depth)), block_at(index)],
                    z_in.at[step - 1, :, block_at(index)], sem_rz, (index, step), peer(step))

    def reduce_mid(index):
        reduce_y(index).wait_recv()
        at = block_at(index)
        sums[lane_y, :, at] = (
            sums[lane_y, :, at].astype(F32) + y_in[:, at].astype(F32)).astype(LOW)
        for step in range(1, depth):
            reduce_z(index, step).start()

    def reduce_end(index):
        at = block_at(index)
        total = sums[lane_y, rows_at(deep), at].astype(F32)
        for step in range(1, depth):
            reduce_z(index, step).wait_recv()
            total = total + z_in[step - 1, :, at].astype(F32)
        grad_ref[:, at] = total

    def halves(tile):
        return [jnp.where(low_half, tile, jnp.zeros_like(tile)),
                jnp.where(low_half, jnp.zeros_like(tile), tile)]

    def group_tile(group, index):
        return w_ref[group, :, index * LANES:(index + 1) * LANES]

    qkv_cols = 3 * tiles * LANES

    def arrange():
        for kind in range(4):
            for group in range(2):
                spot = (kind * tiles + group) * LANES
                wa[:, spot:spot + LANES] = group_tile(group, kind)
        for pair in range(2):
            one, two = (group_tile(group, 4 + pair).astype(F32) for group in range(2))
            spot = (2 * pair * tiles + 2) * LANES
            wa[:, spot:spot + LANES] = jnp.where(low_half, one, flip(two)).astype(LOW)
            spot = ((2 * pair + 1) * tiles + 2) * LANES
            wa[:, spot:spot + LANES] = jnp.where(low_half, flip(one), two).astype(LOW)

    if inside:
        gain_all[deep] = gain_ref[...]
        for step in range(1, depth):
            gather_gain(step).start()
        gather_start(0)
        gather_start(1)
        gather_pass(0)
        gather_start(2)
        for step in range(1, depth):
            gather_gain(step).wait()
        gather_end(0)
        gains = jnp.concatenate([gain_all[place, :, :rows_own] for place in range(depth)], axis=1)
    else:
        gains = gain_ref[...]
    arrange()
    gain1 = gains[0:1, :]
    gain2 = gains[1:2, :]

    def swap(slot, value):
        swap_out[...] = value
        copy = send(swap_out, swap_in.at[slot], sem_c, (slot,), other_core)
        copy.start()
        copy.wait()
        return swap_out[...].astype(F32) + swap_in[slot].astype(F32)

    half = pl.ds(pl.multiple_of(core * half_cols, half_cols), half_cols)

    def hand_over(piece):
        return (
            send(there.at[piece, :, half], here.at[piece, :, half], sem_x, (piece,), other_layer),
            send(there_v.at[piece], here_v.at[piece], sem_v, (piece,), other_layer),
        )

    def hand_on(piece):
        return send(here.at[piece, :, half], here.at[piece, :, half], sem_f, (piece,), other_core)

    def take_over(piece):
        copy, copy_v = hand_over(piece)
        copy.wait_recv()
        passing = hand_on(piece)
        passing.start()
        copy_v.wait_recv()
        passing.wait()

    def emit(piece):
        return (
            pltpu.make_async_copy(there.at[piece], out_ref.at[lane_y, piece], sem_l.at[3 + piece]),
            send(there.at[piece], out_ref.at[lane_y, piece], sem_o, (piece,), other_y),
        )

    def reused(tile_index):
        if tile_index == 0:
            return None
        if tile_index == 1:
            return jnp.logical_and(second, lane >= 0)
        return jnp.logical_and(second, lane >= HEAD)

    def make_bias(piece, count):
        base = piece * PIECE
        query = base + lax.broadcasted_iota(jnp.int32, (1, PIECE), 1)
        begin = start_ref[piece]
        for j in range(count):
            key = base - (count - 1 - j) * PIECE + lax.broadcasted_iota(jnp.int32, (PIECE, 1), 0)
            fine = jnp.logical_and(key >= begin, key <= query)
            bias_s[j] = jnp.where(fine, 0.0, -1e30).astype(F32)

    def attend(piece, count):
        make_bias(piece, count)
        for t in range(tiles):
            parts = []
            for h, query in enumerate(halves(q_s[piece, t])):
                scores = [
                    mm_back(k_s[piece - (count - 1 - j), t], query) + bias_s[j] for j in range(count)
                ]
                top = functools.reduce(
                    jnp.maximum, [jnp.max(s, axis=0, keepdims=True) for s in scores])
                expo = [jnp.exp(s - top) for s in scores]
                total = functools.reduce(
                    jnp.add, [jnp.sum(e, axis=0, keepdims=True) for e in expo])
                mixed = functools.reduce(jnp.add, [
                    mm(vt_s[piece - (count - 1 - j), t, h * HEAD:(h + 1) * HEAD, :], e.astype(LOW))
                    for j, e in enumerate(expo)
                ])
                parts.append(mixed * (1.0 / total))
                lse_s[piece, 2 * t + h] = top + jnp.log(total)
            o_s[piece, t] = jnp.concatenate(parts, axis=0).T.astype(LOW)

    def attend_back(piece, count):
        make_bias(piece, count)
        for t in range(tiles):
            inner = (do_s[t].astype(F32) * o_s[piece, t].astype(F32)).T
            queries = halves(q_s[piece, t])
            grads = halves(do_s[t])
            dq = [0.0, 0.0]
            inners = [jnp.sum(inner[h * HEAD:(h + 1) * HEAD], axis=0, keepdims=True) for h in range(2)]
            for j in range(count):
                at = piece - (count - 1 - j)
                dk_new, dv_new = 0.0, 0.0
                for h in range(2):
                    probs = jnp.exp(
                        mm_back(k_s[at, t], queries[h]) + bias_s[j] - lse_s[piece, 2 * t + h])
                    dprobs = mm_back(v_s[at, t], grads[h])
                    dscores = (probs * (dprobs - inners[h])).astype(LOW)
                    dv_new = dv_new + mm(probs.astype(LOW), grads[h])
                    dk_new = dk_new + mm(dscores, queries[h])
                    dq[h] = dq[h] + mm(kt_s[at, t, h * HEAD:(h + 1) * HEAD, :], dscores)
                spare[at, t] += dk_new
                spare[at, tiles + t] += dv_new
            dq_t = jnp.concatenate(dq, axis=0) * 0.125
            dqkv[piece, :, t * LANES:(t + 1) * LANES] = dq_t.T.astype(LOW)

    def by_count(piece, run):
        for count in range(1, WINDOW + 1):
            fits = piece >= WINDOW - 1 if count == WINDOW else piece == count - 1

            @pl.when(fits)
            def _(count=count):
                run(piece, count)

    def forward_attention(piece):
        @pl.when(second)
        def _():
            take_over(piece)

        rows = jnp.where(first, x_ref[piece], here[piece]).astype(F32)
        plain, factor = normalize(rows)
        plain1[piece] = plain.astype(LOW)
        fac1[piece] = factor
        normed = plain * gain1
        a_t[piece] = normed.T.astype(LOW)
        qkv = mm(normed.astype(LOW), wa[:, :qkv_cols])
        for t in range(tiles):
            q_s[piece, t] = (qkv[:, t * LANES:(t + 1) * LANES].astype(LOW) * 0.125).astype(LOW)
            key = qkv[:, (tiles + t) * LANES:(tiles + t + 1) * LANES].astype(LOW)
            value = qkv[:, (2 * tiles + t) * LANES:(2 * tiles + t + 1) * LANES].astype(LOW)
            mask = reused(t)
            if mask is not None:
                value = jnp.where(mask, here_v[piece, t - 1], value)
                there_v[piece, t - 1] = value
            k_s[piece, t] = key
            v_s[piece, t] = value
            kt_s[piece, t] = key.astype(F32).T.astype(LOW)
            vt_s[piece, t] = value.astype(F32).T.astype(LOW)
        by_count(piece, attend)
        mixed = jnp.concatenate([o_s[piece, t] for t in range(tiles)], axis=1)
        middle = rows + swap(jnp.where(first, lax.rem(piece, 2), 0), mm_back(mixed, wa[:, qkv_cols:]).astype(LOW))
        for t in range(2 * tiles):
            spare[piece, t] = middle[:, t * LANES:(t + 1) * LANES]

    def forward_hidden(piece):
        middle = jnp.concatenate([spare[piece, t] for t in range(2 * tiles)], axis=1)
        plain, factor = normalize(middle)
        plain2[piece] = plain.astype(LOW)
        fac2[piece] = factor
        normed = plain * gain2
        m_t[piece] = normed.T.astype(LOW)
        normed = normed.astype(LOW)
        total = 0.0
        for group in range(2):
            z = mm(normed, w_ref[group, :, hidden:2 * hidden])
            square = z * z
            bent = jnp.tanh(GELU_K * z * (1.0 + GELU_C * square))
            upper = 0.5 * (1.0 + bent)
            acted = (z * upper).astype(LOW)
            slope = upper + 0.5 * z * (1.0 - bent * bent) * (GELU_K * (1.0 + 3.0 * GELU_C * square))
            gd_s[piece, group] = slope.astype(LOW)
            e_s[piece, group] = acted
            total = total + mm_back(acted, w_ref[group, :, 2 * hidden:])
        result = middle + swap(jnp.where(first, lax.rem(piece, 2), 1), total.astype(LOW))
        there[piece] = result.astype(LOW)

        @pl.when(first)
        def _():
            for copy in hand_over(piece):
                copy.start()

        @pl.when(second)
        def _():
            for copy in emit(piece):
                copy.start()

    def forward(step, carry):
        early = step < PIECES

        @pl.when(jnp.logical_xor(early, second))
        def _():
            forward_attention(lax.rem(step, PIECES))

        if inside:
            @pl.when(step == 1)
            def _():
                gather_pass(1)

            @pl.when(step == PIECES - 1)
            def _():
                gather_pass(2)
                gather_end(1)
                gather_end(2)

        @pl.when(jnp.logical_not(early))
        def _():
            forward_hidden(step - PIECES)

        return carry

    lax.fori_loop(0, 2 * PIECES, forward, 0)

    @pl.when(first)
    def _():
        for piece in range(PIECES):
            for copy in hand_over(piece):
                copy.wait_send()

    @pl.when(second)
    def _():
        for piece in range(PIECES):
            for copy in emit(piece):
                copy.wait()

    gain_grad_ref[...] = jnp.zeros_like(gain_grad_ref)
    spare[...] = jnp.zeros_like(spare)

    def hidden_grads(index, carry):
        group, column = index // (hidden // block), index % (hidden // block)
        spot = pl.multiple_of(column * block, block)
        total = 0.0
        other = 0.0
        for piece in range(PIECES):
            total = total + mm(m_t[piece], gd_s[piece, group, :, pl.ds(spot, block)])
            other = other + mm(g_t[piece], e_s[piece, group, :, pl.ds(spot, block)])
        sums[group, :, pl.ds(pl.multiple_of(hidden + spot, block), block)] = total.astype(LOW)
        sums[group, :, pl.ds(pl.multiple_of(2 * hidden + spot, block), block)] = other.astype(LOW)
        return carry

    def head_grads():
        pairs = []
        for kind in range(4):
            total = 0.0
            for piece in range(PIECES):
                if kind < 3:
                    size = tiles * LANES
                    total = total + mm(a_t[piece], dqkv[piece, :, kind * size:(kind + 1) * size])
                else:
                    mixed = jnp.concatenate([o_s[piece, t] for t in range(tiles)], axis=1)
                    total = total + mm(h_t[piece], mixed)
            for group in range(2):
                part = total[:, group * LANES:(group + 1) * LANES].astype(LOW)
                sums[group, :, kind * LANES:(kind + 1) * LANES] = part
            pairs.append(total[:, 2 * LANES:])
        for pair in range(2):
            one, two = pairs[2 * pair:2 * pair + 2]
            spot = (4 + pair) * LANES
            sums[0, :, spot:spot + LANES] = jnp.where(low_half, one, flip(two)).astype(LOW)
            sums[1, :, spot:spot + LANES] = jnp.where(low_half, flip(one), two).astype(LOW)

    per_part = hidden // block
    early_blocks = [per_part + index for index in range(per_part)]
    head_blocks = [index for index in range(per_part)]
    late_blocks = [2 * per_part + index for index in range(per_part)]
    order = early_blocks + head_blocks + late_blocks

    def backward(step, carry):
        piece = PIECES - 1 - step

        @pl.when(first)
        def _():
            take_over(piece)

        grad_low = jnp.where(first, here[piece], x_ref[piece])
        grad = grad_low.astype(F32)
        g_t[piece] = grad.T.astype(LOW)
        total = 0.0
        for group in range(2):
            dz = mm(grad_low, w_ref[group, :, 2 * hidden:]) * gd_s[piece, group].astype(F32)
            dz = dz.astype(LOW)
            gd_s[piece, group] = dz
            total = total + mm_back(dz, w_ref[group, :, hidden:2 * hidden])
        dm = swap(0, total.astype(LOW))

        @pl.when(step == PIECES - 1)
        def _():
            lax.fori_loop(0, 2 * per_part, hidden_grads, 0)
            if inside:
                for index in early_blocks:
                    reduce_y(index).start()

        plain = plain2[piece].astype(F32)
        gain_grad_ref[1:2, :] += jnp.sum(dm * plain, axis=0, keepdims=True)
        middle = grad + norm_back(dm, plain, fac2[piece], gain2)
        h_t[piece] = middle.T.astype(LOW)
        dmixed = mm(middle.astype(LOW), wa[:, qkv_cols:]).astype(LOW)
        for t in range(tiles):
            do_s[t] = dmixed[:, t * LANES:(t + 1) * LANES]
        by_count(piece, attend_back)
        for t in range(tiles):
            dvalue = spare[piece, tiles + t]
            mask = reused(t)
            if mask is not None:
                there_v[piece, t - 1] = dvalue.astype(LOW)
                came = jnp.logical_and(first, jnp.logical_or(t == 1, lane >= HEAD))
                dvalue = jnp.where(came, dvalue + here_v[piece, t - 1].astype(F32), dvalue)
                dvalue = jnp.where(mask, 0.0, dvalue)
            spot = (tiles + t) * LANES
            dqkv[piece, :, spot:spot + LANES] = spare[piece, t].astype(LOW)
            spot = (2 * tiles + t) * LANES
            dqkv[piece, :, spot:spot + LANES] = dvalue.astype(LOW)
        da = swap(1, mm_back(dqkv[piece], wa[:, :qkv_cols]).astype(LOW))
        plain = plain1[piece].astype(F32)
        gain_grad_ref[0:1, :] += jnp.sum(da * plain, axis=0, keepdims=True)
        grad_in = middle + norm_back(da, plain, fac1[piece], gain1)
        there[piece] = grad_in.astype(LOW)

        @pl.when(second)
        def _():
            for copy in hand_over(piece):
                copy.start()

        @pl.when(first)
        def _():
            for copy in emit(piece):
                copy.start()

        return carry

    lax.fori_loop(0, PIECES, backward, 0)
    head_grads()

    if inside:
        gain_copy = send(gain_grad_ref, gain_y, sem_gg, (0,), other_y)
        gain_copy.start()
        reduce_mid(order[0])
        for index in head_blocks:
            reduce_y(index).start()
        gain_copy.wait()
        gain_y[...] = gain_y[...] + gain_grad_ref[...]
        gain_sends = [
            send(gain_y, gain_z.at[step - 1], sem_gg, (step,), peer(step)) for step in range(1, depth)]
        for copy in gain_sends:
            copy.start()
        for index in early_blocks[1:]:
            reduce_mid(index)
        for index in late_blocks:
            reduce_y(index).start()
        for index in head_blocks:
            reduce_mid(index)
        for index in early_blocks + head_blocks:
            reduce_end(index)
        total = gain_y[...]
        for step, copy in enumerate(gain_sends):
            copy.wait()
            total = total + gain_z[step]
        gain_grad_ref[...] = total

        def place(sec, row, unit):
            return (sec * 2 + row) * 2 + unit

        mine = place(section, lane_y, core)
        for half_tile, tile_index in enumerate((2, 5)):
            value_ref[mine, :, half_tile * LANES:(half_tile + 1) * LANES] = (
                grad_ref[:, tile_index * LANES:(tile_index + 1) * LANES].astype(LOW))
        value_x = send(value_ref.at[mine], value_ref.at[mine], sem_va, (0,), other_layer)
        value_x.start()
        reduce_mid(late_blocks[0])
        value_x.wait()
        value_y = []
        for sec in range(2):
            at = place(sec, lane_y, core)
            value_y.append(send(value_ref.at[at], value_ref.at[at], sem_va, (1 + sec,), other_y))
            value_y[-1].start()
        for index in late_blocks[1:]:
            reduce_mid(index)
        for copy in value_y:
            copy.wait()
        value_c = []
        for sec in range(2):
            for row in range(2):
                at = place(sec, row, core)
                value_c.append(
                    send(value_ref.at[at], value_ref.at[at], sem_va, (3 + 2 * sec + row,), other_core))
                value_c[-1].start()
        for index in late_blocks:
            reduce_end(index)
        for copy in value_c:
            copy.wait()
        for index in order:
            reduce_y(index).wait_send()
            for step in range(1, depth):
                reduce_z(index, step).wait_send()

    @pl.when(second)
    def _():
        for piece in range(PIECES):
            for copy in hand_over(piece):
                copy.wait_send()

    @pl.when(first)
    def _():
        for piece in range(PIECES):
            for copy in emit(piece):
                copy.wait()


def run_layers(x_rows, starts, gains, weights, depth, inside):
    width = x_rows.shape[2]
    tiles = width // 2 // LANES
    rows_own = width // depth
    columns = weights.shape[-1]
    blocks = columns // (2 * LANES)
    vmem = pl.BlockSpec(memory_space=pltpu.VMEM)
    anywhere = pl.BlockSpec(memory_space=pl.ANY)
    per_tile = (PIECES, tiles, PIECE, LANES)
    turned = (PIECES, tiles, LANES, PIECE)
    flat = (PIECES, PIECE, width)
    flat_turned = (PIECES, width, PIECE)
    wide = (PIECES, 2, PIECE, width)
    low = lambda shape: pltpu.VMEM(shape, LOW)
    full = lambda shape: pltpu.VMEM(shape, F32)
    dma = lambda *shape: pltpu.SemaphoreType.DMA(shape)
    out_shape = [
        jax.ShapeDtypeStruct((2,) + flat, LOW),
        jax.ShapeDtypeStruct((rows_own, columns), F32) if inside
        else jax.ShapeDtypeStruct(weights.shape, LOW),
        jax.ShapeDtypeStruct((8, width), F32),
    ]
    out_specs = [anywhere, vmem, vmem]
    scratch = [
        low((width, 4 * tiles * LANES)),
        low(per_tile), low(per_tile), low(per_tile), low(turned), low(turned), low(per_tile),
        full((PIECES, 2 * tiles, 1, PIECE)),
        low(flat), low(flat), full((PIECES, PIECE, 1)), full((PIECES, PIECE, 1)),
        low(flat_turned), low(flat_turned), low(flat_turned), low(flat_turned),
        low(wide), low(wide), low((tiles, PIECE, LANES)),
        low((PIECES, PIECE, 3 * tiles * LANES)), full((PIECES, 2 * tiles, PIECE, LANES)),
        full((WINDOW, PIECE, PIECE)),
        low(flat), low((PIECES, 2, PIECE, LANES)), low(flat), low((PIECES, 2, PIECE, LANES)),
        low((PIECE, width)), low((2, PIECE, width)),
        dma(2, PIECES), dma(2, PIECES), dma(2, PIECES), dma(2, 2), dma(2, PIECES), dma(3 + PIECES),
    ]
    if inside:
        out_shape.append(jax.ShapeDtypeStruct((8, rows_own, 2 * LANES), LOW))
        out_specs.append(vmem)
        scratch += [
            low((2, width, columns)), full((depth,) + gains.shape),
            low((2, width, columns)), low((width, columns)), low((depth - 1, rows_own, columns)),
            full((8, width)), full((depth - 1, 8, width)),
            dma(2, 3, depth), dma(2, 3, depth), dma(2, depth), dma(2, blocks),
            dma(2, blocks, depth), dma(2, depth), dma(2, 7),
        ]
    return pl.pallas_call(
        functools.partial(layers_kernel, width, depth, inside),
        out_shape=out_shape,
        in_specs=[vmem, vmem, vmem, anywhere if inside else vmem],
        out_specs=out_specs,
        scratch_shapes=scratch,
        compiler_params=pltpu.CompilerParams(
            collective_id=0, has_side_effects=True, vmem_limit_bytes=63 << 20),
        name="layers",
    )(x_rows, starts, gains, weights)


def pack(parts):
    w_qk, w_value, w_out, w_up, w_down = parts
    query, key, out_t = w_qk[:, 0], w_qk[:, 1], w_out.T
    edge = 2 * HEAD
    return jnp.concatenate(
        [query[:, :edge], key[:, :edge], w_value[:, :edge], out_t[:, :edge],
         query[:, edge:], key[:, edge:], w_value[:, edge:], out_t[:, edge:], w_up, w_down.T],
        axis=1)


def unpack(packed):
    edge = 2 * HEAD
    cut = lambda spot, size: packed[:, spot:spot + size]
    query = jnp.concatenate([cut(0, edge), cut(4 * edge, HEAD)], axis=1)
    key = jnp.concatenate([cut(edge, edge), cut(4 * edge + HEAD, HEAD)], axis=1)
    value = jnp.concatenate([cut(2 * edge, edge), cut(5 * edge, HEAD)], axis=1)
    out_t = jnp.concatenate([cut(3 * edge, edge), cut(5 * edge + HEAD, HEAD)], axis=1)
    hidden = packed.shape[1] // 3
    return (
        jnp.stack([query, key], axis=1), value, out_t.T,
        cut(hidden, hidden), cut(2 * hidden, hidden).T)


def shards(
    ends_in, seq_lengths, norm_gains, qk_weight, value_weight, out_weight, fc_weight, proj_weight
):
    section = lax.axis_index("section")
    lane_y = lax.axis_index("y")
    group = 2 * lane_y + lax.axis_index("core")
    first = section == 0
    cols = qk_weight.shape[3]
    width = ends_in.shape[2]
    fresh = (value_weight.shape[1] - width) // cols
    offset = jnp.where(first, group, width // cols + jnp.minimum(group, fresh - 1)) * cols
    w_value = lax.dynamic_slice_in_dim(value_weight, offset, cols, 1)
    packed = pack((qk_weight[0], w_value, out_weight[0], fc_weight[0], proj_weight[0]))
    depth = lax.axis_size("dp")
    inside = depth > 1 and depth <= 4 and width % (16 * depth) == 0
    if inside:
        weights = packed
        gains = norm_gains[0].astype(F32).T
        gains = jnp.pad(gains, ((0, 6), (0, -gains.shape[1] % LANES)))
    else:
        weights = lax.all_gather(packed, "dp", axis=0, tiled=True)
        weights = lax.all_gather(weights, "y", axis=0)
        gains = lax.all_gather(norm_gains[0], "dp", axis=0, tiled=True).astype(F32).T
        gains = jnp.pad(gains, ((0, 6), (0, 0)))
    x_rows = lax.dynamic_slice_in_dim(ends_in[0], lane_y * MB_TOK, MB_TOK, 0)
    x_rows = x_rows.reshape(PIECES, PIECE, width)
    ends = jnp.cumsum(lax.dynamic_index_in_dim(seq_lengths, lane_y, 0, keepdims=False))
    places = jnp.arange(MB_TOK, dtype=jnp.int32)
    starts = jnp.max(
        jnp.where(ends[None, :] <= places[:, None], ends[None, :], 0), axis=1)
    starts = starts.astype(jnp.int32).reshape(PIECES, 1, PIECE)
    kept = width // cols + fresh
    edge = 2 * HEAD
    results = run_layers(x_rows, starts, gains, weights, depth, inside)
    both = results[0].reshape(2 * MB_TOK, width)
    if inside:
        _, grads, gain_grads, values = results
        rows_own = width // depth
        gain_rows = lax.dynamic_slice_in_dim(
            gain_grads[:2], lax.axis_index("dp") * rows_own, rows_own, 1).T
        values = values[:, :, :cols]
    else:
        _, grads, gain_grads = results
        grads = lax.psum_scatter(grads, "y", scatter_dimension=0, tiled=False)
        grads = lax.psum_scatter(grads, "dp", scatter_dimension=0, tiled=True)
        gain_rows = lax.psum(gain_grads[:2], "y").T
        gain_rows = lax.psum_scatter(gain_rows, "dp", scatter_dimension=0, tiled=True)
        values = lax.all_gather(
            unpack(grads)[1].astype(LOW), ("section", "y", "core"), axis=0)
    d_qk, _, d_out, d_up, d_down = unpack(grads.astype(F32))
    d_value = jnp.concatenate([values[index] for index in range(kept)], axis=1).astype(F32)
    return (
        both[None], gain_rows[:, 0][None], gain_rows[:, 1][None], d_qk[None], d_value,
        d_out[None], d_up[None], d_down[None])


def solution(mesh):
    sections, depth, split = (mesh.shape[name] for name in ("section", "dp", "mp"))
    grid = Mesh(mesh.devices.reshape(sections, depth, split // 2, 2), ("section", "dp", "y", "core"))
    mp = ("y", "core")
    in_specs = (
        P("section", "dp", None),
        P("dp", None),
        P("section", "dp", None),
        P("section", "dp", None, mp),
        P("dp", None),
        P("section", mp, "dp"),
        P("section", "dp", mp),
        P("section", mp, "dp"),
    )
    out_specs = (
        P("section", "dp", None),
        P("section", "dp"),
        P("section", "dp"),
        P("section", "dp", None, mp),
        P("dp", None),
        P("section", mp, "dp"),
        P("section", "dp", mp),
        P("section", mp, "dp"),
    )
    return jax.shard_map(shards, mesh=grid, in_specs=in_specs, out_specs=out_specs, check_vma=False)
```

```python
import functools
import math

import jax
import jax.numpy as jnp
from jax import lax
from jax.experimental import pallas as pl
from jax.experimental.pallas import tpu as pltpu
from jax.sharding import Mesh, PartitionSpec as P

HEAD = 64
MB_TOK = 1024
PIECE = 256
PIECES = MB_TOK // PIECE
WINDOW = 3
PARTS = 6
LANES = 128
EPSILON = 1e-05
GELU_K = math.sqrt(2.0 / math.pi)
GELU_C = 0.044715
MESH = pl.DeviceIdType.MESH
F32 = jnp.float32
LOW = jnp.bfloat16


def mm(left, right):
    return lax.dot_general(left, right, (((1,), (0,)), ((), ())), preferred_element_type=F32)


def mm_back(left, right):
    return lax.dot_general(left, right, (((1,), (1,)), ((), ())), preferred_element_type=F32)


def normalize(rows):
    centred = rows - jnp.mean(rows, axis=1, keepdims=True)
    factor = lax.rsqrt(jnp.mean(centred * centred, axis=1, keepdims=True) + EPSILON)
    return centred * factor, factor


def norm_back(grad, plain, factor, gain):
    scaled = grad * gain
    return factor * (
        scaled
        - jnp.mean(scaled, axis=1, keepdims=True)
        - plain * jnp.mean(scaled * plain, axis=1, keepdims=True)
    )


def flip(tile):
    return pltpu.roll(tile, HEAD, 1)


def layers_kernel(width, depth, inside, *refs):
    refs = list(refs)
    take = lambda count: [refs.pop(0) for _ in range(count)]
    length_ref, x_all, gain_ref, part_ref = take(4)
    out_ref, grad_ref, gain_grad_ref = take(3)
    if inside:
        (value_ref,) = take(1)
    (wa, q_s, k_s, v_s, kt_s, vt_s, o_s, lse_s, plain1, plain2, fac1, fac2,
     a_t, m_t, g_t, h_t, e_s, gd_s, do_s, dqkv, spare, bias_s, x_ref, start_s,
     there, there_v, here, here_v, swap_out, swap_in,
     sem_x, sem_v, sem_f, sem_c, sem_o, sem_oc, sem_l) = take(37)
    if inside:
        (w_ref, gain_all, sums, y_in, z_in, gain_y, gain_z,
         sem_az, sem_ay, sem_gz, sem_ry, sem_rz, sem_gg, sem_va) = take(14)
    else:
        w_ref, sums = part_ref, grad_ref

    section = lax.axis_index("section")
    core = lax.axis_index("core")
    lane_y = lax.axis_index("y")
    deep = lax.axis_index("dp")
    other_layer = {"section": 1 - section}
    other_core = {"core": 1 - core}
    other_y = {"y": 1 - lane_y}
    first = section == 0
    second = jnp.logical_not(first)
    tiles = width // 2 // LANES
    hidden = width
    rows_own = width // depth
    half_cols = width // 2

    def send(src, dst, sems, index, target):
        return pltpu.make_async_remote_copy(
            src_ref=src, dst_ref=dst, send_sem=sems.at[(0,) + index], recv_sem=sems.at[(1,) + index],
            device_id=target, device_id_type=MESH)

    def peer(step):
        return {"dp": lax.rem(deep + step, depth)}

    barrier = pltpu.get_barrier_semaphore()
    friends = [other_layer, other_core, other_y]
    if inside:
        friends = friends + [peer(step) for step in range(1, depth)]
    for friend in friends:
        pl.semaphore_signal(barrier, inc=1, device_id=friend, device_id_type=MESH)
    pl.semaphore_wait(barrier, len(friends))

    lane = lax.broadcasted_iota(jnp.int32, (1, LANES), 1)
    low_half = lane < HEAD

    def rows_at(place):
        return pl.ds(pl.multiple_of(place * rows_own, rows_own), rows_own)

    unit = part_ref.shape[-1] // PARTS
    ways = (1, -1)
    mixed_part = PARTS - 1

    def cols_at(part):
        return pl.ds(part * unit, unit)

    def on_line(place):
        return jnp.logical_and(place >= 0, place < depth)

    def own_copy():
        return pltpu.make_async_copy(part_ref, w_ref.at[lane_y, rows_at(deep)], sem_l.at[PIECES])

    def gather_line(part, row, hop, way):
        place = deep - hop * ways[way]
        home = lane_y if row == 0 else 1 - lane_y
        spot = w_ref.at[home, rows_at(place), cols_at(part)]
        src = part_ref.at[:, cols_at(part)] if row == 0 and hop == 0 else spot
        return send(src, spot, sem_az, (part + row, hop, way), {"dp": deep + ways[way]})

    def line_start(part, row, hop, way):
        @pl.when(jnp.logical_and(on_line(deep - hop * ways[way]), on_line(deep + ways[way])))
        def _():
            gather_line(part, row, hop, way).start()

    def line_sent(part, row, hop, way):
        @pl.when(jnp.logical_and(on_line(deep - hop * ways[way]), on_line(deep + ways[way])))
        def _():
            gather_line(part, row, hop, way).wait_send()

    def gather_y(part, place, own):
        spot = w_ref.at[lane_y, rows_at(place), cols_at(part)]
        src = part_ref.at[:, cols_at(part)] if own else spot
        return send(src, spot, sem_ay, (part, place), other_y)

    def gather_gain(step):
        return send(gain_ref, gain_all.at[deep], sem_gz, (step,), peer(step))

    def gather_start(part):
        for way in range(2):
            line_start(part, 0, 0, way)
        if part != mixed_part:
            gather_y(part, deep, True).start()

    def gather_pass(part, row=0):
        for hop in range(depth - 1):
            for way in range(2):
                place = deep - (hop + 1) * ways[way]

                @pl.when(on_line(place))
                def _(hop=hop, way=way, place=place):
                    gather_line(part, row, hop, way).wait_recv()
                    if hop < depth - 2:
                        line_start(part, row, hop + 1, way)
                    if part != mixed_part:
                        gather_y(part, place, False).start()

    def gather_cross():
        gather_y(mixed_part, deep, True).wait()
        for way in range(2):
            line_start(mixed_part, 1, 0, way)

    def gather_end(part):
        if part != mixed_part:
            for place in range(depth):
                gather_y(part, place, False).wait()
        for row in range(2 if part == mixed_part else 1):
            for hop in range(depth - 1):
                for way in range(2):
                    line_sent(part, row, hop, way)

    block = 2 * LANES
    spans = [(spot, block) for spot in (
        [hidden + index * block for index in range(hidden // block)]
        + [index * block for index in range(hidden // block)]
        + [2 * hidden + index * block for index in range(hidden // block - 1)])]
    spans += [(3 * hidden - block, LANES), (3 * hidden - LANES, LANES)]

    def block_at(index):
        return pl.ds(spans[index][0], spans[index][1])

    def reduce_y(index):
        return send(sums.at[1 - lane_y, :, block_at(index)], y_in.at[:, block_at(index)],
                    sem_ry, (index,), other_y)

    def reduce_z(index, step):
        return send(sums.at[lane_y, rows_at(lax.rem(deep + step, depth)), block_at(index)],
                    z_in.at[step - 1, :, block_at(index)], sem_rz, (index, step), peer(step))

    ahead = 2

    def reduce_mid(index):
        reduce_y(index).wait_recv()
        if index + ahead < len(spans) and index + ahead >= early_blocks:
            reduce_y(index + ahead).start()
        at = block_at(index)
        sums[lane_y, :, at] = (
            sums[lane_y, :, at].astype(F32) + y_in[:, at].astype(F32)).astype(LOW)
        for step in range(1, depth):
            reduce_z(index, step).start()

    def reduce_end(index):
        at = block_at(index)
        total = sums[lane_y, rows_at(deep), at].astype(F32)
        for step in range(1, depth):
            reduce_z(index, step).wait_recv()
            total = total + z_in[step - 1, :, at].astype(F32)
        grad_ref[:, at] = total

    def halves(tile):
        return [jnp.where(low_half, tile, jnp.zeros_like(tile)),
                jnp.where(low_half, jnp.zeros_like(tile), tile)]

    def group_tile(group, index):
        return w_ref[group, :, index * LANES:(index + 1) * LANES]

    qkv_cols = 3 * tiles * LANES

    def arrange():
        for kind in range(4):
            for group in range(2):
                spot = (kind * tiles + group) * LANES
                wa[:, spot:spot + LANES] = group_tile(group, kind)
        for pair in range(2):
            one, two = (group_tile(group, 4 + pair).astype(F32) for group in range(2))
            spot = (2 * pair * tiles + 2) * LANES
            wa[:, spot:spot + LANES] = jnp.where(low_half, one, flip(two)).astype(LOW)
            spot = ((2 * pair + 1) * tiles + 2) * LANES
            wa[:, spot:spot + LANES] = jnp.where(low_half, flip(one), two).astype(LOW)

    x_copy = pltpu.make_async_copy(x_all.at[lane_y], x_ref, sem_l.at[PIECES + 1])
    if inside:
        gather_start(0)
        gather_start(1)
        gather_y(mixed_part, deep, True).start()
        gain_all[deep] = gain_ref[...]
        for step in range(1, depth):
            gather_gain(step).start()
        own_copy().start()
    x_copy.start()

    for piece in range(PIECES):
        place = piece * PIECE + lax.broadcasted_iota(jnp.int32, (1, PIECE), 1)
        begin = jnp.zeros((1, PIECE), jnp.int32)
        end = 0
        for index in range(length_ref.shape[1]):
            end = end + length_ref[lane_y, index]
            begin = jnp.where(place >= end, end, begin)
        start_s[piece] = begin

    if inside:
        gather_pass(0)
        gather_start(2)
        gather_pass(1)
        gather_start(3)
        gather_pass(2)
        gather_start(4)
        for step in range(1, depth):
            gather_gain(step).wait()
        gather_end(0)
        gather_end(1)
        own_copy().wait()
        gains = jnp.concatenate([gain_all[place, :, :rows_own] for place in range(depth)], axis=1)
    else:
        gains = gain_ref[...]
    arrange()
    x_copy.wait()
    gain1 = gains[0:1, :]
    gain2 = gains[1:2, :]

    def swap(slot, value):
        swap_out[...] = value
        copy = send(swap_out, swap_in.at[slot], sem_c, (slot,), other_core)
        copy.start()
        copy.wait()
        return swap_out[...].astype(F32) + swap_in[slot].astype(F32)

    half = pl.ds(pl.multiple_of(core * half_cols, half_cols), half_cols)

    def hand_rows(piece):
        return send(there.at[piece, :, half], here.at[piece, :, half], sem_x, (piece,), other_layer)

    def hand_values(piece):
        return send(there_v.at[piece], here_v.at[piece], sem_v, (piece,), other_layer)

    def hand_over(piece):
        return [hand_rows(piece), hand_values(piece)]

    def hand_on(piece):
        return send(here.at[piece, :, half], here.at[piece, :, half], sem_f, (piece,), other_core)

    def take_start(piece):
        hand_rows(piece).wait_recv()
        hand_on(piece).start()

    def take_values(piece):
        hand_values(piece).wait_recv()

    def emit_here(piece, stage):
        return pltpu.make_async_copy(stage.at[piece], out_ref.at[lane_y, piece], sem_l.at[piece])

    def emit_there(piece, stage):
        return send(stage.at[piece, :, half], out_ref.at[lane_y, piece, :, half],
                    sem_o, (piece,), other_y)

    def emit(piece, stage):
        return [emit_here(piece, stage), emit_there(piece, stage)]

    def emit_on(piece):
        spot = out_ref.at[1 - lane_y, piece, :, half]
        return send(spot, spot, sem_oc, (piece,), other_core)

    def reused(tile_index):
        if tile_index == 0:
            return None
        if tile_index == 1:
            return jnp.logical_and(second, lane >= 0)
        return jnp.logical_and(second, lane >= HEAD)

    def make_bias(piece, count):
        base = piece * PIECE
        query = base + lax.broadcasted_iota(jnp.int32, (1, PIECE), 1)
        begin = start_s[piece]
        for j in range(count):
            key = base - (count - 1 - j) * PIECE + lax.broadcasted_iota(jnp.int32, (PIECE, 1), 0)
            fine = jnp.logical_and(key >= begin, key <= query)
            bias_s[j] = jnp.where(fine, 0.0, -1e30).astype(F32)

    def attend(piece, count):
        make_bias(piece, count)
        for t in range(tiles):
            parts = []
            for h, query in enumerate(halves(q_s[piece, t])):
                scores = [
                    mm_back(k_s[piece - (count - 1 - j), t], query) + bias_s[j] for j in range(count)
                ]
                top = functools.reduce(
                    jnp.maximum, [jnp.max(s, axis=0, keepdims=True) for s in scores])
                expo = [jnp.exp(s - top) for s in scores]
                total = functools.reduce(
                    jnp.add, [jnp.sum(e, axis=0, keepdims=True) for e in expo])
                mixed = functools.reduce(jnp.add, [
                    mm(vt_s[piece - (count - 1 - j), t, h * HEAD:(h + 1) * HEAD, :], e.astype(LOW))
                    for j, e in enumerate(expo)
                ])
                parts.append(mixed * (1.0 / total))
                lse_s[piece, 2 * t + h] = top + jnp.log(total)
            o_s[piece, t] = jnp.concatenate(parts, axis=0).T.astype(LOW)

    def attend_back(piece, count):
        make_bias(piece, count)
        for t in range(tiles):
            inner = (do_s[t].astype(F32) * o_s[piece, t].astype(F32)).T
            queries = halves(q_s[piece, t])
            grads = halves(do_s[t])
            dq = [0.0, 0.0]
            inners = [jnp.sum(inner[h * HEAD:(h + 1) * HEAD], axis=0, keepdims=True) for h in range(2)]
            for j in range(count):
                at = piece - (count - 1 - j)
                dk_new, dv_new = 0.0, 0.0
                for h in range(2):
                    probs = jnp.exp(
                        mm_back(k_s[at, t], queries[h]) + bias_s[j] - lse_s[piece, 2 * t + h])
                    dprobs = mm_back(v_s[at, t], grads[h])
                    dscores = (probs * (dprobs - inners[h])).astype(LOW)
                    dv_new = dv_new + mm(probs.astype(LOW), grads[h])
                    dk_new = dk_new + mm(dscores, queries[h])
                    dq[h] = dq[h] + mm(kt_s[at, t, h * HEAD:(h + 1) * HEAD, :], dscores)
                spare[at, t] += dk_new
                spare[at, tiles + t] += dv_new
            dq_t = jnp.concatenate(dq, axis=0) * 0.125
            dqkv[piece, :, t * LANES:(t + 1) * LANES] = dq_t.T.astype(LOW)

    def by_count(piece, run):
        for count in range(1, WINDOW + 1):
            fits = piece >= WINDOW - 1 if count == WINDOW else piece == count - 1

            @pl.when(fits)
            def _(count=count):
                run(piece, count)

    def forward_attention(piece):
        @pl.when(second)
        def _():
            @pl.when(piece == 0)
            def _():
                take_start(piece)

            hand_on(piece).wait()

        rows = jnp.where(first, x_ref[piece], here[piece]).astype(F32)
        plain, factor = normalize(rows)
        plain1[piece] = plain.astype(LOW)
        fac1[piece] = factor
        normed = plain * gain1
        a_t[piece] = normed.T.astype(LOW)
        qkv = mm(normed.astype(LOW), wa[:, :qkv_cols])

        @pl.when(second)
        def _():
            take_values(piece)

        for t in range(tiles):
            q_s[piece, t] = (qkv[:, t * LANES:(t + 1) * LANES].astype(LOW) * 0.125).astype(LOW)
            key = qkv[:, (tiles + t) * LANES:(tiles + t + 1) * LANES].astype(LOW)
            value = qkv[:, (2 * tiles + t) * LANES:(2 * tiles + t + 1) * LANES].astype(LOW)
            mask = reused(t)
            if mask is not None:
                value = jnp.where(mask, here_v[piece, t - 1], value)
                there_v[piece, t - 1] = value
            k_s[piece, t] = key
            v_s[piece, t] = value
            kt_s[piece, t] = key.astype(F32).T.astype(LOW)
            vt_s[piece, t] = value.astype(F32).T.astype(LOW)
        by_count(piece, attend)
        mixed = jnp.concatenate([o_s[piece, t] for t in range(tiles)], axis=1)
        middle = rows + swap(jnp.where(first, lax.rem(piece, 2), 0), mm_back(mixed, wa[:, qkv_cols:]).astype(LOW))
        for t in range(2 * tiles):
            spare[piece, t] = middle[:, t * LANES:(t + 1) * LANES]

    def forward_hidden(piece):
        middle = jnp.concatenate([spare[piece, t] for t in range(2 * tiles)], axis=1)
        plain, factor = normalize(middle)
        plain2[piece] = plain.astype(LOW)
        fac2[piece] = factor
        normed = plain * gain2
        m_t[piece] = normed.T.astype(LOW)
        normed = normed.astype(LOW)
        total = 0.0
        for group in range(2):
            z = mm(normed, w_ref[group, :, hidden:2 * hidden])
            square = z * z
            bent = jnp.tanh(GELU_K * z * (1.0 + GELU_C * square))
            upper = 0.5 * (1.0 + bent)
            acted = (z * upper).astype(LOW)
            slope = upper + 0.5 * z * (1.0 - bent * bent) * (GELU_K * (1.0 + 3.0 * GELU_C * square))
            gd_s[piece, group] = slope.astype(LOW)
            e_s[piece, group] = acted
            total = total + mm_back(acted, w_ref[group, :, 2 * hidden:])

        @pl.when(jnp.logical_and(second, piece < PIECES - 1))
        def _():
            take_start(piece + 1)

        result = middle + swap(jnp.where(first, lax.rem(piece, 2), 1), total.astype(LOW))
        result = result.astype(LOW)

        @pl.when(first)
        def _():
            there[piece] = result
            for copy in hand_over(piece):
                copy.start()

        @pl.when(second)
        def _():
            here[piece] = result
            for copy in emit(piece, here):
                copy.start()

    def forward(step, carry):
        early = step < PIECES

        @pl.when(jnp.logical_xor(early, second))
        def _():
            forward_attention(lax.rem(step, PIECES))

        if inside:
            @pl.when(step == 0)
            def _():
                gather_pass(3)
                gather_start(5)
                gather_cross()

            @pl.when(step == 1)
            def _():
                gather_pass(4)

            @pl.when(step == 2)
            def _():
                gather_pass(5)
                gather_pass(5, 1)

            @pl.when(step == PIECES - 1)
            def _():
                for part in range(2, PARTS):
                    gather_end(part)

        @pl.when(jnp.logical_not(early))
        def _():
            forward_hidden(step - PIECES)

        return carry

    lax.fori_loop(0, 2 * PIECES, forward, 0)

    @pl.when(first)
    def _():
        for piece in range(PIECES):
            for copy in hand_over(piece):
                copy.wait_send()

    gain_grad_ref[...] = jnp.zeros_like(gain_grad_ref)
    spare[...] = jnp.zeros_like(spare)

    def hidden_grads(index, carry):
        group, column = index // (hidden // block), index % (hidden // block)
        spot = pl.multiple_of(column * block, block)
        total = 0.0
        other = 0.0
        for piece in range(PIECES):
            total = total + mm(m_t[piece], gd_s[piece, group, :, pl.ds(spot, block)])
            other = other + mm(g_t[piece], e_s[piece, group, :, pl.ds(spot, block)])
        sums[group, :, pl.ds(pl.multiple_of(hidden + spot, block), block)] = total.astype(LOW)
        sums[group, :, pl.ds(pl.multiple_of(2 * hidden + spot, block), block)] = other.astype(LOW)
        return carry

    def head_grads():
        pairs = []
        for kind in range(4):
            total = 0.0
            for piece in range(PIECES):
                if kind < 3:
                    size = tiles * LANES
                    total = total + mm(a_t[piece], dqkv[piece, :, kind * size:(kind + 1) * size])
                else:
                    mixed = jnp.concatenate([o_s[piece, t] for t in range(tiles)], axis=1)
                    total = total + mm(h_t[piece], mixed)
            for group in range(2):
                part = total[:, group * LANES:(group + 1) * LANES].astype(LOW)
                sums[group, :, kind * LANES:(kind + 1) * LANES] = part
            pairs.append(total[:, 2 * LANES:])
        for pair in range(2):
            one, two = pairs[2 * pair:2 * pair + 2]
            spot = (4 + pair) * LANES
            sums[0, :, spot:spot + LANES] = jnp.where(low_half, one, flip(two)).astype(LOW)
            sums[1, :, spot:spot + LANES] = jnp.where(low_half, flip(one), two).astype(LOW)

    per_part = hidden // block
    early_blocks = per_part

    def backward(step, carry):
        piece = PIECES - 1 - step

        @pl.when(first)
        def _():
            take_start(piece)
            hand_on(piece).wait()

        grad_low = jnp.where(first, here[piece], x_ref[piece])
        grad = grad_low.astype(F32)
        g_t[piece] = grad.T.astype(LOW)
        total = 0.0
        for group in range(2):
            dz = mm(grad_low, w_ref[group, :, 2 * hidden:]) * gd_s[piece, group].astype(F32)
            dz = dz.astype(LOW)
            gd_s[piece, group] = dz
            total = total + mm_back(dz, w_ref[group, :, hidden:2 * hidden])
        dm = swap(0, total.astype(LOW))

        @pl.when(step == PIECES - 1)
        def _():
            lax.fori_loop(0, 2 * per_part, hidden_grads, 0)
            if inside:
                for index in range(early_blocks):
                    reduce_y(index).start()

        plain = plain2[piece].astype(F32)
        gain_grad_ref[1:2, :] += jnp.sum(dm * plain, axis=0, keepdims=True)
        middle = grad + norm_back(dm, plain, fac2[piece], gain2)
        h_t[piece] = middle.T.astype(LOW)
        dmixed = mm(middle.astype(LOW), wa[:, qkv_cols:]).astype(LOW)
        for t in range(tiles):
            do_s[t] = dmixed[:, t * LANES:(t + 1) * LANES]
        by_count(piece, attend_back)

        @pl.when(first)
        def _():
            take_values(piece)

        for t in range(tiles):
            dvalue = spare[piece, tiles + t]
            mask = reused(t)
            if mask is not None:
                there_v[piece, t - 1] = dvalue.astype(LOW)
                came = jnp.logical_and(first, jnp.logical_or(t == 1, lane >= HEAD))
                dvalue = jnp.where(came, dvalue + here_v[piece, t - 1].astype(F32), dvalue)
                dvalue = jnp.where(mask, 0.0, dvalue)
            spot = (tiles + t) * LANES
            dqkv[piece, :, spot:spot + LANES] = spare[piece, t].astype(LOW)
            spot = (2 * tiles + t) * LANES
            dqkv[piece, :, spot:spot + LANES] = dvalue.astype(LOW)
        da = swap(1, mm_back(dqkv[piece], wa[:, :qkv_cols]).astype(LOW))
        plain = plain1[piece].astype(F32)
        gain_grad_ref[0:1, :] += jnp.sum(da * plain, axis=0, keepdims=True)
        grad_in = middle + norm_back(da, plain, fac1[piece], gain1)
        there[piece] = grad_in.astype(LOW)

        @pl.when(second)
        def _():
            for copy in hand_over(piece):
                copy.start()

        @pl.when(first)
        def _():
            for copy in emit(piece, there):
                copy.start()

        return carry

    lax.fori_loop(0, PIECES, backward, 0)
    head_grads()

    def emit_stage(run):
        @pl.when(first)
        def _():
            run(there)

        @pl.when(second)
        def _():
            run(here)

    def pass_outputs(stage):
        for piece in range(PIECES):
            emit_there(piece, stage).wait_recv()
            emit_on(piece).start()

    def finish_outputs(stage):
        for piece in range(PIECES):
            emit_here(piece, stage).wait()
            emit_there(piece, stage).wait_send()
            emit_on(piece).wait()

    if inside:
        gain_copy = send(gain_grad_ref, gain_y, sem_gg, (0,), other_y)
        gain_copy.start()
        reduce_mid(0)
        gain_copy.wait()
        gain_y[...] = gain_y[...] + gain_grad_ref[...]
        gain_sends = [
            send(gain_y, gain_z.at[step - 1], sem_gg, (step,), peer(step)) for step in range(1, depth)]
        for copy in gain_sends:
            copy.start()
        reduce_mid(1)
        reduce_mid(2)
        reduce_end(0)
        emit_stage(pass_outputs)
        for index in range(3, 6):
            reduce_mid(index)
            reduce_end(index - 2)
        total = gain_y[...]
        for step, copy in enumerate(gain_sends):
            copy.wait()
            total = total + gain_z[step]
        gain_grad_ref[...] = total
        reduce_end(4)
        reduce_mid(6)
        reduce_end(5)

        def place(sec, row, unit):
            return (sec * 2 + row) * 2 + unit

        mine = place(section, lane_y, core)
        for half_tile, tile_index in enumerate((2, 5)):
            value_ref[mine, :, half_tile * LANES:(half_tile + 1) * LANES] = (
                grad_ref[:, tile_index * LANES:(tile_index + 1) * LANES].astype(LOW))
        value_x = send(value_ref.at[mine], value_ref.at[mine], sem_va, (0,), other_layer)
        value_x.start()
        reduce_mid(7)
        value_x.wait()
        value_y = []
        for sec in range(2):
            at = place(sec, lane_y, core)
            value_y.append(send(value_ref.at[at], value_ref.at[at], sem_va, (1 + sec,), other_y))
            value_y[-1].start()
        reduce_end(6)
        reduce_mid(8)
        for copy in value_y:
            copy.wait()
        value_c = []
        for sec in range(2):
            for row in range(2):
                at = place(sec, row, core)
                value_c.append(
                    send(value_ref.at[at], value_ref.at[at], sem_va, (3 + 2 * sec + row,), other_core))
                value_c[-1].start()
        reduce_end(7)
        reduce_mid(9)
        reduce_end(8)
        reduce_end(9)
        for copy in value_c:
            copy.wait()
        for index in range(len(spans)):
            reduce_y(index).wait_send()
            for step in range(1, depth):
                reduce_z(index, step).wait_send()
    else:
        emit_stage(pass_outputs)

    emit_stage(finish_outputs)

    @pl.when(second)
    def _():
        for piece in range(PIECES):
            for copy in hand_over(piece):
                copy.wait_send()


def run_layers(lengths, x_rows, gains, weights, depth, inside):
    width = x_rows.shape[3]
    tiles = width // 2 // LANES
    rows_own = width // depth
    columns = weights.shape[-1]
    blocks = columns // (2 * LANES) + 1
    vmem = pl.BlockSpec(memory_space=pltpu.VMEM)
    anywhere = pl.BlockSpec(memory_space=pl.ANY)
    smem = pl.BlockSpec(memory_space=pltpu.SMEM)
    per_tile = (PIECES, tiles, PIECE, LANES)
    turned = (PIECES, tiles, LANES, PIECE)
    flat = (PIECES, PIECE, width)
    flat_turned = (PIECES, width, PIECE)
    wide = (PIECES, 2, PIECE, width)
    low = lambda shape: pltpu.VMEM(shape, LOW)
    full = lambda shape: pltpu.VMEM(shape, F32)
    dma = lambda *shape: pltpu.SemaphoreType.DMA(shape)
    out_shape = [
        jax.ShapeDtypeStruct((2,) + flat, LOW),
        jax.ShapeDtypeStruct((rows_own, columns), F32) if inside
        else jax.ShapeDtypeStruct(weights.shape, LOW),
        jax.ShapeDtypeStruct((8, width), F32),
    ]
    out_specs = [anywhere, vmem, vmem]
    scratch = [
        low((width, 4 * tiles * LANES)),
        low(per_tile), low(per_tile), low(per_tile), low(turned), low(turned), low(per_tile),
        full((PIECES, 2 * tiles, 1, PIECE)),
        low(flat), low(flat), full((PIECES, PIECE, 1)), full((PIECES, PIECE, 1)),
        low(flat_turned), low(flat_turned), low(flat_turned), low(flat_turned),
        low(wide), low(wide), low((tiles, PIECE, LANES)),
        low((PIECES, PIECE, 3 * tiles * LANES)), full((PIECES, 2 * tiles, PIECE, LANES)),
        full((WINDOW, PIECE, PIECE)), low(flat), pltpu.VMEM((PIECES, 1, PIECE), jnp.int32),
        low(flat), low((PIECES, 2, PIECE, LANES)), low(flat), low((PIECES, 2, PIECE, LANES)),
        low((PIECE, width)), low((2, PIECE, width)),
        dma(2, PIECES), dma(2, PIECES), dma(2, PIECES), dma(2, 2), dma(2, PIECES), dma(2, PIECES),
        dma(2 + PIECES),
    ]
    if inside:
        out_shape.append(jax.ShapeDtypeStruct((8, rows_own, 2 * LANES), LOW))
        out_specs.append(vmem)
        scratch += [
            low((2, width, columns)), full((depth,) + gains.shape),
            low((2, width, columns)), low((width, columns)), low((depth - 1, rows_own, columns)),
            full((8, width)), full((depth - 1, 8, width)),
            dma(2, PARTS + 1, depth - 1, 2), dma(2, PARTS, depth), dma(2, depth), dma(2, blocks),
            dma(2, blocks, depth), dma(2, depth), dma(2, 7),
        ]
    return pl.pallas_call(
        functools.partial(layers_kernel, width, depth, inside),
        out_shape=out_shape,
        in_specs=[smem, anywhere, vmem, anywhere if inside else vmem],
        out_specs=out_specs,
        scratch_shapes=scratch,
        compiler_params=pltpu.CompilerParams(
            collective_id=0, has_side_effects=True, vmem_limit_bytes=63 << 20),
        name="layers",
    )(lengths, x_rows, gains, weights)


def pack(parts):
    w_qk, w_value, w_out, w_up, w_down = parts
    query, key, out_t = w_qk[:, 0], w_qk[:, 1], w_out.T
    edge = 2 * HEAD
    return jnp.concatenate(
        [query[:, :edge], key[:, :edge], w_value[:, :edge], out_t[:, :edge],
         query[:, edge:], key[:, edge:], w_value[:, edge:], out_t[:, edge:], w_up, w_down.T],
        axis=1)


def unpack(packed):
    edge = 2 * HEAD
    cut = lambda spot, size: packed[:, spot:spot + size]
    query = jnp.concatenate([cut(0, edge), cut(4 * edge, HEAD)], axis=1)
    key = jnp.concatenate([cut(edge, edge), cut(4 * edge + HEAD, HEAD)], axis=1)
    value = jnp.concatenate([cut(2 * edge, edge), cut(5 * edge, HEAD)], axis=1)
    out_t = jnp.concatenate([cut(3 * edge, edge), cut(5 * edge + HEAD, HEAD)], axis=1)
    hidden = packed.shape[1] // 3
    return (
        jnp.stack([query, key], axis=1), value, out_t.T,
        cut(hidden, hidden), cut(2 * hidden, hidden).T)


def shards(
    ends_in, seq_lengths, norm_gains, qk_weight, value_weight, out_weight, fc_weight, proj_weight
):
    section = lax.axis_index("section")
    lane_y = lax.axis_index("y")
    group = 2 * lane_y + lax.axis_index("core")
    first = section == 0
    cols = qk_weight.shape[3]
    width = ends_in.shape[2]
    fresh = (value_weight.shape[1] - width) // cols
    offset = jnp.where(first, group, width // cols + jnp.minimum(group, fresh - 1)) * cols
    w_value = lax.dynamic_slice_in_dim(value_weight, offset, cols, 1)
    packed = pack((qk_weight[0], w_value, out_weight[0], fc_weight[0], proj_weight[0]))
    depth = lax.axis_size("dp")
    inside = depth > 1 and depth <= 4 and width % (16 * depth) == 0
    if inside:
        weights = packed
        gains = norm_gains[0].astype(F32).T
        gains = jnp.pad(gains, ((0, 6), (0, -gains.shape[1] % LANES)))
    else:
        weights = lax.all_gather(packed, "dp", axis=0, tiled=True)
        weights = lax.all_gather(weights, "y", axis=0)
        gains = lax.all_gather(norm_gains[0], "dp", axis=0, tiled=True).astype(F32).T
        gains = jnp.pad(gains, ((0, 6), (0, 0)))
    x_rows = ends_in[0].reshape(2, PIECES, PIECE, width)
    kept = width // cols + fresh
    edge = 2 * HEAD
    results = run_layers(seq_lengths, x_rows, gains, weights, depth, inside)
    both = results[0].reshape(2 * MB_TOK, width)
    if inside:
        _, grads, gain_grads, values = results
        rows_own = width // depth
        gain_rows = lax.dynamic_slice_in_dim(
            gain_grads[:2], lax.axis_index("dp") * rows_own, rows_own, 1).T
        values = values[:, :, :cols]
    else:
        _, grads, gain_grads = results
        grads = lax.psum_scatter(grads, "y", scatter_dimension=0, tiled=False)
        grads = lax.psum_scatter(grads, "dp", scatter_dimension=0, tiled=True)
        gain_rows = lax.psum(gain_grads[:2], "y").T
        gain_rows = lax.psum_scatter(gain_rows, "dp", scatter_dimension=0, tiled=True)
        values = lax.all_gather(
            unpack(grads)[1].astype(LOW), ("section", "y", "core"), axis=0)
    d_qk, _, d_out, d_up, d_down = unpack(grads.astype(F32))
    d_value = jnp.concatenate([values[index] for index in range(kept)], axis=1).astype(F32)
    return (
        both[None], gain_rows[:, 0][None], gain_rows[:, 1][None], d_qk[None], d_value,
        d_out[None], d_up[None], d_down[None])


def solution(mesh):
    sections, depth, split = (mesh.shape[name] for name in ("section", "dp", "mp"))
    grid = Mesh(mesh.devices.reshape(sections, depth, split // 2, 2), ("section", "dp", "y", "core"))
    mp = ("y", "core")
    in_specs = (
        P("section", "dp", None),
        P("dp", None),
        P("section", "dp", None),
        P("section", "dp", None, mp),
        P("dp", None),
        P("section", mp, "dp"),
        P("section", "dp", mp),
        P("section", mp, "dp"),
    )
    out_specs = (
        P("section", "dp", None),
        P("section", "dp"),
        P("section", "dp"),
        P("section", "dp", None, mp),
        P("dp", None),
        P("section", mp, "dp"),
        P("section", "dp", mp),
        P("section", mp, "dp"),
    )
    return jax.shard_map(shards, mesh=grid, in_specs=in_specs, out_specs=out_specs, check_vma=False)
```

```python
import functools
import math

import jax
import jax.numpy as jnp
from jax import lax
from jax.experimental import pallas as pl
from jax.experimental.pallas import tpu as pltpu
from jax.sharding import Mesh, PartitionSpec as P

HEAD = 64
MB_TOK = 1024
PIECE = 256
PIECES = MB_TOK // PIECE
WINDOW = 3
PARTS = 6
LANES = 128
EPSILON = 1e-05
GELU_K = math.sqrt(2.0 / math.pi)
GELU_C = 0.044715
MESH = pl.DeviceIdType.MESH
F32 = jnp.float32
LOW = jnp.bfloat16


def mm(left, right):
    return lax.dot_general(left, right, (((1,), (0,)), ((), ())), preferred_element_type=F32)


def mm_back(left, right):
    return lax.dot_general(left, right, (((1,), (1,)), ((), ())), preferred_element_type=F32)


def normalize(rows):
    centred = rows - jnp.mean(rows, axis=1, keepdims=True)
    factor = lax.rsqrt(jnp.mean(centred * centred, axis=1, keepdims=True) + EPSILON)
    return centred * factor, factor


def norm_back(grad, plain, factor, gain):
    scaled = grad * gain
    return factor * (
        scaled
        - jnp.mean(scaled, axis=1, keepdims=True)
        - plain * jnp.mean(scaled * plain, axis=1, keepdims=True)
    )


def flip(tile):
    return pltpu.roll(tile, HEAD, 1)


def layers_kernel(width, depth, inside, *refs):
    refs = list(refs)
    take = lambda count: [refs.pop(0) for _ in range(count)]
    length_ref, x_all, gain_ref = take(3)
    part_refs = take(3 if inside else 1)
    out_ref, grad_ref, gain_grad_ref = take(3)
    if inside:
        (value_ref,) = take(1)
    (wa, q_s, k_s, v_s, turn_s, o_s, lse_s, plain1, plain2, fac1, fac2,
     a_t, m_t, g_t, h_t, e_s, gd_s, do_s, spare, bias_s, x_ref, start_s,
     there, there_v, here, here_v, swap_out, swap_in,
     sem_x, sem_v, sem_f, sem_c, sem_o, sem_oc, sem_l) = take(35)
    if inside:
        (w_ref, gain_all, sums, y_in, z_in, gain_y, gain_z,
         sem_az, sem_ay, sem_gz, sem_ry, sem_rz, sem_rm, sem_gg, sem_va) = take(15)
    else:
        w_ref, sums = part_refs[0], grad_ref

    section = lax.axis_index("section")
    core = lax.axis_index("core")
    lane_y = lax.axis_index("y")
    deep = lax.axis_index("dp")
    other_layer = {"section": 1 - section}
    other_core = {"core": 1 - core}
    other_y = {"y": 1 - lane_y}
    first = section == 0
    second = jnp.logical_not(first)
    tiles = width // 2 // LANES
    hidden = width
    rows_own = width // depth
    half_cols = width // 2

    def send(src, dst, sems, index, target):
        return pltpu.make_async_remote_copy(
            src_ref=src, dst_ref=dst, send_sem=sems.at[(0,) + index], recv_sem=sems.at[(1,) + index],
            device_id=target, device_id_type=MESH)

    def peer(step):
        return {"dp": lax.rem(deep + step, depth)}

    barrier = pltpu.get_barrier_semaphore()
    friends = [other_layer, other_core, other_y]
    if inside:
        friends = friends + [peer(step) for step in range(1, depth)]
        twin = {"dp": deep + 1 - 2 * lax.rem(deep, 2)}
    for friend in friends:
        pl.semaphore_signal(barrier, inc=1, device_id=friend, device_id_type=MESH)
    pl.semaphore_wait(barrier, len(friends))

    lane = lax.broadcasted_iota(jnp.int32, (1, LANES), 1)
    low_half = lane < HEAD

    def rows_at(place):
        return pl.ds(pl.multiple_of(place * rows_own, rows_own), rows_own)

    unit = 3 * hidden // PARTS
    per_ref = PARTS // 3
    ways = (1, -1)
    mixed_part = PARTS - 1

    def cols_at(part):
        return pl.ds(part * unit, unit)

    def on_line(place):
        return jnp.logical_and(place >= 0, place < depth)

    def own_part(part):
        return part_refs[part // per_ref].at[:, pl.ds(part % per_ref * unit, unit)]

    def own_copy(index):
        return pltpu.make_async_copy(
            part_refs[index], w_ref.at[lane_y, rows_at(deep), pl.ds(index * hidden, hidden)],
            sem_l.at[PIECES + index])

    def gather_line(part, row, hop, way):
        place = deep - hop * ways[way]
        home = lane_y if row == 0 else 1 - lane_y
        spot = w_ref.at[home, rows_at(place), cols_at(part)]
        src = own_part(part) if row == 0 and hop == 0 else spot
        return send(src, spot, sem_az, (part + row, hop, way), {"dp": deep + ways[way]})

    def line_start(part, row, hop, way):
        @pl.when(jnp.logical_and(on_line(deep - hop * ways[way]), on_line(deep + ways[way])))
        def _():
            gather_line(part, row, hop, way).start()

    def line_sent(part, row, hop, way):
        @pl.when(jnp.logical_and(on_line(deep - hop * ways[way]), on_line(deep + ways[way])))
        def _():
            gather_line(part, row, hop, way).wait_send()

    def gather_y(part, place, own):
        spot = w_ref.at[lane_y, rows_at(place), cols_at(part)]
        src = own_part(part) if own else spot
        return send(src, spot, sem_ay, (part, place), other_y)

    def gather_gain(step):
        return send(gain_all.at[deep], gain_all.at[deep], sem_gz, (step,), peer(step))

    def gather_start(part):
        for way in range(2):
            line_start(part, 0, 0, way)
        if part != mixed_part:
            gather_y(part, deep, True).start()

    def gather_pass(part, row=0):
        for hop in range(depth - 1):
            for way in range(2):
                place = deep - (hop + 1) * ways[way]

                @pl.when(on_line(place))
                def _(hop=hop, way=way, place=place):
                    gather_line(part, row, hop, way).wait_recv()
                    if hop < depth - 2:
                        line_start(part, row, hop + 1, way)
                    if part != mixed_part:
                        gather_y(part, place, False).start()

    def gather_cross():
        gather_y(mixed_part, deep, True).wait()
        for way in range(2):
            line_start(mixed_part, 1, 0, way)

    def gather_end(part):
        if part != mixed_part:
            for place in range(depth):
                gather_y(part, place, False).wait()
        for row in range(2 if part == mixed_part else 1):
            for hop in range(depth - 1):
                for way in range(2):
                    line_sent(part, row, hop, way)

    block = 2 * LANES
    last = block // 2
    spans = [
        (2 * hidden, block), (2 * hidden + block, last), (hidden, block), (hidden + block, block),
        (block, block), (2 * block, block), (0, block),
        (hidden + 2 * block, last), (hidden + 2 * block + last, last)]
    mixed_at = pl.ds(2 * hidden + block + last, block + last)

    def block_at(index):
        return pl.ds(spans[index][0], spans[index][1])

    def reduce_y(index):
        return send(sums.at[1 - lane_y, :, block_at(index)], y_in.at[:, block_at(index)],
                    sem_ry, (index,), other_y)

    def share_of(near, index):
        own = lax.rem(deep, 2)
        return rows_at((own if near else 1 - own) + 2 * index)

    def reduce_near(index, share):
        at = block_at(index)
        return send(sums.at[lane_y, share_of(False, share), at], z_in.at[share, :, at],
                    sem_rz, (index, share), twin)

    def reduce_far(index):
        at = block_at(index)
        return send(sums.at[lane_y, rows_at(lax.rem(deep + 2, depth)), at], z_in.at[2, :, at],
                    sem_rz, (index, 2), peer(2))

    def reduce_mid(index, following=None):
        reduce_y(index).wait_recv()
        if following is not None:
            reduce_y(following).start()
        at = block_at(index)
        sums[lane_y, :, at] = (
            sums[lane_y, :, at].astype(F32) + y_in[:, at].astype(F32)).astype(LOW)
        for share in range(2):
            reduce_near(index, share).start()

    def reduce_late(index):
        at = block_at(index)
        for share in range(2):
            reduce_near(index, share).wait_recv()
            rows = share_of(True, share)
            sums[lane_y, rows, at] = (
                sums[lane_y, rows, at].astype(F32) + z_in[share, :, at].astype(F32)).astype(LOW)
        reduce_far(index).start()

    def reduce_end(index):
        at = block_at(index)
        reduce_far(index).wait_recv()
        grad_ref[:, at] = (
            sums[lane_y, rows_at(deep), at].astype(F32) + z_in[2, :, at].astype(F32))

    def mixed_home(row, share):
        if row == 0:
            return z_in.at[share, :, mixed_at]
        return y_in.at[rows_at(share), mixed_at]

    def mixed_group(row):
        return lane_y if row == 0 else 1 - lane_y

    def mixed_near(row, share):
        return send(sums.at[mixed_group(row), share_of(False, share), mixed_at],
                    mixed_home(row, share), sem_rm, (row, share), twin)

    def mixed_far(row):
        return send(sums.at[mixed_group(row), rows_at(lax.rem(deep + 2, depth)), mixed_at],
                    mixed_home(row, 2), sem_rm, (row, 2), peer(2))

    def mixed_cross():
        return send(sums.at[1 - lane_y, rows_at(deep), mixed_at], mixed_home(1, 3),
                    sem_rm, (1, 3), other_y)

    def mixed_start():
        for row in range(2):
            for share in range(2):
                mixed_near(row, share).start()

    def mixed_mid():
        for row in range(2):
            for share in range(2):
                mixed_near(row, share).wait_recv()
                rows = share_of(True, share)
                group = mixed_group(row)
                sums[group, rows, mixed_at] = (
                    sums[group, rows, mixed_at].astype(F32)
                    + mixed_home(row, share)[...].astype(F32)).astype(LOW)
            mixed_far(row).start()

    def mixed_late():
        for row in range(2):
            mixed_far(row).wait_recv()
            total = (sums[mixed_group(row), rows_at(deep), mixed_at].astype(F32)
                     + mixed_home(row, 2)[...].astype(F32))
            if row == 0:
                grad_ref[:, mixed_at] = total
            else:
                sums[mixed_group(row), rows_at(deep), mixed_at] = total.astype(LOW)
        mixed_cross().start()

    def mixed_end():
        mixed_cross().wait_recv()
        grad_ref[:, mixed_at] += mixed_home(1, 3)[...].astype(F32)

    def reduce_sent():
        for index in range(len(spans)):
            reduce_y(index).wait_send()
            for share in range(2):
                reduce_near(index, share).wait_send()
            reduce_far(index).wait_send()
        for row in range(2):
            for share in range(2):
                mixed_near(row, share).wait_send()
            mixed_far(row).wait_send()
        mixed_cross().wait_send()

    def halves(tile):
        return [jnp.where(low_half, tile, jnp.zeros_like(tile)),
                jnp.where(low_half, jnp.zeros_like(tile), tile)]

    def group_tile(group, index):
        return w_ref[group, :, index * LANES:(index + 1) * LANES]

    qkv_cols = 3 * tiles * LANES

    def arrange():
        for kind in range(4):
            for group in range(2):
                spot = (kind * tiles + group) * LANES
                wa[:, spot:spot + LANES] = group_tile(group, kind)
        for pair in range(2):
            one, two = (group_tile(group, 4 + pair).astype(F32) for group in range(2))
            spot = (2 * pair * tiles + 2) * LANES
            wa[:, spot:spot + LANES] = jnp.where(low_half, one, flip(two)).astype(LOW)
            spot = ((2 * pair + 1) * tiles + 2) * LANES
            wa[:, spot:spot + LANES] = jnp.where(low_half, flip(one), two).astype(LOW)

    x_copy = pltpu.make_async_copy(x_all.at[lane_y], x_ref, sem_l.at[PIECES + 3])
    if inside:
        gather_start(0)
        gather_start(1)
        gather_y(mixed_part, deep, True).start()
        gain_all[deep, 0:2, 0:rows_own] = gain_ref[...].astype(F32)
        for step in range(1, depth):
            gather_gain(step).start()
        for index in range(3):
            own_copy(index).start()
    x_copy.start()

    for piece in range(PIECES):
        place = piece * PIECE + lax.broadcasted_iota(jnp.int32, (1, PIECE), 1)
        begin = jnp.zeros((1, PIECE), jnp.int32)
        end = 0
        for index in range(length_ref.shape[1]):
            end = end + length_ref[lane_y, index]
            begin = jnp.where(place >= end, end, begin)
        start_s[piece] = begin

    if inside:
        gather_pass(0)
        gather_start(2)
        gather_pass(1)
        gather_start(3)
        gather_pass(2)
        gather_start(4)
        for step in range(1, depth):
            gather_gain(step).wait()
        gather_end(0)
        gather_end(1)
        for index in range(3):
            own_copy(index).wait()
        gains = jnp.concatenate([gain_all[place, :, :rows_own] for place in range(depth)], axis=1)
    else:
        gains = gain_ref[...]
    arrange()
    x_copy.wait()
    gain1 = gains[0:1, :]
    gain2 = gains[1:2, :]

    def swap_copy(leave, enter):
        return send(swap_out.at[leave], swap_in.at[enter], sem_c, (enter,), other_core)

    def swap_start(slots, value):
        swap_out[slots[0]] = value
        swap_copy(*slots).start()

    def swap_end(slots):
        swap_copy(*slots).wait()
        return swap_out[slots[0]].astype(F32) + swap_in[slots[1]].astype(F32)

    def first_slots(piece):
        return lax.rem(piece, 2), piece

    def turned_slots(piece):
        return lax.rem(piece, 2), lax.rem(piece + 2, PIECES)

    def second_slots(piece):
        return 2, PIECES + lax.rem(piece, 2)

    def last_slots(piece):
        return 2, PIECES + lax.rem(piece + 1, 2)

    def put_rows(piece, rows):
        for t in range(2 * tiles):
            spare[piece, t] = rows[:, t * LANES:(t + 1) * LANES]

    def get_rows(piece):
        return jnp.concatenate([spare[piece, t] for t in range(2 * tiles)], axis=1)

    def joined(*stores):
        return jnp.concatenate([store[t] for store in stores for t in range(tiles)], axis=1)

    half = pl.ds(pl.multiple_of(core * half_cols, half_cols), half_cols)

    def hand_rows(piece):
        return send(there.at[piece, :, half], here.at[piece, :, half], sem_x, (piece,), other_layer)

    def hand_values(piece):
        return send(there_v.at[piece], here_v.at[piece], sem_v, (piece,), other_layer)

    def hand_on(piece):
        return send(here.at[piece, :, half], here.at[piece, :, half], sem_f, (piece,), other_core)

    def take_start(piece):
        hand_rows(piece).wait_recv()
        hand_on(piece).start()

    def take_values(piece):
        hand_values(piece).wait_recv()

    def emit_here(piece, stage):
        return pltpu.make_async_copy(stage.at[piece], out_ref.at[lane_y, piece], sem_l.at[piece])

    def emit_there(piece, stage):
        return send(stage.at[piece, :, half], out_ref.at[lane_y, piece, :, half],
                    sem_o, (piece,), other_y)

    def emit(piece, stage):
        return [emit_here(piece, stage), emit_there(piece, stage)]

    def emit_on(piece):
        spot = out_ref.at[1 - lane_y, piece, :, half]
        return send(spot, spot, sem_oc, (piece,), other_core)

    def reused(tile_index):
        if tile_index == 0:
            return None
        if tile_index == 1:
            return jnp.logical_and(second, lane >= 0)
        return jnp.logical_and(second, lane >= HEAD)

    def make_bias(piece, count):
        base = piece * PIECE
        query = base + lax.broadcasted_iota(jnp.int32, (1, PIECE), 1)
        begin = start_s[piece]
        for j in range(count):
            key = base - (count - 1 - j) * PIECE + lax.broadcasted_iota(jnp.int32, (PIECE, 1), 0)
            fine = jnp.logical_and(key >= begin, key <= query)
            bias_s[j] = jnp.where(fine, 0.0, -1e30).astype(F32)

    def attend(piece, count):
        make_bias(piece, count)
        for t in range(tiles):
            parts = []
            for h, query in enumerate(halves(q_s[piece, t])):
                scores = [
                    mm_back(k_s[piece - (count - 1 - j), t], query) + bias_s[j] for j in range(count)
                ]
                top = functools.reduce(
                    jnp.maximum, [jnp.max(s, axis=0, keepdims=True) for s in scores])
                expo = [jnp.exp(s - top) for s in scores]
                total = functools.reduce(
                    jnp.add, [jnp.sum(e, axis=0, keepdims=True) for e in expo])
                mixed = functools.reduce(jnp.add, [
                    mm(turn_s[piece - (count - 1 - j), t, h * HEAD:(h + 1) * HEAD, :], e.astype(LOW))
                    for j, e in enumerate(expo)
                ])
                parts.append(mixed * (1.0 / total))
                lse_s[piece, 2 * t + h] = top + jnp.log(total)
            o_s[piece, t] = jnp.concatenate(parts, axis=0).T.astype(LOW)

    def attend_back(piece, count):
        make_bias(piece, count)
        for t in range(tiles):
            inner = (do_s[t].astype(F32) * o_s[piece, t].astype(F32)).T
            queries = halves(q_s[piece, t])
            grads = halves(do_s[t])
            dq = [0.0, 0.0]
            inners = [jnp.sum(inner[h * HEAD:(h + 1) * HEAD], axis=0, keepdims=True) for h in range(2)]
            for j in range(count):
                at = piece - (count - 1 - j)
                dk_new, dv_new = 0.0, 0.0
                for h in range(2):
                    probs = jnp.exp(
                        mm_back(k_s[at, t], queries[h]) + bias_s[j] - lse_s[piece, 2 * t + h])
                    dprobs = mm_back(v_s[at, t], grads[h])
                    dscores = (probs * (dprobs - inners[h])).astype(LOW)
                    dv_new = dv_new + mm(probs.astype(LOW), grads[h])
                    dk_new = dk_new + mm(dscores, queries[h])
                    dq[h] = dq[h] + mm(turn_s[at, t, h * HEAD:(h + 1) * HEAD, :], dscores)
                spare[at, t] += dk_new
                spare[at, tiles + t] += dv_new
            dq_t = jnp.concatenate(dq, axis=0) * 0.125
            q_s[piece, t] = dq_t.T.astype(LOW)

    def by_count(piece, run):
        for count in range(1, WINDOW + 1):
            fits = piece >= WINDOW - 1 if count == WINDOW else piece == count - 1

            @pl.when(fits)
            def _(count=count):
                run(piece, count)

    def forward_attention(piece):
        @pl.when(second)
        def _():
            @pl.when(piece < 2)
            def _():
                take_start(piece)

            hand_on(piece).wait()

        rows = jnp.where(first, x_ref[piece], here[piece]).astype(F32)
        plain, factor = normalize(rows)
        plain1[piece] = plain.astype(LOW)
        fac1[piece] = factor
        normed = plain * gain1
        a_t[piece] = normed.T.astype(LOW)
        qkv = mm(normed.astype(LOW), wa[:, :qkv_cols])

        @pl.when(second)
        def _():
            take_values(piece)

        for t in range(tiles):
            q_s[piece, t] = (qkv[:, t * LANES:(t + 1) * LANES].astype(LOW) * 0.125).astype(LOW)
            key = qkv[:, (tiles + t) * LANES:(tiles + t + 1) * LANES].astype(LOW)
            value = qkv[:, (2 * tiles + t) * LANES:(2 * tiles + t + 1) * LANES].astype(LOW)
            mask = reused(t)
            if mask is not None:
                value = jnp.where(mask, here_v[piece, t - 1], value)
                there_v[piece, t - 1] = value
            k_s[piece, t] = key
            v_s[piece, t] = value
            turn_s[piece, t] = value.astype(F32).T.astype(LOW)

        @pl.when(first)
        def _():
            hand_values(piece).start()

        by_count(piece, attend)
        put_rows(piece, rows)
        swap_start(first_slots(piece), mm_back(joined(o_s.at[piece]), wa[:, qkv_cols:]).astype(LOW))

    def forward_middle(piece):
        put_rows(piece, get_rows(piece) + swap_end(first_slots(piece)))

    def forward_hidden(piece):
        plain, factor = normalize(get_rows(piece))
        plain2[piece] = plain.astype(LOW)
        fac2[piece] = factor
        normed = plain * gain2
        m_t[piece] = normed.T.astype(LOW)
        normed = normed.astype(LOW)
        total = 0.0
        for group in range(2):
            z = mm(normed, w_ref[group, :, hidden:2 * hidden])
            square = z * z
            bent = jnp.tanh(GELU_K * z * (1.0 + GELU_C * square))
            upper = 0.5 * (1.0 + bent)
            acted = (z * upper).astype(LOW)
            slope = upper + 0.5 * z * (1.0 - bent * bent) * (GELU_K * (1.0 + 3.0 * GELU_C * square))
            gd_s[piece, group] = slope.astype(LOW)
            e_s[piece, group] = acted
            total = total + mm_back(acted, w_ref[group, :, 2 * hidden:])
        swap_start(second_slots(piece), total.astype(LOW))

    def forward_result(piece):
        result = (get_rows(piece) + swap_end(second_slots(piece))).astype(LOW)

        @pl.when(first)
        def _():
            there[piece] = result
            hand_rows(piece).start()

        @pl.when(second)
        def _():
            here[piece] = result
            for copy in emit(piece, here):
                copy.start()

    def within(step, low_end, high_end):
        return jnp.logical_and(step >= low_end, step < high_end)

    def forward(step, carry):
        lag = jnp.where(first, 0, PIECES)
        place = step - lag

        @pl.when(within(place, 0, PIECES))
        def _():
            forward_attention(place)

        if inside:
            @pl.when(step == 0)
            def _():
                gather_pass(3)
                gather_start(5)
                gather_cross()

            @pl.when(step == 1)
            def _():
                gather_pass(4)

            @pl.when(step == 2)
            def _():
                gather_pass(5)
                gather_pass(5, 1)

            @pl.when(step == PIECES - 1)
            def _():
                for part in range(2, PARTS):
                    gather_end(part)

        @pl.when(jnp.logical_and(second, within(place, 2, PIECES + 1)))
        def _():
            forward_result(place - 2)

        @pl.when(within(place, 1, PIECES + 1))
        def _():
            forward_middle(place - 1)

        hidden_place = jnp.where(first, place - PIECES, place - 1)

        @pl.when(within(hidden_place, 0, PIECES))
        def _():
            @pl.when(jnp.logical_and(second, hidden_place < PIECES - 2))
            def _():
                take_start(hidden_place + 2)

            forward_hidden(hidden_place)

            @pl.when(first)
            def _():
                forward_result(hidden_place)

        return carry

    lax.fori_loop(0, 2 * PIECES + 1, forward, 0)

    @pl.when(first)
    def _():
        for piece in range(PIECES):
            hand_rows(piece).wait_send()
            hand_values(piece).wait_send()

    gain_grad_ref[...] = jnp.zeros_like(gain_grad_ref)

    def hidden_grads(left, right, base):
        def one(index, carry):
            group, column = index // (hidden // block), index % (hidden // block)
            spot = pl.multiple_of(column * block, block)
            total = 0.0
            for piece in range(PIECES):
                total = total + mm(left[piece], right[piece, group, :, pl.ds(spot, block)])
            sums[group, :, pl.ds(pl.multiple_of(base + spot, block), block)] = total.astype(LOW)
            return carry

        lax.fori_loop(0, 2 * (hidden // block), one, 0)

    def head_grads():
        pairs = []
        for kind in range(4):
            total = 0.0
            for piece in range(PIECES):
                if kind < 3:
                    total = total + mm(a_t[piece], joined((q_s, k_s, v_s)[kind].at[piece]))
                else:
                    total = total + mm(h_t[piece], joined(o_s.at[piece]))
            for group in range(2):
                part = total[:, group * LANES:(group + 1) * LANES].astype(LOW)
                sums[group, :, kind * LANES:(kind + 1) * LANES] = part
            pairs.append(total[:, 2 * LANES:])
        for pair in range(2):
            one, two = pairs[2 * pair:2 * pair + 2]
            spot = (4 + pair) * LANES
            sums[0, :, spot:spot + LANES] = jnp.where(low_half, one, flip(two)).astype(LOW)
            sums[1, :, spot:spot + LANES] = jnp.where(low_half, flip(one), two).astype(LOW)

    def grad_rows(piece):
        return jnp.where(first, here[piece], x_ref[piece])

    def backward_hidden(piece):
        @pl.when(first)
        def _():
            take_start(piece)
            hand_on(piece).wait()

        grad_low = grad_rows(piece)
        g_t[piece] = grad_low.astype(F32).T.astype(LOW)

        @pl.when(piece == 0)
        def _():
            hidden_grads(g_t, e_s, 2 * hidden)
            if inside:
                reduce_y(0).start()
                reduce_y(1).start()
                mixed_start()

        total = 0.0
        for group in range(2):
            dz = mm(grad_low, w_ref[group, :, 2 * hidden:]) * gd_s[piece, group].astype(F32)
            dz = dz.astype(LOW)
            gd_s[piece, group] = dz
            total = total + mm_back(dz, w_ref[group, :, hidden:2 * hidden])
        swap_start(turned_slots(piece), total.astype(LOW))

        @pl.when(piece == 0)
        def _():
            hidden_grads(m_t, gd_s, hidden)
            if inside:
                reduce_y(2).start()

    def backward_attention(piece):
        dm = swap_end(turned_slots(piece))
        plain = plain2[piece].astype(F32)
        gain_grad_ref[1:2, :] += jnp.sum(dm * plain, axis=0, keepdims=True)
        middle = grad_rows(piece).astype(F32) + norm_back(dm, plain, fac2[piece], gain2)
        h_t[piece] = middle.T.astype(LOW)
        dmixed = mm(middle.astype(LOW), wa[:, qkv_cols:]).astype(LOW)
        for t in range(tiles):
            do_s[t] = dmixed[:, t * LANES:(t + 1) * LANES]
        by_count(piece, attend_back)
        for t in range(1, tiles):
            there_v[piece, t - 1] = spare[piece, tiles + t].astype(LOW)

        @pl.when(first)
        def _():
            hand_values(piece).wait_recv()

        @pl.when(second)
        def _():
            hand_values(piece).start()

        for t in range(tiles):
            dvalue = spare[piece, tiles + t]
            mask = reused(t)
            if mask is not None:
                came = jnp.logical_and(first, jnp.logical_or(t == 1, lane >= HEAD))
                dvalue = jnp.where(came, dvalue + here_v[piece, t - 1].astype(F32), dvalue)
                dvalue = jnp.where(mask, 0.0, dvalue)
            k_s[piece, t] = spare[piece, t].astype(LOW)
            v_s[piece, t] = dvalue.astype(LOW)
        put_rows(piece, middle)
        terms = joined(q_s.at[piece], k_s.at[piece], v_s.at[piece])
        swap_start(last_slots(piece), mm_back(terms, wa[:, :qkv_cols]).astype(LOW))

    def backward_result(piece):
        da = swap_end(last_slots(piece))
        plain = plain1[piece].astype(F32)
        gain_grad_ref[0:1, :] += jnp.sum(da * plain, axis=0, keepdims=True)
        there[piece] = (get_rows(piece) + norm_back(da, plain, fac1[piece], gain1)).astype(LOW)

        @pl.when(second)
        def _():
            hand_rows(piece).start()

        @pl.when(first)
        def _():
            for copy in emit(piece, there):
                copy.start()

    def backward(step, carry):
        @pl.when(step < PIECES)
        def _():
            backward_hidden(PIECES - 1 - step)

        @pl.when(step == 0)
        def _():
            @pl.when(second)
            def _():
                forward_result(PIECES - 1)

            spare[...] = jnp.zeros_like(spare)
            for piece in range(PIECES):
                for t in range(tiles):
                    turn_s[piece, t] = k_s[piece, t].astype(F32).T.astype(LOW)

        if inside:
            @pl.when(step == PIECES)
            def _():
                mixed_mid()
                reduce_mid(0, 3)
                reduce_mid(1)

        @pl.when(step >= 2)
        def _():
            backward_result(PIECES + 1 - step)

        @pl.when(step >= 1)
        def _():
            backward_attention(PIECES - step)

        return carry

    lax.fori_loop(0, PIECES + 1, backward, 0)
    head_grads()
    if inside:
        reduce_y(4).start()
    backward_result(0)

    def emit_stage(run):
        @pl.when(first)
        def _():
            run(there)

        @pl.when(second)
        def _():
            run(here)

    def pass_outputs(stage):
        for piece in range(PIECES):
            emit_there(piece, stage).wait_recv()
            emit_on(piece).start()

    def finish_outputs(stage):
        for piece in range(PIECES):
            emit_here(piece, stage).wait()
            emit_there(piece, stage).wait_send()
            emit_on(piece).wait()

    if inside:
        gain_copy = send(gain_grad_ref, gain_y, sem_gg, (0,), other_y)
        gain_copy.start()
        reduce_late(0)
        mixed_late()
        reduce_mid(2, 5)
        reduce_late(1)
        gain_copy.wait()
        gain_y[...] = gain_y[...] + gain_grad_ref[...]
        gain_sends = [
            send(gain_y, gain_z.at[step - 1], sem_gg, (step,), peer(step)) for step in range(1, depth)]
        for copy in gain_sends:
            copy.start()
        reduce_mid(3, 6)
        reduce_late(2)
        reduce_end(0)
        reduce_mid(4, 7)
        reduce_late(3)
        reduce_end(1)
        reduce_end(2)
        total = gain_y[...]
        for step, copy in enumerate(gain_sends):
            copy.wait()
            total = total + gain_z[step]
        gain_grad_ref[...] = total
        reduce_mid(5, 8)
        reduce_late(4)
        reduce_end(3)
        emit_stage(pass_outputs)
        reduce_mid(6)
        reduce_late(5)
        reduce_end(4)
        reduce_mid(7)
        reduce_late(6)
        reduce_end(5)

        def place(sec, row, unit):
            return (sec * 2 + row) * 2 + unit

        mine = place(section, lane_y, core)
        for half_tile, tile_index in enumerate((2, 5)):
            value_ref[mine, :, half_tile * LANES:(half_tile + 1) * LANES] = (
                grad_ref[:, tile_index * LANES:(tile_index + 1) * LANES].astype(LOW))
        value_x = send(value_ref.at[mine], value_ref.at[mine], sem_va, (0,), other_layer)
        value_x.start()
        mixed_end()
        reduce_mid(8)
        reduce_late(7)
        reduce_end(6)
        value_x.wait()
        value_y = []
        for sec in range(2):
            at = place(sec, lane_y, core)
            value_y.append(send(value_ref.at[at], value_ref.at[at], sem_va, (1 + sec,), other_y))
            value_y[-1].start()
        reduce_late(8)
        reduce_end(7)
        for copy in value_y:
            copy.wait()
        value_c = []
        for sec in range(2):
            for row in range(2):
                at = place(sec, row, core)
                value_c.append(
                    send(value_ref.at[at], value_ref.at[at], sem_va, (3 + 2 * sec + row,), other_core))
                value_c[-1].start()
        reduce_end(8)
        for copy in value_c:
            copy.wait()
        reduce_sent()
    else:
        emit_stage(pass_outputs)

    emit_stage(finish_outputs)

    @pl.when(second)
    def _():
        for piece in range(PIECES):
            hand_rows(piece).wait_send()
            hand_values(piece).wait_send()


def run_layers(lengths, x_rows, gains, weights, depth, inside):
    width = x_rows.shape[3]
    tiles = width // 2 // LANES
    rows_own = width // depth
    columns = 3 * width
    vmem = pl.BlockSpec(memory_space=pltpu.VMEM)
    anywhere = pl.BlockSpec(memory_space=pl.ANY)
    smem = pl.BlockSpec(memory_space=pltpu.SMEM)
    per_tile = (PIECES, tiles, PIECE, LANES)
    turned = (PIECES, tiles, LANES, PIECE)
    flat = (PIECES, PIECE, width)
    flat_turned = (PIECES, width, PIECE)
    wide = (PIECES, 2, PIECE, width)
    low = lambda shape: pltpu.VMEM(shape, LOW)
    full = lambda shape: pltpu.VMEM(shape, F32)
    dma = lambda *shape: pltpu.SemaphoreType.DMA(shape)
    out_shape = [
        jax.ShapeDtypeStruct((2,) + flat, LOW),
        jax.ShapeDtypeStruct((rows_own, columns), F32) if inside
        else jax.ShapeDtypeStruct(weights[0].shape, LOW),
        jax.ShapeDtypeStruct((8, width), F32),
    ]
    out_specs = [anywhere, vmem, vmem]
    scratch = [
        low((width, 4 * tiles * LANES)),
        low(per_tile), low(per_tile), low(per_tile), low(turned), low(per_tile),
        full((PIECES, 2 * tiles, 1, PIECE)),
        low(flat), low(flat), full((PIECES, PIECE, 1)), full((PIECES, PIECE, 1)),
        low(flat_turned), low(flat_turned), low(flat_turned), low(flat_turned),
        low(wide), low(wide), low((tiles, PIECE, LANES)),
        full((PIECES, 2 * tiles, PIECE, LANES)),
        full((WINDOW, PIECE, PIECE)), low(flat), pltpu.VMEM((PIECES, 1, PIECE), jnp.int32),
        low(flat), low((PIECES, 2, PIECE, LANES)), low(flat), low((PIECES, 2, PIECE, LANES)),
        low((3, PIECE, width)), low((PIECES + 2, PIECE, width)),
        dma(2, PIECES), dma(2, PIECES), dma(2, PIECES), dma(2, PIECES + 2), dma(2, PIECES),
        dma(2, PIECES), dma(4 + PIECES),
    ]
    if inside:
        out_shape.append(jax.ShapeDtypeStruct((8, rows_own, 2 * LANES), LOW))
        out_specs.append(vmem)
        scratch += [
            low((2, width, columns)), full((depth, 8, -(-rows_own // LANES) * LANES)),
            low((2, width, columns)), low((width, columns)), low((depth - 1, rows_own, columns)),
            full((8, width)), full((depth - 1, 8, width)),
            dma(2, PARTS + 1, depth - 1, 2), dma(2, PARTS, depth), dma(2, depth), dma(2, 9),
            dma(2, 9, 3), dma(2, 2, 4), dma(2, depth), dma(2, 7),
        ]
    return pl.pallas_call(
        functools.partial(layers_kernel, width, depth, inside),
        out_shape=out_shape,
        in_specs=[smem, anywhere, vmem] + [anywhere if inside else vmem] * len(weights),
        out_specs=out_specs,
        scratch_shapes=scratch,
        compiler_params=pltpu.CompilerParams(
            collective_id=0, has_side_effects=True, vmem_limit_bytes=63 << 20),
        name="layers",
    )(lengths, x_rows, gains, *weights)


def pack(w_qk, w_value, w_out):
    query, key, out_t = w_qk[:, 0], w_qk[:, 1], w_out.T
    edge = 2 * HEAD
    return jnp.concatenate(
        [query[:, :edge], key[:, :edge], w_value[:, :edge], out_t[:, :edge],
         query[:, edge:], key[:, edge:], w_value[:, edge:], out_t[:, edge:]],
        axis=1)


def unpack(packed):
    edge = 2 * HEAD
    cut = lambda spot, size: packed[:, spot:spot + size]
    query = jnp.concatenate([cut(0, edge), cut(4 * edge, HEAD)], axis=1)
    key = jnp.concatenate([cut(edge, edge), cut(4 * edge + HEAD, HEAD)], axis=1)
    value = jnp.concatenate([cut(2 * edge, edge), cut(5 * edge, HEAD)], axis=1)
    out_t = jnp.concatenate([cut(3 * edge, edge), cut(5 * edge + HEAD, HEAD)], axis=1)
    hidden = packed.shape[1] // 3
    return (
        jnp.stack([query, key], axis=1), value, out_t.T,
        cut(hidden, hidden), cut(2 * hidden, hidden).T)


def shards(
    ends_in, seq_lengths, norm_gains, qk_weight, value_weight, out_weight, fc_weight, proj_weight
):
    section = lax.axis_index("section")
    lane_y = lax.axis_index("y")
    group = 2 * lane_y + lax.axis_index("core")
    first = section == 0
    cols = qk_weight.shape[3]
    width = ends_in.shape[2]
    fresh = (value_weight.shape[1] - width) // cols
    offset = jnp.where(first, group, width // cols + jnp.minimum(group, fresh - 1)) * cols
    w_value = lax.dynamic_slice_in_dim(value_weight, offset, cols, 1)
    parts = [pack(qk_weight[0], w_value, out_weight[0]), fc_weight[0], proj_weight[0].T]
    depth = lax.axis_size("dp")
    inside = depth == 4 and width % (16 * depth) == 0
    if inside:
        weights = parts
        gains = norm_gains[0].T
    else:
        weights = lax.all_gather(jnp.concatenate(parts, axis=1), "dp", axis=0, tiled=True)
        weights = [lax.all_gather(weights, "y", axis=0)]
        gains = lax.all_gather(norm_gains[0], "dp", axis=0, tiled=True).astype(F32).T
    x_rows = ends_in[0].reshape(2, PIECES, PIECE, width)
    kept = width // cols + fresh
    edge = 2 * HEAD
    results = run_layers(seq_lengths, x_rows, gains, weights, depth, inside)
    both = results[0].reshape(2 * MB_TOK, width)
    if inside:
        _, grads, gain_grads, values = results
        rows_own = width // depth
        gain_rows = lax.dynamic_slice_in_dim(
            gain_grads[:2], lax.axis_index("dp") * rows_own, rows_own, 1).T
        values = values[:, :, :cols]
    else:
        _, grads, gain_grads = results
        grads = lax.psum_scatter(grads, "y", scatter_dimension=0, tiled=False)
        grads = lax.psum_scatter(grads, "dp", scatter_dimension=0, tiled=True)
        gain_rows = lax.psum(gain_grads[:2], "y").T
        gain_rows = lax.psum_scatter(gain_rows, "dp", scatter_dimension=0, tiled=True)
        values = lax.all_gather(
            unpack(grads)[1].astype(LOW), ("section", "y", "core"), axis=0)
    d_qk, _, d_out, d_up, d_down = unpack(grads.astype(F32))
    d_value = jnp.concatenate([values[index] for index in range(kept)], axis=1).astype(F32)
    return (
        both[None], gain_rows[:, 0][None], gain_rows[:, 1][None], d_qk[None], d_value,
        d_out[None], d_up[None], d_down[None])


def solution(mesh):
    sections, depth, split = (mesh.shape[name] for name in ("section", "dp", "mp"))
    grid = Mesh(mesh.devices.reshape(sections, depth, split // 2, 2), ("section", "dp", "y", "core"))
    mp = ("y", "core")
    in_specs = (
        P("section", "dp", None),
        P("dp", None),
        P("section", "dp", None),
        P("section", "dp", None, mp),
        P("dp", None),
        P("section", mp, "dp"),
        P("section", "dp", mp),
        P("section", mp, "dp"),
    )
    out_specs = (
        P("section", "dp", None),
        P("section", "dp"),
        P("section", "dp"),
        P("section", "dp", None, mp),
        P("dp", None),
        P("section", mp, "dp"),
        P("section", "dp", mp),
        P("section", mp, "dp"),
    )
    return jax.shard_map(shards, mesh=grid, in_specs=in_specs, out_specs=out_specs, check_vma=False)
```

```python
import functools
import math

import jax
import jax.numpy as jnp
from jax import lax
from jax.experimental import pallas as pl
from jax.experimental.pallas import tpu as pltpu
from jax.sharding import Mesh, PartitionSpec as P

HEAD = 64
MB_TOK = 1024
PIECE = 256
PIECES = MB_TOK // PIECE
WINDOW = 3
PARTS = 6
LANES = 128
EPSILON = 1e-05
GELU_K = math.sqrt(2.0 / math.pi)
GELU_C = 0.044715
MESH = pl.DeviceIdType.MESH
F32 = jnp.float32
LOW = jnp.bfloat16


def mm(left, right):
    return lax.dot_general(left, right, (((1,), (0,)), ((), ())), preferred_element_type=F32)


def mm_back(left, right):
    return lax.dot_general(left, right, (((1,), (1,)), ((), ())), preferred_element_type=F32)


def normalize(rows):
    centred = rows - jnp.mean(rows, axis=1, keepdims=True)
    factor = lax.rsqrt(jnp.mean(centred * centred, axis=1, keepdims=True) + EPSILON)
    return centred * factor, factor


def norm_back(grad, plain, factor, gain):
    scaled = grad * gain
    return factor * (
        scaled
        - jnp.mean(scaled, axis=1, keepdims=True)
        - plain * jnp.mean(scaled * plain, axis=1, keepdims=True)
    )


def flip(tile):
    return pltpu.roll(tile, HEAD, 1)


def layers_kernel(width, depth, inside, *refs):
    refs = list(refs)
    take = lambda count: [refs.pop(0) for _ in range(count)]
    length_ref, x_all, gain_ref = take(3)
    part_refs = take(3 if inside else 1)
    out_ref, grad_ref, gain_grad_ref = take(3)
    if inside:
        (value_ref,) = take(1)
    (wa, q_s, k_s, v_s, turn_s, o_s, lse_s, plain1, plain2, fac1, fac2,
     a_t, m_t, g_t, h_t, e_s, gd_s, do_s, spare, bias_s, x_ref, start_s,
     there, there_v, here, here_v, swap_out, swap_in,
     sem_x, sem_v, sem_f, sem_c, sem_o, sem_oc, sem_l) = take(35)
    if inside:
        (w_ref, gain_all, sums, y_in, z_in, gain_y, gain_z,
         sem_az, sem_ay, sem_gz, sem_ry, sem_rz, sem_rm, sem_gg, sem_va) = take(15)
    else:
        w_ref, sums = part_refs[0], grad_ref

    section = lax.axis_index("section")
    core = lax.axis_index("core")
    lane_y = lax.axis_index("y")
    deep = lax.axis_index("dp")
    other_layer = {"section": 1 - section}
    other_core = {"core": 1 - core}
    other_y = {"y": 1 - lane_y}
    first = section == 0
    second = jnp.logical_not(first)
    tiles = width // 2 // LANES
    hidden = width
    rows_own = width // depth
    half_cols = width // 2

    def send(src, dst, sems, index, target):
        return pltpu.make_async_remote_copy(
            src_ref=src, dst_ref=dst, send_sem=sems.at[(0,) + index], recv_sem=sems.at[(1,) + index],
            device_id=target, device_id_type=MESH)

    def peer(step):
        return {"dp": lax.rem(deep + step, depth)}

    barrier = pltpu.get_barrier_semaphore()
    friends = [other_layer, other_core, other_y]
    if inside:
        friends = friends + [peer(step) for step in range(1, depth)]
        twin = {"dp": deep + 1 - 2 * lax.rem(deep, 2)}
    for friend in friends:
        pl.semaphore_signal(barrier, inc=1, device_id=friend, device_id_type=MESH)
    pl.semaphore_wait(barrier, len(friends))

    lane = lax.broadcasted_iota(jnp.int32, (1, LANES), 1)
    low_half = lane < HEAD

    def rows_at(place):
        return pl.ds(pl.multiple_of(place * rows_own, rows_own), rows_own)

    unit = 3 * hidden // PARTS
    per_ref = PARTS // 3
    ways = (1, -1)
    mixed_part = PARTS - 1

    def cols_at(part):
        return pl.ds(part * unit, unit)

    def on_line(place):
        return jnp.logical_and(place >= 0, place < depth)

    def own_part(part):
        return part_refs[part // per_ref].at[:, pl.ds(part % per_ref * unit, unit)]

    def own_copy(index):
        return pltpu.make_async_copy(
            part_refs[index], w_ref.at[lane_y, rows_at(deep), pl.ds(index * hidden, hidden)],
            sem_l.at[PIECES + index])

    def gather_line(part, row, hop, way):
        place = deep - hop * ways[way]
        home = lane_y if row == 0 else 1 - lane_y
        spot = w_ref.at[home, rows_at(place), cols_at(part)]
        src = own_part(part) if row == 0 and hop == 0 else spot
        return send(src, spot, sem_az, (part + row, hop, way), {"dp": deep + ways[way]})

    def line_start(part, row, hop, way):
        @pl.when(jnp.logical_and(on_line(deep - hop * ways[way]), on_line(deep + ways[way])))
        def _():
            gather_line(part, row, hop, way).start()

    def line_sent(part, row, hop, way):
        @pl.when(jnp.logical_and(on_line(deep - hop * ways[way]), on_line(deep + ways[way])))
        def _():
            gather_line(part, row, hop, way).wait_send()

    def gather_y(part, place, own):
        spot = w_ref.at[lane_y, rows_at(place), cols_at(part)]
        src = own_part(part) if own else spot
        return send(src, spot, sem_ay, (part, place), other_y)

    def gather_gain(step):
        return send(gain_all.at[deep], gain_all.at[deep], sem_gz, (step,), peer(step))

    def gather_start(part):
        for way in range(2):
            line_start(part, 0, 0, way)
        if part != mixed_part:
            gather_y(part, deep, True).start()

    def gather_pass(part, row=0, hops=None):
        for hop in range(depth - 1) if hops is None else hops:
            for way in range(2):
                place = deep - (hop + 1) * ways[way]

                @pl.when(on_line(place))
                def _(hop=hop, way=way, place=place):
                    gather_line(part, row, hop, way).wait_recv()
                    if hop < depth - 2:
                        line_start(part, row, hop + 1, way)
                    if part != mixed_part:
                        gather_y(part, place, False).start()

    def gather_cross():
        gather_y(mixed_part, deep, True).wait()
        for way in range(2):
            line_start(mixed_part, 1, 0, way)

    def gather_end(part):
        if part != mixed_part:
            for place in range(depth):
                gather_y(part, place, False).wait()
        for row in range(2 if part == mixed_part else 1):
            for hop in range(depth - 1):
                for way in range(2):
                    line_sent(part, row, hop, way)

    block = 2 * LANES
    last = block // 2
    spans = [
        (2 * hidden, block), (2 * hidden + block, last), (hidden, block), (hidden + block, block),
        (block, block), (2 * block, block), (0, block),
        (hidden + 2 * block, last), (hidden + 2 * block + last, last)]
    mixed_at = pl.ds(2 * hidden + block + last, block + last)

    def block_at(index):
        return pl.ds(spans[index][0], spans[index][1])

    def reduce_y(index):
        return send(sums.at[1 - lane_y, :, block_at(index)], y_in.at[:, block_at(index)],
                    sem_ry, (index,), other_y)

    def share_of(near, index):
        own = lax.rem(deep, 2)
        return rows_at((own if near else 1 - own) + 2 * index)

    def reduce_near(index, share):
        at = block_at(index)
        return send(sums.at[lane_y, share_of(False, share), at], z_in.at[share, :, at],
                    sem_rz, (index, share), twin)

    def reduce_far(index):
        at = block_at(index)
        return send(sums.at[lane_y, rows_at(lax.rem(deep + 2, depth)), at], z_in.at[2, :, at],
                    sem_rz, (index, 2), peer(2))

    def reduce_mid(index, following=None):
        reduce_y(index).wait_recv()
        if following is not None:
            reduce_y(following).start()
        at = block_at(index)
        sums[lane_y, :, at] = (
            sums[lane_y, :, at].astype(F32) + y_in[:, at].astype(F32)).astype(LOW)
        for share in range(2):
            reduce_near(index, share).start()

    def reduce_late(index):
        at = block_at(index)
        for share in range(2):
            reduce_near(index, share).wait_recv()
            rows = share_of(True, share)
            sums[lane_y, rows, at] = (
                sums[lane_y, rows, at].astype(F32) + z_in[share, :, at].astype(F32)).astype(LOW)
        reduce_far(index).start()

    def reduce_end(index):
        at = block_at(index)
        reduce_far(index).wait_recv()
        grad_ref[:, at] = (
            sums[lane_y, rows_at(deep), at].astype(F32) + z_in[2, :, at].astype(F32))

    def mixed_home(row, share):
        if row == 0:
            return z_in.at[share, :, mixed_at]
        return y_in.at[rows_at(share), mixed_at]

    def mixed_group(row):
        return lane_y if row == 0 else 1 - lane_y

    def mixed_near(row, share):
        return send(sums.at[mixed_group(row), share_of(False, share), mixed_at],
                    mixed_home(row, share), sem_rm, (row, share), twin)

    def mixed_far(row):
        return send(sums.at[mixed_group(row), rows_at(lax.rem(deep + 2, depth)), mixed_at],
                    mixed_home(row, 2), sem_rm, (row, 2), peer(2))

    def mixed_cross():
        return send(sums.at[1 - lane_y, rows_at(deep), mixed_at], mixed_home(1, 3),
                    sem_rm, (1, 3), other_y)

    def mixed_start():
        for row in range(2):
            for share in range(2):
                mixed_near(row, share).start()

    def mixed_mid():
        for row in range(2):
            for share in range(2):
                mixed_near(row, share).wait_recv()
                rows = share_of(True, share)
                group = mixed_group(row)
                sums[group, rows, mixed_at] = (
                    sums[group, rows, mixed_at].astype(F32)
                    + mixed_home(row, share)[...].astype(F32)).astype(LOW)
            mixed_far(row).start()

    def mixed_late():
        for row in range(2):
            mixed_far(row).wait_recv()
            total = (sums[mixed_group(row), rows_at(deep), mixed_at].astype(F32)
                     + mixed_home(row, 2)[...].astype(F32))
            if row == 0:
                grad_ref[:, mixed_at] = total
            else:
                sums[mixed_group(row), rows_at(deep), mixed_at] = total.astype(LOW)
        mixed_cross().start()

    def mixed_end():
        mixed_cross().wait_recv()
        grad_ref[:, mixed_at] += mixed_home(1, 3)[...].astype(F32)

    def reduce_sent():
        for index in range(len(spans)):
            reduce_y(index).wait_send()
            for share in range(2):
                reduce_near(index, share).wait_send()
            reduce_far(index).wait_send()
        for row in range(2):
            for share in range(2):
                mixed_near(row, share).wait_send()
            mixed_far(row).wait_send()
        mixed_cross().wait_send()

    def halves(tile):
        return [jnp.where(low_half, tile, jnp.zeros_like(tile)),
                jnp.where(low_half, jnp.zeros_like(tile), tile)]

    def group_tile(group, index):
        return w_ref[group, :, index * LANES:(index + 1) * LANES]

    qkv_cols = 3 * tiles * LANES

    def arrange():
        for kind in range(4):
            for group in range(2):
                spot = (kind * tiles + group) * LANES
                wa[:, spot:spot + LANES] = group_tile(group, kind)
        for pair in range(2):
            one, two = (group_tile(group, 4 + pair).astype(F32) for group in range(2))
            spot = (2 * pair * tiles + 2) * LANES
            wa[:, spot:spot + LANES] = jnp.where(low_half, one, flip(two)).astype(LOW)
            spot = ((2 * pair + 1) * tiles + 2) * LANES
            wa[:, spot:spot + LANES] = jnp.where(low_half, flip(one), two).astype(LOW)

    x_copy = pltpu.make_async_copy(x_all.at[lane_y], x_ref, sem_l.at[PIECES + 3])
    if inside:
        gather_start(0)
        gather_start(1)
        gather_y(mixed_part, deep, True).start()
        gain_all[deep, 0:2, 0:rows_own] = gain_ref[...].astype(F32)
        for step in range(1, depth):
            gather_gain(step).start()
        for index in range(3):
            own_copy(index).start()
    x_copy.start()

    for piece in range(PIECES):
        place = piece * PIECE + lax.broadcasted_iota(jnp.int32, (1, PIECE), 1)
        begin = jnp.zeros((1, PIECE), jnp.int32)
        end = 0
        for index in range(length_ref.shape[1]):
            end = end + length_ref[lane_y, index]
            begin = jnp.where(place >= end, end, begin)
        start_s[piece] = begin

    if inside:
        gather_pass(0)
        gather_start(2)
        gather_pass(1)
        gather_start(3)
        gather_pass(2)
        gather_start(4)
        for step in range(1, depth):
            gather_gain(step).wait()
        gather_end(0)
        gather_end(1)
        for index in range(3):
            own_copy(index).wait()
        gains = jnp.concatenate([gain_all[place, :, :rows_own] for place in range(depth)], axis=1)
    else:
        gains = gain_ref[...]
    arrange()
    x_copy.wait()
    gain1 = gains[0:1, :]
    gain2 = gains[1:2, :]

    def swap_copy(leave, enter):
        return send(swap_out.at[leave], swap_in.at[enter], sem_c, (enter,), other_core)

    def swap_start(slots, value):
        swap_out[slots[0]] = value
        swap_copy(*slots).start()

    def swap_end(slots):
        swap_copy(*slots).wait()
        return swap_out[slots[0]].astype(F32) + swap_in[slots[1]].astype(F32)

    def first_slots(piece):
        return lax.rem(piece, 2), piece

    def turned_slots(piece):
        return lax.rem(piece, 2), lax.rem(piece + 2, PIECES)

    def second_slots(piece):
        return 2, PIECES + lax.rem(piece, 2)

    def last_slots(piece):
        return 2, PIECES + lax.rem(piece + 1, 2)

    def put_rows(piece, rows):
        for t in range(2 * tiles):
            spare[piece, t] = rows[:, t * LANES:(t + 1) * LANES]

    def get_rows(piece):
        return jnp.concatenate([spare[piece, t] for t in range(2 * tiles)], axis=1)

    def joined(*stores):
        return jnp.concatenate([store[t] for store in stores for t in range(tiles)], axis=1)

    half = pl.ds(pl.multiple_of(core * half_cols, half_cols), half_cols)

    def hand_rows(piece):
        return send(there.at[piece, :, half], here.at[piece, :, half], sem_x, (piece,), other_layer)

    def hand_values(piece):
        return send(there_v.at[piece], here_v.at[piece], sem_v, (piece,), other_layer)

    def hand_on(piece):
        return send(here.at[piece, :, half], here.at[piece, :, half], sem_f, (piece,), other_core)

    def take_start(piece):
        hand_rows(piece).wait_recv()
        hand_on(piece).start()

    def take_values(piece):
        hand_values(piece).wait_recv()

    def emit_here(piece, stage):
        return pltpu.make_async_copy(stage.at[piece], out_ref.at[lane_y, piece], sem_l.at[piece])

    def emit_there(piece, stage):
        return send(stage.at[piece, :, half], out_ref.at[lane_y, piece, :, half],
                    sem_o, (piece,), other_y)

    def emit(piece, stage):
        return [emit_here(piece, stage), emit_there(piece, stage)]

    def emit_on(piece):
        spot = out_ref.at[1 - lane_y, piece, :, half]
        return send(spot, spot, sem_oc, (piece,), other_core)

    def reused(tile_index):
        if tile_index == 0:
            return None
        if tile_index == 1:
            return jnp.logical_and(second, lane >= 0)
        return jnp.logical_and(second, lane >= HEAD)

    def make_bias(piece, count):
        base = piece * PIECE
        query = base + lax.broadcasted_iota(jnp.int32, (1, PIECE), 1)
        begin = start_s[piece]
        for j in range(count):
            key = base - (count - 1 - j) * PIECE + lax.broadcasted_iota(jnp.int32, (PIECE, 1), 0)
            fine = jnp.logical_and(key >= begin, key <= query)
            bias_s[j] = jnp.where(fine, 0.0, -1e30).astype(F32)

    def attend(piece, count):
        make_bias(piece, count)
        for t in range(tiles):
            parts = []
            for h, query in enumerate(halves(q_s[piece, t])):
                scores = [
                    mm_back(k_s[piece - (count - 1 - j), t], query) + bias_s[j] for j in range(count)
                ]
                top = functools.reduce(
                    jnp.maximum, [jnp.max(s, axis=0, keepdims=True) for s in scores])
                expo = [jnp.exp(s - top) for s in scores]
                total = functools.reduce(
                    jnp.add, [jnp.sum(e, axis=0, keepdims=True) for e in expo])
                mixed = functools.reduce(jnp.add, [
                    mm(turn_s[piece - (count - 1 - j), t, h * HEAD:(h + 1) * HEAD, :], e.astype(LOW))
                    for j, e in enumerate(expo)
                ])
                parts.append(mixed * (1.0 / total))
                lse_s[piece, 2 * t + h] = top + jnp.log(total)
            o_s[piece, t] = jnp.concatenate(parts, axis=0).T.astype(LOW)

    def attend_back(piece, count):
        make_bias(piece, count)
        for t in range(tiles):
            inner = (do_s[t].astype(F32) * o_s[piece, t].astype(F32)).T
            queries = halves(q_s[piece, t])
            grads = halves(do_s[t])
            dq = [0.0, 0.0]
            inners = [jnp.sum(inner[h * HEAD:(h + 1) * HEAD], axis=0, keepdims=True) for h in range(2)]
            for j in range(count):
                at = piece - (count - 1 - j)
                dk_new, dv_new = 0.0, 0.0
                for h in range(2):
                    probs = jnp.exp(
                        mm_back(k_s[at, t], queries[h]) + bias_s[j] - lse_s[piece, 2 * t + h])
                    dprobs = mm_back(v_s[at, t], grads[h])
                    dscores = (probs * (dprobs - inners[h])).astype(LOW)
                    dv_new = dv_new + mm(probs.astype(LOW), grads[h])
                    dk_new = dk_new + mm(dscores, queries[h])
                    dq[h] = dq[h] + mm(turn_s[at, t, h * HEAD:(h + 1) * HEAD, :], dscores)
                spare[at, t] += dk_new
                spare[at, tiles + t] += dv_new
            dq_t = jnp.concatenate(dq, axis=0) * 0.125
            q_s[piece, t] = dq_t.T.astype(LOW)

    def by_count(piece, run):
        for count in range(1, WINDOW + 1):
            fits = piece >= WINDOW - 1 if count == WINDOW else piece == count - 1

            @pl.when(fits)
            def _(count=count):
                run(piece, count)

    def forward_attention(piece):
        @pl.when(second)
        def _():
            @pl.when(piece < 2)
            def _():
                take_start(piece)

            hand_on(piece).wait()

        rows = jnp.where(first, x_ref[piece], here[piece]).astype(F32)
        plain, factor = normalize(rows)
        plain1[piece] = plain.astype(LOW)
        fac1[piece] = factor
        normed = plain * gain1
        a_t[piece] = normed.T.astype(LOW)
        qkv = mm(normed.astype(LOW), wa[:, :qkv_cols])

        @pl.when(second)
        def _():
            take_values(piece)

        for t in range(tiles):
            q_s[piece, t] = (qkv[:, t * LANES:(t + 1) * LANES].astype(LOW) * 0.125).astype(LOW)
            key = qkv[:, (tiles + t) * LANES:(tiles + t + 1) * LANES].astype(LOW)
            value = qkv[:, (2 * tiles + t) * LANES:(2 * tiles + t + 1) * LANES].astype(LOW)
            mask = reused(t)
            if mask is not None:
                value = jnp.where(mask, here_v[piece, t - 1], value)
                there_v[piece, t - 1] = value
            k_s[piece, t] = key
            v_s[piece, t] = value
            turn_s[piece, t] = value.astype(F32).T.astype(LOW)

        @pl.when(first)
        def _():
            hand_values(piece).start()

        by_count(piece, attend)
        put_rows(piece, rows)
        swap_start(first_slots(piece), mm_back(joined(o_s.at[piece]), wa[:, qkv_cols:]).astype(LOW))

    def forward_middle(piece):
        put_rows(piece, get_rows(piece) + swap_end(first_slots(piece)))

    def forward_spread(piece):
        plain, factor = normalize(get_rows(piece))
        plain2[piece] = plain.astype(LOW)
        fac2[piece] = factor
        normed = plain * gain2
        m_t[piece] = normed.T.astype(LOW)
        normed = normed.astype(LOW)
        for group in range(2):
            z = mm(normed, w_ref[group, :, hidden:2 * hidden])
            square = z * z
            bent = jnp.tanh(GELU_K * z * (1.0 + GELU_C * square))
            upper = 0.5 * (1.0 + bent)
            slope = upper + 0.5 * z * (1.0 - bent * bent) * (GELU_K * (1.0 + 3.0 * GELU_C * square))
            gd_s[piece, group] = slope.astype(LOW)
            e_s[piece, group] = (z * upper).astype(LOW)

    def forward_fold(piece):
        total = 0.0
        for group in range(2):
            total = total + mm_back(e_s[piece, group], w_ref[group, :, 2 * hidden:])
        swap_start(second_slots(piece), total.astype(LOW))

    def forward_result(piece):
        result = (get_rows(piece) + swap_end(second_slots(piece))).astype(LOW)

        @pl.when(first)
        def _():
            there[piece] = result
            hand_rows(piece).start()

        @pl.when(second)
        def _():
            here[piece] = result
            for copy in emit(piece, here):
                copy.start()

    def within(step, low_end, high_end):
        return jnp.logical_and(step >= low_end, step < high_end)

    lag = jnp.where(first, 0, 2 * PIECES)

    def forward(step, carry):
        place = step - lag

        @pl.when(within(place, 0, PIECES))
        def _():
            forward_attention(place)

        if inside:
            @pl.when(step == 1)
            def _():
                gather_pass(3)
                gather_start(5)
                gather_cross()

            @pl.when(step == PIECES - 1)
            def _():
                gather_pass(4)
                gather_end(2)
                gather_end(3)

            for hop in range(depth - 1):
                @pl.when(step == PIECES + hop)
                def _(hop=hop):
                    gather_pass(5, 0, [hop])
                    gather_pass(5, 1, [hop])

            @pl.when(step == 2 * PIECES - 1)
            def _():
                gather_end(4)
                gather_end(5)

        @pl.when(jnp.logical_and(second, within(place, 2, PIECES + 1)))
        def _():
            forward_result(place - 2)

        @pl.when(within(place, 1, PIECES + 1))
        def _():
            forward_middle(place - 1)

        spread_place = place - jnp.where(first, PIECES, 1)

        @pl.when(within(spread_place, 0, PIECES))
        def _():
            forward_spread(spread_place)

        fold_place = place - jnp.where(first, 2 * PIECES, 1)

        @pl.when(within(fold_place, 0, PIECES))
        def _():
            @pl.when(jnp.logical_and(second, fold_place < PIECES - 2))
            def _():
                take_start(fold_place + 2)

            forward_fold(fold_place)

            @pl.when(first)
            def _():
                forward_result(fold_place)

        return carry

    lax.fori_loop(0, 3 * PIECES + 1, forward, 0)

    @pl.when(first)
    def _():
        for piece in range(PIECES):
            hand_rows(piece).wait_send()
            hand_values(piece).wait_send()

    gain_grad_ref[...] = jnp.zeros_like(gain_grad_ref)

    def hidden_grads(left, right, base):
        def one(index, carry):
            group, column = index // (hidden // block), index % (hidden // block)
            spot = pl.multiple_of(column * block, block)
            total = 0.0
            for piece in range(PIECES):
                total = total + mm(left[piece], right[piece, group, :, pl.ds(spot, block)])
            sums[group, :, pl.ds(pl.multiple_of(base + spot, block), block)] = total.astype(LOW)
            return carry

        lax.fori_loop(0, 2 * (hidden // block), one, 0)

    def head_grads():
        pairs = []
        for kind in range(4):
            total = 0.0
            for piece in range(PIECES):
                if kind < 3:
                    total = total + mm(a_t[piece], joined((q_s, k_s, v_s)[kind].at[piece]))
                else:
                    total = total + mm(h_t[piece], joined(o_s.at[piece]))
            for group in range(2):
                part = total[:, group * LANES:(group + 1) * LANES].astype(LOW)
                sums[group, :, kind * LANES:(kind + 1) * LANES] = part
            pairs.append(total[:, 2 * LANES:])
        for pair in range(2):
            one, two = pairs[2 * pair:2 * pair + 2]
            spot = (4 + pair) * LANES
            sums[0, :, spot:spot + LANES] = jnp.where(low_half, one, flip(two)).astype(LOW)
            sums[1, :, spot:spot + LANES] = jnp.where(low_half, flip(one), two).astype(LOW)

    def down_grads():
        hidden_grads(g_t, e_s, 2 * hidden)
        if inside:
            reduce_y(0).start()
            reduce_y(1).start()
            mixed_start()

    def up_grads():
        hidden_grads(m_t, gd_s, hidden)
        if inside:
            reduce_y(2).start()

    def reduce_open():
        if inside:
            mixed_mid()
            reduce_mid(0, 3)

    def grad_rows(piece):
        return jnp.where(first, here[piece], x_ref[piece])

    def backward_hidden(piece):
        @pl.when(first)
        def _():
            take_start(piece)
            hand_on(piece).wait()

        grad_low = grad_rows(piece)
        g_t[piece] = grad_low.astype(F32).T.astype(LOW)

        @pl.when(jnp.logical_and(first, piece == 0))
        def _():
            down_grads()

        total = 0.0
        for group in range(2):
            dz = mm(grad_low, w_ref[group, :, 2 * hidden:]) * gd_s[piece, group].astype(F32)
            dz = dz.astype(LOW)
            gd_s[piece, group] = dz
            total = total + mm_back(dz, w_ref[group, :, hidden:2 * hidden])
        swap_start(turned_slots(piece), total.astype(LOW))

        @pl.when(jnp.logical_and(first, piece == 0))
        def _():
            up_grads()

    def backward_attention(piece):
        dm = swap_end(turned_slots(piece))
        plain = plain2[piece].astype(F32)
        gain_grad_ref[1:2, :] += jnp.sum(dm * plain, axis=0, keepdims=True)
        middle = grad_rows(piece).astype(F32) + norm_back(dm, plain, fac2[piece], gain2)
        h_t[piece] = middle.T.astype(LOW)
        dmixed = mm(middle.astype(LOW), wa[:, qkv_cols:]).astype(LOW)
        for t in range(tiles):
            do_s[t] = dmixed[:, t * LANES:(t + 1) * LANES]
        by_count(piece, attend_back)
        for t in range(1, tiles):
            there_v[piece, t - 1] = spare[piece, tiles + t].astype(LOW)

        @pl.when(first)
        def _():
            hand_values(piece).wait_recv()

        @pl.when(second)
        def _():
            hand_values(piece).start()

        for t in range(tiles):
            dvalue = spare[piece, tiles + t]
            mask = reused(t)
            if mask is not None:
                came = jnp.logical_and(first, jnp.logical_or(t == 1, lane >= HEAD))
                dvalue = jnp.where(came, dvalue + here_v[piece, t - 1].astype(F32), dvalue)
                dvalue = jnp.where(mask, 0.0, dvalue)
            k_s[piece, t] = spare[piece, t].astype(LOW)
            v_s[piece, t] = dvalue.astype(LOW)
        put_rows(piece, middle)
        terms = joined(q_s.at[piece], k_s.at[piece], v_s.at[piece])
        swap_start(last_slots(piece), mm_back(terms, wa[:, :qkv_cols]).astype(LOW))

    def backward_result(piece):
        da = swap_end(last_slots(piece))
        plain = plain1[piece].astype(F32)
        gain_grad_ref[0:1, :] += jnp.sum(da * plain, axis=0, keepdims=True)
        there[piece] = (get_rows(piece) + norm_back(da, plain, fac1[piece], gain1)).astype(LOW)

        @pl.when(second)
        def _():
            hand_rows(piece).start()

        @pl.when(first)
        def _():
            for copy in emit(piece, there):
                copy.start()

    def backward(step, carry):
        turn = step // 2
        even = lax.rem(step, 2) == 0

        @pl.when(jnp.logical_and(jnp.logical_xor(even, first), turn < PIECES))
        def _():
            backward_hidden(PIECES - 1 - turn)

        @pl.when(step == 0)
        def _():
            @pl.when(second)
            def _():
                forward_result(PIECES - 1)

            spare[...] = jnp.zeros_like(spare)
            for piece in range(PIECES):
                for t in range(tiles):
                    turn_s[piece, t] = k_s[piece, t].astype(F32).T.astype(LOW)

        @pl.when(jnp.logical_and(first, step == 2 * PIECES))
        def _():
            reduce_open()

        @pl.when(jnp.logical_and(jnp.logical_xor(even, second), turn >= 1))
        def _():
            @pl.when(turn >= 2)
            def _():
                backward_result(PIECES + 1 - turn)

            backward_attention(PIECES - turn)

        return carry

    lax.fori_loop(0, 2 * PIECES + 2, backward, 0)
    backward_result(0)

    @pl.when(second)
    def _():
        down_grads()
        up_grads()
        reduce_open()

    head_grads()
    if inside:
        reduce_y(4).start()
        reduce_mid(1)

    def emit_stage(run):
        @pl.when(first)
        def _():
            run(there)

        @pl.when(second)
        def _():
            run(here)

    def pass_outputs(stage):
        for piece in range(PIECES):
            emit_there(piece, stage).wait_recv()
            emit_on(piece).start()

    def finish_outputs(stage):
        for piece in range(PIECES):
            emit_here(piece, stage).wait()
            emit_there(piece, stage).wait_send()
            emit_on(piece).wait()

    if inside:
        gain_copy = send(gain_grad_ref, gain_y, sem_gg, (0,), other_y)
        gain_copy.start()
        reduce_late(0)
        mixed_late()
        reduce_mid(2, 5)
        reduce_late(1)
        gain_copy.wait()
        gain_y[...] = gain_y[...] + gain_grad_ref[...]
        gain_sends = [
            send(gain_y, gain_z.at[step - 1], sem_gg, (step,), peer(step)) for step in range(1, depth)]
        for copy in gain_sends:
            copy.start()
        reduce_mid(3, 6)
        reduce_late(2)
        reduce_end(0)
        reduce_mid(4, 7)
        reduce_late(3)
        reduce_end(1)
        reduce_end(2)
        total = gain_y[...]
        for step, copy in enumerate(gain_sends):
            copy.wait()
            total = total + gain_z[step]
        gain_grad_ref[...] = total
        reduce_mid(5, 8)
        reduce_late(4)
        reduce_end(3)
        emit_stage(pass_outputs)
        reduce_mid(6)
        reduce_late(5)
        reduce_end(4)
        reduce_mid(7)
        reduce_late(6)
        reduce_end(5)

        def place(sec, row, unit):
            return (sec * 2 + row) * 2 + unit

        mine = place(section, lane_y, core)
        for half_tile, tile_index in enumerate((2, 5)):
            value_ref[mine, :, half_tile * LANES:(half_tile + 1) * LANES] = (
                grad_ref[:, tile_index * LANES:(tile_index + 1) * LANES].astype(LOW))
        value_x = send(value_ref.at[mine], value_ref.at[mine], sem_va, (0,), other_layer)
        value_x.start()
        mixed_end()
        reduce_mid(8)
        reduce_late(7)
        reduce_end(6)
        value_x.wait()
        value_y = []
        for sec in range(2):
            at = place(sec, lane_y, core)
            value_y.append(send(value_ref.at[at], value_ref.at[at], sem_va, (1 + sec,), other_y))
            value_y[-1].start()
        reduce_late(8)
        reduce_end(7)
        for copy in value_y:
            copy.wait()
        value_c = []
        for sec in range(2):
            for row in range(2):
                at = place(sec, row, core)
                value_c.append(
                    send(value_ref.at[at], value_ref.at[at], sem_va, (3 + 2 * sec + row,), other_core))
                value_c[-1].start()
        reduce_end(8)
        for copy in value_c:
            copy.wait()
        reduce_sent()
    else:
        emit_stage(pass_outputs)

    emit_stage(finish_outputs)

    @pl.when(second)
    def _():
        for piece in range(PIECES):
            hand_rows(piece).wait_send()
            hand_values(piece).wait_send()


def run_layers(lengths, x_rows, gains, weights, depth, inside):
    width = x_rows.shape[3]
    tiles = width // 2 // LANES
    rows_own = width // depth
    columns = 3 * width
    vmem = pl.BlockSpec(memory_space=pltpu.VMEM)
    anywhere = pl.BlockSpec(memory_space=pl.ANY)
    smem = pl.BlockSpec(memory_space=pltpu.SMEM)
    per_tile = (PIECES, tiles, PIECE, LANES)
    turned = (PIECES, tiles, LANES, PIECE)
    flat = (PIECES, PIECE, width)
    flat_turned = (PIECES, width, PIECE)
    wide = (PIECES, 2, PIECE, width)
    low = lambda shape: pltpu.VMEM(shape, LOW)
    full = lambda shape: pltpu.VMEM(shape, F32)
    dma = lambda *shape: pltpu.SemaphoreType.DMA(shape)
    out_shape = [
        jax.ShapeDtypeStruct((2,) + flat, LOW),
        jax.ShapeDtypeStruct((rows_own, columns), F32) if inside
        else jax.ShapeDtypeStruct(weights[0].shape, LOW),
        jax.ShapeDtypeStruct((8, width), F32),
    ]
    out_specs = [anywhere, vmem, vmem]
    scratch = [
        low((width, 4 * tiles * LANES)),
        low(per_tile), low(per_tile), low(per_tile), low(turned), low(per_tile),
        full((PIECES, 2 * tiles, 1, PIECE)),
        low(flat), low(flat), full((PIECES, PIECE, 1)), full((PIECES, PIECE, 1)),
        low(flat_turned), low(flat_turned), low(flat_turned), low(flat_turned),
        low(wide), low(wide), low((tiles, PIECE, LANES)),
        full((PIECES, 2 * tiles, PIECE, LANES)),
        full((WINDOW, PIECE, PIECE)), low(flat), pltpu.VMEM((PIECES, 1, PIECE), jnp.int32),
        low(flat), low((PIECES, 2, PIECE, LANES)), low(flat), low((PIECES, 2, PIECE, LANES)),
        low((3, PIECE, width)), low((PIECES + 2, PIECE, width)),
        dma(2, PIECES), dma(2, PIECES), dma(2, PIECES), dma(2, PIECES + 2), dma(2, PIECES),
        dma(2, PIECES), dma(4 + PIECES),
    ]
    if inside:
        out_shape.append(jax.ShapeDtypeStruct((8, rows_own, 2 * LANES), LOW))
        out_specs.append(vmem)
        scratch += [
            low((2, width, columns)), full((depth, 8, -(-rows_own // LANES) * LANES)),
            low((2, width, columns)), low((width, columns)), low((depth - 1, rows_own, columns)),
            full((8, width)), full((depth - 1, 8, width)),
            dma(2, PARTS + 1, depth - 1, 2), dma(2, PARTS, depth), dma(2, depth), dma(2, 9),
            dma(2, 9, 3), dma(2, 2, 4), dma(2, depth), dma(2, 7),
        ]
    return pl.pallas_call(
        functools.partial(layers_kernel, width, depth, inside),
        out_shape=out_shape,
        in_specs=[smem, anywhere, vmem] + [anywhere if inside else vmem] * len(weights),
        out_specs=out_specs,
        scratch_shapes=scratch,
        compiler_params=pltpu.CompilerParams(
            collective_id=0, has_side_effects=True, vmem_limit_bytes=63 << 20),
        name="layers",
    )(lengths, x_rows, gains, *weights)


def pack(w_qk, w_value, w_out):
    query, key, out_t = w_qk[:, 0], w_qk[:, 1], w_out.T
    edge = 2 * HEAD
    return jnp.concatenate(
        [query[:, :edge], key[:, :edge], w_value[:, :edge], out_t[:, :edge],
         query[:, edge:], key[:, edge:], w_value[:, edge:], out_t[:, edge:]],
        axis=1)


def unpack(packed):
    edge = 2 * HEAD
    cut = lambda spot, size: packed[:, spot:spot + size]
    query = jnp.concatenate([cut(0, edge), cut(4 * edge, HEAD)], axis=1)
    key = jnp.concatenate([cut(edge, edge), cut(4 * edge + HEAD, HEAD)], axis=1)
    value = jnp.concatenate([cut(2 * edge, edge), cut(5 * edge, HEAD)], axis=1)
    out_t = jnp.concatenate([cut(3 * edge, edge), cut(5 * edge + HEAD, HEAD)], axis=1)
    hidden = packed.shape[1] // 3
    return (
        jnp.stack([query, key], axis=1), value, out_t.T,
        cut(hidden, hidden), cut(2 * hidden, hidden).T)


def shards(
    ends_in, seq_lengths, norm_gains, qk_weight, value_weight, out_weight, fc_weight, proj_weight
):
    section = lax.axis_index("section")
    lane_y = lax.axis_index("y")
    group = 2 * lane_y + lax.axis_index("core")
    first = section == 0
    cols = qk_weight.shape[3]
    width = ends_in.shape[2]
    fresh = (value_weight.shape[1] - width) // cols
    offset = jnp.where(first, group, width // cols + jnp.minimum(group, fresh - 1)) * cols
    w_value = lax.dynamic_slice_in_dim(value_weight, offset, cols, 1)
    parts = [pack(qk_weight[0], w_value, out_weight[0]), fc_weight[0], proj_weight[0].T]
    depth = lax.axis_size("dp")
    inside = depth == 4 and width % (16 * depth) == 0
    if inside:
        weights = parts
        gains = norm_gains[0].T
    else:
        weights = lax.all_gather(jnp.concatenate(parts, axis=1), "dp", axis=0, tiled=True)
        weights = [lax.all_gather(weights, "y", axis=0)]
        gains = lax.all_gather(norm_gains[0], "dp", axis=0, tiled=True).astype(F32).T
    x_rows = ends_in[0].reshape(2, PIECES, PIECE, width)
    kept = width // cols + fresh
    edge = 2 * HEAD
    results = run_layers(seq_lengths, x_rows, gains, weights, depth, inside)
    both = results[0].reshape(2 * MB_TOK, width)
    if inside:
        _, grads, gain_grads, values = results
        rows_own = width // depth
        gain_rows = lax.dynamic_slice_in_dim(
            gain_grads[:2], lax.axis_index("dp") * rows_own, rows_own, 1).T
        values = values[:, :, :cols]
    else:
        _, grads, gain_grads = results
        grads = lax.psum_scatter(grads, "y", scatter_dimension=0, tiled=False)
        grads = lax.psum_scatter(grads, "dp", scatter_dimension=0, tiled=True)
        gain_rows = lax.psum(gain_grads[:2], "y").T
        gain_rows = lax.psum_scatter(gain_rows, "dp", scatter_dimension=0, tiled=True)
        values = lax.all_gather(
            unpack(grads)[1].astype(LOW), ("section", "y", "core"), axis=0)
    d_qk, _, d_out, d_up, d_down = unpack(grads.astype(F32))
    d_value = jnp.concatenate([values[index] for index in range(kept)], axis=1).astype(F32)
    return (
        both[None], gain_rows[:, 0][None], gain_rows[:, 1][None], d_qk[None], d_value,
        d_out[None], d_up[None], d_down[None])


def solution(mesh):
    sections, depth, split = (mesh.shape[name] for name in ("section", "dp", "mp"))
    grid = Mesh(mesh.devices.reshape(sections, depth, split // 2, 2), ("section", "dp", "y", "core"))
    mp = ("y", "core")
    in_specs = (
        P("section", "dp", None),
        P("dp", None),
        P("section", "dp", None),
        P("section", "dp", None, mp),
        P("dp", None),
        P("section", mp, "dp"),
        P("section", "dp", mp),
        P("section", mp, "dp"),
    )
    out_specs = (
        P("section", "dp", None),
        P("section", "dp"),
        P("section", "dp"),
        P("section", "dp", None, mp),
        P("dp", None),
        P("section", mp, "dp"),
        P("section", "dp", mp),
        P("section", mp, "dp"),
    )
    return jax.shard_map(shards, mesh=grid, in_specs=in_specs, out_specs=out_specs, check_vma=False)
```

```python
import functools
import math

import jax
import jax.numpy as jnp
from jax import lax
from jax.experimental import pallas as pl
from jax.experimental.pallas import tpu as pltpu
from jax.sharding import Mesh, PartitionSpec as P

HEAD = 64
MB_TOK = 1024
PIECE = 256
PIECES = MB_TOK // PIECE
WINDOW = 3
PARTS = 6
LANES = 128
EPSILON = 1e-05
GELU_K = math.sqrt(2.0 / math.pi)
GELU_C = 0.044715
MESH = pl.DeviceIdType.MESH
F32 = jnp.float32
LOW = jnp.bfloat16


def mm(left, right):
    return lax.dot_general(left, right, (((1,), (0,)), ((), ())), preferred_element_type=F32)


def mm_back(left, right):
    return lax.dot_general(left, right, (((1,), (1,)), ((), ())), preferred_element_type=F32)


def normalize(rows):
    centred = rows - jnp.mean(rows, axis=1, keepdims=True)
    factor = lax.rsqrt(jnp.mean(centred * centred, axis=1, keepdims=True) + EPSILON)
    return centred * factor, factor


def norm_back(grad, plain, factor, gain):
    scaled = grad * gain
    return factor * (
        scaled
        - jnp.mean(scaled, axis=1, keepdims=True)
        - plain * jnp.mean(scaled * plain, axis=1, keepdims=True)
    )


def flip(tile):
    return pltpu.roll(tile, HEAD, 1)


def layers_kernel(width, depth, inside, *refs):
    refs = list(refs)
    take = lambda count: [refs.pop(0) for _ in range(count)]
    length_ref, x_all, gain_ref = take(3)
    part_refs = take(3 if inside else 1)
    out_ref, grad_ref, gain_grad_ref = take(3)
    if inside:
        (value_ref,) = take(1)
    (wa, q_s, k_s, v_s, turn_s, o_s, lse_s, plain1, plain2, fac1, fac2,
     a_t, m_t, g_t, h_t, e_s, gd_s, do_s, spare, bias_s, x_ref, start_s,
     there, there_v, here, here_v, swap_out, swap_in,
     sem_x, sem_v, sem_f, sem_c, sem_o, sem_oc, sem_l) = take(35)
    if inside:
        (w_ref, gain_all, sums, y_in, z_in, gain_y, gain_z,
         sem_az, sem_ay, sem_gz, sem_ry, sem_rz, sem_rm, sem_gg, sem_va) = take(15)
    else:
        w_ref, sums = part_refs[0], grad_ref

    section = lax.axis_index("section")
    core = lax.axis_index("core")
    lane_y = lax.axis_index("y")
    deep = lax.axis_index("dp")
    other_layer = {"section": 1 - section}
    other_core = {"core": 1 - core}
    other_y = {"y": 1 - lane_y}
    first = section == 0
    second = jnp.logical_not(first)
    tiles = width // 2 // LANES
    hidden = width
    rows_own = width // depth
    half_cols = width // 2

    def send(src, dst, sems, index, target):
        return pltpu.make_async_remote_copy(
            src_ref=src, dst_ref=dst, send_sem=sems.at[(0,) + index], recv_sem=sems.at[(1,) + index],
            device_id=target, device_id_type=MESH)

    def peer(step):
        return {"dp": lax.rem(deep + step, depth)}

    barrier = pltpu.get_barrier_semaphore()
    friends = [other_layer, other_core, other_y]
    if inside:
        friends = friends + [peer(step) for step in range(1, depth)]
        twin = {"dp": deep + 1 - 2 * lax.rem(deep, 2)}
    for friend in friends:
        pl.semaphore_signal(barrier, inc=1, device_id=friend, device_id_type=MESH)
    pl.semaphore_wait(barrier, len(friends))

    lane = lax.broadcasted_iota(jnp.int32, (1, LANES), 1)
    low_half = lane < HEAD

    def rows_at(place):
        return pl.ds(pl.multiple_of(place * rows_own, rows_own), rows_own)

    unit = 3 * hidden // PARTS
    per_ref = PARTS // 3
    ways = (1, -1)
    mixed_part = PARTS - 1

    def cols_at(part):
        return pl.ds(part * unit, unit)

    def on_line(place):
        return jnp.logical_and(place >= 0, place < depth)

    def own_part(part):
        return part_refs[part // per_ref].at[:, pl.ds(part % per_ref * unit, unit)]

    def own_copy(index):
        return pltpu.make_async_copy(
            part_refs[index], w_ref.at[lane_y, rows_at(deep), pl.ds(index * hidden, hidden)],
            sem_l.at[PIECES + index])

    def gather_line(part, row, hop, way):
        place = deep - hop * ways[way]
        home = lane_y if row == 0 else 1 - lane_y
        spot = w_ref.at[home, rows_at(place), cols_at(part)]
        src = own_part(part) if row == 0 and hop == 0 else spot
        return send(src, spot, sem_az, (part + row, hop, way), {"dp": deep + ways[way]})

    def line_start(part, row, hop, way):
        @pl.when(jnp.logical_and(on_line(deep - hop * ways[way]), on_line(deep + ways[way])))
        def _():
            gather_line(part, row, hop, way).start()

    def line_sent(part, row, hop, way):
        @pl.when(jnp.logical_and(on_line(deep - hop * ways[way]), on_line(deep + ways[way])))
        def _():
            gather_line(part, row, hop, way).wait_send()

    def gather_y(part, place, own):
        spot = w_ref.at[lane_y, rows_at(place), cols_at(part)]
        src = own_part(part) if own else spot
        return send(src, spot, sem_ay, (part, place), other_y)

    def gather_gain(step):
        return send(gain_all.at[deep], gain_all.at[deep], sem_gz, (step,), peer(step))

    def gather_start(part):
        for way in range(2):
            line_start(part, 0, 0, way)
        if part != mixed_part:
            gather_y(part, deep, True).start()

    def gather_pass(part, row=0, hops=None):
        for hop in range(depth - 1) if hops is None else hops:
            for way in range(2):
                place = deep - (hop + 1) * ways[way]

                @pl.when(on_line(place))
                def _(hop=hop, way=way, place=place):
                    gather_line(part, row, hop, way).wait_recv()
                    if hop < depth - 2:
                        line_start(part, row, hop + 1, way)
                    if part != mixed_part:
                        gather_y(part, place, False).start()

    def gather_cross():
        gather_y(mixed_part, deep, True).wait()
        for way in range(2):
            line_start(mixed_part, 1, 0, way)

    def gather_end(part):
        if part != mixed_part:
            for place in range(depth):
                gather_y(part, place, False).wait()
        for row in range(2 if part == mixed_part else 1):
            for hop in range(depth - 1):
                for way in range(2):
                    line_sent(part, row, hop, way)

    block = 2 * LANES
    last = block // 2
    spans = [
        (2 * hidden, block), (hidden, block), (hidden + block, block),
        (block, block), (2 * block, block), (0, block),
        (hidden + 2 * block, last), (hidden + 2 * block + last, last)]
    mixed_at = pl.ds(2 * hidden + block, 2 * block)

    def block_at(index):
        return pl.ds(spans[index][0], spans[index][1])

    def reduce_y(index):
        return send(sums.at[1 - lane_y, :, block_at(index)], y_in.at[:, block_at(index)],
                    sem_ry, (index,), other_y)

    def share_of(near, index):
        own = lax.rem(deep, 2)
        return rows_at((own if near else 1 - own) + 2 * index)

    def reduce_near(index, share):
        at = block_at(index)
        return send(sums.at[lane_y, share_of(False, share), at], z_in.at[share, :, at],
                    sem_rz, (index, share), twin)

    def reduce_far(index):
        at = block_at(index)
        return send(sums.at[lane_y, rows_at(lax.rem(deep + 2, depth)), at], z_in.at[2, :, at],
                    sem_rz, (index, 2), peer(2))

    def reduce_mid(index, following=None):
        reduce_y(index).wait_recv()
        if following is not None:
            reduce_y(following).start()
        at = block_at(index)
        sums[lane_y, :, at] = (
            sums[lane_y, :, at].astype(F32) + y_in[:, at].astype(F32)).astype(LOW)
        for share in range(2):
            reduce_near(index, share).start()

    def reduce_late(index):
        at = block_at(index)
        for share in range(2):
            reduce_near(index, share).wait_recv()
            rows = share_of(True, share)
            sums[lane_y, rows, at] = (
                sums[lane_y, rows, at].astype(F32) + z_in[share, :, at].astype(F32)).astype(LOW)
        reduce_far(index).start()

    def reduce_end(index):
        at = block_at(index)
        reduce_far(index).wait_recv()
        grad_ref[:, at] = (
            sums[lane_y, rows_at(deep), at].astype(F32) + z_in[2, :, at].astype(F32))

    def mixed_home(row, share):
        if row == 0:
            return z_in.at[share, :, mixed_at]
        return y_in.at[rows_at(share), mixed_at]

    def mixed_group(row):
        return lane_y if row == 0 else 1 - lane_y

    def mixed_near(row, share):
        return send(sums.at[mixed_group(row), share_of(False, share), mixed_at],
                    mixed_home(row, share), sem_rm, (row, share), twin)

    def mixed_far(row):
        return send(sums.at[mixed_group(row), rows_at(lax.rem(deep + 2, depth)), mixed_at],
                    mixed_home(row, 2), sem_rm, (row, 2), peer(2))

    def mixed_cross():
        return send(sums.at[1 - lane_y, rows_at(deep), mixed_at], mixed_home(1, 3),
                    sem_rm, (1, 3), other_y)

    def mixed_start():
        for row in range(2):
            for share in range(2):
                mixed_near(row, share).start()

    def mixed_mid():
        for row in range(2):
            for share in range(2):
                mixed_near(row, share).wait_recv()
                rows = share_of(True, share)
                group = mixed_group(row)
                sums[group, rows, mixed_at] = (
                    sums[group, rows, mixed_at].astype(F32)
                    + mixed_home(row, share)[...].astype(F32)).astype(LOW)
            mixed_far(row).start()

    def mixed_late():
        for row in range(2):
            mixed_far(row).wait_recv()
            total = (sums[mixed_group(row), rows_at(deep), mixed_at].astype(F32)
                     + mixed_home(row, 2)[...].astype(F32))
            if row == 0:
                grad_ref[:, mixed_at] = total
            else:
                sums[mixed_group(row), rows_at(deep), mixed_at] = total.astype(LOW)
        mixed_cross().start()

    def mixed_end():
        mixed_cross().wait_recv()
        grad_ref[:, mixed_at] += mixed_home(1, 3)[...].astype(F32)

    def reduce_sent():
        for index in range(len(spans)):
            reduce_y(index).wait_send()
            for share in range(2):
                reduce_near(index, share).wait_send()
            reduce_far(index).wait_send()
        for row in range(2):
            for share in range(2):
                mixed_near(row, share).wait_send()
            mixed_far(row).wait_send()
        mixed_cross().wait_send()

    def halves(tile):
        return [jnp.where(low_half, tile, jnp.zeros_like(tile)),
                jnp.where(low_half, jnp.zeros_like(tile), tile)]

    def group_tile(group, index):
        return w_ref[group, :, index * LANES:(index + 1) * LANES]

    qkv_cols = 3 * tiles * LANES

    def arrange():
        for kind in range(4):
            for group in range(2):
                spot = (kind * tiles + group) * LANES
                wa[:, spot:spot + LANES] = group_tile(group, kind)
        for pair in range(2):
            one, two = (group_tile(group, 4 + pair).astype(F32) for group in range(2))
            spot = (2 * pair * tiles + 2) * LANES
            wa[:, spot:spot + LANES] = jnp.where(low_half, one, flip(two)).astype(LOW)
            spot = ((2 * pair + 1) * tiles + 2) * LANES
            wa[:, spot:spot + LANES] = jnp.where(low_half, flip(one), two).astype(LOW)

    x_copy = pltpu.make_async_copy(x_all.at[lane_y], x_ref, sem_l.at[PIECES + 3])
    if inside:
        gather_start(0)
        gather_start(1)
        gather_y(mixed_part, deep, True).start()
        gain_all[deep, 0:2, 0:rows_own] = gain_ref[...].astype(F32)
        for step in range(1, depth):
            gather_gain(step).start()
        for index in range(3):
            own_copy(index).start()
    x_copy.start()

    for piece in range(PIECES):
        place = piece * PIECE + lax.broadcasted_iota(jnp.int32, (1, PIECE), 1)
        begin = jnp.zeros((1, PIECE), jnp.int32)
        end = 0
        for index in range(length_ref.shape[1]):
            end = end + length_ref[lane_y, index]
            begin = jnp.where(place >= end, end, begin)
        start_s[piece] = begin

    if inside:
        gather_pass(0)
        gather_start(2)
        gather_pass(1)
        gather_start(3)
        gather_pass(2, 0, [0, 1])
        gather_start(4)
        for step in range(1, depth):
            gather_gain(step).wait()
        gather_end(0)
        gather_end(1)
        gather_pass(2, 0, [2])
        gather_pass(3, 0, [0])
        for index in range(3):
            own_copy(index).wait()
        gains = jnp.concatenate([gain_all[place, :, :rows_own] for place in range(depth)], axis=1)
    else:
        gains = gain_ref[...]
    arrange()
    x_copy.wait()
    gain1 = gains[0:1, :]
    gain2 = gains[1:2, :]

    def swap_copy(leave, enter):
        return send(swap_out.at[leave], swap_in.at[enter], sem_c, (enter,), other_core)

    def swap_start(slots, value):
        swap_out[slots[0]] = value
        swap_copy(*slots).start()

    def swap_end(slots):
        swap_copy(*slots).wait()
        return swap_out[slots[0]].astype(F32) + swap_in[slots[1]].astype(F32)

    def first_slots(piece):
        return lax.rem(piece, 2), piece

    def turned_slots(piece):
        return lax.rem(piece, 2), lax.rem(piece + 2, PIECES)

    def second_slots(piece):
        return 2, PIECES + lax.rem(piece, 2)

    def last_slots(piece):
        return 2, PIECES + lax.rem(piece + 1, 2)

    def put_rows(piece, rows):
        for t in range(2 * tiles):
            spare[piece, t] = rows[:, t * LANES:(t + 1) * LANES]

    def get_rows(piece):
        return jnp.concatenate([spare[piece, t] for t in range(2 * tiles)], axis=1)

    def joined(*stores):
        return jnp.concatenate([store[t] for store in stores for t in range(tiles)], axis=1)

    half = pl.ds(pl.multiple_of(core * half_cols, half_cols), half_cols)

    def hand_rows(piece):
        return send(there.at[piece, :, half], here.at[piece, :, half], sem_x, (piece,), other_layer)

    def hand_values(piece):
        return send(there_v.at[piece], here_v.at[piece], sem_v, (piece,), other_layer)

    def hand_on(piece):
        return send(here.at[piece, :, half], here.at[piece, :, half], sem_f, (piece,), other_core)

    def take_start(piece):
        hand_rows(piece).wait_recv()
        hand_on(piece).start()

    def take_values(piece):
        hand_values(piece).wait_recv()

    def emit_here(piece, stage):
        return pltpu.make_async_copy(stage.at[piece], out_ref.at[lane_y, piece], sem_l.at[piece])

    def emit_there(piece, stage):
        return send(stage.at[piece, :, half], out_ref.at[lane_y, piece, :, half],
                    sem_o, (piece,), other_y)

    def emit(piece, stage):
        return [emit_here(piece, stage), emit_there(piece, stage)]

    def emit_on(piece):
        spot = out_ref.at[1 - lane_y, piece, :, half]
        return send(spot, spot, sem_oc, (piece,), other_core)

    def reused(tile_index):
        if tile_index == 0:
            return None
        if tile_index == 1:
            return jnp.logical_and(second, lane >= 0)
        return jnp.logical_and(second, lane >= HEAD)

    def make_bias(piece, count):
        base = piece * PIECE
        query = base + lax.broadcasted_iota(jnp.int32, (1, PIECE), 1)
        begin = start_s[piece]
        for j in range(count):
            key = base - (count - 1 - j) * PIECE + lax.broadcasted_iota(jnp.int32, (PIECE, 1), 0)
            fine = jnp.logical_and(key >= begin, key <= query)
            bias_s[j] = jnp.where(fine, 0.0, -1e30).astype(F32)

    def attend(piece, count):
        make_bias(piece, count)
        for t in range(tiles):
            parts = []
            for h, query in enumerate(halves(q_s[piece, t])):
                scores = [
                    mm_back(k_s[piece - (count - 1 - j), t], query) + bias_s[j] for j in range(count)
                ]
                top = functools.reduce(
                    jnp.maximum, [jnp.max(s, axis=0, keepdims=True) for s in scores])
                expo = [jnp.exp(s - top) for s in scores]
                total = functools.reduce(
                    jnp.add, [jnp.sum(e, axis=0, keepdims=True) for e in expo])
                mixed = functools.reduce(jnp.add, [
                    mm(turn_s[piece - (count - 1 - j), t, h * HEAD:(h + 1) * HEAD, :], e.astype(LOW))
                    for j, e in enumerate(expo)
                ])
                parts.append(mixed * (1.0 / total))
                lse_s[piece, 2 * t + h] = top + jnp.log(total)
            o_s[piece, t] = jnp.concatenate(parts, axis=0).T.astype(LOW)

    def attend_back(piece, count):
        make_bias(piece, count)
        for t in range(tiles):
            inner = (do_s[t].astype(F32) * o_s[piece, t].astype(F32)).T
            queries = halves(q_s[piece, t])
            grads = halves(do_s[t])
            dq = [0.0, 0.0]
            inners = [jnp.sum(inner[h * HEAD:(h + 1) * HEAD], axis=0, keepdims=True) for h in range(2)]
            for j in range(count):
                at = piece - (count - 1 - j)
                dk_new, dv_new = 0.0, 0.0
                for h in range(2):
                    probs = jnp.exp(
                        mm_back(k_s[at, t], queries[h]) + bias_s[j] - lse_s[piece, 2 * t + h])
                    dprobs = mm_back(v_s[at, t], grads[h])
                    dscores = (probs * (dprobs - inners[h])).astype(LOW)
                    dv_new = dv_new + mm(probs.astype(LOW), grads[h])
                    dk_new = dk_new + mm(dscores, queries[h])
                    dq[h] = dq[h] + mm(turn_s[at, t, h * HEAD:(h + 1) * HEAD, :], dscores)
                spare[at, t] += dk_new
                spare[at, tiles + t] += dv_new
            dq_t = jnp.concatenate(dq, axis=0) * 0.125
            q_s[piece, t] = dq_t.T.astype(LOW)

    def by_count(piece, run):
        for count in range(1, WINDOW + 1):
            fits = piece >= WINDOW - 1 if count == WINDOW else piece == count - 1

            @pl.when(fits)
            def _(count=count):
                run(piece, count)

    def forward_attention(piece):
        @pl.when(second)
        def _():
            @pl.when(piece < 2)
            def _():
                take_start(piece)

            hand_on(piece).wait()

        rows = jnp.where(first, x_ref[piece], here[piece]).astype(F32)
        plain, factor = normalize(rows)
        plain1[piece] = plain.astype(LOW)
        fac1[piece] = factor
        normed = plain * gain1
        a_t[piece] = normed.T.astype(LOW)
        qkv = mm(normed.astype(LOW), wa[:, :qkv_cols])

        @pl.when(second)
        def _():
            take_values(piece)

        for t in range(tiles):
            q_s[piece, t] = (qkv[:, t * LANES:(t + 1) * LANES].astype(LOW) * 0.125).astype(LOW)
            key = qkv[:, (tiles + t) * LANES:(tiles + t + 1) * LANES].astype(LOW)
            value = qkv[:, (2 * tiles + t) * LANES:(2 * tiles + t + 1) * LANES].astype(LOW)
            mask = reused(t)
            if mask is not None:
                value = jnp.where(mask, here_v[piece, t - 1], value)
                there_v[piece, t - 1] = value
            k_s[piece, t] = key
            v_s[piece, t] = value
            turn_s[piece, t] = value.astype(F32).T.astype(LOW)

        @pl.when(first)
        def _():
            hand_values(piece).start()

        by_count(piece, attend)
        put_rows(piece, rows)
        swap_start(first_slots(piece), mm_back(joined(o_s.at[piece]), wa[:, qkv_cols:]).astype(LOW))

    def forward_middle(piece):
        put_rows(piece, get_rows(piece) + swap_end(first_slots(piece)))

    def forward_spread(piece):
        plain, factor = normalize(get_rows(piece))
        plain2[piece] = plain.astype(LOW)
        fac2[piece] = factor
        normed = plain * gain2
        m_t[piece] = normed.T.astype(LOW)
        normed = normed.astype(LOW)
        for group in range(2):
            z = mm(normed, w_ref[group, :, hidden:2 * hidden])
            square = z * z
            bent = jnp.tanh(GELU_K * z * (1.0 + GELU_C * square))
            upper = 0.5 * (1.0 + bent)
            slope = upper + 0.5 * z * (1.0 - bent * bent) * (GELU_K * (1.0 + 3.0 * GELU_C * square))
            gd_s[piece, group] = slope.astype(LOW)
            e_s[piece, group] = (z * upper).astype(LOW)

    def forward_fold(piece):
        total = 0.0
        for group in range(2):
            total = total + mm_back(e_s[piece, group], w_ref[group, :, 2 * hidden:])
        swap_start(second_slots(piece), total.astype(LOW))

    def forward_result(piece):
        result = (get_rows(piece) + swap_end(second_slots(piece))).astype(LOW)

        @pl.when(first)
        def _():
            there[piece] = result
            hand_rows(piece).start()

        @pl.when(second)
        def _():
            here[piece] = result
            for copy in emit(piece, here):
                copy.start()

    def within(step, low_end, high_end):
        return jnp.logical_and(step >= low_end, step < high_end)

    lag = jnp.where(first, 0, 2 * PIECES)

    def forward(step, carry):
        place = step - lag

        @pl.when(within(place, 0, PIECES))
        def _():
            forward_attention(place)

        if inside:
            @pl.when(step == 0)
            def _():
                gather_pass(3, 0, [1])
                gather_start(5)
                gather_cross()

            @pl.when(step == 1)
            def _():
                gather_pass(3, 0, [2])
                gather_pass(4, 0, [0])

            @pl.when(step == 2)
            def _():
                gather_pass(4, 0, [1])
                gather_pass(5, 0, [0])
                gather_pass(5, 1, [0])

            @pl.when(step == 3)
            def _():
                gather_pass(4, 0, [2])
                gather_pass(5, 0, [1])
                gather_pass(5, 1, [1])
                gather_end(2)
                gather_end(3)

            @pl.when(step == 2 * PIECES - 2)
            def _():
                gather_pass(5, 0, [2])
                gather_pass(5, 1, [2])

            @pl.when(step == 2 * PIECES - 1)
            def _():
                gather_end(4)
                gather_end(5)

        @pl.when(jnp.logical_and(second, within(place, 2, PIECES + 1)))
        def _():
            forward_result(place - 2)

        @pl.when(within(place, 1, PIECES + 1))
        def _():
            forward_middle(place - 1)

        spread_place = place - jnp.where(first, PIECES, 1)

        @pl.when(within(spread_place, 0, PIECES))
        def _():
            forward_spread(spread_place)

        fold_place = place - jnp.where(first, 2 * PIECES, 1)

        @pl.when(within(fold_place, 0, PIECES))
        def _():
            @pl.when(jnp.logical_and(second, fold_place < PIECES - 2))
            def _():
                take_start(fold_place + 2)

            forward_fold(fold_place)

            @pl.when(first)
            def _():
                forward_result(fold_place)

        return carry

    lax.fori_loop(0, 3 * PIECES + 1, forward, 0)

    @pl.when(first)
    def _():
        for piece in range(PIECES):
            hand_rows(piece).wait_send()
            hand_values(piece).wait_send()

    gain_grad_ref[...] = jnp.zeros_like(gain_grad_ref)

    def hidden_grads(left, right, base):
        def one(index, carry):
            group, column = index // (hidden // block), index % (hidden // block)
            spot = pl.multiple_of(column * block, block)
            total = 0.0
            for piece in range(PIECES):
                total = total + mm(left[piece], right[piece, group, :, pl.ds(spot, block)])
            sums[group, :, pl.ds(pl.multiple_of(base + spot, block), block)] = total.astype(LOW)
            return carry

        lax.fori_loop(0, 2 * (hidden // block), one, 0)

    def head_grads():
        pairs = []
        for kind in range(4):
            total = 0.0
            for piece in range(PIECES):
                if kind < 3:
                    total = total + mm(a_t[piece], joined((q_s, k_s, v_s)[kind].at[piece]))
                else:
                    total = total + mm(h_t[piece], joined(o_s.at[piece]))
            for group in range(2):
                part = total[:, group * LANES:(group + 1) * LANES].astype(LOW)
                sums[group, :, kind * LANES:(kind + 1) * LANES] = part
            pairs.append(total[:, 2 * LANES:])
        for pair in range(2):
            one, two = pairs[2 * pair:2 * pair + 2]
            spot = (4 + pair) * LANES
            sums[0, :, spot:spot + LANES] = jnp.where(low_half, one, flip(two)).astype(LOW)
            sums[1, :, spot:spot + LANES] = jnp.where(low_half, flip(one), two).astype(LOW)

    def down_grads():
        hidden_grads(g_t, e_s, 2 * hidden)
        if inside:
            reduce_y(0).start()
            mixed_start()

    def up_grads():
        hidden_grads(m_t, gd_s, hidden)
        if inside:
            reduce_y(1).start()
            reduce_y(2).start()

    def grad_rows(piece):
        return jnp.where(first, here[piece], x_ref[piece])

    def backward_hidden(piece):
        @pl.when(first)
        def _():
            take_start(piece)
            hand_on(piece).wait()

        grad_low = grad_rows(piece)
        g_t[piece] = grad_low.astype(F32).T.astype(LOW)

        @pl.when(jnp.logical_and(first, piece == 0))
        def _():
            down_grads()

        total = 0.0
        for group in range(2):
            dz = mm(grad_low, w_ref[group, :, 2 * hidden:]) * gd_s[piece, group].astype(F32)
            dz = dz.astype(LOW)
            gd_s[piece, group] = dz
            total = total + mm_back(dz, w_ref[group, :, hidden:2 * hidden])
        swap_start(turned_slots(piece), total.astype(LOW))

        @pl.when(jnp.logical_and(first, piece == 0))
        def _():
            up_grads()

    def backward_attention(piece):
        dm = swap_end(turned_slots(piece))
        plain = plain2[piece].astype(F32)
        gain_grad_ref[1:2, :] += jnp.sum(dm * plain, axis=0, keepdims=True)
        middle = grad_rows(piece).astype(F32) + norm_back(dm, plain, fac2[piece], gain2)
        h_t[piece] = middle.T.astype(LOW)
        dmixed = mm(middle.astype(LOW), wa[:, qkv_cols:]).astype(LOW)
        for t in range(tiles):
            do_s[t] = dmixed[:, t * LANES:(t + 1) * LANES]
        by_count(piece, attend_back)
        for t in range(1, tiles):
            there_v[piece, t - 1] = spare[piece, tiles + t].astype(LOW)

        @pl.when(first)
        def _():
            hand_values(piece).wait_recv()

        @pl.when(second)
        def _():
            hand_values(piece).start()

        for t in range(tiles):
            dvalue = spare[piece, tiles + t]
            mask = reused(t)
            if mask is not None:
                came = jnp.logical_and(first, jnp.logical_or(t == 1, lane >= HEAD))
                dvalue = jnp.where(came, dvalue + here_v[piece, t - 1].astype(F32), dvalue)
                dvalue = jnp.where(mask, 0.0, dvalue)
            k_s[piece, t] = spare[piece, t].astype(LOW)
            v_s[piece, t] = dvalue.astype(LOW)
        put_rows(piece, middle)
        terms = joined(q_s.at[piece], k_s.at[piece], v_s.at[piece])
        swap_start(last_slots(piece), mm_back(terms, wa[:, :qkv_cols]).astype(LOW))

    def backward_result(piece):
        da = swap_end(last_slots(piece))
        plain = plain1[piece].astype(F32)
        gain_grad_ref[0:1, :] += jnp.sum(da * plain, axis=0, keepdims=True)
        there[piece] = (get_rows(piece) + norm_back(da, plain, fac1[piece], gain1)).astype(LOW)

        @pl.when(second)
        def _():
            hand_rows(piece).start()

        @pl.when(first)
        def _():
            for copy in emit(piece, there):
                copy.start()

    def backward(step, carry):
        turn = step // 2
        even = lax.rem(step, 2) == 0

        @pl.when(jnp.logical_and(jnp.logical_xor(even, first), turn < PIECES))
        def _():
            backward_hidden(PIECES - 1 - turn)

        @pl.when(step == 0)
        def _():
            @pl.when(second)
            def _():
                forward_result(PIECES - 1)

            spare[...] = jnp.zeros_like(spare)
            for piece in range(PIECES):
                for t in range(tiles):
                    turn_s[piece, t] = k_s[piece, t].astype(F32).T.astype(LOW)

        @pl.when(jnp.logical_and(jnp.logical_xor(even, second), turn >= 1))
        def _():
            @pl.when(turn >= 2)
            def _():
                backward_result(PIECES + 1 - turn)

            backward_attention(PIECES - turn)

        return carry

    lax.fori_loop(0, 2 * PIECES + 2, backward, 0)
    backward_result(0)

    @pl.when(second)
    def _():
        down_grads()
        up_grads()

    head_grads()

    def emit_stage(run):
        @pl.when(first)
        def _():
            run(there)

        @pl.when(second)
        def _():
            run(here)

    def pass_outputs(stage):
        for piece in range(PIECES):
            emit_there(piece, stage).wait_recv()
            emit_on(piece).start()

    def finish_outputs(stage):
        for piece in range(PIECES):
            emit_here(piece, stage).wait()
            emit_there(piece, stage).wait_send()
            emit_on(piece).wait()

    if inside:
        gain_copy = send(gain_grad_ref, gain_y, sem_gg, (0,), other_y)
        gain_copy.start()
        reduce_y(3).start()
        mixed_mid()
        reduce_mid(0, 4)
        gain_copy.wait()
        gain_y[...] = gain_y[...] + gain_grad_ref[...]
        gain_sends = [
            send(gain_y, gain_z.at[step - 1], sem_gg, (step,), peer(step)) for step in range(1, depth)]
        for copy in gain_sends:
            copy.start()
        reduce_mid(1)
        reduce_late(0)
        reduce_mid(2, 5)
        mixed_late()
        reduce_late(1)
        reduce_mid(3, 6)
        reduce_end(0)
        reduce_late(2)
        reduce_mid(4, 7)
        reduce_end(1)
        reduce_late(3)
        reduce_end(2)
        total = gain_y[...]
        for step, copy in enumerate(gain_sends):
            copy.wait()
            total = total + gain_z[step]
        gain_grad_ref[...] = total
        reduce_mid(5)
        reduce_late(4)
        reduce_end(3)
        emit_stage(pass_outputs)
        reduce_mid(6)
        reduce_late(5)
        reduce_end(4)

        def place(sec, row, unit):
            return (sec * 2 + row) * 2 + unit

        mine = place(section, lane_y, core)
        for half_tile, tile_index in enumerate((2, 5)):
            value_ref[mine, :, half_tile * LANES:(half_tile + 1) * LANES] = (
                grad_ref[:, tile_index * LANES:(tile_index + 1) * LANES].astype(LOW))
        value_x = send(value_ref.at[mine], value_ref.at[mine], sem_va, (0,), other_layer)
        value_x.start()
        mixed_end()
        reduce_mid(7)
        reduce_late(6)
        reduce_end(5)
        value_x.wait()
        value_y = []
        for sec in range(2):
            at = place(sec, lane_y, core)
            value_y.append(send(value_ref.at[at], value_ref.at[at], sem_va, (1 + sec,), other_y))
            value_y[-1].start()
        reduce_late(7)
        reduce_end(6)
        for copy in value_y:
            copy.wait()
        value_c = []
        for sec in range(2):
            for row in range(2):
                at = place(sec, row, core)
                value_c.append(
                    send(value_ref.at[at], value_ref.at[at], sem_va, (3 + 2 * sec + row,), other_core))
                value_c[-1].start()
        reduce_end(7)
        for copy in value_c:
            copy.wait()
        reduce_sent()
    else:
        emit_stage(pass_outputs)

    emit_stage(finish_outputs)

    @pl.when(second)
    def _():
        for piece in range(PIECES):
            hand_rows(piece).wait_send()
            hand_values(piece).wait_send()


def run_layers(lengths, x_rows, gains, weights, depth, inside):
    width = x_rows.shape[3]
    tiles = width // 2 // LANES
    rows_own = width // depth
    columns = 3 * width
    vmem = pl.BlockSpec(memory_space=pltpu.VMEM)
    anywhere = pl.BlockSpec(memory_space=pl.ANY)
    smem = pl.BlockSpec(memory_space=pltpu.SMEM)
    per_tile = (PIECES, tiles, PIECE, LANES)
    turned = (PIECES, tiles, LANES, PIECE)
    flat = (PIECES, PIECE, width)
    flat_turned = (PIECES, width, PIECE)
    wide = (PIECES, 2, PIECE, width)
    low = lambda shape: pltpu.VMEM(shape, LOW)
    full = lambda shape: pltpu.VMEM(shape, F32)
    dma = lambda *shape: pltpu.SemaphoreType.DMA(shape)
    out_shape = [
        jax.ShapeDtypeStruct((2,) + flat, LOW),
        jax.ShapeDtypeStruct((rows_own, columns), F32) if inside
        else jax.ShapeDtypeStruct(weights[0].shape, LOW),
        jax.ShapeDtypeStruct((8, width), F32),
    ]
    out_specs = [anywhere, vmem, vmem]
    scratch = [
        low((width, 4 * tiles * LANES)),
        low(per_tile), low(per_tile), low(per_tile), low(turned), low(per_tile),
        full((PIECES, 2 * tiles, 1, PIECE)),
        low(flat), low(flat), full((PIECES, PIECE, 1)), full((PIECES, PIECE, 1)),
        low(flat_turned), low(flat_turned), low(flat_turned), low(flat_turned),
        low(wide), low(wide), low((tiles, PIECE, LANES)),
        full((PIECES, 2 * tiles, PIECE, LANES)),
        full((WINDOW, PIECE, PIECE)), low(flat), pltpu.VMEM((PIECES, 1, PIECE), jnp.int32),
        low(flat), low((PIECES, 2, PIECE, LANES)), low(flat), low((PIECES, 2, PIECE, LANES)),
        low((3, PIECE, width)), low((PIECES + 2, PIECE, width)),
        dma(2, PIECES), dma(2, PIECES), dma(2, PIECES), dma(2, PIECES + 2), dma(2, PIECES),
        dma(2, PIECES), dma(4 + PIECES),
    ]
    if inside:
        out_shape.append(jax.ShapeDtypeStruct((8, rows_own, 2 * LANES), LOW))
        out_specs.append(vmem)
        scratch += [
            low((2, width, columns)), full((depth, 8, -(-rows_own // LANES) * LANES)),
            low((2, width, columns)), low((width, columns)), low((depth - 1, rows_own, columns)),
            full((8, width)), full((depth - 1, 8, width)),
            dma(2, PARTS + 1, depth - 1, 2), dma(2, PARTS, depth), dma(2, depth), dma(2, 8),
            dma(2, 8, 3), dma(2, 2, 4), dma(2, depth), dma(2, 7),
        ]
    return pl.pallas_call(
        functools.partial(layers_kernel, width, depth, inside),
        out_shape=out_shape,
        in_specs=[smem, anywhere, vmem] + [anywhere if inside else vmem] * len(weights),
        out_specs=out_specs,
        scratch_shapes=scratch,
        compiler_params=pltpu.CompilerParams(
            collective_id=0, has_side_effects=True, vmem_limit_bytes=63 << 20),
        name="layers",
    )(lengths, x_rows, gains, *weights)


def pack(w_qk, w_value, w_out):
    query, key, out_t = w_qk[:, 0], w_qk[:, 1], w_out.T
    edge = 2 * HEAD
    return jnp.concatenate(
        [query[:, :edge], key[:, :edge], w_value[:, :edge], out_t[:, :edge],
         query[:, edge:], key[:, edge:], w_value[:, edge:], out_t[:, edge:]],
        axis=1)


def unpack(packed):
    edge = 2 * HEAD
    cut = lambda spot, size: packed[:, spot:spot + size]
    query = jnp.concatenate([cut(0, edge), cut(4 * edge, HEAD)], axis=1)
    key = jnp.concatenate([cut(edge, edge), cut(4 * edge + HEAD, HEAD)], axis=1)
    value = jnp.concatenate([cut(2 * edge, edge), cut(5 * edge, HEAD)], axis=1)
    out_t = jnp.concatenate([cut(3 * edge, edge), cut(5 * edge + HEAD, HEAD)], axis=1)
    hidden = packed.shape[1] // 3
    return (
        jnp.stack([query, key], axis=1), value, out_t.T,
        cut(hidden, hidden), cut(2 * hidden, hidden).T)


def shards(
    ends_in, seq_lengths, norm_gains, qk_weight, value_weight, out_weight, fc_weight, proj_weight
):
    section = lax.axis_index("section")
    lane_y = lax.axis_index("y")
    group = 2 * lane_y + lax.axis_index("core")
    first = section == 0
    cols = qk_weight.shape[3]
    width = ends_in.shape[2]
    fresh = (value_weight.shape[1] - width) // cols
    offset = jnp.where(first, group, width // cols + jnp.minimum(group, fresh - 1)) * cols
    w_value = lax.dynamic_slice_in_dim(value_weight, offset, cols, 1)
    parts = [pack(qk_weight[0], w_value, out_weight[0]), fc_weight[0], proj_weight[0].T]
    depth = lax.axis_size("dp")
    inside = depth == 4 and width % (16 * depth) == 0
    if inside:
        weights = parts
        gains = norm_gains[0].T
    else:
        weights = lax.all_gather(jnp.concatenate(parts, axis=1), "dp", axis=0, tiled=True)
        weights = [lax.all_gather(weights, "y", axis=0)]
        gains = lax.all_gather(norm_gains[0], "dp", axis=0, tiled=True).astype(F32).T
    x_rows = ends_in[0].reshape(2, PIECES, PIECE, width)
    kept = width // cols + fresh
    edge = 2 * HEAD
    results = run_layers(seq_lengths, x_rows, gains, weights, depth, inside)
    both = results[0].reshape(2 * MB_TOK, width)
    if inside:
        _, grads, gain_grads, values = results
        rows_own = width // depth
        gain_rows = lax.dynamic_slice_in_dim(
            gain_grads[:2], lax.axis_index("dp") * rows_own, rows_own, 1).T
        values = values[:, :, :cols]
    else:
        _, grads, gain_grads = results
        grads = lax.psum_scatter(grads, "y", scatter_dimension=0, tiled=False)
        grads = lax.psum_scatter(grads, "dp", scatter_dimension=0, tiled=True)
        gain_rows = lax.psum(gain_grads[:2], "y").T
        gain_rows = lax.psum_scatter(gain_rows, "dp", scatter_dimension=0, tiled=True)
        values = lax.all_gather(
            unpack(grads)[1].astype(LOW), ("section", "y", "core"), axis=0)
    d_qk, _, d_out, d_up, d_down = unpack(grads.astype(F32))
    d_value = jnp.concatenate([values[index] for index in range(kept)], axis=1).astype(F32)
    return (
        both[None], gain_rows[:, 0][None], gain_rows[:, 1][None], d_qk[None], d_value,
        d_out[None], d_up[None], d_down[None])


def solution(mesh):
    sections, depth, split = (mesh.shape[name] for name in ("section", "dp", "mp"))
    grid = Mesh(mesh.devices.reshape(sections, depth, split // 2, 2), ("section", "dp", "y", "core"))
    mp = ("y", "core")
    in_specs = (
        P("section", "dp", None),
        P("dp", None),
        P("section", "dp", None),
        P("section", "dp", None, mp),
        P("dp", None),
        P("section", mp, "dp"),
        P("section", "dp", mp),
        P("section", mp, "dp"),
    )
    out_specs = (
        P("section", "dp", None),
        P("section", "dp"),
        P("section", "dp"),
        P("section", "dp", None, mp),
        P("dp", None),
        P("section", mp, "dp"),
        P("section", "dp", mp),
        P("section", mp, "dp"),
    )
    return jax.shard_map(shards, mesh=grid, in_specs=in_specs, out_specs=out_specs, check_vma=False)
```

```python
import functools
import math

import jax
import jax.numpy as jnp
from jax import lax
from jax.experimental import pallas as pl
from jax.experimental.pallas import tpu as pltpu
from jax.sharding import Mesh, PartitionSpec as P

HEAD = 64
MB_TOK = 1024
PIECE = 256
PIECES = MB_TOK // PIECE
WINDOW = 3
PARTS = 6
LANES = 128
EPSILON = 1e-05
GELU_K = math.sqrt(2.0 / math.pi)
GELU_C = 0.044715
MESH = pl.DeviceIdType.MESH
F32 = jnp.float32
LOW = jnp.bfloat16


def mm(left, right):
    return lax.dot_general(left, right, (((1,), (0,)), ((), ())), preferred_element_type=F32)


def mm_back(left, right):
    return lax.dot_general(left, right, (((1,), (1,)), ((), ())), preferred_element_type=F32)


def normalize(rows):
    centred = rows - jnp.mean(rows, axis=1, keepdims=True)
    factor = lax.rsqrt(jnp.mean(centred * centred, axis=1, keepdims=True) + EPSILON)
    return centred * factor, factor


def norm_back(grad, plain, factor, gain):
    scaled = grad * gain
    return factor * (
        scaled
        - jnp.mean(scaled, axis=1, keepdims=True)
        - plain * jnp.mean(scaled * plain, axis=1, keepdims=True)
    )


def flip(tile):
    return pltpu.roll(tile, HEAD, 1)


def layers_kernel(width, depth, inside, *refs):
    refs = list(refs)
    take = lambda count: [refs.pop(0) for _ in range(count)]
    length_ref, x_all, gain_ref = take(3)
    part_refs = take(3 if inside else 1)
    out_ref, grad_ref, gain_grad_ref = take(3)
    if inside:
        head_out, gain_out, value_out = take(3)
    (wa, q_s, k_s, v_s, turn_s, o_s, lse_s, plain1, plain2, fac_s,
     a_t, m_t, g_t, h_t, e_s, gd_s, do_s, spare, bias_s, x_ref, start_s,
     there, there_v, here, here_v, swap_out, swap_in,
     sem_x, sem_v, sem_f, sem_c, sem_o, sem_oc, sem_l) = take(34)
    if inside:
        (w_ref, gain_all, sums, y_in, z_in, gain_y, gain_z, value_ref,
         sem_az, sem_ay, sem_gz, sem_ry, sem_rz, sem_rm, sem_gg, sem_va) = take(16)
    else:
        w_ref, sums = part_refs[0], grad_ref

    section = lax.axis_index("section")
    core = lax.axis_index("core")
    lane_y = lax.axis_index("y")
    deep = lax.axis_index("dp")
    other_layer = {"section": 1 - section}
    other_core = {"core": 1 - core}
    other_y = {"y": 1 - lane_y}
    first = section == 0
    second = jnp.logical_not(first)
    tiles = width // 2 // LANES
    hidden = width
    rows_own = width // depth
    half_cols = width // 2

    def send(src, dst, sems, index, target):
        return pltpu.make_async_remote_copy(
            src_ref=src, dst_ref=dst, send_sem=sems.at[(0,) + index], recv_sem=sems.at[(1,) + index],
            device_id=target, device_id_type=MESH)

    def peer(step):
        return {"dp": lax.rem(deep + step, depth)}

    barrier = pltpu.get_barrier_semaphore()
    friends = [other_layer, other_core, other_y]
    if inside:
        friends = friends + [peer(step) for step in range(1, depth)]
        twin = {"dp": deep + 1 - 2 * lax.rem(deep, 2)}
    for friend in friends:
        pl.semaphore_signal(barrier, inc=1, device_id=friend, device_id_type=MESH)
    pl.semaphore_wait(barrier, len(friends))

    lane = lax.broadcasted_iota(jnp.int32, (1, LANES), 1)
    low_half = lane < HEAD

    def rows_at(place):
        return pl.ds(pl.multiple_of(place * rows_own, rows_own), rows_own)

    unit = 3 * hidden // PARTS
    per_ref = PARTS // 3
    ways = (1, -1)
    mixed_part = PARTS - 1

    def cols_at(part):
        return pl.ds(part * unit, unit)

    def on_line(place):
        return jnp.logical_and(place >= 0, place < depth)

    def own_part(part):
        return part_refs[part // per_ref].at[:, pl.ds(part % per_ref * unit, unit)]

    def own_copy(index):
        return pltpu.make_async_copy(
            part_refs[index], w_ref.at[lane_y, rows_at(deep), pl.ds(index * hidden, hidden)],
            sem_l.at[PIECES + index])

    def gather_line(part, row, hop, way):
        place = deep - hop * ways[way]
        home = lane_y if row == 0 else 1 - lane_y
        spot = w_ref.at[home, rows_at(place), cols_at(part)]
        src = own_part(part) if row == 0 and hop == 0 else spot
        return send(src, spot, sem_az, (part + row, hop, way), {"dp": deep + ways[way]})

    def line_start(part, row, hop, way):
        @pl.when(jnp.logical_and(on_line(deep - hop * ways[way]), on_line(deep + ways[way])))
        def _():
            gather_line(part, row, hop, way).start()

    def line_sent(part, row, hop, way):
        @pl.when(jnp.logical_and(on_line(deep - hop * ways[way]), on_line(deep + ways[way])))
        def _():
            gather_line(part, row, hop, way).wait_send()

    def gather_y(part, place, own):
        spot = w_ref.at[lane_y, rows_at(place), cols_at(part)]
        src = own_part(part) if own else spot
        return send(src, spot, sem_ay, (part, place), other_y)

    def gather_gain(step):
        return send(gain_all.at[deep], gain_all.at[deep], sem_gz, (step,), peer(step))

    def gather_start(part):
        for way in range(2):
            line_start(part, 0, 0, way)
        if part != mixed_part:
            gather_y(part, deep, True).start()

    def gather_pass(part, row=0, hops=None):
        for hop in range(depth - 1) if hops is None else hops:
            for way in range(2):
                place = deep - (hop + 1) * ways[way]

                @pl.when(on_line(place))
                def _(hop=hop, way=way, place=place):
                    gather_line(part, row, hop, way).wait_recv()
                    if hop < depth - 2:
                        line_start(part, row, hop + 1, way)
                    if part != mixed_part:
                        gather_y(part, place, False).start()

    def gather_cross():
        gather_y(mixed_part, deep, True).wait()
        for way in range(2):
            line_start(mixed_part, 1, 0, way)

    def gather_end(part):
        if part != mixed_part:
            for place in range(depth):
                gather_y(part, place, False).wait()
        for row in range(2 if part == mixed_part else 1):
            for hop in range(depth - 1):
                for way in range(2):
                    line_sent(part, row, hop, way)

    block = 2 * LANES
    last = block // 2
    spans = [
        (2 * hidden, block), (hidden, block), (hidden + block, block),
        (block, block), (2 * block, block), (0, block),
        (hidden + 2 * block, last), (hidden + 2 * block + last, last)]
    mixed_at = pl.ds(2 * hidden + block, 2 * block)
    mixed_out = pl.ds(hidden + block, 2 * block)

    def block_at(index):
        return pl.ds(spans[index][0], spans[index][1])

    def reduce_y(index):
        return send(sums.at[1 - lane_y, :, block_at(index)], y_in.at[:, block_at(index)],
                    sem_ry, (index,), other_y)

    def share_of(near, index):
        own = lax.rem(deep, 2)
        return rows_at((own if near else 1 - own) + 2 * index)

    def reduce_near(index, share):
        at = block_at(index)
        return send(sums.at[lane_y, share_of(False, share), at], z_in.at[share, :, at],
                    sem_rz, (index, share), twin)

    def reduce_far(index):
        at = block_at(index)
        return send(sums.at[lane_y, rows_at(lax.rem(deep + 2, depth)), at], z_in.at[2, :, at],
                    sem_rz, (index, 2), peer(2))

    def reduce_mid(index, following=None):
        reduce_y(index).wait_recv()
        if following is not None:
            reduce_y(following).start()
        at = block_at(index)
        sums[lane_y, :, at] = (
            sums[lane_y, :, at].astype(F32) + y_in[:, at].astype(F32)).astype(LOW)
        for share in range(2):
            reduce_near(index, share).start()

    def reduce_late(index):
        at = block_at(index)
        for share in range(2):
            reduce_near(index, share).wait_recv()
            rows = share_of(True, share)
            sums[lane_y, rows, at] = (
                sums[lane_y, rows, at].astype(F32) + z_in[share, :, at].astype(F32)).astype(LOW)
        reduce_far(index).start()

    def summed(at):
        return sums[lane_y, rows_at(deep), at].astype(F32) + z_in[2, :, at].astype(F32)

    def head_tile(index):
        return summed(pl.ds(index * LANES, LANES))

    def reduce_end(index):
        at = block_at(index)
        reduce_far(index).wait_recv()
        spot, size = spans[index]
        if spot >= hidden:
            grad_ref[:, spot - hidden:spot - hidden + size] = summed(at)

    def mixed_home(row, share):
        if row == 0:
            return z_in.at[share, :, mixed_at]
        return y_in.at[rows_at(share), mixed_at]

    def mixed_group(row):
        return lane_y if row == 0 else 1 - lane_y

    def mixed_near(row, share):
        return send(sums.at[mixed_group(row), share_of(False, share), mixed_at],
                    mixed_home(row, share), sem_rm, (row, share), twin)

    def mixed_far(row):
        return send(sums.at[mixed_group(row), rows_at(lax.rem(deep + 2, depth)), mixed_at],
                    mixed_home(row, 2), sem_rm, (row, 2), peer(2))

    def mixed_cross():
        return send(sums.at[1 - lane_y, rows_at(deep), mixed_at], mixed_home(1, 3),
                    sem_rm, (1, 3), other_y)

    def mixed_start():
        for row in range(2):
            for share in range(2):
                mixed_near(row, share).start()

    def mixed_mid():
        for row in range(2):
            for share in range(2):
                mixed_near(row, share).wait_recv()
                rows = share_of(True, share)
                group = mixed_group(row)
                sums[group, rows, mixed_at] = (
                    sums[group, rows, mixed_at].astype(F32)
                    + mixed_home(row, share)[...].astype(F32)).astype(LOW)
            mixed_far(row).start()

    def mixed_late():
        for row in range(2):
            mixed_far(row).wait_recv()
            total = (sums[mixed_group(row), rows_at(deep), mixed_at].astype(F32)
                     + mixed_home(row, 2)[...].astype(F32))
            if row == 0:
                grad_ref[:, mixed_out] = total
            else:
                sums[mixed_group(row), rows_at(deep), mixed_at] = total.astype(LOW)

    def mixed_end():
        mixed_cross().wait_recv()
        grad_ref[:, mixed_out] += mixed_home(1, 3)[...].astype(F32)

    def reduce_sent():
        for index in range(len(spans)):
            reduce_y(index).wait_send()
            for share in range(2):
                reduce_near(index, share).wait_send()
            reduce_far(index).wait_send()
        for row in range(2):
            for share in range(2):
                mixed_near(row, share).wait_send()
            mixed_far(row).wait_send()
        mixed_cross().wait_send()

    def halves(tile):
        return [jnp.where(low_half, tile, jnp.zeros_like(tile)),
                jnp.where(low_half, jnp.zeros_like(tile), tile)]

    def group_tile(group, index):
        return w_ref[group, :, index * LANES:(index + 1) * LANES]

    qkv_cols = 3 * tiles * LANES

    def arrange():
        for kind in range(4):
            for group in range(2):
                spot = (kind * tiles + group) * LANES
                wa[:, spot:spot + LANES] = group_tile(group, kind)
        for pair in range(2):
            one, two = (group_tile(group, 4 + pair).astype(F32) for group in range(2))
            spot = (2 * pair * tiles + 2) * LANES
            wa[:, spot:spot + LANES] = jnp.where(low_half, one, flip(two)).astype(LOW)
            spot = ((2 * pair + 1) * tiles + 2) * LANES
            wa[:, spot:spot + LANES] = jnp.where(low_half, flip(one), two).astype(LOW)

    x_copy = pltpu.make_async_copy(x_all.at[lane_y], x_ref, sem_l.at[PIECES + 3])
    if inside:
        gather_start(0)
        gather_start(1)
        gather_y(mixed_part, deep, True).start()
        gain_all[deep, 0:2, 0:rows_own] = gain_ref[...].astype(F32)
        for step in range(1, depth):
            gather_gain(step).start()
        for index in range(3):
            own_copy(index).start()
    x_copy.start()

    for piece in range(PIECES):
        place = piece * PIECE + lax.broadcasted_iota(jnp.int32, (1, PIECE), 1)
        begin = jnp.zeros((1, PIECE), jnp.int32)
        end = 0
        for index in range(length_ref.shape[1]):
            end = end + length_ref[lane_y, index]
            begin = jnp.where(place >= end, end, begin)
        start_s[piece] = begin

    if inside:
        gather_pass(0)
        gather_start(2)
        gather_pass(1)
        gather_start(3)
        gather_pass(2, 0, [0, 1])
        gather_start(4)
        for step in range(1, depth):
            gather_gain(step).wait()
        gather_end(0)
        gather_end(1)
        gather_pass(2, 0, [2])
        gather_pass(3, 0, [0])
        for index in range(3):
            own_copy(index).wait()
        gains = jnp.concatenate([gain_all[place, :, :rows_own] for place in range(depth)], axis=1)
    else:
        gains = gain_ref[...]
    arrange()
    x_copy.wait()
    gain1 = gains[0:1, :]
    gain2 = gains[1:2, :]

    def swap_copy(leave, enter):
        return send(swap_out.at[leave], swap_in.at[enter], sem_c, (enter,), other_core)

    def swap_start(slots, value):
        swap_out[slots[0]] = value
        swap_copy(*slots).start()

    def swap_end(slots):
        swap_copy(*slots).wait()
        return swap_out[slots[0]].astype(F32) + swap_in[slots[1]].astype(F32)

    def first_slots(piece):
        return lax.rem(piece, 2), piece

    def turned_slots(piece):
        return lax.rem(piece, 2), lax.rem(piece + 2, PIECES)

    def second_slots(piece):
        return 2, PIECES + lax.rem(piece, 2)

    def last_slots(piece):
        return 2, PIECES + lax.rem(piece + 1, 2)

    def put_rows(piece, rows):
        for t in range(2 * tiles):
            spare[piece, t] = rows[:, t * LANES:(t + 1) * LANES]

    def get_rows(piece):
        return jnp.concatenate([spare[piece, t] for t in range(2 * tiles)], axis=1)

    def joined(*stores):
        return jnp.concatenate([store[t] for store in stores for t in range(tiles)], axis=1)

    half = pl.ds(pl.multiple_of(core * half_cols, half_cols), half_cols)

    def hand_rows(piece):
        return send(there.at[piece, :, half], here.at[piece, :, half], sem_x, (piece,), other_layer)

    def hand_values(piece):
        return send(there_v.at[piece], here_v.at[piece], sem_v, (piece,), other_layer)

    def hand_on(piece):
        return send(here.at[piece, :, half], here.at[piece, :, half], sem_f, (piece,), other_core)

    def take_start(piece):
        hand_rows(piece).wait_recv()
        hand_on(piece).start()

    def take_values(piece):
        hand_values(piece).wait_recv()

    def emit_here(piece, stage):
        return pltpu.make_async_copy(stage.at[piece], out_ref.at[lane_y, piece], sem_l.at[piece])

    def emit_there(piece, stage):
        return send(stage.at[piece, :, half], out_ref.at[lane_y, piece, :, half],
                    sem_o, (piece,), other_y)

    def emit(piece, stage):
        return [emit_here(piece, stage), emit_there(piece, stage)]

    def emit_on(piece):
        spot = out_ref.at[1 - lane_y, piece, :, half]
        return send(spot, spot, sem_oc, (piece,), other_core)

    def reused(tile_index):
        if tile_index == 0:
            return None
        if tile_index == 1:
            return jnp.logical_and(second, lane >= 0)
        return jnp.logical_and(second, lane >= HEAD)

    def make_bias(piece, count):
        base = piece * PIECE
        query = base + lax.broadcasted_iota(jnp.int32, (1, PIECE), 1)
        begin = start_s[piece]
        for j in range(count):
            key = base - (count - 1 - j) * PIECE + lax.broadcasted_iota(jnp.int32, (PIECE, 1), 0)
            fine = jnp.logical_and(key >= begin, key <= query)
            bias_s[j] = jnp.where(fine, 0.0, -1e30).astype(F32)

    def attend(piece, count):
        make_bias(piece, count)
        for t in range(tiles):
            parts = []
            for h, query in enumerate(halves(q_s[piece, t])):
                scores = [
                    mm_back(k_s[piece - (count - 1 - j), t], query) + bias_s[j] for j in range(count)
                ]
                top = functools.reduce(
                    jnp.maximum, [jnp.max(s, axis=0, keepdims=True) for s in scores])
                expo = [jnp.exp(s - top) for s in scores]
                total = functools.reduce(
                    jnp.add, [jnp.sum(e, axis=0, keepdims=True) for e in expo])
                mixed = functools.reduce(jnp.add, [
                    mm(turn_s[piece - (count - 1 - j), t, h * HEAD:(h + 1) * HEAD, :], e.astype(LOW))
                    for j, e in enumerate(expo)
                ])
                parts.append(mixed * (1.0 / total))
                lse_s[piece, 2 * t + h] = top + jnp.log(total)
            o_s[piece, t] = jnp.concatenate(parts, axis=0).T.astype(LOW)

    def attend_back(piece, count):
        make_bias(piece, count)
        for t in range(tiles):
            inner = (do_s[t].astype(F32) * o_s[piece, t].astype(F32)).T
            queries = halves(q_s[piece, t])
            grads = halves(do_s[t])
            dq = [0.0, 0.0]
            inners = [jnp.sum(inner[h * HEAD:(h + 1) * HEAD], axis=0, keepdims=True) for h in range(2)]
            for j in range(count):
                at = piece - (count - 1 - j)
                dk_new, dv_new = 0.0, 0.0
                for h in range(2):
                    probs = jnp.exp(
                        mm_back(k_s[at, t], queries[h]) + bias_s[j] - lse_s[piece, 2 * t + h])
                    dprobs = mm_back(v_s[at, t], grads[h])
                    dscores = (probs * (dprobs - inners[h])).astype(LOW)
                    dv_new = dv_new + mm(probs.astype(LOW), grads[h])
                    dk_new = dk_new + mm(dscores, queries[h])
                    dq[h] = dq[h] + mm(turn_s[at, t, h * HEAD:(h + 1) * HEAD, :], dscores)
                spare[at, t] += dk_new
                spare[at, tiles + t] += dv_new
            dq_t = jnp.concatenate(dq, axis=0) * 0.125
            q_s[piece, t] = dq_t.T.astype(LOW)

    def by_count(piece, run):
        for count in range(1, WINDOW + 1):
            fits = piece >= WINDOW - 1 if count == WINDOW else piece == count - 1

            @pl.when(fits)
            def _(count=count):
                run(piece, count)

    def forward_attention(piece):
        @pl.when(second)
        def _():
            @pl.when(piece < 2)
            def _():
                take_start(piece)

            hand_on(piece).wait()

        rows = jnp.where(first, x_ref[piece], here[piece]).astype(F32)
        plain, factor = normalize(rows)
        plain1[piece] = plain.astype(LOW)
        fac_s[piece, :, 0:1] = factor
        normed = plain * gain1
        a_t[piece] = normed.T.astype(LOW)
        qkv = mm(normed.astype(LOW), wa[:, :qkv_cols])

        @pl.when(second)
        def _():
            take_values(piece)

        for t in range(tiles):
            q_s[piece, t] = (qkv[:, t * LANES:(t + 1) * LANES].astype(LOW) * 0.125).astype(LOW)
            key = qkv[:, (tiles + t) * LANES:(tiles + t + 1) * LANES].astype(LOW)
            value = qkv[:, (2 * tiles + t) * LANES:(2 * tiles + t + 1) * LANES].astype(LOW)
            mask = reused(t)
            if mask is not None:
                value = jnp.where(mask, here_v[piece, t - 1], value)
                there_v[piece, t - 1] = value
            k_s[piece, t] = key
            v_s[piece, t] = value
            turn_s[piece, t] = value.astype(F32).T.astype(LOW)

        @pl.when(first)
        def _():
            hand_values(piece).start()

        by_count(piece, attend)
        put_rows(piece, rows)
        swap_start(first_slots(piece), mm_back(joined(o_s.at[piece]), wa[:, qkv_cols:]).astype(LOW))

    def forward_middle(piece):
        put_rows(piece, get_rows(piece) + swap_end(first_slots(piece)))

    def forward_spread(piece):
        plain, factor = normalize(get_rows(piece))
        plain2[piece] = plain.astype(LOW)
        fac_s[piece, :, 1:2] = factor
        normed = plain * gain2
        m_t[piece] = normed.T.astype(LOW)
        normed = normed.astype(LOW)
        for group in range(2):
            z = mm(normed, w_ref[group, :, hidden:2 * hidden])
            square = z * z
            bent = jnp.tanh(GELU_K * z * (1.0 + GELU_C * square))
            upper = 0.5 * (1.0 + bent)
            slope = upper + 0.5 * z * (1.0 - bent * bent) * (GELU_K * (1.0 + 3.0 * GELU_C * square))
            gd_s[piece, group] = slope.astype(LOW)
            e_s[piece, group] = (z * upper).astype(LOW)

    def forward_fold(piece):
        total = 0.0
        for group in range(2):
            total = total + mm_back(e_s[piece, group], w_ref[group, :, 2 * hidden:])
        swap_start(second_slots(piece), total.astype(LOW))

    def forward_result(piece):
        result = (get_rows(piece) + swap_end(second_slots(piece))).astype(LOW)

        @pl.when(first)
        def _():
            there[piece] = result
            hand_rows(piece).start()

        @pl.when(second)
        def _():
            here[piece] = result
            for copy in emit(piece, here):
                copy.start()

    def within(step, low_end, high_end):
        return jnp.logical_and(step >= low_end, step < high_end)

    lag = jnp.where(first, 0, 2 * PIECES)

    def forward(step, carry):
        place = step - lag

        @pl.when(within(place, 0, PIECES))
        def _():
            forward_attention(place)

        if inside:
            @pl.when(step == 0)
            def _():
                gather_pass(3, 0, [1])
                gather_start(5)
                gather_cross()

            @pl.when(step == 1)
            def _():
                gather_pass(3, 0, [2])
                gather_pass(4, 0, [0])

            @pl.when(step == 2)
            def _():
                gather_pass(4, 0, [1])
                gather_pass(5, 0, [0])
                gather_pass(5, 1, [0])

            @pl.when(step == 3)
            def _():
                gather_pass(4, 0, [2])
                gather_pass(5, 0, [1])
                gather_pass(5, 1, [1])
                gather_end(2)
                gather_end(3)

            @pl.when(step == 2 * PIECES - 2)
            def _():
                gather_pass(5, 0, [2])
                gather_pass(5, 1, [2])

            @pl.when(step == 2 * PIECES - 1)
            def _():
                gather_end(4)
                gather_end(5)

        @pl.when(jnp.logical_and(second, within(place, 2, PIECES + 1)))
        def _():
            forward_result(place - 2)

        @pl.when(within(place, 1, PIECES + 1))
        def _():
            forward_middle(place - 1)

        spread_place = place - jnp.where(first, PIECES, 1)

        @pl.when(within(spread_place, 0, PIECES))
        def _():
            forward_spread(spread_place)

        fold_place = place - jnp.where(first, 2 * PIECES, 1)

        @pl.when(within(fold_place, 0, PIECES))
        def _():
            @pl.when(jnp.logical_and(second, fold_place < PIECES - 2))
            def _():
                take_start(fold_place + 2)

            forward_fold(fold_place)

            @pl.when(first)
            def _():
                forward_result(fold_place)

        return carry

    lax.fori_loop(0, 3 * PIECES + 1, forward, 0)

    @pl.when(first)
    def _():
        for piece in range(PIECES):
            hand_rows(piece).wait_send()
            hand_values(piece).wait_send()

    gain_grad_ref[...] = jnp.zeros_like(gain_grad_ref)

    def hidden_grads(left, right, base):
        def one(index, carry):
            group, column = index // (hidden // block), index % (hidden // block)
            spot = pl.multiple_of(column * block, block)
            total = 0.0
            for piece in range(PIECES):
                total = total + mm(left[piece], right[piece, group, :, pl.ds(spot, block)])
            sums[group, :, pl.ds(pl.multiple_of(base + spot, block), block)] = total.astype(LOW)
            return carry

        lax.fori_loop(0, 2 * (hidden // block), one, 0)

    def head_grads():
        pairs = []
        for kind in range(4):
            total = 0.0
            for piece in range(PIECES):
                if kind < 3:
                    total = total + mm(a_t[piece], joined((q_s, k_s, v_s)[kind].at[piece]))
                else:
                    total = total + mm(h_t[piece], joined(o_s.at[piece]))
            for group in range(2):
                part = total[:, group * LANES:(group + 1) * LANES].astype(LOW)
                sums[group, :, kind * LANES:(kind + 1) * LANES] = part
            pairs.append(total[:, 2 * LANES:])
        for pair in range(2):
            one, two = pairs[2 * pair:2 * pair + 2]
            spot = (4 + pair) * LANES
            sums[0, :, spot:spot + LANES] = jnp.where(low_half, one, flip(two)).astype(LOW)
            sums[1, :, spot:spot + LANES] = jnp.where(low_half, flip(one), two).astype(LOW)

    def down_grads():
        hidden_grads(g_t, e_s, 2 * hidden)
        if inside:
            reduce_y(0).start()
            mixed_start()

    def up_grads():
        hidden_grads(m_t, gd_s, hidden)
        if inside:
            reduce_y(1).start()
            reduce_y(2).start()

    def grad_rows(piece):
        return jnp.where(first, here[piece], x_ref[piece])

    def backward_hidden(piece):
        @pl.when(first)
        def _():
            @pl.when(piece == PIECES - 1)
            def _():
                take_start(piece)

            hand_on(piece).wait()

        grad_low = grad_rows(piece)
        g_t[piece] = grad_low.astype(F32).T.astype(LOW)

        @pl.when(jnp.logical_and(first, piece == 0))
        def _():
            down_grads()

        total = 0.0
        for group in range(2):
            dz = mm(grad_low, w_ref[group, :, 2 * hidden:]) * gd_s[piece, group].astype(F32)
            dz = dz.astype(LOW)
            gd_s[piece, group] = dz
            total = total + mm_back(dz, w_ref[group, :, hidden:2 * hidden])
        swap_start(turned_slots(piece), total.astype(LOW))

        @pl.when(jnp.logical_and(first, piece == 0))
        def _():
            up_grads()

    def backward_attention(piece):
        dm = swap_end(turned_slots(piece))
        plain = plain2[piece].astype(F32)
        gain_grad_ref[1:2, :] += jnp.sum(dm * plain, axis=0, keepdims=True)
        middle = grad_rows(piece).astype(F32) + norm_back(dm, plain, fac_s[piece, :, 1:2], gain2)
        h_t[piece] = middle.T.astype(LOW)
        dmixed = mm(middle.astype(LOW), wa[:, qkv_cols:]).astype(LOW)
        for t in range(tiles):
            do_s[t] = dmixed[:, t * LANES:(t + 1) * LANES]
        by_count(piece, attend_back)
        for t in range(1, tiles):
            there_v[piece, t - 1] = spare[piece, tiles + t].astype(LOW)

        @pl.when(first)
        def _():
            hand_values(piece).wait_recv()

        @pl.when(second)
        def _():
            hand_values(piece).start()

        for t in range(tiles):
            dvalue = spare[piece, tiles + t]
            mask = reused(t)
            if mask is not None:
                came = jnp.logical_and(first, jnp.logical_or(t == 1, lane >= HEAD))
                dvalue = jnp.where(came, dvalue + here_v[piece, t - 1].astype(F32), dvalue)
                dvalue = jnp.where(mask, 0.0, dvalue)
            k_s[piece, t] = spare[piece, t].astype(LOW)
            v_s[piece, t] = dvalue.astype(LOW)
        put_rows(piece, middle)
        terms = joined(q_s.at[piece], k_s.at[piece], v_s.at[piece])
        swap_start(last_slots(piece), mm_back(terms, wa[:, :qkv_cols]).astype(LOW))

    def backward_result(piece):
        da = swap_end(last_slots(piece))
        plain = plain1[piece].astype(F32)
        gain_grad_ref[0:1, :] += jnp.sum(da * plain, axis=0, keepdims=True)
        there[piece] = (get_rows(piece) + norm_back(da, plain, fac_s[piece, :, 0:1], gain1)).astype(LOW)

        @pl.when(second)
        def _():
            hand_rows(piece).start()

        @pl.when(first)
        def _():
            for copy in emit(piece, there):
                copy.start()

    def backward(step, carry):
        turn = step // 2
        even = lax.rem(step, 2) == 0

        @pl.when(jnp.logical_and(jnp.logical_xor(even, first), turn < PIECES))
        def _():
            backward_hidden(PIECES - 1 - turn)

        @pl.when(step == 0)
        def _():
            @pl.when(second)
            def _():
                forward_result(PIECES - 1)

            spare[...] = jnp.zeros_like(spare)
            for piece in range(PIECES):
                for t in range(tiles):
                    turn_s[piece, t] = k_s[piece, t].astype(F32).T.astype(LOW)

        @pl.when(jnp.logical_and(jnp.logical_xor(even, second), turn >= 1))
        def _():
            @pl.when(turn >= 2)
            def _():
                backward_result(PIECES + 1 - turn)

            @pl.when(jnp.logical_and(first, turn < PIECES))
            def _():
                take_start(PIECES - 1 - turn)

            backward_attention(PIECES - turn)

        return carry

    lax.fori_loop(0, 2 * PIECES + 2, backward, 0)
    backward_result(0)

    @pl.when(second)
    def _():
        down_grads()
        up_grads()

    head_grads()

    def emit_stage(run):
        @pl.when(first)
        def _():
            run(there)

        @pl.when(second)
        def _():
            run(here)

    def pass_outputs(stage):
        for piece in range(PIECES):
            emit_there(piece, stage).wait_recv()
            emit_on(piece).start()

    def finish_outputs(stage):
        for piece in range(PIECES):
            emit_here(piece, stage).wait()
            emit_there(piece, stage).wait_send()
            emit_on(piece).wait()

    if inside:
        gain_copy = send(gain_grad_ref, gain_y, sem_gg, (0,), other_y)
        gain_copy.start()
        reduce_y(3).start()
        mixed_mid()
        reduce_mid(0, 4)
        gain_copy.wait()
        gain_y[...] = gain_y[...] + gain_grad_ref[...]
        gain_sends = [
            send(gain_y, gain_z.at[step - 1], sem_gg, (step,), peer(step)) for step in range(1, depth)]
        for copy in gain_sends:
            copy.start()
        reduce_mid(1)
        reduce_late(0)
        reduce_mid(2, 5)
        mixed_late()
        reduce_late(1)
        reduce_mid(3, 6)
        reduce_end(0)
        reduce_late(2)
        reduce_mid(4, 7)
        reduce_end(1)
        reduce_late(3)
        reduce_end(2)
        total = gain_y[...]
        for step, copy in enumerate(gain_sends):
            copy.wait()
            total = total + gain_z[step]
        gain_out[...] = functools.reduce(jnp.add, [
            jnp.where(deep == index, total[0:2, index * rows_own:(index + 1) * rows_own], 0.0)
            for index in range(depth)])
        reduce_mid(5)
        reduce_late(4)
        reduce_end(3)
        emit_stage(pass_outputs)
        reduce_mid(6)
        mixed_cross().start()
        reduce_late(5)
        reduce_end(4)

        def place(sec, row, unit):
            return (sec * 2 + row) * 2 + unit

        mine = place(section, lane_y, core)
        for half_tile, tile_index in enumerate((2, 5)):
            value_ref[mine, :, half_tile * LANES:(half_tile + 1) * LANES] = (
                head_tile(tile_index).astype(LOW))
        value_y = send(value_ref.at[mine], value_ref.at[mine], sem_va, (0,), other_y)
        value_y.start()
        reduce_mid(7)
        reduce_late(6)
        reduce_end(5)
        value_y.wait()
        value_x = []
        for row in range(2):
            at = place(section, row, core)
            value_x.append(send(value_ref.at[at], value_ref.at[at], sem_va, (1 + row,), other_layer))
            value_x[-1].start()
        reduce_late(7)
        reduce_end(6)
        for copy in value_x:
            copy.wait()
        value_c = []
        for sec in range(2):
            for row in range(2):
                at = place(sec, row, core)
                value_c.append(
                    send(value_ref.at[at], value_ref.at[at], sem_va, (3 + 2 * sec + row,), other_core))
                value_c[-1].start()
        mixed_end()
        reduce_end(7)
        edge = 2 * HEAD

        def columns(kind, pair, upper):
            rest = head_tile(pair)
            return jnp.concatenate(
                [head_tile(kind), rest[:, HEAD:] if upper else rest[:, :HEAD]], axis=1)

        head_out[0] = columns(0, 4, False)
        head_out[1] = columns(1, 4, True)
        head_out[2] = columns(3, 5, True)
        for copy in value_c:
            copy.wait()
        value_out[...] = jnp.concatenate(
            [value_ref[index, :, :edge + HEAD] for index in range(value_out.shape[1] // (edge + HEAD))],
            axis=1).astype(F32)
        reduce_sent()
    else:
        emit_stage(pass_outputs)

    emit_stage(finish_outputs)

    @pl.when(second)
    def _():
        for piece in range(PIECES):
            hand_rows(piece).wait_send()
            hand_values(piece).wait_send()


def run_layers(lengths, x_rows, gains, weights, cols, value_cols, depth, inside):
    width = x_rows.shape[3]
    tiles = width // 2 // LANES
    rows_own = width // depth
    columns = 3 * width
    vmem = pl.BlockSpec(memory_space=pltpu.VMEM)
    anywhere = pl.BlockSpec(memory_space=pl.ANY)
    smem = pl.BlockSpec(memory_space=pltpu.SMEM)
    per_tile = (PIECES, tiles, PIECE, LANES)
    turned = (PIECES, tiles, LANES, PIECE)
    flat = (PIECES, PIECE, width)
    flat_turned = (PIECES, width, PIECE)
    wide = (PIECES, 2, PIECE, width)
    low = lambda shape: pltpu.VMEM(shape, LOW)
    full = lambda shape: pltpu.VMEM(shape, F32)
    dma = lambda *shape: pltpu.SemaphoreType.DMA(shape)
    out_shape = [
        jax.ShapeDtypeStruct((2,) + flat, LOW),
        jax.ShapeDtypeStruct((rows_own, 2 * width), F32) if inside
        else jax.ShapeDtypeStruct(weights[0].shape, LOW),
        jax.ShapeDtypeStruct((8, width), F32),
    ]
    out_specs = [anywhere, vmem, vmem]
    scratch = [
        low((width, 4 * tiles * LANES)),
        low(per_tile), low(per_tile), low(per_tile), low(turned), low(per_tile),
        full((PIECES, 2 * tiles, 1, PIECE)),
        low(flat), low(flat), full((PIECES, PIECE, 2)),
        low(flat_turned), low(flat_turned), low(flat_turned), low(flat_turned),
        low(wide), low(wide), low((tiles, PIECE, LANES)),
        full((PIECES, 2 * tiles, PIECE, LANES)),
        full((WINDOW, PIECE, PIECE)), low(flat), pltpu.VMEM((PIECES, 1, PIECE), jnp.int32),
        low(flat), low((PIECES, 2, PIECE, LANES)), low(flat), low((PIECES, 2, PIECE, LANES)),
        low((3, PIECE, width)), low((PIECES + 2, PIECE, width)),
        dma(2, PIECES), dma(2, PIECES), dma(2, PIECES), dma(2, PIECES + 2), dma(2, PIECES),
        dma(2, PIECES), dma(4 + PIECES),
    ]
    if inside:
        out_shape += [
            jax.ShapeDtypeStruct((3, rows_own, cols), F32),
            jax.ShapeDtypeStruct((2, rows_own), F32),
            jax.ShapeDtypeStruct((rows_own, value_cols), F32)]
        out_specs += [vmem] * 3
        scratch += [
            low((2, width, columns)), full((depth, 8, -(-rows_own // LANES) * LANES)),
            low((2, width, columns)), low((width, columns)), low((depth - 1, rows_own, columns)),
            full((8, width)), full((depth - 1, 8, width)),
            low((8, rows_own, 2 * LANES)),
            dma(2, PARTS + 1, depth - 1, 2), dma(2, PARTS, depth), dma(2, depth), dma(2, 8),
            dma(2, 8, 3), dma(2, 2, 4), dma(2, depth), dma(2, 7),
        ]
    return pl.pallas_call(
        functools.partial(layers_kernel, width, depth, inside),
        out_shape=out_shape,
        in_specs=[smem, anywhere, vmem] + [anywhere if inside else vmem] * len(weights),
        out_specs=out_specs,
        scratch_shapes=scratch,
        compiler_params=pltpu.CompilerParams(
            collective_id=0, has_side_effects=True, vmem_limit_bytes=63 << 20),
        name="layers",
    )(lengths, x_rows, gains, *weights)


def pack(w_qk, w_value, w_out):
    query, key, out_t = w_qk[:, 0], w_qk[:, 1], w_out.T
    edge = 2 * HEAD
    return jnp.concatenate(
        [query[:, :edge], key[:, :edge], w_value[:, :edge], out_t[:, :edge],
         query[:, edge:], key[:, edge:], w_value[:, edge:], out_t[:, edge:]],
        axis=1)


def unpack(packed):
    edge = 2 * HEAD
    cut = lambda spot, size: packed[:, spot:spot + size]
    query = jnp.concatenate([cut(0, edge), cut(4 * edge, HEAD)], axis=1)
    key = jnp.concatenate([cut(edge, edge), cut(4 * edge + HEAD, HEAD)], axis=1)
    value = jnp.concatenate([cut(2 * edge, edge), cut(5 * edge, HEAD)], axis=1)
    out_t = jnp.concatenate([cut(3 * edge, edge), cut(5 * edge + HEAD, HEAD)], axis=1)
    hidden = packed.shape[1] // 3
    return (
        jnp.stack([query, key], axis=1), value, out_t.T,
        cut(hidden, hidden), cut(2 * hidden, hidden).T)


def shards(
    ends_in, seq_lengths, norm_gains, qk_weight, value_weight, out_weight, fc_weight, proj_weight
):
    section = lax.axis_index("section")
    lane_y = lax.axis_index("y")
    group = 2 * lane_y + lax.axis_index("core")
    first = section == 0
    cols = qk_weight.shape[3]
    width = ends_in.shape[2]
    fresh = (value_weight.shape[1] - width) // cols
    offset = jnp.where(first, group, width // cols + jnp.minimum(group, fresh - 1)) * cols
    w_value = lax.dynamic_slice_in_dim(value_weight, offset, cols, 1)
    parts = [pack(qk_weight[0], w_value, out_weight[0]), fc_weight[0], proj_weight[0].T]
    depth = lax.axis_size("dp")
    inside = depth == 4 and width % (16 * depth) == 0
    if inside:
        weights = parts
        gains = norm_gains[0].T
    else:
        weights = lax.all_gather(jnp.concatenate(parts, axis=1), "dp", axis=0, tiled=True)
        weights = [lax.all_gather(weights, "y", axis=0)]
        gains = lax.all_gather(norm_gains[0], "dp", axis=0, tiled=True).astype(F32).T
    x_rows = ends_in[0].reshape(2, PIECES, PIECE, width)
    kept = width // cols + fresh
    results = run_layers(
        seq_lengths, x_rows, gains, weights, cols, value_weight.shape[1], depth, inside)
    both = results[0].reshape(2 * MB_TOK, width)
    if inside:
        _, grads, _, heads, gain_rows, d_value = results
        attn_gain, mlp_gain = gain_rows[0], gain_rows[1]
        d_qk = jnp.stack([heads[0], heads[1]], axis=1)
        d_out = heads[2].T
        d_up, d_down = grads[:, :width], grads[:, width:].T
    else:
        _, grads, gain_grads = results
        grads = lax.psum_scatter(grads, "y", scatter_dimension=0, tiled=False)
        grads = lax.psum_scatter(grads, "dp", scatter_dimension=0, tiled=True)
        gain_rows = lax.psum(gain_grads[:2], "y").T
        gain_rows = lax.psum_scatter(gain_rows, "dp", scatter_dimension=0, tiled=True)
        attn_gain, mlp_gain = gain_rows[:, 0], gain_rows[:, 1]
        d_qk, d_value, d_out, d_up, d_down = unpack(grads.astype(F32))
        values = lax.all_gather(d_value.astype(LOW), ("section", "y", "core"), axis=0)
        d_value = jnp.concatenate([values[index] for index in range(kept)], axis=1).astype(F32)
    return (
        both[None], attn_gain[None], mlp_gain[None], d_qk[None], d_value,
        d_out[None], d_up[None], d_down[None])


def solution(mesh):
    sections, depth, split = (mesh.shape[name] for name in ("section", "dp", "mp"))
    grid = Mesh(mesh.devices.reshape(sections, depth, split // 2, 2), ("section", "dp", "y", "core"))
    mp = ("y", "core")
    in_specs = (
        P("section", "dp", None),
        P("dp", None),
        P("section", "dp", None),
        P("section", "dp", None, mp),
        P("dp", None),
        P("section", mp, "dp"),
        P("section", "dp", mp),
        P("section", mp, "dp"),
    )
    out_specs = (
        P("section", "dp", None),
        P("section", "dp"),
        P("section", "dp"),
        P("section", "dp", None, mp),
        P("dp", None),
        P("section", mp, "dp"),
        P("section", "dp", mp),
        P("section", mp, "dp"),
    )
    return jax.shard_map(shards, mesh=grid, in_specs=in_specs, out_specs=out_specs, check_vma=False)
```

```python
import functools
import math

import jax
import jax.numpy as jnp
from jax import lax
from jax.experimental import pallas as pl
from jax.experimental.pallas import tpu as pltpu
from jax.sharding import Mesh, PartitionSpec as P

HEAD = 64
MB_TOK = 1024
PIECE = 256
PIECES = MB_TOK // PIECE
WINDOW = 3
PARTS = 6
LANES = 128
EPSILON = 1e-05
GELU_K = math.sqrt(2.0 / math.pi)
GELU_C = 0.044715
MESH = pl.DeviceIdType.MESH
F32 = jnp.float32
LOW = jnp.bfloat16


def mm(left, right):
    return lax.dot_general(left, right, (((1,), (0,)), ((), ())), preferred_element_type=F32)


def mm_back(left, right):
    return lax.dot_general(left, right, (((1,), (1,)), ((), ())), preferred_element_type=F32)


def normalize(rows):
    centred = rows - jnp.mean(rows, axis=1, keepdims=True)
    factor = lax.rsqrt(jnp.mean(centred * centred, axis=1, keepdims=True) + EPSILON)
    return centred * factor, factor


def norm_back(grad, plain, factor, gain):
    scaled = grad * gain
    return factor * (
        scaled
        - jnp.mean(scaled, axis=1, keepdims=True)
        - plain * jnp.mean(scaled * plain, axis=1, keepdims=True)
    )


def flip(tile):
    return pltpu.roll(tile, HEAD, 1)


def layers_kernel(width, depth, inside, *refs):
    refs = list(refs)
    take = lambda count: [refs.pop(0) for _ in range(count)]
    length_ref, x_all, gain_ref = take(3)
    part_refs = take(3 if inside else 1)
    out_ref, grad_ref, gain_grad_ref = take(3)
    if inside:
        head_out, gain_out, value_out = take(3)
    (wa, q_s, k_s, v_s, turn_s, o_s, lse_s, plain1, plain2, fac_s,
     a_t, m_t, g_t, h_t, e_s, gd_s, do_s, spare, bias_s, x_ref, start_s,
     there, there_v, here, here_v, swap_out, swap_in,
     sem_x, sem_v, sem_f, sem_c, sem_o, sem_oc, sem_l) = take(34)
    if inside:
        (w_ref, gain_all, sums, y_in, z_in, gain_y, gain_z, value_ref,
         sem_az, sem_ay, sem_gz, sem_ry, sem_rz, sem_rm, sem_gg, sem_va) = take(16)
    else:
        w_ref, sums = part_refs[0], grad_ref

    section = lax.axis_index("section")
    core = lax.axis_index("core")
    lane_y = lax.axis_index("y")
    deep = lax.axis_index("dp")
    other_layer = {"section": 1 - section}
    other_core = {"core": 1 - core}
    other_y = {"y": 1 - lane_y}
    first = section == 0
    second = jnp.logical_not(first)
    tiles = width // 2 // LANES
    hidden = width
    rows_own = width // depth
    half_cols = width // 2

    def send(src, dst, sems, index, target):
        return pltpu.make_async_remote_copy(
            src_ref=src, dst_ref=dst, send_sem=sems.at[(0,) + index], recv_sem=sems.at[(1,) + index],
            device_id=target, device_id_type=MESH)

    def peer(step):
        return {"dp": lax.rem(deep + step, depth)}

    barrier = pltpu.get_barrier_semaphore()
    friends = [other_layer, other_core, other_y]
    if inside:
        friends = friends + [peer(step) for step in range(1, depth)]
        twin = {"dp": deep + 1 - 2 * lax.rem(deep, 2)}
    for friend in friends:
        pl.semaphore_signal(barrier, inc=1, device_id=friend, device_id_type=MESH)
    pl.semaphore_wait(barrier, len(friends))

    lane = lax.broadcasted_iota(jnp.int32, (1, LANES), 1)
    low_half = lane < HEAD

    def rows_at(place):
        return pl.ds(pl.multiple_of(place * rows_own, rows_own), rows_own)

    unit = 3 * hidden // PARTS
    per_ref = PARTS // 3
    ways = (1, -1)
    mixed_part = PARTS - 1

    def cols_at(part):
        return pl.ds(part * unit, unit)

    def on_line(place):
        return jnp.logical_and(place >= 0, place < depth)

    def own_part(part):
        return part_refs[part // per_ref].at[:, pl.ds(part % per_ref * unit, unit)]

    def own_copy(index):
        return pltpu.make_async_copy(
            part_refs[index], w_ref.at[lane_y, rows_at(deep), pl.ds(index * hidden, hidden)],
            sem_l.at[PIECES + index])

    def gather_line(part, row, hop, way):
        place = deep - hop * ways[way]
        home = lane_y if row == 0 else 1 - lane_y
        spot = w_ref.at[home, rows_at(place), cols_at(part)]
        src = own_part(part) if row == 0 and hop == 0 else spot
        return send(src, spot, sem_az, (part + row, hop, way), {"dp": deep + ways[way]})

    def line_start(part, row, hop, way):
        @pl.when(jnp.logical_and(on_line(deep - hop * ways[way]), on_line(deep + ways[way])))
        def _():
            gather_line(part, row, hop, way).start()

    def line_sent(part, row, hop, way):
        @pl.when(jnp.logical_and(on_line(deep - hop * ways[way]), on_line(deep + ways[way])))
        def _():
            gather_line(part, row, hop, way).wait_send()

    def gather_y(part, place, own):
        spot = w_ref.at[lane_y, rows_at(place), cols_at(part)]
        src = own_part(part) if own else spot
        return send(src, spot, sem_ay, (part, place), other_y)

    def gather_gain(step):
        return send(gain_all.at[deep], gain_all.at[deep], sem_gz, (step,), peer(step))

    def gather_start(part):
        for way in range(2):
            line_start(part, 0, 0, way)
        if part != mixed_part:
            gather_y(part, deep, True).start()

    def gather_pass(part, row=0, hops=None):
        for hop in range(depth - 1) if hops is None else hops:
            for way in range(2):
                place = deep - (hop + 1) * ways[way]

                @pl.when(on_line(place))
                def _(hop=hop, way=way, place=place):
                    gather_line(part, row, hop, way).wait_recv()
                    if hop < depth - 2:
                        line_start(part, row, hop + 1, way)
                    if part != mixed_part:
                        gather_y(part, place, False).start()

    def gather_cross():
        gather_y(mixed_part, deep, True).wait()
        for way in range(2):
            line_start(mixed_part, 1, 0, way)

    def gather_end(part):
        if part != mixed_part:
            for place in range(depth):
                gather_y(part, place, False).wait()
        for row in range(2 if part == mixed_part else 1):
            for hop in range(depth - 1):
                for way in range(2):
                    line_sent(part, row, hop, way)

    block = 2 * LANES
    last = block // 2
    spans = [
        (2 * hidden, block), (hidden, block), (hidden + block, block),
        (block, block), (2 * block, block), (0, block),
        (hidden + 2 * block, last), (hidden + 2 * block + last, last)]
    mixed_at = pl.ds(2 * hidden + block, 2 * block)
    mixed_out = pl.ds(hidden + block, 2 * block)

    def block_at(index):
        return pl.ds(spans[index][0], spans[index][1])

    def reduce_y(index):
        return send(sums.at[1 - lane_y, :, block_at(index)], y_in.at[:, block_at(index)],
                    sem_ry, (index,), other_y)

    def share_of(near, index):
        own = lax.rem(deep, 2)
        return rows_at((own if near else 1 - own) + 2 * index)

    def reduce_near(index, share):
        at = block_at(index)
        return send(sums.at[lane_y, share_of(False, share), at], z_in.at[share, :, at],
                    sem_rz, (index, share), twin)

    def reduce_far(index):
        at = block_at(index)
        return send(sums.at[lane_y, rows_at(lax.rem(deep + 2, depth)), at], z_in.at[2, :, at],
                    sem_rz, (index, 2), peer(2))

    def reduce_mid(index, following=None):
        reduce_y(index).wait_recv()
        if following is not None:
            reduce_y(following).start()
        at = block_at(index)
        sums[lane_y, :, at] = (
            sums[lane_y, :, at].astype(F32) + y_in[:, at].astype(F32)).astype(LOW)
        for share in range(2):
            reduce_near(index, share).start()

    def reduce_late(index):
        at = block_at(index)
        for share in range(2):
            reduce_near(index, share).wait_recv()
            rows = share_of(True, share)
            sums[lane_y, rows, at] = (
                sums[lane_y, rows, at].astype(F32) + z_in[share, :, at].astype(F32)).astype(LOW)
        reduce_far(index).start()

    def summed(at):
        return sums[lane_y, rows_at(deep), at].astype(F32) + z_in[2, :, at].astype(F32)

    def head_tile(index):
        return summed(pl.ds(index * LANES, LANES))

    def reduce_end(index):
        at = block_at(index)
        reduce_far(index).wait_recv()
        spot, size = spans[index]
        if spot >= hidden:
            grad_ref[:, spot - hidden:spot - hidden + size] = summed(at)

    def mixed_home(row, share):
        if row == 0:
            return z_in.at[share, :, mixed_at]
        return y_in.at[rows_at(share), mixed_at]

    def mixed_group(row):
        return lane_y if row == 0 else 1 - lane_y

    def mixed_near(row, share):
        return send(sums.at[mixed_group(row), share_of(False, share), mixed_at],
                    mixed_home(row, share), sem_rm, (row, share), twin)

    def mixed_far(row):
        return send(sums.at[mixed_group(row), rows_at(lax.rem(deep + 2, depth)), mixed_at],
                    mixed_home(row, 2), sem_rm, (row, 2), peer(2))

    def mixed_cross():
        return send(sums.at[1 - lane_y, rows_at(deep), mixed_at], mixed_home(1, 3),
                    sem_rm, (1, 3), other_y)

    def mixed_start():
        for row in range(2):
            for share in range(2):
                mixed_near(row, share).start()

    def mixed_mid():
        for row in range(2):
            for share in range(2):
                mixed_near(row, share).wait_recv()
                rows = share_of(True, share)
                group = mixed_group(row)
                sums[group, rows, mixed_at] = (
                    sums[group, rows, mixed_at].astype(F32)
                    + mixed_home(row, share)[...].astype(F32)).astype(LOW)
            mixed_far(row).start()

    def mixed_late():
        for row in range(2):
            mixed_far(row).wait_recv()
            total = (sums[mixed_group(row), rows_at(deep), mixed_at].astype(F32)
                     + mixed_home(row, 2)[...].astype(F32))
            if row == 0:
                grad_ref[:, mixed_out] = total
            else:
                sums[mixed_group(row), rows_at(deep), mixed_at] = total.astype(LOW)

    def mixed_end():
        mixed_cross().wait_recv()
        grad_ref[:, mixed_out] += mixed_home(1, 3)[...].astype(F32)

    def reduce_sent():
        for index in range(len(spans)):
            reduce_y(index).wait_send()
            for share in range(2):
                reduce_near(index, share).wait_send()
            reduce_far(index).wait_send()
        for row in range(2):
            for share in range(2):
                mixed_near(row, share).wait_send()
            mixed_far(row).wait_send()
        mixed_cross().wait_send()

    def halves(tile):
        return [jnp.where(low_half, tile, jnp.zeros_like(tile)),
                jnp.where(low_half, jnp.zeros_like(tile), tile)]

    def group_tile(group, index):
        return w_ref[group, :, index * LANES:(index + 1) * LANES]

    qkv_cols = 3 * tiles * LANES

    def arrange():
        for kind in range(4):
            for group in range(2):
                spot = (kind * tiles + group) * LANES
                wa[:, spot:spot + LANES] = group_tile(group, kind)
        for pair in range(2):
            one, two = (group_tile(group, 4 + pair).astype(F32) for group in range(2))
            spot = (2 * pair * tiles + 2) * LANES
            wa[:, spot:spot + LANES] = jnp.where(low_half, one, flip(two)).astype(LOW)
            spot = ((2 * pair + 1) * tiles + 2) * LANES
            wa[:, spot:spot + LANES] = jnp.where(low_half, flip(one), two).astype(LOW)

    x_copy = pltpu.make_async_copy(x_all.at[lane_y], x_ref, sem_l.at[PIECES + 3])
    if inside:
        gather_start(0)
        gather_start(1)
        gather_y(mixed_part, deep, True).start()
        gain_all[deep, 0:2, 0:rows_own] = gain_ref[...].astype(F32)
        for step in range(1, depth):
            gather_gain(step).start()
        for index in range(3):
            own_copy(index).start()
    x_copy.start()

    for piece in range(PIECES):
        place = piece * PIECE + lax.broadcasted_iota(jnp.int32, (1, PIECE), 1)
        begin = jnp.zeros((1, PIECE), jnp.int32)
        end = 0
        for index in range(length_ref.shape[1]):
            end = end + length_ref[lane_y, index]
            begin = jnp.where(place >= end, end, begin)
        start_s[piece] = begin

    if inside:
        gather_pass(0)
        gather_start(2)
        gather_pass(1)
        gather_start(3)
        gather_pass(2, 0, [0, 1])
        gather_start(4)
        for step in range(1, depth):
            gather_gain(step).wait()
        gather_end(0)
        gather_end(1)
        gather_pass(2, 0, [2])
        gather_pass(3, 0, [0])
        for index in range(3):
            own_copy(index).wait()
        gains = jnp.concatenate([gain_all[place, :, :rows_own] for place in range(depth)], axis=1)
    else:
        gains = gain_ref[...]
    arrange()
    x_copy.wait()
    gain1 = gains[0:1, :]
    gain2 = gains[1:2, :]

    def swap_copy(leave, enter):
        return send(swap_out.at[leave], swap_in.at[enter], sem_c, (enter,), other_core)

    def swap_start(slots, value):
        swap_out[slots[0]] = value
        swap_copy(*slots).start()

    def swap_end(slots):
        swap_copy(*slots).wait()
        return swap_out[slots[0]].astype(F32) + swap_in[slots[1]].astype(F32)

    def first_slots(piece):
        return lax.rem(piece, 2), piece

    def turned_slots(piece):
        return lax.rem(piece, 2), lax.rem(piece + 2, PIECES)

    def second_slots(piece):
        return 2, PIECES + lax.rem(piece, 2)

    def last_slots(piece):
        return 2, PIECES + lax.rem(piece + 1, 2)

    def put_rows(piece, rows):
        for t in range(2 * tiles):
            spare[piece, t] = rows[:, t * LANES:(t + 1) * LANES]

    def get_rows(piece):
        return jnp.concatenate([spare[piece, t] for t in range(2 * tiles)], axis=1)

    def joined(*stores):
        return jnp.concatenate([store[t] for store in stores for t in range(tiles)], axis=1)

    half = pl.ds(pl.multiple_of(core * half_cols, half_cols), half_cols)

    def hand_rows(piece):
        return send(there.at[piece, :, half], here.at[piece, :, half], sem_x, (piece,), other_layer)

    def hand_values(piece):
        return send(there_v.at[piece], here_v.at[piece], sem_v, (piece,), other_layer)

    def hand_on(piece):
        return send(here.at[piece, :, half], here.at[piece, :, half], sem_f, (piece,), other_core)

    def take_start(piece):
        hand_rows(piece).wait_recv()
        hand_on(piece).start()

    def take_values(piece):
        hand_values(piece).wait_recv()

    def emit_here(piece, stage):
        return pltpu.make_async_copy(stage.at[piece], out_ref.at[lane_y, piece], sem_l.at[piece])

    def emit_there(piece, stage):
        return send(stage.at[piece, :, half], out_ref.at[lane_y, piece, :, half],
                    sem_o, (piece,), other_y)

    def emit(piece, stage):
        return [emit_here(piece, stage), emit_there(piece, stage)]

    def emit_on(piece):
        spot = out_ref.at[1 - lane_y, piece, :, half]
        return send(spot, spot, sem_oc, (piece,), other_core)

    def reused(tile_index):
        if tile_index == 0:
            return None
        if tile_index == 1:
            return jnp.logical_and(second, lane >= 0)
        return jnp.logical_and(second, lane >= HEAD)

    def make_bias(piece, count):
        base = piece * PIECE
        query = base + lax.broadcasted_iota(jnp.int32, (1, PIECE), 1)
        begin = start_s[piece]
        for j in range(count):
            key = base - (count - 1 - j) * PIECE + lax.broadcasted_iota(jnp.int32, (PIECE, 1), 0)
            fine = jnp.logical_and(key >= begin, key <= query)
            bias_s[j] = jnp.where(fine, 0.0, -1e30).astype(F32)

    def attend(piece, count):
        make_bias(piece, count)
        for t in range(tiles):
            parts = []
            for h, query in enumerate(halves(q_s[piece, t])):
                scores = [
                    mm_back(k_s[piece - (count - 1 - j), t], query) + bias_s[j] for j in range(count)
                ]
                top = functools.reduce(
                    jnp.maximum, [jnp.max(s, axis=0, keepdims=True) for s in scores])
                expo = [jnp.exp(s - top) for s in scores]
                total = functools.reduce(
                    jnp.add, [jnp.sum(e, axis=0, keepdims=True) for e in expo])
                mixed = functools.reduce(jnp.add, [
                    mm(turn_s[piece - (count - 1 - j), t, h * HEAD:(h + 1) * HEAD, :], e.astype(LOW))
                    for j, e in enumerate(expo)
                ])
                parts.append(mixed * (1.0 / total))
                lse_s[piece, 2 * t + h] = top + jnp.log(total)
            o_s[piece, t] = jnp.concatenate(parts, axis=0).T.astype(LOW)

    def attend_back(piece, count):
        make_bias(piece, count)
        for t in range(tiles):
            inner = (do_s[t].astype(F32) * o_s[piece, t].astype(F32)).T
            queries = halves(q_s[piece, t])
            grads = halves(do_s[t])
            dq = [0.0, 0.0]
            inners = [jnp.sum(inner[h * HEAD:(h + 1) * HEAD], axis=0, keepdims=True) for h in range(2)]
            for j in range(count):
                at = piece - (count - 1 - j)
                dk_new, dv_new = 0.0, 0.0
                for h in range(2):
                    probs = jnp.exp(
                        mm_back(k_s[at, t], queries[h]) + bias_s[j] - lse_s[piece, 2 * t + h])
                    dprobs = mm_back(v_s[at, t], grads[h])
                    dscores = (probs * (dprobs - inners[h])).astype(LOW)
                    dv_new = dv_new + mm(probs.astype(LOW), grads[h])
                    dk_new = dk_new + mm(dscores, queries[h])
                    dq[h] = dq[h] + mm(turn_s[at, t, h * HEAD:(h + 1) * HEAD, :], dscores)
                spare[at, t] += dk_new
                spare[at, tiles + t] += dv_new
            dq_t = jnp.concatenate(dq, axis=0) * 0.125
            q_s[piece, t] = dq_t.T.astype(LOW)

    def by_count(piece, run):
        for count in range(1, WINDOW + 1):
            fits = piece >= WINDOW - 1 if count == WINDOW else piece == count - 1

            @pl.when(fits)
            def _(count=count):
                run(piece, count)

    def forward_attention(piece):
        @pl.when(second)
        def _():
            @pl.when(piece < 2)
            def _():
                take_start(piece)

            hand_on(piece).wait()

        rows = jnp.where(first, x_ref[piece], here[piece]).astype(F32)
        plain, factor = normalize(rows)
        plain1[piece] = plain.astype(LOW)
        fac_s[piece, :, 0:1] = factor
        normed = plain * gain1
        a_t[piece] = normed.T.astype(LOW)
        qkv = mm(normed.astype(LOW), wa[:, :qkv_cols])

        @pl.when(second)
        def _():
            take_values(piece)

        for t in range(tiles):
            q_s[piece, t] = (qkv[:, t * LANES:(t + 1) * LANES].astype(LOW) * 0.125).astype(LOW)
            key = qkv[:, (tiles + t) * LANES:(tiles + t + 1) * LANES].astype(LOW)
            value = qkv[:, (2 * tiles + t) * LANES:(2 * tiles + t + 1) * LANES].astype(LOW)
            mask = reused(t)
            if mask is not None:
                value = jnp.where(mask, here_v[piece, t - 1], value)
                there_v[piece, t - 1] = value
            k_s[piece, t] = key
            v_s[piece, t] = value
            turn_s[piece, t] = value.astype(F32).T.astype(LOW)

        @pl.when(first)
        def _():
            hand_values(piece).start()

        by_count(piece, attend)
        put_rows(piece, rows)
        swap_start(first_slots(piece), mm_back(joined(o_s.at[piece]), wa[:, qkv_cols:]).astype(LOW))

    def forward_middle(piece):
        put_rows(piece, get_rows(piece) + swap_end(first_slots(piece)))

    def forward_spread(piece):
        plain, factor = normalize(get_rows(piece))
        plain2[piece] = plain.astype(LOW)
        fac_s[piece, :, 1:2] = factor
        normed = plain * gain2
        m_t[piece] = normed.T.astype(LOW)
        normed = normed.astype(LOW)
        for group in range(2):
            z = mm(normed, w_ref[group, :, hidden:2 * hidden])
            square = z * z
            bent = jnp.tanh(GELU_K * z * (1.0 + GELU_C * square))
            upper = 0.5 * (1.0 + bent)
            slope = upper + 0.5 * z * (1.0 - bent * bent) * (GELU_K * (1.0 + 3.0 * GELU_C * square))
            slope = jnp.where(first, slope, slope * gd_s[piece, group].astype(F32))
            gd_s[piece, group] = slope.astype(LOW)
            e_s[piece, group] = (z * upper).astype(LOW)

    def forward_ahead(piece, carry):
        grad_low = x_ref[piece]
        g_t[piece] = grad_low.astype(F32).T.astype(LOW)
        for group in range(2):
            gd_s[piece, group] = mm(grad_low, w_ref[group, :, 2 * hidden:]).astype(LOW)
        return carry

    def forward_fold(piece):
        total = 0.0
        for group in range(2):
            total = total + mm_back(e_s[piece, group], w_ref[group, :, 2 * hidden:])
        swap_start(second_slots(piece), total.astype(LOW))

    def forward_result(piece):
        result = (get_rows(piece) + swap_end(second_slots(piece))).astype(LOW)

        @pl.when(first)
        def _():
            there[piece] = result
            hand_rows(piece).start()

        @pl.when(second)
        def _():
            here[piece] = result
            for copy in emit(piece, here):
                copy.start()

    def within(step, low_end, high_end):
        return jnp.logical_and(step >= low_end, step < high_end)

    lag = jnp.where(first, 0, 2 * PIECES)

    def forward(step, carry):
        place = step - lag

        @pl.when(within(place, 0, PIECES))
        def _():
            forward_attention(place)

        if inside:
            @pl.when(step == 0)
            def _():
                gather_pass(3, 0, [1])
                gather_start(5)
                gather_cross()

            @pl.when(step == 1)
            def _():
                gather_pass(3, 0, [2])
                gather_pass(4, 0, [0])

            @pl.when(step == 2)
            def _():
                gather_pass(4, 0, [1])
                gather_pass(5, 0, [0])
                gather_pass(5, 1, [0])

            @pl.when(step == 3)
            def _():
                gather_pass(4, 0, [2])
                gather_pass(5, 0, [1])
                gather_pass(5, 1, [1])
                gather_end(2)
                gather_end(3)

            @pl.when(step == 2 * PIECES - 2)
            def _():
                gather_pass(5, 0, [2])
                gather_pass(5, 1, [2])

            @pl.when(step == 2 * PIECES - 1)
            def _():
                gather_end(4)
                gather_end(5)

        @pl.when(jnp.logical_and(second, step == 2 * PIECES - 1))
        def _():
            lax.fori_loop(0, PIECES, forward_ahead, 0)

        @pl.when(jnp.logical_and(second, within(place, 2, PIECES + 1)))
        def _():
            forward_result(place - 2)

        @pl.when(within(place, 1, PIECES + 1))
        def _():
            forward_middle(place - 1)

        spread_place = place - jnp.where(first, PIECES, 1)

        @pl.when(within(spread_place, 0, PIECES))
        def _():
            forward_spread(spread_place)

        fold_place = place - jnp.where(first, 2 * PIECES, 1)

        @pl.when(within(fold_place, 0, PIECES))
        def _():
            @pl.when(jnp.logical_and(second, fold_place < PIECES - 2))
            def _():
                take_start(fold_place + 2)

            forward_fold(fold_place)

            @pl.when(first)
            def _():
                forward_result(fold_place)

        return carry

    lax.fori_loop(0, 3 * PIECES + 1, forward, 0)

    @pl.when(first)
    def _():
        for piece in range(PIECES):
            hand_rows(piece).wait_send()
            hand_values(piece).wait_send()

    gain_grad_ref[...] = jnp.zeros_like(gain_grad_ref)

    def hidden_grads(left, right, base, low_end, high_end):
        def one(index, carry):
            group, column = lax.rem(index, 2), index // 2
            spot = pl.multiple_of(column * block, block)
            total = 0.0
            for piece in range(PIECES):
                total = total + mm(left[piece], right[piece, group, :, pl.ds(spot, block)])
            sums[group, :, pl.ds(pl.multiple_of(base + spot, block), block)] = total.astype(LOW)
            return carry

        lax.fori_loop(2 * low_end, 2 * high_end, one, 0)

    def head_grads():
        pairs = []
        for kind in range(4):
            total = 0.0
            for piece in range(PIECES):
                if kind < 3:
                    total = total + mm(a_t[piece], joined((q_s, k_s, v_s)[kind].at[piece]))
                else:
                    total = total + mm(h_t[piece], joined(o_s.at[piece]))
            for group in range(2):
                part = total[:, group * LANES:(group + 1) * LANES].astype(LOW)
                sums[group, :, kind * LANES:(kind + 1) * LANES] = part
            pairs.append(total[:, 2 * LANES:])
        for pair in range(2):
            one, two = pairs[2 * pair:2 * pair + 2]
            spot = (4 + pair) * LANES
            sums[0, :, spot:spot + LANES] = jnp.where(low_half, one, flip(two)).astype(LOW)
            sums[1, :, spot:spot + LANES] = jnp.where(low_half, flip(one), two).astype(LOW)

    columns_in = hidden // block

    def down_grads():
        hidden_grads(g_t, e_s, 2 * hidden, 0, 1)
        if inside:
            reduce_y(0).start()
        hidden_grads(g_t, e_s, 2 * hidden, 1, columns_in)
        if inside:
            mixed_start()

    def up_grads():
        hidden_grads(m_t, gd_s, hidden, 0, columns_in)
        if inside:
            reduce_y(1).start()
            reduce_y(2).start()

    def grad_rows(piece):
        return jnp.where(first, here[piece], x_ref[piece])

    def backward_hidden(piece):
        @pl.when(first)
        def _():
            @pl.when(jnp.logical_or(piece == PIECES - 1, piece == 0))
            def _():
                take_start(piece)

            hand_on(piece).wait()

            grad_low = here[piece]
            g_t[piece] = grad_low.astype(F32).T.astype(LOW)

            @pl.when(piece == 0)
            def _():
                down_grads()

            for group in range(2):
                dz = mm(grad_low, w_ref[group, :, 2 * hidden:]) * gd_s[piece, group].astype(F32)
                gd_s[piece, group] = dz.astype(LOW)

        total = 0.0
        for group in range(2):
            total = total + mm_back(gd_s[piece, group], w_ref[group, :, hidden:2 * hidden])
        swap_start(turned_slots(piece), total.astype(LOW))

        @pl.when(jnp.logical_and(first, piece == 0))
        def _():
            up_grads()

    def backward_attention(piece):
        dm = swap_end(turned_slots(piece))
        plain = plain2[piece].astype(F32)
        gain_grad_ref[1:2, :] += jnp.sum(dm * plain, axis=0, keepdims=True)
        middle = grad_rows(piece).astype(F32) + norm_back(dm, plain, fac_s[piece, :, 1:2], gain2)
        h_t[piece] = middle.T.astype(LOW)
        dmixed = mm(middle.astype(LOW), wa[:, qkv_cols:]).astype(LOW)
        for t in range(tiles):
            do_s[t] = dmixed[:, t * LANES:(t + 1) * LANES]
        by_count(piece, attend_back)
        for t in range(1, tiles):
            there_v[piece, t - 1] = spare[piece, tiles + t].astype(LOW)

        @pl.when(first)
        def _():
            hand_values(piece).wait_recv()

        @pl.when(second)
        def _():
            hand_values(piece).start()

        for t in range(tiles):
            dvalue = spare[piece, tiles + t]
            mask = reused(t)
            if mask is not None:
                came = jnp.logical_and(first, jnp.logical_or(t == 1, lane >= HEAD))
                dvalue = jnp.where(came, dvalue + here_v[piece, t - 1].astype(F32), dvalue)
                dvalue = jnp.where(mask, 0.0, dvalue)
            k_s[piece, t] = spare[piece, t].astype(LOW)
            v_s[piece, t] = dvalue.astype(LOW)
        put_rows(piece, middle)
        terms = joined(q_s.at[piece], k_s.at[piece], v_s.at[piece])
        swap_start(last_slots(piece), mm_back(terms, wa[:, :qkv_cols]).astype(LOW))

    def backward_result(piece):
        da = swap_end(last_slots(piece))
        plain = plain1[piece].astype(F32)
        gain_grad_ref[0:1, :] += jnp.sum(da * plain, axis=0, keepdims=True)
        there[piece] = (get_rows(piece) + norm_back(da, plain, fac_s[piece, :, 0:1], gain1)).astype(LOW)

        @pl.when(second)
        def _():
            hand_rows(piece).start()

        @pl.when(first)
        def _():
            for copy in emit(piece, there):
                copy.start()

    last_ahead = 2 * PIECES - 2

    def backward(step, carry):
        turn = step // 2
        even = lax.rem(step, 2) == 0
        hidden_first = jnp.logical_or(
            step == last_ahead, jnp.logical_and(jnp.logical_not(even), step < last_ahead))
        hidden_second = jnp.logical_and(even, turn < PIECES)
        hidden_piece = PIECES - 1 - jnp.where(step == last_ahead, PIECES - 1, turn)

        @pl.when(jnp.where(first, hidden_first, hidden_second))
        def _():
            backward_hidden(hidden_piece)

        @pl.when(step == 0)
        def _():
            @pl.when(second)
            def _():
                forward_result(PIECES - 1)

            spare[...] = jnp.zeros_like(spare)
            for piece in range(PIECES):
                for t in range(tiles):
                    turn_s[piece, t] = k_s[piece, t].astype(F32).T.astype(LOW)

        mixed_first = jnp.logical_or(
            jnp.logical_and(step > last_ahead, step <= 2 * PIECES),
            jnp.logical_and(even, jnp.logical_and(step >= 2, step < last_ahead)))
        mixed_second = jnp.logical_and(jnp.logical_not(even), turn >= 1)
        place = PIECES - jnp.where(
            first, jnp.where(step > last_ahead, step - last_ahead + PIECES - 2, turn), turn)

        @pl.when(jnp.where(first, mixed_first, mixed_second))
        def _():
            @pl.when(place < PIECES - 1)
            def _():
                backward_result(place + 1)

            @pl.when(jnp.logical_and(first, place >= 2))
            def _():
                take_start(place - 1)

            backward_attention(place)

        return carry

    lax.fori_loop(0, 2 * PIECES + 2, backward, 0)
    backward_result(0)

    @pl.when(second)
    def _():
        down_grads()
        up_grads()

    head_grads()

    def emit_stage(run):
        @pl.when(first)
        def _():
            run(there)

        @pl.when(second)
        def _():
            run(here)

    def pass_outputs(stage):
        for piece in range(PIECES):
            emit_there(piece, stage).wait_recv()
            emit_on(piece).start()

    def finish_outputs(stage):
        for piece in range(PIECES):
            emit_here(piece, stage).wait()
            emit_there(piece, stage).wait_send()
            emit_on(piece).wait()

    if inside:
        gain_copy = send(gain_grad_ref, gain_y, sem_gg, (0,), other_y)
        gain_copy.start()
        reduce_y(3).start()
        mixed_mid()
        reduce_mid(0, 4)
        gain_copy.wait()
        gain_y[...] = gain_y[...] + gain_grad_ref[...]
        gain_sends = [
            send(gain_y, gain_z.at[step - 1], sem_gg, (step,), peer(step)) for step in range(1, depth)]
        for copy in gain_sends:
            copy.start()
        reduce_mid(1)
        reduce_late(0)
        reduce_mid(2, 5)
        mixed_late()
        reduce_late(1)
        reduce_mid(3, 6)
        reduce_end(0)
        reduce_late(2)
        reduce_mid(4, 7)
        reduce_end(1)
        reduce_late(3)
        reduce_end(2)
        total = gain_y[...]
        for step, copy in enumerate(gain_sends):
            copy.wait()
            total = total + gain_z[step]
        gain_out[...] = functools.reduce(jnp.add, [
            jnp.where(deep == index, total[0:2, index * rows_own:(index + 1) * rows_own], 0.0)
            for index in range(depth)])
        reduce_mid(5)
        reduce_late(4)
        reduce_end(3)
        emit_stage(pass_outputs)
        reduce_mid(6)
        mixed_cross().start()
        reduce_late(5)
        reduce_end(4)

        def place(sec, row, unit):
            return (sec * 2 + row) * 2 + unit

        mine = place(section, lane_y, core)
        for half_tile, tile_index in enumerate((2, 5)):
            value_ref[mine, :, half_tile * LANES:(half_tile + 1) * LANES] = (
                head_tile(tile_index).astype(LOW))
        value_y = send(value_ref.at[mine], value_ref.at[mine], sem_va, (0,), other_y)
        value_y.start()
        reduce_mid(7)
        reduce_late(6)
        reduce_end(5)
        value_y.wait()
        value_x = []
        for row in range(2):
            at = place(section, row, core)
            value_x.append(send(value_ref.at[at], value_ref.at[at], sem_va, (1 + row,), other_layer))
            value_x[-1].start()
        reduce_late(7)
        reduce_end(6)
        for copy in value_x:
            copy.wait()
        value_c = []
        for sec in range(2):
            for row in range(2):
                at = place(sec, row, core)
                value_c.append(
                    send(value_ref.at[at], value_ref.at[at], sem_va, (3 + 2 * sec + row,), other_core))
                value_c[-1].start()
        mixed_end()
        reduce_end(7)
        edge = 2 * HEAD

        def columns(kind, pair, upper):
            rest = head_tile(pair)
            return jnp.concatenate(
                [head_tile(kind), rest[:, HEAD:] if upper else rest[:, :HEAD]], axis=1)

        head_out[0] = columns(0, 4, False)
        head_out[1] = columns(1, 4, True)
        head_out[2] = columns(3, 5, True)
        for copy in value_c:
            copy.wait()
        value_out[...] = jnp.concatenate(
            [value_ref[index, :, :edge + HEAD] for index in range(value_out.shape[1] // (edge + HEAD))],
            axis=1).astype(F32)
        reduce_sent()
    else:
        emit_stage(pass_outputs)

    emit_stage(finish_outputs)

    @pl.when(second)
    def _():
        for piece in range(PIECES):
            hand_rows(piece).wait_send()
            hand_values(piece).wait_send()


def run_layers(lengths, x_rows, gains, weights, cols, value_cols, depth, inside):
    width = x_rows.shape[3]
    tiles = width // 2 // LANES
    rows_own = width // depth
    columns = 3 * width
    vmem = pl.BlockSpec(memory_space=pltpu.VMEM)
    anywhere = pl.BlockSpec(memory_space=pl.ANY)
    smem = pl.BlockSpec(memory_space=pltpu.SMEM)
    per_tile = (PIECES, tiles, PIECE, LANES)
    turned = (PIECES, tiles, LANES, PIECE)
    flat = (PIECES, PIECE, width)
    flat_turned = (PIECES, width, PIECE)
    wide = (PIECES, 2, PIECE, width)
    low = lambda shape: pltpu.VMEM(shape, LOW)
    full = lambda shape: pltpu.VMEM(shape, F32)
    dma = lambda *shape: pltpu.SemaphoreType.DMA(shape)
    out_shape = [
        jax.ShapeDtypeStruct((2,) + flat, LOW),
        jax.ShapeDtypeStruct((rows_own, 2 * width), F32) if inside
        else jax.ShapeDtypeStruct(weights[0].shape, LOW),
        jax.ShapeDtypeStruct((8, width), F32),
    ]
    out_specs = [anywhere, vmem, vmem]
    scratch = [
        low((width, 4 * tiles * LANES)),
        low(per_tile), low(per_tile), low(per_tile), low(turned), low(per_tile),
        full((PIECES, 2 * tiles, 1, PIECE)),
        low(flat), low(flat), full((PIECES, PIECE, 2)),
        low(flat_turned), low(flat_turned), low(flat_turned), low(flat_turned),
        low(wide), low(wide), low((tiles, PIECE, LANES)),
        full((PIECES, 2 * tiles, PIECE, LANES)),
        full((WINDOW, PIECE, PIECE)), low(flat), pltpu.VMEM((PIECES, 1, PIECE), jnp.int32),
        low(flat), low((PIECES, 2, PIECE, LANES)), low(flat), low((PIECES, 2, PIECE, LANES)),
        low((3, PIECE, width)), low((PIECES + 2, PIECE, width)),
        dma(2, PIECES), dma(2, PIECES), dma(2, PIECES), dma(2, PIECES + 2), dma(2, PIECES),
        dma(2, PIECES), dma(4 + PIECES),
    ]
    if inside:
        out_shape += [
            jax.ShapeDtypeStruct((3, rows_own, cols), F32),
            jax.ShapeDtypeStruct((2, rows_own), F32),
            jax.ShapeDtypeStruct((rows_own, value_cols), F32)]
        out_specs += [vmem] * 3
        scratch += [
            low((2, width, columns)), full((depth, 8, -(-rows_own // LANES) * LANES)),
            low((2, width, columns)), low((width, columns)), low((depth - 1, rows_own, columns)),
            full((8, width)), full((depth - 1, 8, width)),
            low((8, rows_own, 2 * LANES)),
            dma(2, PARTS + 1, depth - 1, 2), dma(2, PARTS, depth), dma(2, depth), dma(2, 8),
            dma(2, 8, 3), dma(2, 2, 4), dma(2, depth), dma(2, 7),
        ]
    return pl.pallas_call(
        functools.partial(layers_kernel, width, depth, inside),
        out_shape=out_shape,
        in_specs=[smem, anywhere, vmem] + [anywhere if inside else vmem] * len(weights),
        out_specs=out_specs,
        scratch_shapes=scratch,
        compiler_params=pltpu.CompilerParams(
            collective_id=0, has_side_effects=True, vmem_limit_bytes=63 << 20),
        name="layers",
    )(lengths, x_rows, gains, *weights)


def pack(w_qk, w_value, w_out):
    query, key, out_t = w_qk[:, 0], w_qk[:, 1], w_out.T
    edge = 2 * HEAD
    return jnp.concatenate(
        [query[:, :edge], key[:, :edge], w_value[:, :edge], out_t[:, :edge],
         query[:, edge:], key[:, edge:], w_value[:, edge:], out_t[:, edge:]],
        axis=1)


def unpack(packed):
    edge = 2 * HEAD
    cut = lambda spot, size: packed[:, spot:spot + size]
    query = jnp.concatenate([cut(0, edge), cut(4 * edge, HEAD)], axis=1)
    key = jnp.concatenate([cut(edge, edge), cut(4 * edge + HEAD, HEAD)], axis=1)
    value = jnp.concatenate([cut(2 * edge, edge), cut(5 * edge, HEAD)], axis=1)
    out_t = jnp.concatenate([cut(3 * edge, edge), cut(5 * edge + HEAD, HEAD)], axis=1)
    hidden = packed.shape[1] // 3
    return (
        jnp.stack([query, key], axis=1), value, out_t.T,
        cut(hidden, hidden), cut(2 * hidden, hidden).T)


def shards(
    ends_in, seq_lengths, norm_gains, qk_weight, value_weight, out_weight, fc_weight, proj_weight
):
    section = lax.axis_index("section")
    lane_y = lax.axis_index("y")
    group = 2 * lane_y + lax.axis_index("core")
    first = section == 0
    cols = qk_weight.shape[3]
    width = ends_in.shape[2]
    fresh = (value_weight.shape[1] - width) // cols
    offset = jnp.where(first, group, width // cols + jnp.minimum(group, fresh - 1)) * cols
    w_value = lax.dynamic_slice_in_dim(value_weight, offset, cols, 1)
    parts = [pack(qk_weight[0], w_value, out_weight[0]), fc_weight[0], proj_weight[0].T]
    depth = lax.axis_size("dp")
    inside = depth == 4 and width % (16 * depth) == 0
    if inside:
        weights = parts
        gains = norm_gains[0].T
    else:
        weights = lax.all_gather(jnp.concatenate(parts, axis=1), "dp", axis=0, tiled=True)
        weights = [lax.all_gather(weights, "y", axis=0)]
        gains = lax.all_gather(norm_gains[0], "dp", axis=0, tiled=True).astype(F32).T
    x_rows = ends_in[0].reshape(2, PIECES, PIECE, width)
    kept = width // cols + fresh
    results = run_layers(
        seq_lengths, x_rows, gains, weights, cols, value_weight.shape[1], depth, inside)
    both = results[0].reshape(2 * MB_TOK, width)
    if inside:
        _, grads, _, heads, gain_rows, d_value = results
        attn_gain, mlp_gain = gain_rows[0], gain_rows[1]
        d_qk = jnp.stack([heads[0], heads[1]], axis=1)
        d_out = heads[2].T
        d_up, d_down = grads[:, :width], grads[:, width:].T
    else:
        _, grads, gain_grads = results
        grads = lax.psum_scatter(grads, "y", scatter_dimension=0, tiled=False)
        grads = lax.psum_scatter(grads, "dp", scatter_dimension=0, tiled=True)
        gain_rows = lax.psum(gain_grads[:2], "y").T
        gain_rows = lax.psum_scatter(gain_rows, "dp", scatter_dimension=0, tiled=True)
        attn_gain, mlp_gain = gain_rows[:, 0], gain_rows[:, 1]
        d_qk, d_value, d_out, d_up, d_down = unpack(grads.astype(F32))
        values = lax.all_gather(d_value.astype(LOW), ("section", "y", "core"), axis=0)
        d_value = jnp.concatenate([values[index] for index in range(kept)], axis=1).astype(F32)
    return (
        both[None], attn_gain[None], mlp_gain[None], d_qk[None], d_value,
        d_out[None], d_up[None], d_down[None])


def solution(mesh):
    sections, depth, split = (mesh.shape[name] for name in ("section", "dp", "mp"))
    grid = Mesh(mesh.devices.reshape(sections, depth, split // 2, 2), ("section", "dp", "y", "core"))
    mp = ("y", "core")
    in_specs = (
        P("section", "dp", None),
        P("dp", None),
        P("section", "dp", None),
        P("section", "dp", None, mp),
        P("dp", None),
        P("section", mp, "dp"),
        P("section", "dp", mp),
        P("section", mp, "dp"),
    )
    out_specs = (
        P("section", "dp", None),
        P("section", "dp"),
        P("section", "dp"),
        P("section", "dp", None, mp),
        P("dp", None),
        P("section", mp, "dp"),
        P("section", "dp", mp),
        P("section", mp, "dp"),
    )
    return jax.shard_map(shards, mesh=grid, in_specs=in_specs, out_specs=out_specs, check_vma=False)
```

```python
import functools
import math

import jax
import jax.numpy as jnp
from jax import lax
from jax.experimental import pallas as pl
from jax.experimental.pallas import tpu as pltpu
from jax.sharding import Mesh, PartitionSpec as P

HEAD = 64
MB_TOK = 1024
PIECE = 256
PIECES = MB_TOK // PIECE
WINDOW = 3
PARTS = 6
LANES = 128
EPSILON = 1e-05
GELU_K = math.sqrt(2.0 / math.pi)
GELU_C = 0.044715
MESH = pl.DeviceIdType.MESH
F32 = jnp.float32
LOW = jnp.bfloat16


def mm(left, right):
    return lax.dot_general(left, right, (((1,), (0,)), ((), ())), preferred_element_type=F32)


def mm_back(left, right):
    return lax.dot_general(left, right, (((1,), (1,)), ((), ())), preferred_element_type=F32)


def normalize(rows):
    centred = rows - jnp.mean(rows, axis=1, keepdims=True)
    factor = lax.rsqrt(jnp.mean(centred * centred, axis=1, keepdims=True) + EPSILON)
    return centred * factor, factor


def norm_back(grad, plain, factor, gain):
    scaled = grad * gain
    return factor * (
        scaled
        - jnp.mean(scaled, axis=1, keepdims=True)
        - plain * jnp.mean(scaled * plain, axis=1, keepdims=True)
    )


def flip(tile):
    return pltpu.roll(tile, HEAD, 1)


def layers_kernel(width, depth, inside, *refs):
    refs = list(refs)
    take = lambda count: [refs.pop(0) for _ in range(count)]
    length_ref, x_all, gain_ref = take(3)
    part_refs = take(3 if inside else 1)
    out_ref, grad_ref, gain_grad_ref = take(3)
    if inside:
        head_out, gain_out, value_out = take(3)
    (wa, q_s, k_s, v_s, turn_s, o_s, lse_s, plain1, plain2, fac_s,
     a_t, m_t, g_t, h_t, e_s, gd_s, do_s, spare, bias_s, x_ref, start_s,
     there, there_v, here, here_v, swap_out, swap_in,
     sem_x, sem_v, sem_f, sem_c, sem_o, sem_oc, sem_l) = take(34)
    if inside:
        (w_ref, gain_all, sums, y_in, z_in, gain_y, gain_z, value_ref,
         sem_az, sem_ay, sem_gz, sem_ry, sem_rz, sem_rm, sem_gg, sem_va) = take(16)
    else:
        w_ref, sums = part_refs[0], grad_ref

    section = lax.axis_index("section")
    core = lax.axis_index("core")
    lane_y = lax.axis_index("y")
    deep = lax.axis_index("dp")
    other_layer = {"section": 1 - section}
    other_core = {"core": 1 - core}
    other_y = {"y": 1 - lane_y}
    first = section == 0
    second = jnp.logical_not(first)
    tiles = width // 2 // LANES
    hidden = width
    rows_own = width // depth
    half_cols = width // 2

    def send(src, dst, sems, index, target):
        return pltpu.make_async_remote_copy(
            src_ref=src, dst_ref=dst, send_sem=sems.at[(0,) + index], recv_sem=sems.at[(1,) + index],
            device_id=target, device_id_type=MESH)

    def peer(step):
        return {"dp": lax.rem(deep + step, depth)}

    barrier = pltpu.get_barrier_semaphore()
    friends = [other_layer, other_core, other_y]
    if inside:
        friends = friends + [peer(step) for step in range(1, depth)]
        twin = {"dp": deep + 1 - 2 * lax.rem(deep, 2)}
    for friend in friends:
        pl.semaphore_signal(barrier, inc=1, device_id=friend, device_id_type=MESH)
    pl.semaphore_wait(barrier, len(friends))

    lane = lax.broadcasted_iota(jnp.int32, (1, LANES), 1)
    low_half = lane < HEAD

    def rows_at(place):
        return pl.ds(pl.multiple_of(place * rows_own, rows_own), rows_own)

    unit = 3 * hidden // PARTS
    per_ref = PARTS // 3
    ways = (1, -1)
    mixed_part = PARTS - 1

    def cols_at(part):
        return pl.ds(part * unit, unit)

    def on_line(place):
        return jnp.logical_and(place >= 0, place < depth)

    def own_part(part):
        return part_refs[part // per_ref].at[:, pl.ds(part % per_ref * unit, unit)]

    def own_copy(index):
        return pltpu.make_async_copy(
            part_refs[index], w_ref.at[lane_y, rows_at(deep), pl.ds(index * hidden, hidden)],
            sem_l.at[PIECES + index])

    def gather_line(part, row, hop, way):
        place = deep - hop * ways[way]
        home = lane_y if row == 0 else 1 - lane_y
        spot = w_ref.at[home, rows_at(place), cols_at(part)]
        src = own_part(part) if row == 0 and hop == 0 else spot
        return send(src, spot, sem_az, (part + row, hop, way), {"dp": deep + ways[way]})

    def line_start(part, row, hop, way):
        @pl.when(jnp.logical_and(on_line(deep - hop * ways[way]), on_line(deep + ways[way])))
        def _():
            gather_line(part, row, hop, way).start()

    def line_sent(part, row, hop, way):
        @pl.when(jnp.logical_and(on_line(deep - hop * ways[way]), on_line(deep + ways[way])))
        def _():
            gather_line(part, row, hop, way).wait_send()

    def gather_y(part, place, own):
        spot = w_ref.at[lane_y, rows_at(place), cols_at(part)]
        src = own_part(part) if own else spot
        return send(src, spot, sem_ay, (part, place), other_y)

    def gather_gain(step):
        return send(gain_all.at[deep], gain_all.at[deep], sem_gz, (step,), peer(step))

    def gather_start(part):
        for way in range(2):
            line_start(part, 0, 0, way)
        if part != mixed_part:
            gather_y(part, deep, True).start()

    def gather_pass(part, row=0, hops=None):
        for hop in range(depth - 1) if hops is None else hops:
            for way in range(2):
                place = deep - (hop + 1) * ways[way]

                @pl.when(on_line(place))
                def _(hop=hop, way=way, place=place):
                    gather_line(part, row, hop, way).wait_recv()
                    if hop < depth - 2:
                        line_start(part, row, hop + 1, way)
                    if part != mixed_part:
                        gather_y(part, place, False).start()

    def gather_cross():
        gather_y(mixed_part, deep, True).wait()
        for way in range(2):
            line_start(mixed_part, 1, 0, way)

    def gather_end(part):
        if part != mixed_part:
            for place in range(depth):
                gather_y(part, place, False).wait()
        for row in range(2 if part == mixed_part else 1):
            for hop in range(depth - 1):
                for way in range(2):
                    line_sent(part, row, hop, way)

    block = 2 * LANES
    last = block // 2
    spans = [
        (2 * hidden, block), (hidden, block), (hidden + block, block),
        (block, block), (2 * block, block), (0, block),
        (hidden + 2 * block, last), (hidden + 2 * block + last, last)]
    mixed_at = pl.ds(2 * hidden + block, 2 * block)
    mixed_out = pl.ds(hidden + block, 2 * block)

    def block_at(index):
        return pl.ds(spans[index][0], spans[index][1])

    def reduce_y(index):
        return send(sums.at[1 - lane_y, :, block_at(index)], y_in.at[:, block_at(index)],
                    sem_ry, (index,), other_y)

    def share_of(near, index):
        own = lax.rem(deep, 2)
        return rows_at((own if near else 1 - own) + 2 * index)

    def reduce_near(index, share):
        at = block_at(index)
        return send(sums.at[lane_y, share_of(False, share), at], z_in.at[share, :, at],
                    sem_rz, (index, share), twin)

    def reduce_far(index):
        at = block_at(index)
        return send(sums.at[lane_y, rows_at(lax.rem(deep + 2, depth)), at], z_in.at[2, :, at],
                    sem_rz, (index, 2), peer(2))

    def reduce_mid(index, following=None):
        reduce_y(index).wait_recv()
        if following is not None:
            reduce_y(following).start()
        at = block_at(index)
        sums[lane_y, :, at] = (
            sums[lane_y, :, at].astype(F32) + y_in[:, at].astype(F32)).astype(LOW)
        for share in range(2):
            reduce_near(index, share).start()

    def reduce_late(index):
        at = block_at(index)
        for share in range(2):
            reduce_near(index, share).wait_recv()
            rows = share_of(True, share)
            sums[lane_y, rows, at] = (
                sums[lane_y, rows, at].astype(F32) + z_in[share, :, at].astype(F32)).astype(LOW)
        reduce_far(index).start()

    def summed(at):
        return sums[lane_y, rows_at(deep), at].astype(F32) + z_in[2, :, at].astype(F32)

    def head_tile(index):
        return summed(pl.ds(index * LANES, LANES))

    def reduce_end(index):
        at = block_at(index)
        reduce_far(index).wait_recv()
        spot, size = spans[index]
        if spot >= hidden:
            grad_ref[:, spot - hidden:spot - hidden + size] = summed(at)

    def mixed_home(row, share):
        if row == 0:
            return z_in.at[share, :, mixed_at]
        return y_in.at[rows_at(share), mixed_at]

    def mixed_group(row):
        return lane_y if row == 0 else 1 - lane_y

    def mixed_near(row, share):
        return send(sums.at[mixed_group(row), share_of(False, share), mixed_at],
                    mixed_home(row, share), sem_rm, (row, share), twin)

    def mixed_far(row):
        return send(sums.at[mixed_group(row), rows_at(lax.rem(deep + 2, depth)), mixed_at],
                    mixed_home(row, 2), sem_rm, (row, 2), peer(2))

    def mixed_cross():
        return send(sums.at[1 - lane_y, rows_at(deep), mixed_at], mixed_home(1, 3),
                    sem_rm, (1, 3), other_y)

    def mixed_start():
        for row in range(2):
            for share in range(2):
                mixed_near(row, share).start()

    def mixed_mid():
        for row in range(2):
            for share in range(2):
                mixed_near(row, share).wait_recv()
                rows = share_of(True, share)
                group = mixed_group(row)
                sums[group, rows, mixed_at] = (
                    sums[group, rows, mixed_at].astype(F32)
                    + mixed_home(row, share)[...].astype(F32)).astype(LOW)
            mixed_far(row).start()

    def mixed_late():
        for row in range(2):
            mixed_far(row).wait_recv()
            total = (sums[mixed_group(row), rows_at(deep), mixed_at].astype(F32)
                     + mixed_home(row, 2)[...].astype(F32))
            if row == 0:
                grad_ref[:, mixed_out] = total
            else:
                sums[mixed_group(row), rows_at(deep), mixed_at] = total.astype(LOW)

    def mixed_end():
        mixed_cross().wait_recv()
        grad_ref[:, mixed_out] += mixed_home(1, 3)[...].astype(F32)

    def reduce_sent():
        for index in range(len(spans)):
            reduce_y(index).wait_send()
            for share in range(2):
                reduce_near(index, share).wait_send()
            reduce_far(index).wait_send()
        for row in range(2):
            for share in range(2):
                mixed_near(row, share).wait_send()
            mixed_far(row).wait_send()
        mixed_cross().wait_send()

    def halves(tile):
        return [jnp.where(low_half, tile, jnp.zeros_like(tile)),
                jnp.where(low_half, jnp.zeros_like(tile), tile)]

    def group_tile(group, index):
        return w_ref[group, :, index * LANES:(index + 1) * LANES]

    qkv_cols = 3 * tiles * LANES

    def arrange():
        for kind in range(4):
            for group in range(2):
                spot = (kind * tiles + group) * LANES
                wa[:, spot:spot + LANES] = group_tile(group, kind)
        for pair in range(2):
            one, two = (group_tile(group, 4 + pair).astype(F32) for group in range(2))
            spot = (2 * pair * tiles + 2) * LANES
            wa[:, spot:spot + LANES] = jnp.where(low_half, one, flip(two)).astype(LOW)
            spot = ((2 * pair + 1) * tiles + 2) * LANES
            wa[:, spot:spot + LANES] = jnp.where(low_half, flip(one), two).astype(LOW)

    x_copy = pltpu.make_async_copy(x_all.at[lane_y], x_ref, sem_l.at[PIECES + 3])
    if inside:
        gather_start(0)
        gather_start(1)
        gather_y(mixed_part, deep, True).start()
        gain_all[deep, 0:2, 0:rows_own] = gain_ref[...].astype(F32)
        for step in range(1, depth):
            gather_gain(step).start()
        for index in range(3):
            own_copy(index).start()
    x_copy.start()

    for piece in range(PIECES):
        place = piece * PIECE + lax.broadcasted_iota(jnp.int32, (1, PIECE), 1)
        begin = jnp.zeros((1, PIECE), jnp.int32)
        end = 0
        for index in range(length_ref.shape[1]):
            end = end + length_ref[lane_y, index]
            begin = jnp.where(place >= end, end, begin)
        start_s[piece] = begin

    if inside:
        gather_pass(0)
        gather_start(2)
        gather_pass(1)
        gather_start(3)
        gather_pass(2, 0, [0, 1])
        gather_start(4)
        for step in range(1, depth):
            gather_gain(step).wait()
        gather_end(0)
        gather_end(1)
        gather_pass(2, 0, [2])
        gather_pass(3, 0, [0])
        for index in range(3):
            own_copy(index).wait()
        gains = jnp.concatenate([gain_all[place, :, :rows_own] for place in range(depth)], axis=1)
    else:
        gains = gain_ref[...]
    arrange()
    x_copy.wait()
    gain1 = gains[0:1, :]
    gain2 = gains[1:2, :]

    def swap_copy(leave, enter):
        return send(swap_out.at[leave], swap_in.at[enter], sem_c, (enter,), other_core)

    def swap_start(slots, value):
        swap_out[slots[0]] = value
        swap_copy(*slots).start()

    def swap_end(slots):
        swap_copy(*slots).wait()
        return swap_out[slots[0]].astype(F32) + swap_in[slots[1]].astype(F32)

    def first_slots(piece):
        return lax.rem(piece, 2), piece

    def turned_slots(piece):
        return lax.rem(piece, 2), lax.rem(piece + 2, PIECES)

    def second_slots(piece):
        return 2, PIECES + lax.rem(piece, 2)

    def last_slots(piece):
        return 2, PIECES + lax.rem(piece + 1, 2)

    def put_rows(piece, rows):
        for t in range(2 * tiles):
            spare[piece, t] = rows[:, t * LANES:(t + 1) * LANES]

    def get_rows(piece):
        return jnp.concatenate([spare[piece, t] for t in range(2 * tiles)], axis=1)

    def joined(*stores):
        return jnp.concatenate([store[t] for store in stores for t in range(tiles)], axis=1)

    half = pl.ds(pl.multiple_of(core * half_cols, half_cols), half_cols)

    def hand_rows(piece):
        return send(there.at[piece, :, half], here.at[piece, :, half], sem_x, (piece,), other_layer)

    def hand_values(piece):
        return send(there_v.at[piece], here_v.at[piece], sem_v, (piece,), other_layer)

    def hand_on(piece):
        return send(here.at[piece, :, half], here.at[piece, :, half], sem_f, (piece,), other_core)

    def take_start(piece):
        hand_rows(piece).wait_recv()
        hand_on(piece).start()

    def take_values(piece):
        hand_values(piece).wait_recv()

    def emit_here(piece, stage):
        return pltpu.make_async_copy(stage.at[piece], out_ref.at[lane_y, piece], sem_l.at[piece])

    def emit_there(piece, stage):
        return send(stage.at[piece, :, half], out_ref.at[lane_y, piece, :, half],
                    sem_o, (piece,), other_y)

    def emit(piece, stage):
        return [emit_here(piece, stage), emit_there(piece, stage)]

    def emit_on(piece):
        spot = out_ref.at[1 - lane_y, piece, :, half]
        return send(spot, spot, sem_oc, (piece,), other_core)

    def reused(tile_index):
        if tile_index == 0:
            return None
        if tile_index == 1:
            return jnp.logical_and(second, lane >= 0)
        return jnp.logical_and(second, lane >= HEAD)

    def make_bias(piece, count):
        base = piece * PIECE
        query = base + lax.broadcasted_iota(jnp.int32, (1, PIECE), 1)
        begin = start_s[piece]
        for j in range(count):
            key = base - (count - 1 - j) * PIECE + lax.broadcasted_iota(jnp.int32, (PIECE, 1), 0)
            fine = jnp.logical_and(key >= begin, key <= query)
            bias_s[j] = jnp.where(fine, 0.0, -1e30).astype(F32)

    def attend(piece, count):
        make_bias(piece, count)
        for t in range(tiles):
            parts = []
            for h, query in enumerate(halves(q_s[piece, t])):
                scores = [
                    mm_back(k_s[piece - (count - 1 - j), t], query) + bias_s[j] for j in range(count)
                ]
                top = functools.reduce(
                    jnp.maximum, [jnp.max(s, axis=0, keepdims=True) for s in scores])
                expo = [jnp.exp(s - top) for s in scores]
                total = functools.reduce(
                    jnp.add, [jnp.sum(e, axis=0, keepdims=True) for e in expo])
                mixed = functools.reduce(jnp.add, [
                    mm(turn_s[piece - (count - 1 - j), t, h * HEAD:(h + 1) * HEAD, :], e.astype(LOW))
                    for j, e in enumerate(expo)
                ])
                parts.append(mixed * (1.0 / total))
                lse_s[piece, 2 * t + h] = top + jnp.log(total)
            o_s[piece, t] = jnp.concatenate(parts, axis=0).T.astype(LOW)

    def attend_back(piece, count):
        make_bias(piece, count)
        for t in range(tiles):
            inner = (do_s[t].astype(F32) * o_s[piece, t].astype(F32)).T
            queries = halves(q_s[piece, t])
            grads = halves(do_s[t])
            dq = [0.0, 0.0]
            inners = [jnp.sum(inner[h * HEAD:(h + 1) * HEAD], axis=0, keepdims=True) for h in range(2)]
            for j in range(count):
                at = piece - (count - 1 - j)
                dk_new, dv_new = 0.0, 0.0
                for h in range(2):
                    probs = jnp.exp(
                        mm_back(k_s[at, t], queries[h]) + bias_s[j] - lse_s[piece, 2 * t + h])
                    dprobs = mm_back(v_s[at, t], grads[h])
                    dscores = (probs * (dprobs - inners[h])).astype(LOW)
                    dv_new = dv_new + mm(probs.astype(LOW), grads[h])
                    dk_new = dk_new + mm(dscores, queries[h])
                    dq[h] = dq[h] + mm(turn_s[at, t, h * HEAD:(h + 1) * HEAD, :], dscores)
                spare[at, t] += dk_new
                spare[at, tiles + t] += dv_new
            dq_t = jnp.concatenate(dq, axis=0) * 0.125
            q_s[piece, t] = dq_t.T.astype(LOW)

    def by_count(piece, run):
        for count in range(1, WINDOW + 1):
            fits = piece >= WINDOW - 1 if count == WINDOW else piece == count - 1

            @pl.when(fits)
            def _(count=count):
                run(piece, count)

    def forward_attention(piece):
        @pl.when(second)
        def _():
            @pl.when(piece < 2)
            def _():
                take_start(piece)

            hand_on(piece).wait()

        rows = jnp.where(first, x_ref[piece], here[piece]).astype(F32)
        plain, factor = normalize(rows)
        plain1[piece] = plain.astype(LOW)
        fac_s[piece, :, 0:1] = factor
        normed = plain * gain1
        a_t[piece] = normed.T.astype(LOW)
        qkv = mm(normed.astype(LOW), wa[:, :qkv_cols])

        @pl.when(second)
        def _():
            take_values(piece)

        for t in range(tiles):
            q_s[piece, t] = (qkv[:, t * LANES:(t + 1) * LANES].astype(LOW) * 0.125).astype(LOW)
            key = qkv[:, (tiles + t) * LANES:(tiles + t + 1) * LANES].astype(LOW)
            value = qkv[:, (2 * tiles + t) * LANES:(2 * tiles + t + 1) * LANES].astype(LOW)
            mask = reused(t)
            if mask is not None:
                value = jnp.where(mask, here_v[piece, t - 1], value)
                there_v[piece, t - 1] = value
            k_s[piece, t] = key
            v_s[piece, t] = value
            turn_s[piece, t] = value.astype(F32).T.astype(LOW)

        @pl.when(first)
        def _():
            hand_values(piece).start()

        by_count(piece, attend)
        put_rows(piece, rows)
        swap_start(first_slots(piece), mm_back(joined(o_s.at[piece]), wa[:, qkv_cols:]).astype(LOW))

    def forward_middle(piece):
        put_rows(piece, get_rows(piece) + swap_end(first_slots(piece)))

    def forward_spread(piece):
        plain, factor = normalize(get_rows(piece))
        plain2[piece] = plain.astype(LOW)
        fac_s[piece, :, 1:2] = factor
        normed = plain * gain2
        m_t[piece] = normed.T.astype(LOW)
        normed = normed.astype(LOW)
        for group in range(2):
            z = mm(normed, w_ref[group, :, hidden:2 * hidden])
            square = z * z
            bent = jnp.tanh(GELU_K * z * (1.0 + GELU_C * square))
            upper = 0.5 * (1.0 + bent)
            slope = upper + 0.5 * z * (1.0 - bent * bent) * (GELU_K * (1.0 + 3.0 * GELU_C * square))
            slope = jnp.where(first, slope, slope * gd_s[piece, group].astype(F32))
            gd_s[piece, group] = slope.astype(LOW)
            e_s[piece, group] = (z * upper).astype(LOW)

    def forward_ahead(piece, carry):
        grad_low = x_ref[piece]
        g_t[piece] = grad_low.astype(F32).T.astype(LOW)
        for group in range(2):
            gd_s[piece, group] = mm(grad_low, w_ref[group, :, 2 * hidden:]).astype(LOW)
        return carry

    def forward_fold(piece):
        total = 0.0
        for group in range(2):
            total = total + mm_back(e_s[piece, group], w_ref[group, :, 2 * hidden:])
        swap_start(second_slots(piece), total.astype(LOW))

    def forward_result(piece):
        result = (get_rows(piece) + swap_end(second_slots(piece))).astype(LOW)

        @pl.when(first)
        def _():
            there[piece] = result
            hand_rows(piece).start()

        @pl.when(second)
        def _():
            here[piece] = result
            for copy in emit(piece, here):
                copy.start()

    def within(step, low_end, high_end):
        return jnp.logical_and(step >= low_end, step < high_end)

    lag = jnp.where(first, 0, 2 * PIECES)

    def forward(step, carry):
        place = step - lag

        @pl.when(within(place, 0, PIECES))
        def _():
            forward_attention(place)

        if inside:
            @pl.when(step == 0)
            def _():
                gather_pass(3, 0, [1])
                gather_start(5)
                gather_cross()

            @pl.when(step == 1)
            def _():
                gather_pass(3, 0, [2])
                gather_pass(4, 0, [0])

            @pl.when(step == 2)
            def _():
                gather_pass(4, 0, [1])
                gather_pass(5, 0, [0])
                gather_pass(5, 1, [0])

            @pl.when(step == 3)
            def _():
                gather_pass(4, 0, [2])
                gather_pass(5, 0, [1])
                gather_pass(5, 1, [1])
                gather_end(2)
                gather_end(3)

            @pl.when(step == 2 * PIECES - 2)
            def _():
                gather_pass(5, 0, [2])
                gather_pass(5, 1, [2])

            @pl.when(step == 2 * PIECES - 1)
            def _():
                gather_end(4)
                gather_end(5)

        @pl.when(jnp.logical_and(second, step == 2 * PIECES - 1))
        def _():
            lax.fori_loop(0, PIECES, forward_ahead, 0)

        @pl.when(jnp.logical_and(second, within(place, 2, PIECES + 1)))
        def _():
            forward_result(place - 2)

        @pl.when(within(place, 1, PIECES + 1))
        def _():
            forward_middle(place - 1)

        spread_place = place - jnp.where(first, PIECES, 1)

        @pl.when(within(spread_place, 0, PIECES))
        def _():
            forward_spread(spread_place)

        fold_place = place - jnp.where(first, 2 * PIECES, 1)

        @pl.when(within(fold_place, 0, PIECES))
        def _():
            @pl.when(jnp.logical_and(second, fold_place < PIECES - 2))
            def _():
                take_start(fold_place + 2)

            forward_fold(fold_place)

            @pl.when(first)
            def _():
                forward_result(fold_place)

        return carry

    lax.fori_loop(0, 3 * PIECES + 1, forward, 0)

    @pl.when(first)
    def _():
        for piece in range(PIECES):
            hand_rows(piece).wait_send()
            hand_values(piece).wait_send()

    gain_grad_ref[...] = jnp.zeros_like(gain_grad_ref)

    def hidden_grads(left, right, base, low_end, high_end):
        def one(index, carry):
            group, column = lax.rem(index, 2), index // 2
            spot = pl.multiple_of(column * block, block)
            total = 0.0
            for piece in range(PIECES):
                total = total + mm(left[piece], right[piece, group, :, pl.ds(spot, block)])
            sums[group, :, pl.ds(pl.multiple_of(base + spot, block), block)] = total.astype(LOW)
            return carry

        lax.fori_loop(2 * low_end, 2 * high_end, one, 0)

    def head_grads():
        pairs = []
        for kind in range(4):
            total = 0.0
            for piece in range(PIECES):
                if kind < 3:
                    total = total + mm(a_t[piece], joined((q_s, k_s, v_s)[kind].at[piece]))
                else:
                    total = total + mm(h_t[piece], joined(o_s.at[piece]))
            for group in range(2):
                part = total[:, group * LANES:(group + 1) * LANES].astype(LOW)
                sums[group, :, kind * LANES:(kind + 1) * LANES] = part
            pairs.append(total[:, 2 * LANES:])
        for pair in range(2):
            one, two = pairs[2 * pair:2 * pair + 2]
            spot = (4 + pair) * LANES
            sums[0, :, spot:spot + LANES] = jnp.where(low_half, one, flip(two)).astype(LOW)
            sums[1, :, spot:spot + LANES] = jnp.where(low_half, flip(one), two).astype(LOW)

    columns_in = hidden // block

    def down_grads():
        hidden_grads(g_t, e_s, 2 * hidden, 0, 1)
        if inside:
            reduce_y(0).start()
        hidden_grads(g_t, e_s, 2 * hidden, 1, columns_in)
        if inside:
            mixed_start()

    def up_grads():
        hidden_grads(m_t, gd_s, hidden, 0, columns_in)
        if inside:
            reduce_y(1).start()
            reduce_y(2).start()

    def grad_rows(piece):
        return jnp.where(first, here[piece], x_ref[piece])

    def backward_hidden(piece):
        @pl.when(first)
        def _():
            @pl.when(jnp.logical_or(piece == PIECES - 1, piece == 0))
            def _():
                take_start(piece)

            hand_on(piece).wait()

            grad_low = here[piece]
            g_t[piece] = grad_low.astype(F32).T.astype(LOW)

            @pl.when(piece == 0)
            def _():
                down_grads()

            for group in range(2):
                dz = mm(grad_low, w_ref[group, :, 2 * hidden:]) * gd_s[piece, group].astype(F32)
                gd_s[piece, group] = dz.astype(LOW)

        total = 0.0
        for group in range(2):
            total = total + mm_back(gd_s[piece, group], w_ref[group, :, hidden:2 * hidden])
        swap_start(turned_slots(piece), total.astype(LOW))

        @pl.when(jnp.logical_and(first, piece == 0))
        def _():
            up_grads()

    def backward_attention(piece):
        dm = swap_end(turned_slots(piece))
        plain = plain2[piece].astype(F32)
        gain_grad_ref[1:2, :] += jnp.sum(dm * plain, axis=0, keepdims=True)
        middle = grad_rows(piece).astype(F32) + norm_back(dm, plain, fac_s[piece, :, 1:2], gain2)
        h_t[piece] = middle.T.astype(LOW)
        dmixed = mm(middle.astype(LOW), wa[:, qkv_cols:]).astype(LOW)
        for t in range(tiles):
            do_s[t] = dmixed[:, t * LANES:(t + 1) * LANES]
        by_count(piece, attend_back)
        for t in range(1, tiles):
            there_v[piece, t - 1] = spare[piece, tiles + t].astype(LOW)

        @pl.when(first)
        def _():
            hand_values(piece).wait_recv()

        @pl.when(second)
        def _():
            hand_values(piece).start()

        for t in range(tiles):
            dvalue = spare[piece, tiles + t]
            mask = reused(t)
            if mask is not None:
                came = jnp.logical_and(first, jnp.logical_or(t == 1, lane >= HEAD))
                dvalue = jnp.where(came, dvalue + here_v[piece, t - 1].astype(F32), dvalue)
                dvalue = jnp.where(mask, 0.0, dvalue)
            k_s[piece, t] = spare[piece, t].astype(LOW)
            v_s[piece, t] = dvalue.astype(LOW)
        put_rows(piece, middle)
        terms = joined(q_s.at[piece], k_s.at[piece], v_s.at[piece])
        swap_start(last_slots(piece), mm_back(terms, wa[:, :qkv_cols]).astype(LOW))

    def backward_result(piece):
        da = swap_end(last_slots(piece))
        plain = plain1[piece].astype(F32)
        gain_grad_ref[0:1, :] += jnp.sum(da * plain, axis=0, keepdims=True)
        there[piece] = (get_rows(piece) + norm_back(da, plain, fac_s[piece, :, 0:1], gain1)).astype(LOW)

        @pl.when(second)
        def _():
            hand_rows(piece).start()

        @pl.when(first)
        def _():
            emit_here(piece, there).start()

            @pl.when(piece >= 2)
            def _():
                emit_there(piece, there).start()

    last_ahead = 2 * PIECES - 2

    def backward(step, carry):
        turn = step // 2
        even = lax.rem(step, 2) == 0
        hidden_first = jnp.logical_or(
            step == last_ahead, jnp.logical_and(jnp.logical_not(even), step < last_ahead))
        hidden_second = jnp.logical_and(even, turn < PIECES)
        hidden_piece = PIECES - 1 - jnp.where(step == last_ahead, PIECES - 1, turn)

        @pl.when(jnp.where(first, hidden_first, hidden_second))
        def _():
            backward_hidden(hidden_piece)

        @pl.when(step == 0)
        def _():
            @pl.when(second)
            def _():
                forward_result(PIECES - 1)

            spare[...] = jnp.zeros_like(spare)
            for piece in range(PIECES):
                for t in range(tiles):
                    turn_s[piece, t] = k_s[piece, t].astype(F32).T.astype(LOW)

        mixed_first = jnp.logical_or(
            jnp.logical_and(step > last_ahead, step <= 2 * PIECES),
            jnp.logical_and(even, jnp.logical_and(step >= 2, step < last_ahead)))
        mixed_second = jnp.logical_and(jnp.logical_not(even), turn >= 1)
        place = PIECES - jnp.where(
            first, jnp.where(step > last_ahead, step - last_ahead + PIECES - 2, turn), turn)

        @pl.when(jnp.where(first, mixed_first, mixed_second))
        def _():
            @pl.when(place < PIECES - 1)
            def _():
                backward_result(place + 1)

            @pl.when(jnp.logical_and(first, place >= 2))
            def _():
                take_start(place - 1)

            backward_attention(place)

        return carry

    lax.fori_loop(0, 2 * PIECES + 2, backward, 0)
    backward_result(0)

    @pl.when(second)
    def _():
        down_grads()
        up_grads()

    head_grads()

    def emit_stage(run):
        @pl.when(first)
        def _():
            run(there)

        @pl.when(second)
        def _():
            run(here)

    def late_outputs():
        @pl.when(first)
        def _():
            for piece in range(2):
                emit_there(piece, there).start()

    def pass_outputs(pieces):
        def one(stage):
            for piece in pieces:
                emit_there(piece, stage).wait_recv()
                emit_on(piece).start()

        emit_stage(one)

    def finish_outputs(stage):
        for piece in range(PIECES):
            emit_here(piece, stage).wait()
            emit_there(piece, stage).wait_send()
            emit_on(piece).wait()

    if inside:
        gain_copy = send(gain_grad_ref, gain_y, sem_gg, (0,), other_y)
        gain_copy.start()
        reduce_y(3).start()
        mixed_mid()
        reduce_mid(0, 4)
        gain_copy.wait()
        gain_y[...] = gain_y[...] + gain_grad_ref[...]
        gain_sends = [
            send(gain_y, gain_z.at[step - 1], sem_gg, (step,), peer(step)) for step in range(1, depth)]
        for copy in gain_sends:
            copy.start()
        reduce_mid(1)
        reduce_late(0)
        reduce_mid(2, 5)
        mixed_late()
        reduce_late(1)
        reduce_mid(3, 6)
        reduce_end(0)
        reduce_late(2)
        reduce_mid(4, 7)
        reduce_end(1)
        reduce_late(3)
        reduce_end(2)
        total = gain_y[...]
        for step, copy in enumerate(gain_sends):
            copy.wait()
            total = total + gain_z[step]
        gain_out[...] = functools.reduce(jnp.add, [
            jnp.where(deep == index, total[0:2, index * rows_own:(index + 1) * rows_own], 0.0)
            for index in range(depth)])
        reduce_mid(5)
        reduce_late(4)
        reduce_end(3)
        pass_outputs((3, 2))
        reduce_mid(6)
        mixed_cross().start()
        reduce_late(5)
        reduce_end(4)

        def place(sec, row, unit):
            return (sec * 2 + row) * 2 + unit

        mine = place(section, lane_y, core)
        for half_tile, tile_index in enumerate((2, 5)):
            value_ref[mine, :, half_tile * LANES:(half_tile + 1) * LANES] = (
                head_tile(tile_index).astype(LOW))
        value_y = send(value_ref.at[mine], value_ref.at[mine], sem_va, (0,), other_y)
        value_y.start()
        reduce_mid(7)
        late_outputs()
        value_y.wait()
        value_x = []
        for row in range(2):
            at = place(section, row, core)
            value_x.append(send(value_ref.at[at], value_ref.at[at], sem_va, (1 + row,), other_layer))
            value_x[-1].start()
        reduce_late(6)
        reduce_end(5)
        reduce_late(7)
        for copy in value_x:
            copy.wait()
        value_c = []
        for sec in range(2):
            for row in range(2):
                at = place(sec, row, core)
                value_c.append(
                    send(value_ref.at[at], value_ref.at[at], sem_va, (3 + 2 * sec + row,), other_core))
                value_c[-1].start()
        reduce_end(6)
        mixed_end()
        reduce_end(7)
        pass_outputs((1, 0))
        edge = 2 * HEAD

        def columns(kind, pair, upper):
            rest = head_tile(pair)
            return jnp.concatenate(
                [head_tile(kind), rest[:, HEAD:] if upper else rest[:, :HEAD]], axis=1)

        head_out[0] = columns(0, 4, False)
        head_out[1] = columns(1, 4, True)
        head_out[2] = columns(3, 5, True)
        for copy in value_c:
            copy.wait()
        value_out[...] = jnp.concatenate(
            [value_ref[index, :, :edge + HEAD] for index in range(value_out.shape[1] // (edge + HEAD))],
            axis=1).astype(F32)
        reduce_sent()
    else:
        late_outputs()
        pass_outputs(range(PIECES))

    emit_stage(finish_outputs)

    @pl.when(second)
    def _():
        for piece in range(PIECES):
            hand_rows(piece).wait_send()
            hand_values(piece).wait_send()


def run_layers(lengths, x_rows, gains, weights, cols, value_cols, depth, inside):
    width = x_rows.shape[3]
    tiles = width // 2 // LANES
    rows_own = width // depth
    columns = 3 * width
    vmem = pl.BlockSpec(memory_space=pltpu.VMEM)
    anywhere = pl.BlockSpec(memory_space=pl.ANY)
    smem = pl.BlockSpec(memory_space=pltpu.SMEM)
    per_tile = (PIECES, tiles, PIECE, LANES)
    turned = (PIECES, tiles, LANES, PIECE)
    flat = (PIECES, PIECE, width)
    flat_turned = (PIECES, width, PIECE)
    wide = (PIECES, 2, PIECE, width)
    low = lambda shape: pltpu.VMEM(shape, LOW)
    full = lambda shape: pltpu.VMEM(shape, F32)
    dma = lambda *shape: pltpu.SemaphoreType.DMA(shape)
    out_shape = [
        jax.ShapeDtypeStruct((2,) + flat, LOW),
        jax.ShapeDtypeStruct((rows_own, 2 * width), F32) if inside
        else jax.ShapeDtypeStruct(weights[0].shape, LOW),
        jax.ShapeDtypeStruct((8, width), F32),
    ]
    out_specs = [anywhere, vmem, vmem]
    scratch = [
        low((width, 4 * tiles * LANES)),
        low(per_tile), low(per_tile), low(per_tile), low(turned), low(per_tile),
        full((PIECES, 2 * tiles, 1, PIECE)),
        low(flat), low(flat), full((PIECES, PIECE, 2)),
        low(flat_turned), low(flat_turned), low(flat_turned), low(flat_turned),
        low(wide), low(wide), low((tiles, PIECE, LANES)),
        full((PIECES, 2 * tiles, PIECE, LANES)),
        full((WINDOW, PIECE, PIECE)), low(flat), pltpu.VMEM((PIECES, 1, PIECE), jnp.int32),
        low(flat), low((PIECES, 2, PIECE, LANES)), low(flat), low((PIECES, 2, PIECE, LANES)),
        low((3, PIECE, width)), low((PIECES + 2, PIECE, width)),
        dma(2, PIECES), dma(2, PIECES), dma(2, PIECES), dma(2, PIECES + 2), dma(2, PIECES),
        dma(2, PIECES), dma(4 + PIECES),
    ]
    if inside:
        out_shape += [
            jax.ShapeDtypeStruct((3, rows_own, cols), F32),
            jax.ShapeDtypeStruct((2, rows_own), F32),
            jax.ShapeDtypeStruct((rows_own, value_cols), F32)]
        out_specs += [vmem] * 3
        scratch += [
            low((2, width, columns)), full((depth, 8, -(-rows_own // LANES) * LANES)),
            low((2, width, columns)), low((width, columns)), low((depth - 1, rows_own, columns)),
            full((8, width)), full((depth - 1, 8, width)),
            low((8, rows_own, 2 * LANES)),
            dma(2, PARTS + 1, depth - 1, 2), dma(2, PARTS, depth), dma(2, depth), dma(2, 8),
            dma(2, 8, 3), dma(2, 2, 4), dma(2, depth), dma(2, 7),
        ]
    return pl.pallas_call(
        functools.partial(layers_kernel, width, depth, inside),
        out_shape=out_shape,
        in_specs=[smem, anywhere, vmem] + [anywhere if inside else vmem] * len(weights),
        out_specs=out_specs,
        scratch_shapes=scratch,
        compiler_params=pltpu.CompilerParams(
            collective_id=0, has_side_effects=True, vmem_limit_bytes=63 << 20),
        name="layers",
    )(lengths, x_rows, gains, *weights)


def pack(w_qk, w_value, w_out):
    query, key, out_t = w_qk[:, 0], w_qk[:, 1], w_out.T
    edge = 2 * HEAD
    return jnp.concatenate(
        [query[:, :edge], key[:, :edge], w_value[:, :edge], out_t[:, :edge],
         query[:, edge:], key[:, edge:], w_value[:, edge:], out_t[:, edge:]],
        axis=1)


def unpack(packed):
    edge = 2 * HEAD
    cut = lambda spot, size: packed[:, spot:spot + size]
    query = jnp.concatenate([cut(0, edge), cut(4 * edge, HEAD)], axis=1)
    key = jnp.concatenate([cut(edge, edge), cut(4 * edge + HEAD, HEAD)], axis=1)
    value = jnp.concatenate([cut(2 * edge, edge), cut(5 * edge, HEAD)], axis=1)
    out_t = jnp.concatenate([cut(3 * edge, edge), cut(5 * edge + HEAD, HEAD)], axis=1)
    hidden = packed.shape[1] // 3
    return (
        jnp.stack([query, key], axis=1), value, out_t.T,
        cut(hidden, hidden), cut(2 * hidden, hidden).T)


def shards(
    ends_in, seq_lengths, norm_gains, qk_weight, value_weight, out_weight, fc_weight, proj_weight
):
    section = lax.axis_index("section")
    lane_y = lax.axis_index("y")
    group = 2 * lane_y + lax.axis_index("core")
    first = section == 0
    cols = qk_weight.shape[3]
    width = ends_in.shape[2]
    fresh = (value_weight.shape[1] - width) // cols
    offset = jnp.where(first, group, width // cols + jnp.minimum(group, fresh - 1)) * cols
    w_value = lax.dynamic_slice_in_dim(value_weight, offset, cols, 1)
    parts = [pack(qk_weight[0], w_value, out_weight[0]), fc_weight[0], proj_weight[0].T]
    depth = lax.axis_size("dp")
    inside = depth == 4 and width % (16 * depth) == 0
    if inside:
        weights = parts
        gains = norm_gains[0].T
    else:
        weights = lax.all_gather(jnp.concatenate(parts, axis=1), "dp", axis=0, tiled=True)
        weights = [lax.all_gather(weights, "y", axis=0)]
        gains = lax.all_gather(norm_gains[0], "dp", axis=0, tiled=True).astype(F32).T
    x_rows = ends_in[0].reshape(2, PIECES, PIECE, width)
    kept = width // cols + fresh
    results = run_layers(
        seq_lengths, x_rows, gains, weights, cols, value_weight.shape[1], depth, inside)
    both = results[0].reshape(2 * MB_TOK, width)
    if inside:
        _, grads, _, heads, gain_rows, d_value = results
        attn_gain, mlp_gain = gain_rows[0], gain_rows[1]
        d_qk = jnp.stack([heads[0], heads[1]], axis=1)
        d_out = heads[2].T
        d_up, d_down = grads[:, :width], grads[:, width:].T
    else:
        _, grads, gain_grads = results
        grads = lax.psum_scatter(grads, "y", scatter_dimension=0, tiled=False)
        grads = lax.psum_scatter(grads, "dp", scatter_dimension=0, tiled=True)
        gain_rows = lax.psum(gain_grads[:2], "y").T
        gain_rows = lax.psum_scatter(gain_rows, "dp", scatter_dimension=0, tiled=True)
        attn_gain, mlp_gain = gain_rows[:, 0], gain_rows[:, 1]
        d_qk, d_value, d_out, d_up, d_down = unpack(grads.astype(F32))
        values = lax.all_gather(d_value.astype(LOW), ("section", "y", "core"), axis=0)
        d_value = jnp.concatenate([values[index] for index in range(kept)], axis=1).astype(F32)
    return (
        both[None], attn_gain[None], mlp_gain[None], d_qk[None], d_value,
        d_out[None], d_up[None], d_down[None])


def solution(mesh):
    sections, depth, split = (mesh.shape[name] for name in ("section", "dp", "mp"))
    grid = Mesh(mesh.devices.reshape(sections, depth, split // 2, 2), ("section", "dp", "y", "core"))
    mp = ("y", "core")
    in_specs = (
        P("section", "dp", None),
        P("dp", None),
        P("section", "dp", None),
        P("section", "dp", None, mp),
        P("dp", None),
        P("section", mp, "dp"),
        P("section", "dp", mp),
        P("section", mp, "dp"),
    )
    out_specs = (
        P("section", "dp", None),
        P("section", "dp"),
        P("section", "dp"),
        P("section", "dp", None, mp),
        P("dp", None),
        P("section", mp, "dp"),
        P("section", "dp", mp),
        P("section", mp, "dp"),
    )
    return jax.shard_map(shards, mesh=grid, in_specs=in_specs, out_specs=out_specs, check_vma=False)
```

```python
import functools
import math

import jax
import jax.numpy as jnp
from jax import lax
from jax.experimental import pallas as pl
from jax.experimental.pallas import tpu as pltpu
from jax.sharding import Mesh, PartitionSpec as P

HEAD = 64
MB_TOK = 1024
PIECE = 256
PIECES = MB_TOK // PIECE
WINDOW = 3
PARTS = 6
LANES = 128
EPSILON = 1e-05
GELU_K = math.sqrt(2.0 / math.pi)
GELU_C = 0.044715
MESH = pl.DeviceIdType.MESH
F32 = jnp.float32
LOW = jnp.bfloat16


def mm(left, right):
    return lax.dot_general(left, right, (((1,), (0,)), ((), ())), preferred_element_type=F32)


def mm_back(left, right):
    return lax.dot_general(left, right, (((1,), (1,)), ((), ())), preferred_element_type=F32)


def normalize(rows):
    centred = rows - jnp.mean(rows, axis=1, keepdims=True)
    factor = lax.rsqrt(jnp.mean(centred * centred, axis=1, keepdims=True) + EPSILON)
    return centred * factor, factor


def norm_back(grad, plain, factor, gain):
    scaled = grad * gain
    return factor * (
        scaled
        - jnp.mean(scaled, axis=1, keepdims=True)
        - plain * jnp.mean(scaled * plain, axis=1, keepdims=True)
    )


def flip(tile):
    return pltpu.roll(tile, HEAD, 1)


def layers_kernel(width, depth, inside, *refs):
    refs = list(refs)
    take = lambda count: [refs.pop(0) for _ in range(count)]
    length_ref, x_all, gain_ref = take(3)
    part_refs = take(3 if inside else 1)
    out_ref, grad_ref, gain_grad_ref = take(3)
    if inside:
        head_out, gain_out, value_out = take(3)
    (wa, q_s, k_s, v_s, turn_s, o_s, lse_s, plain1, plain2, fac_s,
     a_t, m_t, g_t, h_t, e_s, gd_s, do_s, spare, bias_s, x_ref, start_s,
     there, there_v, here, here_v, swap_out, swap_in,
     sem_x, sem_v, sem_f, sem_c, sem_o, sem_oc, sem_l) = take(34)
    if inside:
        (w_ref, gain_all, sums, y_in, z_in, gain_y, gain_z, value_ref,
         sem_az, sem_ay, sem_gz, sem_ry, sem_rz, sem_rm, sem_gg, sem_va) = take(16)
    else:
        w_ref, sums = part_refs[0], grad_ref

    section = lax.axis_index("section")
    core = lax.axis_index("core")
    lane_y = lax.axis_index("y")
    deep = lax.axis_index("dp")
    other_layer = {"section": 1 - section}
    other_core = {"core": 1 - core}
    other_y = {"y": 1 - lane_y}
    first = section == 0
    second = jnp.logical_not(first)
    tiles = width // 2 // LANES
    hidden = width
    rows_own = width // depth
    half_cols = width // 2

    def send(src, dst, sems, index, target):
        return pltpu.make_async_remote_copy(
            src_ref=src, dst_ref=dst, send_sem=sems.at[(0,) + index], recv_sem=sems.at[(1,) + index],
            device_id=target, device_id_type=MESH)

    def peer(step):
        return {"dp": lax.rem(deep + step, depth)}

    barrier = pltpu.get_barrier_semaphore()
    friends = [other_layer, other_core, other_y]
    if inside:
        friends = friends + [peer(step) for step in range(1, depth)]
        twin = {"dp": deep + 1 - 2 * lax.rem(deep, 2)}
    for friend in friends:
        pl.semaphore_signal(barrier, inc=1, device_id=friend, device_id_type=MESH)
    pl.semaphore_wait(barrier, len(friends))

    lane = lax.broadcasted_iota(jnp.int32, (1, LANES), 1)
    low_half = lane < HEAD

    def rows_at(place):
        return pl.ds(pl.multiple_of(place * rows_own, rows_own), rows_own)

    unit = 3 * hidden // PARTS
    per_ref = PARTS // 3
    ways = (1, -1)
    mixed_part = PARTS - 1

    def cols_at(part):
        return pl.ds(part * unit, unit)

    def on_line(place):
        return jnp.logical_and(place >= 0, place < depth)

    def own_part(part):
        return part_refs[part // per_ref].at[:, pl.ds(part % per_ref * unit, unit)]

    def own_copy(index):
        return pltpu.make_async_copy(
            part_refs[index], w_ref.at[lane_y, rows_at(deep), pl.ds(index * hidden, hidden)],
            sem_l.at[PIECES + index])

    def gather_line(part, row, hop, way):
        place = deep - hop * ways[way]
        home = lane_y if row == 0 else 1 - lane_y
        spot = w_ref.at[home, rows_at(place), cols_at(part)]
        src = own_part(part) if row == 0 and hop == 0 else spot
        return send(src, spot, sem_az, (part + row, hop, way), {"dp": deep + ways[way]})

    def line_start(part, row, hop, way):
        @pl.when(jnp.logical_and(on_line(deep - hop * ways[way]), on_line(deep + ways[way])))
        def _():
            gather_line(part, row, hop, way).start()

    def line_sent(part, row, hop, way):
        @pl.when(jnp.logical_and(on_line(deep - hop * ways[way]), on_line(deep + ways[way])))
        def _():
            gather_line(part, row, hop, way).wait_send()

    def gather_y(part, place, own):
        spot = w_ref.at[lane_y, rows_at(place), cols_at(part)]
        src = own_part(part) if own else spot
        return send(src, spot, sem_ay, (part, place), other_y)

    def gather_gain(step):
        return send(gain_all.at[deep], gain_all.at[deep], sem_gz, (step,), peer(step))

    def gather_start(part):
        for way in range(2):
            line_start(part, 0, 0, way)
        if part != mixed_part:
            gather_y(part, deep, True).start()

    def gather_pass(part, row=0, hops=None):
        for hop in range(depth - 1) if hops is None else hops:
            for way in range(2):
                place = deep - (hop + 1) * ways[way]

                @pl.when(on_line(place))
                def _(hop=hop, way=way, place=place):
                    gather_line(part, row, hop, way).wait_recv()
                    if hop < depth - 2:
                        line_start(part, row, hop + 1, way)
                    if part != mixed_part:
                        gather_y(part, place, False).start()

    def gather_cross():
        gather_y(mixed_part, deep, True).wait()
        for way in range(2):
            line_start(mixed_part, 1, 0, way)

    def gather_end(part):
        if part != mixed_part:
            for place in range(depth):
                gather_y(part, place, False).wait()
        for row in range(2 if part == mixed_part else 1):
            for hop in range(depth - 1):
                for way in range(2):
                    line_sent(part, row, hop, way)

    block = 2 * LANES
    last = block // 2
    spans = [
        (2 * hidden, block), (hidden, block), (hidden + block, block),
        (block, block), (2 * block, block), (0, block),
        (hidden + 2 * block, last), (hidden + 2 * block + last, last)]
    mixed_at = pl.ds(2 * hidden + block, 2 * block)
    mixed_out = pl.ds(hidden + block, 2 * block)

    def block_at(index):
        return pl.ds(spans[index][0], spans[index][1])

    def reduce_y(index):
        return send(sums.at[1 - lane_y, :, block_at(index)], y_in.at[:, block_at(index)],
                    sem_ry, (index,), other_y)

    def share_of(near, index):
        own = lax.rem(deep, 2)
        return rows_at((own if near else 1 - own) + 2 * index)

    def reduce_near(index, share):
        at = block_at(index)
        return send(sums.at[lane_y, share_of(False, share), at], z_in.at[share, :, at],
                    sem_rz, (index, share), twin)

    def reduce_far(index):
        at = block_at(index)
        return send(sums.at[lane_y, rows_at(lax.rem(deep + 2, depth)), at], z_in.at[2, :, at],
                    sem_rz, (index, 2), peer(2))

    def reduce_mid(index, following=None):
        reduce_y(index).wait_recv()
        if following is not None:
            reduce_y(following).start()
        at = block_at(index)
        sums[lane_y, :, at] = (
            sums[lane_y, :, at].astype(F32) + y_in[:, at].astype(F32)).astype(LOW)
        for share in range(2):
            reduce_near(index, share).start()

    def reduce_late(index):
        at = block_at(index)
        for share in range(2):
            reduce_near(index, share).wait_recv()
            rows = share_of(True, share)
            sums[lane_y, rows, at] = (
                sums[lane_y, rows, at].astype(F32) + z_in[share, :, at].astype(F32)).astype(LOW)
        reduce_far(index).start()

    def summed(at):
        return sums[lane_y, rows_at(deep), at].astype(F32) + z_in[2, :, at].astype(F32)

    def head_tile(index):
        return summed(pl.ds(index * LANES, LANES))

    def reduce_end(index):
        at = block_at(index)
        reduce_far(index).wait_recv()
        spot, size = spans[index]
        if spot >= hidden:
            grad_ref[:, spot - hidden:spot - hidden + size] = summed(at)

    def mixed_home(row, share):
        if row == 0:
            return z_in.at[share, :, mixed_at]
        return y_in.at[rows_at(share), mixed_at]

    def mixed_group(row):
        return lane_y if row == 0 else 1 - lane_y

    def mixed_near(row, share):
        return send(sums.at[mixed_group(row), share_of(False, share), mixed_at],
                    mixed_home(row, share), sem_rm, (row, share), twin)

    def mixed_far(row):
        return send(sums.at[mixed_group(row), rows_at(lax.rem(deep + 2, depth)), mixed_at],
                    mixed_home(row, 2), sem_rm, (row, 2), peer(2))

    def mixed_cross():
        return send(sums.at[1 - lane_y, rows_at(deep), mixed_at], mixed_home(1, 3),
                    sem_rm, (1, 3), other_y)

    def mixed_start():
        for row in range(2):
            for share in range(2):
                mixed_near(row, share).start()

    def mixed_mid():
        for row in range(2):
            for share in range(2):
                mixed_near(row, share).wait_recv()
                rows = share_of(True, share)
                group = mixed_group(row)
                sums[group, rows, mixed_at] = (
                    sums[group, rows, mixed_at].astype(F32)
                    + mixed_home(row, share)[...].astype(F32)).astype(LOW)
            mixed_far(row).start()

    def mixed_late():
        for row in range(2):
            mixed_far(row).wait_recv()
            total = (sums[mixed_group(row), rows_at(deep), mixed_at].astype(F32)
                     + mixed_home(row, 2)[...].astype(F32))
            if row == 0:
                grad_ref[:, mixed_out] = total
            else:
                sums[mixed_group(row), rows_at(deep), mixed_at] = total.astype(LOW)

    def mixed_end():
        mixed_cross().wait_recv()
        grad_ref[:, mixed_out] += mixed_home(1, 3)[...].astype(F32)

    def reduce_sent():
        for index in range(len(spans)):
            reduce_y(index).wait_send()
            for share in range(2):
                reduce_near(index, share).wait_send()
            reduce_far(index).wait_send()
        for row in range(2):
            for share in range(2):
                mixed_near(row, share).wait_send()
            mixed_far(row).wait_send()
        mixed_cross().wait_send()

    def halves(tile):
        return [jnp.where(low_half, tile, jnp.zeros_like(tile)),
                jnp.where(low_half, jnp.zeros_like(tile), tile)]

    def group_tile(group, index):
        return w_ref[group, :, index * LANES:(index + 1) * LANES]

    qkv_cols = 3 * tiles * LANES

    def arrange():
        for kind in range(4):
            for group in range(2):
                spot = (kind * tiles + group) * LANES
                wa[:, spot:spot + LANES] = group_tile(group, kind)
        for pair in range(2):
            one, two = (group_tile(group, 4 + pair).astype(F32) for group in range(2))
            spot = (2 * pair * tiles + 2) * LANES
            wa[:, spot:spot + LANES] = jnp.where(low_half, one, flip(two)).astype(LOW)
            spot = ((2 * pair + 1) * tiles + 2) * LANES
            wa[:, spot:spot + LANES] = jnp.where(low_half, flip(one), two).astype(LOW)

    x_copy = pltpu.make_async_copy(x_all.at[lane_y], x_ref, sem_l.at[PIECES + 3])
    if inside:
        gather_start(0)
        gather_start(1)
        gather_y(mixed_part, deep, True).start()
        gain_all[deep, 0:2, 0:rows_own] = gain_ref[...].astype(F32)
        for step in range(1, depth):
            gather_gain(step).start()
        for index in range(3):
            own_copy(index).start()
    x_copy.start()

    for piece in range(PIECES):
        place = piece * PIECE + lax.broadcasted_iota(jnp.int32, (1, PIECE), 1)
        begin = jnp.zeros((1, PIECE), jnp.int32)
        end = 0
        for index in range(length_ref.shape[1]):
            end = end + length_ref[lane_y, index]
            begin = jnp.where(place >= end, end, begin)
        start_s[piece] = begin

    if inside:
        gather_pass(0)
        gather_start(2)
        gather_pass(1)
        gather_start(3)
        gather_pass(2, 0, [0, 1])
        gather_start(4)
        for step in range(1, depth):
            gather_gain(step).wait()
        gather_end(0)
        gather_end(1)
        gather_pass(2, 0, [2])
        gather_pass(3, 0, [0])
        for index in range(3):
            own_copy(index).wait()
        gains = jnp.concatenate([gain_all[place, :, :rows_own] for place in range(depth)], axis=1)
    else:
        gains = gain_ref[...]
    arrange()
    x_copy.wait()
    gain1 = gains[0:1, :]
    gain2 = gains[1:2, :]

    def swap_copy(leave, enter):
        return send(swap_out.at[leave], swap_in.at[enter], sem_c, (enter,), other_core)

    def swap_start(slots, value):
        swap_out[slots[0]] = value
        swap_copy(*slots).start()

    def swap_end(slots):
        swap_copy(*slots).wait()
        return swap_out[slots[0]].astype(F32) + swap_in[slots[1]].astype(F32)

    def first_slots(piece):
        return lax.rem(piece, 2), piece

    def turned_slots(piece):
        return lax.rem(piece, 2), lax.rem(piece + 2, PIECES)

    def second_slots(piece):
        return 2, PIECES + lax.rem(piece, 2)

    def last_slots(piece):
        return 2, PIECES + lax.rem(piece + 1, 2)

    def put_rows(piece, rows):
        for t in range(2 * tiles):
            spare[piece, t] = rows[:, t * LANES:(t + 1) * LANES]

    def get_rows(piece):
        return jnp.concatenate([spare[piece, t] for t in range(2 * tiles)], axis=1)

    def joined(*stores):
        return jnp.concatenate([store[t] for store in stores for t in range(tiles)], axis=1)

    half = pl.ds(pl.multiple_of(core * half_cols, half_cols), half_cols)

    def hand_rows(piece):
        return send(there.at[piece, :, half], here.at[piece, :, half], sem_x, (piece,), other_layer)

    def hand_values(piece):
        return send(there_v.at[piece], here_v.at[piece], sem_v, (piece,), other_layer)

    def hand_on(piece):
        return send(here.at[piece, :, half], here.at[piece, :, half], sem_f, (piece,), other_core)

    def take_start(piece):
        hand_rows(piece).wait_recv()
        hand_on(piece).start()

    def take_values(piece):
        hand_values(piece).wait_recv()

    def emit_here(piece, stage):
        return pltpu.make_async_copy(stage.at[piece], out_ref.at[lane_y, piece], sem_l.at[piece])

    def emit_there(piece, stage):
        return send(stage.at[piece, :, half], out_ref.at[lane_y, piece, :, half],
                    sem_o, (piece,), other_y)

    def emit(piece, stage):
        return [emit_here(piece, stage), emit_there(piece, stage)]

    def emit_on(piece):
        spot = out_ref.at[1 - lane_y, piece, :, half]
        return send(spot, spot, sem_oc, (piece,), other_core)

    def reused(tile_index):
        if tile_index == 0:
            return None
        if tile_index == 1:
            return jnp.logical_and(second, lane >= 0)
        return jnp.logical_and(second, lane >= HEAD)

    def make_bias(piece, count):
        base = piece * PIECE
        query = base + lax.broadcasted_iota(jnp.int32, (1, PIECE), 1)
        begin = start_s[piece]
        for j in range(count):
            key = base - (count - 1 - j) * PIECE + lax.broadcasted_iota(jnp.int32, (PIECE, 1), 0)
            fine = jnp.logical_and(key >= begin, key <= query)
            bias_s[j] = jnp.where(fine, 0.0, -1e30).astype(F32)

    def attend(piece, count):
        make_bias(piece, count)
        for t in range(tiles):
            parts = []
            for h, query in enumerate(halves(q_s[piece, t])):
                scores = [
                    mm_back(k_s[piece - (count - 1 - j), t], query) + bias_s[j] for j in range(count)
                ]
                top = functools.reduce(
                    jnp.maximum, [jnp.max(s, axis=0, keepdims=True) for s in scores])
                expo = [jnp.exp(s - top) for s in scores]
                total = functools.reduce(
                    jnp.add, [jnp.sum(e, axis=0, keepdims=True) for e in expo])
                mixed = functools.reduce(jnp.add, [
                    mm(turn_s[piece - (count - 1 - j), t, h * HEAD:(h + 1) * HEAD, :], e.astype(LOW))
                    for j, e in enumerate(expo)
                ])
                parts.append(mixed * (1.0 / total))
                lse_s[piece, 2 * t + h] = top + jnp.log(total)
            o_s[piece, t] = jnp.concatenate(parts, axis=0).T.astype(LOW)

    def attend_back(piece, count):
        make_bias(piece, count)
        for t in range(tiles):
            inner = (do_s[t].astype(F32) * o_s[piece, t].astype(F32)).T
            queries = halves(q_s[piece, t])
            grads = halves(do_s[t])
            dq = [0.0, 0.0]
            inners = [jnp.sum(inner[h * HEAD:(h + 1) * HEAD], axis=0, keepdims=True) for h in range(2)]
            for j in range(count):
                at = piece - (count - 1 - j)
                dk_new, dv_new = 0.0, 0.0
                for h in range(2):
                    probs = jnp.exp(
                        mm_back(k_s[at, t], queries[h]) + bias_s[j] - lse_s[piece, 2 * t + h])
                    dprobs = mm_back(v_s[at, t], grads[h])
                    dscores = (probs * (dprobs - inners[h])).astype(LOW)
                    dv_new = dv_new + mm(probs.astype(LOW), grads[h])
                    dk_new = dk_new + mm(dscores, queries[h])
                    dq[h] = dq[h] + mm(turn_s[at, t, h * HEAD:(h + 1) * HEAD, :], dscores)
                spare[at, t] += dk_new
                spare[at, tiles + t] += dv_new
            dq_t = jnp.concatenate(dq, axis=0) * 0.125
            q_s[piece, t] = dq_t.T.astype(LOW)

    def by_count(piece, run):
        for count in range(1, WINDOW + 1):
            fits = piece >= WINDOW - 1 if count == WINDOW else piece == count - 1

            @pl.when(fits)
            def _(count=count):
                run(piece, count)

    def forward_attention(piece):
        @pl.when(second)
        def _():
            @pl.when(piece < 2)
            def _():
                take_start(piece)

            hand_on(piece).wait()

        rows = jnp.where(first, x_ref[piece], here[piece]).astype(F32)
        plain, factor = normalize(rows)
        plain1[piece] = plain.astype(LOW)
        fac_s[piece, :, 0:1] = factor
        normed = plain * gain1
        a_t[piece] = normed.T.astype(LOW)
        qkv = mm(normed.astype(LOW), wa[:, :qkv_cols])

        @pl.when(second)
        def _():
            take_values(piece)

        for t in range(tiles):
            q_s[piece, t] = (qkv[:, t * LANES:(t + 1) * LANES].astype(LOW) * 0.125).astype(LOW)
            key = qkv[:, (tiles + t) * LANES:(tiles + t + 1) * LANES].astype(LOW)
            value = qkv[:, (2 * tiles + t) * LANES:(2 * tiles + t + 1) * LANES].astype(LOW)
            mask = reused(t)
            if mask is not None:
                value = jnp.where(mask, here_v[piece, t - 1], value)
                there_v[piece, t - 1] = value
            k_s[piece, t] = key
            v_s[piece, t] = value
            turn_s[piece, t] = value.astype(F32).T.astype(LOW)

        @pl.when(first)
        def _():
            hand_values(piece).start()

        by_count(piece, attend)
        put_rows(piece, rows)
        swap_start(first_slots(piece), mm_back(joined(o_s.at[piece]), wa[:, qkv_cols:]).astype(LOW))

    def forward_middle(piece):
        put_rows(piece, get_rows(piece) + swap_end(first_slots(piece)))

    def forward_spread(piece):
        plain, factor = normalize(get_rows(piece))
        plain2[piece] = plain.astype(LOW)
        fac_s[piece, :, 1:2] = factor
        normed = plain * gain2
        m_t[piece] = normed.T.astype(LOW)
        normed = normed.astype(LOW)
        for group in range(2):
            z = mm(normed, w_ref[group, :, hidden:2 * hidden])
            square = z * z
            bent = jnp.tanh(GELU_K * z * (1.0 + GELU_C * square))
            upper = 0.5 * (1.0 + bent)
            slope = upper + 0.5 * z * (1.0 - bent * bent) * (GELU_K * (1.0 + 3.0 * GELU_C * square))
            slope = jnp.where(first, slope, slope * gd_s[piece, group].astype(F32))
            gd_s[piece, group] = slope.astype(LOW)
            e_s[piece, group] = (z * upper).astype(LOW)

    def forward_ahead(piece, carry):
        grad_low = x_ref[piece]
        g_t[piece] = grad_low.astype(F32).T.astype(LOW)
        for group in range(2):
            gd_s[piece, group] = mm(grad_low, w_ref[group, :, 2 * hidden:]).astype(LOW)
        return carry

    def forward_fold(piece):
        total = 0.0
        for group in range(2):
            total = total + mm_back(e_s[piece, group], w_ref[group, :, 2 * hidden:])
        swap_start(second_slots(piece), total.astype(LOW))

    def forward_result(piece):
        result = (get_rows(piece) + swap_end(second_slots(piece))).astype(LOW)

        @pl.when(first)
        def _():
            there[piece] = result
            hand_rows(piece).start()

        @pl.when(second)
        def _():
            here[piece] = result
            for copy in emit(piece, here):
                copy.start()

    def within(step, low_end, high_end):
        return jnp.logical_and(step >= low_end, step < high_end)

    lag = jnp.where(first, 0, 2 * PIECES)

    def forward(step, carry):
        place = step - lag

        @pl.when(within(place, 0, PIECES))
        def _():
            forward_attention(place)

        if inside:
            @pl.when(step == 0)
            def _():
                gather_pass(3, 0, [1])
                gather_start(5)
                gather_cross()

            @pl.when(step == 1)
            def _():
                gather_pass(3, 0, [2])
                gather_pass(4, 0, [0])

            @pl.when(step == 2)
            def _():
                gather_pass(4, 0, [1])
                gather_pass(5, 0, [0])
                gather_pass(5, 1, [0])

            @pl.when(step == 3)
            def _():
                gather_pass(4, 0, [2])
                gather_pass(5, 0, [1])
                gather_pass(5, 1, [1])
                gather_end(2)
                gather_end(3)

            @pl.when(step == 2 * PIECES - 2)
            def _():
                gather_pass(5, 0, [2])
                gather_pass(5, 1, [2])

            @pl.when(step == 2 * PIECES - 1)
            def _():
                gather_end(4)
                gather_end(5)

        @pl.when(jnp.logical_and(second, step == 2 * PIECES - 1))
        def _():
            lax.fori_loop(0, PIECES, forward_ahead, 0)

        @pl.when(jnp.logical_and(second, within(place, 2, PIECES + 1)))
        def _():
            forward_result(place - 2)

        @pl.when(within(place, 1, PIECES + 1))
        def _():
            forward_middle(place - 1)

        spread_place = place - jnp.where(first, PIECES, 1)

        @pl.when(within(spread_place, 0, PIECES))
        def _():
            forward_spread(spread_place)

        fold_place = place - jnp.where(first, 2 * PIECES, 1)

        @pl.when(within(fold_place, 0, PIECES))
        def _():
            @pl.when(jnp.logical_and(second, fold_place < PIECES - 2))
            def _():
                take_start(fold_place + 2)

            forward_fold(fold_place)

            @pl.when(first)
            def _():
                forward_result(fold_place)

        return carry

    lax.fori_loop(0, 3 * PIECES + 1, forward, 0)

    @pl.when(first)
    def _():
        for piece in range(PIECES):
            hand_rows(piece).wait_send()
            hand_values(piece).wait_send()

    gain_grad_ref[...] = jnp.zeros_like(gain_grad_ref)

    def hidden_grads(left, right, base, low_end, high_end):
        def one(index, carry):
            group, column = lax.rem(index, 2), index // 2
            spot = pl.multiple_of(column * block, block)
            total = 0.0
            for piece in range(PIECES):
                total = total + mm(left[piece], right[piece, group, :, pl.ds(spot, block)])
            sums[group, :, pl.ds(pl.multiple_of(base + spot, block), block)] = total.astype(LOW)
            return carry

        lax.fori_loop(2 * low_end, 2 * high_end, one, 0)

    def head_grads():
        pairs = []
        for kind in range(4):
            total = 0.0
            for piece in range(PIECES):
                if kind < 3:
                    total = total + mm(a_t[piece], joined((q_s, k_s, v_s)[kind].at[piece]))
                else:
                    total = total + mm(h_t[piece], joined(o_s.at[piece]))
            for group in range(2):
                part = total[:, group * LANES:(group + 1) * LANES].astype(LOW)
                sums[group, :, kind * LANES:(kind + 1) * LANES] = part
            pairs.append(total[:, 2 * LANES:])
        for pair in range(2):
            one, two = pairs[2 * pair:2 * pair + 2]
            spot = (4 + pair) * LANES
            sums[0, :, spot:spot + LANES] = jnp.where(low_half, one, flip(two)).astype(LOW)
            sums[1, :, spot:spot + LANES] = jnp.where(low_half, flip(one), two).astype(LOW)

    columns_in = hidden // block

    def down_grads():
        hidden_grads(g_t, e_s, 2 * hidden, 0, 1)
        if inside:
            reduce_y(0).start()
        hidden_grads(g_t, e_s, 2 * hidden, 1, columns_in)
        if inside:
            mixed_start()

    def up_grads():
        hidden_grads(m_t, gd_s, hidden, 0, columns_in)
        if inside:
            reduce_y(1).start()
            reduce_y(2).start()

    def grad_rows(piece):
        return jnp.where(first, here[piece], x_ref[piece])

    def backward_hidden(piece):
        @pl.when(first)
        def _():
            @pl.when(jnp.logical_or(piece == PIECES - 1, piece == 0))
            def _():
                take_start(piece)

            hand_on(piece).wait()

            grad_low = here[piece]
            g_t[piece] = grad_low.astype(F32).T.astype(LOW)

            @pl.when(piece == 0)
            def _():
                down_grads()

            for group in range(2):
                dz = mm(grad_low, w_ref[group, :, 2 * hidden:]) * gd_s[piece, group].astype(F32)
                gd_s[piece, group] = dz.astype(LOW)

        total = 0.0
        for group in range(2):
            total = total + mm_back(gd_s[piece, group], w_ref[group, :, hidden:2 * hidden])
        swap_start(turned_slots(piece), total.astype(LOW))

        @pl.when(jnp.logical_and(first, piece == 0))
        def _():
            up_grads()

    def backward_attention(piece):
        dm = swap_end(turned_slots(piece))
        plain = plain2[piece].astype(F32)
        gain_grad_ref[1:2, :] += jnp.sum(dm * plain, axis=0, keepdims=True)
        middle = grad_rows(piece).astype(F32) + norm_back(dm, plain, fac_s[piece, :, 1:2], gain2)
        h_t[piece] = middle.T.astype(LOW)
        dmixed = mm(middle.astype(LOW), wa[:, qkv_cols:]).astype(LOW)
        for t in range(tiles):
            do_s[t] = dmixed[:, t * LANES:(t + 1) * LANES]
        by_count(piece, attend_back)
        for t in range(1, tiles):
            there_v[piece, t - 1] = spare[piece, tiles + t].astype(LOW)

        @pl.when(first)
        def _():
            hand_values(piece).wait_recv()

        @pl.when(second)
        def _():
            hand_values(piece).start()

        for t in range(tiles):
            dvalue = spare[piece, tiles + t]
            mask = reused(t)
            if mask is not None:
                came = jnp.logical_and(first, jnp.logical_or(t == 1, lane >= HEAD))
                dvalue = jnp.where(came, dvalue + here_v[piece, t - 1].astype(F32), dvalue)
                dvalue = jnp.where(mask, 0.0, dvalue)
            k_s[piece, t] = spare[piece, t].astype(LOW)
            v_s[piece, t] = dvalue.astype(LOW)
        put_rows(piece, middle)
        terms = joined(q_s.at[piece], k_s.at[piece], v_s.at[piece])
        swap_start(last_slots(piece), mm_back(terms, wa[:, :qkv_cols]).astype(LOW))

    def backward_result(piece):
        da = swap_end(last_slots(piece))
        plain = plain1[piece].astype(F32)
        gain_grad_ref[0:1, :] += jnp.sum(da * plain, axis=0, keepdims=True)
        there[piece] = (get_rows(piece) + norm_back(da, plain, fac_s[piece, :, 0:1], gain1)).astype(LOW)

        @pl.when(second)
        def _():
            hand_rows(piece).start()

        @pl.when(first)
        def _():
            emit_here(piece, there).start()

            @pl.when(piece >= 2)
            def _():
                emit_there(piece, there).start()

    last_ahead = 2 * PIECES - 2

    def backward(step, carry):
        turn = step // 2
        even = lax.rem(step, 2) == 0
        hidden_first = jnp.logical_or(
            step == last_ahead, jnp.logical_and(jnp.logical_not(even), step < last_ahead))
        hidden_second = jnp.logical_and(even, turn < PIECES)
        hidden_piece = PIECES - 1 - jnp.where(step == last_ahead, PIECES - 1, turn)

        @pl.when(jnp.logical_and(first, step == last_ahead))
        def _():
            backward_result(2)

        @pl.when(jnp.where(first, hidden_first, hidden_second))
        def _():
            backward_hidden(hidden_piece)

        @pl.when(step == 0)
        def _():
            @pl.when(second)
            def _():
                forward_result(PIECES - 1)

            spare[...] = jnp.zeros_like(spare)
            for piece in range(PIECES):
                for t in range(tiles):
                    turn_s[piece, t] = k_s[piece, t].astype(F32).T.astype(LOW)

        mixed_first = jnp.logical_or(
            jnp.logical_and(step > last_ahead, step <= 2 * PIECES),
            jnp.logical_and(even, jnp.logical_and(step >= 2, step < last_ahead)))
        mixed_second = jnp.logical_and(jnp.logical_not(even), turn >= 1)
        place = PIECES - jnp.where(
            first, jnp.where(step > last_ahead, step - last_ahead + PIECES - 2, turn), turn)

        @pl.when(jnp.where(first, mixed_first, mixed_second))
        def _():
            @pl.when(jnp.logical_and(
                place < PIECES - 1, jnp.logical_or(second, step != last_ahead + 1)))
            def _():
                backward_result(place + 1)

            @pl.when(jnp.logical_and(first, place >= 2))
            def _():
                take_start(place - 1)

            backward_attention(place)

        return carry

    lax.fori_loop(0, 2 * PIECES + 2, backward, 0)
    backward_result(0)

    @pl.when(second)
    def _():
        down_grads()
        up_grads()

    head_grads()

    def emit_stage(run):
        @pl.when(first)
        def _():
            run(there)

        @pl.when(second)
        def _():
            run(here)

    def late_outputs():
        @pl.when(first)
        def _():
            for piece in range(2):
                emit_there(piece, there).start()

    def pass_outputs(pieces):
        def one(stage):
            for piece in pieces:
                emit_there(piece, stage).wait_recv()
                emit_on(piece).start()

        emit_stage(one)

    def finish_outputs(stage):
        for piece in range(PIECES):
            emit_here(piece, stage).wait()
            emit_there(piece, stage).wait_send()
            emit_on(piece).wait()

    if inside:
        gain_copy = send(gain_grad_ref, gain_y, sem_gg, (0,), other_y)
        gain_copy.start()
        reduce_y(3).start()
        mixed_mid()
        reduce_mid(0, 4)
        gain_copy.wait()
        gain_y[...] = gain_y[...] + gain_grad_ref[...]
        gain_sends = [
            send(gain_y, gain_z.at[step - 1], sem_gg, (step,), peer(step)) for step in range(1, depth)]
        for copy in gain_sends:
            copy.start()
        reduce_mid(1)
        reduce_late(0)
        reduce_mid(2, 5)
        mixed_late()
        reduce_late(1)
        reduce_mid(3, 6)
        reduce_end(0)
        reduce_late(2)
        reduce_mid(4, 7)
        reduce_end(1)
        reduce_late(3)
        reduce_end(2)
        total = gain_y[...]
        for step, copy in enumerate(gain_sends):
            copy.wait()
            total = total + gain_z[step]
        gain_out[...] = functools.reduce(jnp.add, [
            jnp.where(deep == index, total[0:2, index * rows_own:(index + 1) * rows_own], 0.0)
            for index in range(depth)])
        reduce_mid(5)
        reduce_late(4)
        reduce_end(3)
        pass_outputs((3, 2))
        reduce_mid(6)
        mixed_cross().start()
        reduce_late(5)
        reduce_end(4)

        def place(sec, row, unit):
            return (sec * 2 + row) * 2 + unit

        mine = place(section, lane_y, core)
        for half_tile, tile_index in enumerate((2, 5)):
            value_ref[mine, :, half_tile * LANES:(half_tile + 1) * LANES] = (
                head_tile(tile_index).astype(LOW))
        value_y = send(value_ref.at[mine], value_ref.at[mine], sem_va, (0,), other_y)
        value_y.start()
        reduce_mid(7)
        late_outputs()
        value_y.wait()
        value_x = []
        for row in range(2):
            at = place(section, row, core)
            value_x.append(send(value_ref.at[at], value_ref.at[at], sem_va, (1 + row,), other_layer))
            value_x[-1].start()
        reduce_late(6)
        reduce_end(5)
        reduce_late(7)
        for copy in value_x:
            copy.wait()
        value_c = []
        for sec in range(2):
            for row in range(2):
                at = place(sec, row, core)
                value_c.append(
                    send(value_ref.at[at], value_ref.at[at], sem_va, (3 + 2 * sec + row,), other_core))
                value_c[-1].start()
        reduce_end(6)
        mixed_end()
        reduce_end(7)
        pass_outputs((1, 0))
        edge = 2 * HEAD

        def columns(kind, pair, upper):
            rest = head_tile(pair)
            return jnp.concatenate(
                [head_tile(kind), rest[:, HEAD:] if upper else rest[:, :HEAD]], axis=1)

        head_out[0] = columns(0, 4, False)
        head_out[1] = columns(1, 4, True)
        head_out[2] = columns(3, 5, True)
        for copy in value_c:
            copy.wait()
        value_out[...] = jnp.concatenate(
            [value_ref[index, :, :edge + HEAD] for index in range(value_out.shape[1] // (edge + HEAD))],
            axis=1).astype(F32)
        reduce_sent()
    else:
        late_outputs()
        pass_outputs(range(PIECES))

    emit_stage(finish_outputs)

    @pl.when(second)
    def _():
        for piece in range(PIECES):
            hand_rows(piece).wait_send()
            hand_values(piece).wait_send()


def run_layers(lengths, x_rows, gains, weights, cols, value_cols, depth, inside):
    width = x_rows.shape[3]
    tiles = width // 2 // LANES
    rows_own = width // depth
    columns = 3 * width
    vmem = pl.BlockSpec(memory_space=pltpu.VMEM)
    anywhere = pl.BlockSpec(memory_space=pl.ANY)
    smem = pl.BlockSpec(memory_space=pltpu.SMEM)
    per_tile = (PIECES, tiles, PIECE, LANES)
    turned = (PIECES, tiles, LANES, PIECE)
    flat = (PIECES, PIECE, width)
    flat_turned = (PIECES, width, PIECE)
    wide = (PIECES, 2, PIECE, width)
    low = lambda shape: pltpu.VMEM(shape, LOW)
    full = lambda shape: pltpu.VMEM(shape, F32)
    dma = lambda *shape: pltpu.SemaphoreType.DMA(shape)
    out_shape = [
        jax.ShapeDtypeStruct((2,) + flat, LOW),
        jax.ShapeDtypeStruct((rows_own, 2 * width), F32) if inside
        else jax.ShapeDtypeStruct(weights[0].shape, LOW),
        jax.ShapeDtypeStruct((8, width), F32),
    ]
    out_specs = [anywhere, vmem, vmem]
    scratch = [
        low((width, 4 * tiles * LANES)),
        low(per_tile), low(per_tile), low(per_tile), low(turned), low(per_tile),
        full((PIECES, 2 * tiles, 1, PIECE)),
        low(flat), low(flat), full((PIECES, PIECE, 2)),
        low(flat_turned), low(flat_turned), low(flat_turned), low(flat_turned),
        low(wide), low(wide), low((tiles, PIECE, LANES)),
        full((PIECES, 2 * tiles, PIECE, LANES)),
        full((WINDOW, PIECE, PIECE)), low(flat), pltpu.VMEM((PIECES, 1, PIECE), jnp.int32),
        low(flat), low((PIECES, 2, PIECE, LANES)), low(flat), low((PIECES, 2, PIECE, LANES)),
        low((3, PIECE, width)), low((PIECES + 2, PIECE, width)),
        dma(2, PIECES), dma(2, PIECES), dma(2, PIECES), dma(2, PIECES + 2), dma(2, PIECES),
        dma(2, PIECES), dma(4 + PIECES),
    ]
    if inside:
        out_shape += [
            jax.ShapeDtypeStruct((3, rows_own, cols), F32),
            jax.ShapeDtypeStruct((2, rows_own), F32),
            jax.ShapeDtypeStruct((rows_own, value_cols), F32)]
        out_specs += [vmem] * 3
        scratch += [
            low((2, width, columns)), full((depth, 8, -(-rows_own // LANES) * LANES)),
            low((2, width, columns)), low((width, columns)), low((depth - 1, rows_own, columns)),
            full((8, width)), full((depth - 1, 8, width)),
            low((8, rows_own, 2 * LANES)),
            dma(2, PARTS + 1, depth - 1, 2), dma(2, PARTS, depth), dma(2, depth), dma(2, 8),
            dma(2, 8, 3), dma(2, 2, 4), dma(2, depth), dma(2, 7),
        ]
    return pl.pallas_call(
        functools.partial(layers_kernel, width, depth, inside),
        out_shape=out_shape,
        in_specs=[smem, anywhere, vmem] + [anywhere if inside else vmem] * len(weights),
        out_specs=out_specs,
        scratch_shapes=scratch,
        compiler_params=pltpu.CompilerParams(
            collective_id=0, has_side_effects=True, vmem_limit_bytes=63 << 20),
        name="layers",
    )(lengths, x_rows, gains, *weights)


def pack(w_qk, w_value, w_out):
    query, key, out_t = w_qk[:, 0], w_qk[:, 1], w_out.T
    edge = 2 * HEAD
    return jnp.concatenate(
        [query[:, :edge], key[:, :edge], w_value[:, :edge], out_t[:, :edge],
         query[:, edge:], key[:, edge:], w_value[:, edge:], out_t[:, edge:]],
        axis=1)


def unpack(packed):
    edge = 2 * HEAD
    cut = lambda spot, size: packed[:, spot:spot + size]
    query = jnp.concatenate([cut(0, edge), cut(4 * edge, HEAD)], axis=1)
    key = jnp.concatenate([cut(edge, edge), cut(4 * edge + HEAD, HEAD)], axis=1)
    value = jnp.concatenate([cut(2 * edge, edge), cut(5 * edge, HEAD)], axis=1)
    out_t = jnp.concatenate([cut(3 * edge, edge), cut(5 * edge + HEAD, HEAD)], axis=1)
    hidden = packed.shape[1] // 3
    return (
        jnp.stack([query, key], axis=1), value, out_t.T,
        cut(hidden, hidden), cut(2 * hidden, hidden).T)


def shards(
    ends_in, seq_lengths, norm_gains, qk_weight, value_weight, out_weight, fc_weight, proj_weight
):
    section = lax.axis_index("section")
    lane_y = lax.axis_index("y")
    group = 2 * lane_y + lax.axis_index("core")
    first = section == 0
    cols = qk_weight.shape[3]
    width = ends_in.shape[2]
    fresh = (value_weight.shape[1] - width) // cols
    offset = jnp.where(first, group, width // cols + jnp.minimum(group, fresh - 1)) * cols
    w_value = lax.dynamic_slice_in_dim(value_weight, offset, cols, 1)
    parts = [pack(qk_weight[0], w_value, out_weight[0]), fc_weight[0], proj_weight[0].T]
    depth = lax.axis_size("dp")
    inside = depth == 4 and width % (16 * depth) == 0
    if inside:
        weights = parts
        gains = norm_gains[0].T
    else:
        weights = lax.all_gather(jnp.concatenate(parts, axis=1), "dp", axis=0, tiled=True)
        weights = [lax.all_gather(weights, "y", axis=0)]
        gains = lax.all_gather(norm_gains[0], "dp", axis=0, tiled=True).astype(F32).T
    x_rows = ends_in[0].reshape(2, PIECES, PIECE, width)
    kept = width // cols + fresh
    results = run_layers(
        seq_lengths, x_rows, gains, weights, cols, value_weight.shape[1], depth, inside)
    both = results[0].reshape(2 * MB_TOK, width)
    if inside:
        _, grads, _, heads, gain_rows, d_value = results
        attn_gain, mlp_gain = gain_rows[0], gain_rows[1]
        d_qk = jnp.stack([heads[0], heads[1]], axis=1)
        d_out = heads[2].T
        d_up, d_down = grads[:, :width], grads[:, width:].T
    else:
        _, grads, gain_grads = results
        grads = lax.psum_scatter(grads, "y", scatter_dimension=0, tiled=False)
        grads = lax.psum_scatter(grads, "dp", scatter_dimension=0, tiled=True)
        gain_rows = lax.psum(gain_grads[:2], "y").T
        gain_rows = lax.psum_scatter(gain_rows, "dp", scatter_dimension=0, tiled=True)
        attn_gain, mlp_gain = gain_rows[:, 0], gain_rows[:, 1]
        d_qk, d_value, d_out, d_up, d_down = unpack(grads.astype(F32))
        values = lax.all_gather(d_value.astype(LOW), ("section", "y", "core"), axis=0)
        d_value = jnp.concatenate([values[index] for index in range(kept)], axis=1).astype(F32)
    return (
        both[None], attn_gain[None], mlp_gain[None], d_qk[None], d_value,
        d_out[None], d_up[None], d_down[None])


def solution(mesh):
    sections, depth, split = (mesh.shape[name] for name in ("section", "dp", "mp"))
    grid = Mesh(mesh.devices.reshape(sections, depth, split // 2, 2), ("section", "dp", "y", "core"))
    mp = ("y", "core")
    in_specs = (
        P("section", "dp", None),
        P("dp", None),
        P("section", "dp", None),
        P("section", "dp", None, mp),
        P("dp", None),
        P("section", mp, "dp"),
        P("section", "dp", mp),
        P("section", mp, "dp"),
    )
    out_specs = (
        P("section", "dp", None),
        P("section", "dp"),
        P("section", "dp"),
        P("section", "dp", None, mp),
        P("dp", None),
        P("section", mp, "dp"),
        P("section", "dp", mp),
        P("section", mp, "dp"),
    )
    return jax.shard_map(shards, mesh=grid, in_specs=in_specs, out_specs=out_specs, check_vma=False)
```

```python
import functools
import math

import jax
import jax.numpy as jnp
from jax import lax
from jax.experimental import pallas as pl
from jax.experimental.pallas import tpu as pltpu
from jax.sharding import Mesh, PartitionSpec as P

HEAD = 64
MB_TOK = 1024
PIECE = 256
PIECES = MB_TOK // PIECE
WINDOW = 3
PARTS = 6
LANES = 128
EPSILON = 1e-05
GELU_K = math.sqrt(2.0 / math.pi)
GELU_C = 0.044715
MESH = pl.DeviceIdType.MESH
F32 = jnp.float32
LOW = jnp.bfloat16


def mm(left, right):
    return lax.dot_general(left, right, (((1,), (0,)), ((), ())), preferred_element_type=F32)


def mm_back(left, right):
    return lax.dot_general(left, right, (((1,), (1,)), ((), ())), preferred_element_type=F32)


def normalize(rows):
    centred = rows - jnp.mean(rows, axis=1, keepdims=True)
    factor = lax.rsqrt(jnp.mean(centred * centred, axis=1, keepdims=True) + EPSILON)
    return centred * factor, factor


def norm_back(grad, plain, factor, gain):
    scaled = grad * gain
    return factor * (
        scaled
        - jnp.mean(scaled, axis=1, keepdims=True)
        - plain * jnp.mean(scaled * plain, axis=1, keepdims=True)
    )


def flip(tile):
    return pltpu.roll(tile, HEAD, 1)


def layers_kernel(width, depth, inside, *refs):
    refs = list(refs)
    take = lambda count: [refs.pop(0) for _ in range(count)]
    length_ref, x_all, gain_ref = take(3)
    part_refs = take(3 if inside else 1)
    out_ref, grad_ref, gain_grad_ref = take(3)
    if inside:
        head_out, gain_out, value_out = take(3)
    (wa, q_s, k_s, v_s, turn_s, o_s, lse_s, plain1, plain2, fac_s,
     a_t, m_t, g_t, h_t, e_s, gd_s, do_s, spare, bias_s, x_ref, start_s,
     there, there_v, here, here_v, swap_out, swap_in,
     sem_x, sem_v, sem_f, sem_c, sem_o, sem_oc, sem_l) = take(34)
    if inside:
        (w_ref, gain_all, sums, y_in, z_in, gain_y, gain_z, value_ref,
         sem_az, sem_ay, sem_gz, sem_ry, sem_rz, sem_rm, sem_gg, sem_va) = take(16)
    else:
        w_ref, sums = part_refs[0], grad_ref

    section = lax.axis_index("section")
    core = lax.axis_index("core")
    lane_y = lax.axis_index("y")
    deep = lax.axis_index("dp")
    other_layer = {"section": 1 - section}
    other_core = {"core": 1 - core}
    other_y = {"y": 1 - lane_y}
    first = section == 0
    second = jnp.logical_not(first)
    tiles = width // 2 // LANES
    hidden = width
    rows_own = width // depth
    half_cols = width // 2

    def send(src, dst, sems, index, target):
        return pltpu.make_async_remote_copy(
            src_ref=src, dst_ref=dst, send_sem=sems.at[(0,) + index], recv_sem=sems.at[(1,) + index],
            device_id=target, device_id_type=MESH)

    def peer(step):
        return {"dp": lax.rem(deep + step, depth)}

    barrier = pltpu.get_barrier_semaphore()
    friends = [other_layer, other_core, other_y]
    if inside:
        friends = friends + [peer(step) for step in range(1, depth)]
        twin = {"dp": deep + 1 - 2 * lax.rem(deep, 2)}
    for friend in friends:
        pl.semaphore_signal(barrier, inc=1, device_id=friend, device_id_type=MESH)
    pl.semaphore_wait(barrier, len(friends))

    lane = lax.broadcasted_iota(jnp.int32, (1, LANES), 1)
    low_half = lane < HEAD

    def rows_at(place):
        return pl.ds(pl.multiple_of(place * rows_own, rows_own), rows_own)

    unit = 3 * hidden // PARTS
    per_ref = PARTS // 3
    ways = (1, -1)
    mixed_part = PARTS - 1

    def cols_at(part):
        return pl.ds(part * unit, unit)

    def on_line(place):
        return jnp.logical_and(place >= 0, place < depth)

    def own_part(part):
        return part_refs[part // per_ref].at[:, pl.ds(part % per_ref * unit, unit)]

    def own_copy(index):
        return pltpu.make_async_copy(
            part_refs[index], w_ref.at[lane_y, rows_at(deep), pl.ds(index * hidden, hidden)],
            sem_l.at[PIECES + index])

    def gather_line(part, row, hop, way):
        place = deep - hop * ways[way]
        home = lane_y if row == 0 else 1 - lane_y
        spot = w_ref.at[home, rows_at(place), cols_at(part)]
        src = own_part(part) if row == 0 and hop == 0 else spot
        return send(src, spot, sem_az, (part + row, hop, way), {"dp": deep + ways[way]})

    def line_start(part, row, hop, way):
        @pl.when(jnp.logical_and(on_line(deep - hop * ways[way]), on_line(deep + ways[way])))
        def _():
            gather_line(part, row, hop, way).start()

    def line_sent(part, row, hop, way):
        @pl.when(jnp.logical_and(on_line(deep - hop * ways[way]), on_line(deep + ways[way])))
        def _():
            gather_line(part, row, hop, way).wait_send()

    def gather_y(part, place, own):
        spot = w_ref.at[lane_y, rows_at(place), cols_at(part)]
        src = own_part(part) if own else spot
        return send(src, spot, sem_ay, (part, place), other_y)

    def gather_gain(step):
        return send(gain_all.at[deep], gain_all.at[deep], sem_gz, (step,), peer(step))

    def gather_start(part):
        for way in range(2):
            line_start(part, 0, 0, way)
        if part != mixed_part:
            gather_y(part, deep, True).start()

    def gather_pass(part, row=0, hops=None):
        for hop in range(depth - 1) if hops is None else hops:
            for way in range(2):
                place = deep - (hop + 1) * ways[way]

                @pl.when(on_line(place))
                def _(hop=hop, way=way, place=place):
                    gather_line(part, row, hop, way).wait_recv()
                    if hop < depth - 2:
                        line_start(part, row, hop + 1, way)
                    if part != mixed_part:
                        gather_y(part, place, False).start()

    def gather_cross():
        gather_y(mixed_part, deep, True).wait()
        for way in range(2):
            line_start(mixed_part, 1, 0, way)

    def gather_end(part):
        if part != mixed_part:
            for place in range(depth):
                gather_y(part, place, False).wait()
        for row in range(2 if part == mixed_part else 1):
            for hop in range(depth - 1):
                for way in range(2):
                    line_sent(part, row, hop, way)

    block = 2 * LANES
    last = block // 2
    spans = [
        (2 * hidden, block), (hidden, block), (hidden + block, block),
        (block, block), (2 * block, block), (0, block),
        (hidden + 2 * block, last), (hidden + 2 * block + last, last)]
    mixed_at = pl.ds(2 * hidden + block, 2 * block)
    mixed_out = pl.ds(hidden + block, 2 * block)

    def block_at(index):
        return pl.ds(spans[index][0], spans[index][1])

    def reduce_y(index):
        return send(sums.at[1 - lane_y, :, block_at(index)], y_in.at[:, block_at(index)],
                    sem_ry, (index,), other_y)

    def share_of(near, index):
        own = lax.rem(deep, 2)
        return rows_at((own if near else 1 - own) + 2 * index)

    def reduce_near(index, share):
        at = block_at(index)
        return send(sums.at[lane_y, share_of(False, share), at], z_in.at[share, :, at],
                    sem_rz, (index, share), twin)

    def reduce_far(index):
        at = block_at(index)
        return send(sums.at[lane_y, rows_at(lax.rem(deep + 2, depth)), at], z_in.at[2, :, at],
                    sem_rz, (index, 2), peer(2))

    def reduce_mid(index, following=None):
        reduce_y(index).wait_recv()
        if following is not None:
            reduce_y(following).start()
        at = block_at(index)
        sums[lane_y, :, at] = (
            sums[lane_y, :, at].astype(F32) + y_in[:, at].astype(F32)).astype(LOW)
        for share in range(2):
            reduce_near(index, share).start()

    def reduce_late(index):
        at = block_at(index)
        for share in range(2):
            reduce_near(index, share).wait_recv()
            rows = share_of(True, share)
            sums[lane_y, rows, at] = (
                sums[lane_y, rows, at].astype(F32) + z_in[share, :, at].astype(F32)).astype(LOW)
        reduce_far(index).start()

    def summed(at):
        return sums[lane_y, rows_at(deep), at].astype(F32) + z_in[2, :, at].astype(F32)

    def head_tile(index):
        return summed(pl.ds(index * LANES, LANES))

    def reduce_end(index):
        at = block_at(index)
        reduce_far(index).wait_recv()
        spot, size = spans[index]
        if spot >= hidden:
            grad_ref[:, spot - hidden:spot - hidden + size] = summed(at)

    def mixed_home(row, share):
        if row == 0:
            return z_in.at[share, :, mixed_at]
        return y_in.at[rows_at(share), mixed_at]

    def mixed_group(row):
        return lane_y if row == 0 else 1 - lane_y

    def mixed_near(row, share):
        return send(sums.at[mixed_group(row), share_of(False, share), mixed_at],
                    mixed_home(row, share), sem_rm, (row, share), twin)

    def mixed_far(row):
        return send(sums.at[mixed_group(row), rows_at(lax.rem(deep + 2, depth)), mixed_at],
                    mixed_home(row, 2), sem_rm, (row, 2), peer(2))

    def mixed_cross():
        return send(sums.at[1 - lane_y, rows_at(deep), mixed_at], mixed_home(1, 3),
                    sem_rm, (1, 3), other_y)

    def mixed_start():
        for row in range(2):
            for share in range(2):
                mixed_near(row, share).start()

    def mixed_mid():
        for row in range(2):
            for share in range(2):
                mixed_near(row, share).wait_recv()
                rows = share_of(True, share)
                group = mixed_group(row)
                sums[group, rows, mixed_at] = (
                    sums[group, rows, mixed_at].astype(F32)
                    + mixed_home(row, share)[...].astype(F32)).astype(LOW)
            mixed_far(row).start()

    def mixed_late():
        for row in range(2):
            mixed_far(row).wait_recv()
            total = (sums[mixed_group(row), rows_at(deep), mixed_at].astype(F32)
                     + mixed_home(row, 2)[...].astype(F32))
            if row == 0:
                grad_ref[:, mixed_out] = total
            else:
                sums[mixed_group(row), rows_at(deep), mixed_at] = total.astype(LOW)

    def mixed_end():
        mixed_cross().wait_recv()
        grad_ref[:, mixed_out] += mixed_home(1, 3)[...].astype(F32)

    def reduce_sent():
        for index in range(len(spans)):
            reduce_y(index).wait_send()
            for share in range(2):
                reduce_near(index, share).wait_send()
            reduce_far(index).wait_send()
        for row in range(2):
            for share in range(2):
                mixed_near(row, share).wait_send()
            mixed_far(row).wait_send()
        mixed_cross().wait_send()

    def halves(tile):
        return [jnp.where(low_half, tile, jnp.zeros_like(tile)),
                jnp.where(low_half, jnp.zeros_like(tile), tile)]

    def group_tile(group, index):
        return w_ref[group, :, index * LANES:(index + 1) * LANES]

    qkv_cols = 3 * tiles * LANES

    def arrange():
        for kind in range(4):
            for group in range(2):
                spot = (kind * tiles + group) * LANES
                wa[:, spot:spot + LANES] = group_tile(group, kind)
        for pair in range(2):
            one, two = (group_tile(group, 4 + pair).astype(F32) for group in range(2))
            spot = (2 * pair * tiles + 2) * LANES
            wa[:, spot:spot + LANES] = jnp.where(low_half, one, flip(two)).astype(LOW)
            spot = ((2 * pair + 1) * tiles + 2) * LANES
            wa[:, spot:spot + LANES] = jnp.where(low_half, flip(one), two).astype(LOW)

    x_copy = pltpu.make_async_copy(x_all.at[lane_y], x_ref, sem_l.at[PIECES + 3])
    if inside:
        gather_start(0)
        gather_start(1)
        gather_y(mixed_part, deep, True).start()
        gain_all[deep, 0:2, 0:rows_own] = gain_ref[...].astype(F32)
        for step in range(1, depth):
            gather_gain(step).start()
        for index in range(3):
            own_copy(index).start()
    x_copy.start()

    for piece in range(PIECES):
        place = piece * PIECE + lax.broadcasted_iota(jnp.int32, (1, PIECE), 1)
        begin = jnp.zeros((1, PIECE), jnp.int32)
        end = 0
        for index in range(length_ref.shape[1]):
            end = end + length_ref[lane_y, index]
            begin = jnp.where(place >= end, end, begin)
        start_s[piece] = begin

    if inside:
        gather_pass(0)
        gather_start(2)
        gather_pass(1)
        gather_start(3)
        gather_pass(2, 0, [0, 1])
        gather_start(4)
        for step in range(1, depth):
            gather_gain(step).wait()
        gather_end(0)
        gather_end(1)
        gather_pass(2, 0, [2])
        gather_pass(3, 0, [0])
        for index in range(3):
            own_copy(index).wait()
        gains = jnp.concatenate([gain_all[place, :, :rows_own] for place in range(depth)], axis=1)
    else:
        gains = gain_ref[...]
    arrange()
    x_copy.wait()
    gain1 = gains[0:1, :]
    gain2 = gains[1:2, :]

    def swap_copy(leave, enter):
        return send(swap_out.at[leave], swap_in.at[enter], sem_c, (enter,), other_core)

    def swap_start(slots, value):
        swap_out[slots[0]] = value
        swap_copy(*slots).start()

    def swap_end(slots):
        swap_copy(*slots).wait()
        return swap_out[slots[0]].astype(F32) + swap_in[slots[1]].astype(F32)

    def first_slots(piece):
        return lax.rem(piece, 2), piece

    def turned_slots(piece):
        return lax.rem(piece, 2), lax.rem(piece + 2, PIECES)

    def second_slots(piece):
        return 2, PIECES + lax.rem(piece, 2)

    def last_slots(piece):
        return 2, PIECES + lax.rem(piece + 1, 2)

    def put_rows(piece, rows):
        for t in range(2 * tiles):
            spare[piece, t] = rows[:, t * LANES:(t + 1) * LANES]

    def get_rows(piece):
        return jnp.concatenate([spare[piece, t] for t in range(2 * tiles)], axis=1)

    def joined(*stores):
        return jnp.concatenate([store[t] for store in stores for t in range(tiles)], axis=1)

    half = pl.ds(pl.multiple_of(core * half_cols, half_cols), half_cols)

    def hand_rows(piece):
        return send(there.at[piece, :, half], here.at[piece, :, half], sem_x, (piece,), other_layer)

    def hand_values(piece):
        return send(there_v.at[piece], here_v.at[piece], sem_v, (piece,), other_layer)

    def hand_on(piece):
        return send(here.at[piece, :, half], here.at[piece, :, half], sem_f, (piece,), other_core)

    def take_start(piece):
        hand_rows(piece).wait_recv()
        hand_on(piece).start()

    def take_values(piece):
        hand_values(piece).wait_recv()

    def emit_here(piece, stage):
        return pltpu.make_async_copy(stage.at[piece], out_ref.at[lane_y, piece], sem_l.at[piece])

    def emit_there(piece, stage):
        return send(stage.at[piece, :, half], out_ref.at[lane_y, piece, :, half],
                    sem_o, (piece,), other_y)

    def emit(piece, stage):
        return [emit_here(piece, stage), emit_there(piece, stage)]

    def emit_on(piece):
        spot = out_ref.at[1 - lane_y, piece, :, half]
        return send(spot, spot, sem_oc, (piece,), other_core)

    def reused(tile_index):
        if tile_index == 0:
            return None
        if tile_index == 1:
            return jnp.logical_and(second, lane >= 0)
        return jnp.logical_and(second, lane >= HEAD)

    def make_bias(piece, count):
        base = piece * PIECE
        query = base + lax.broadcasted_iota(jnp.int32, (1, PIECE), 1)
        begin = start_s[piece]
        for j in range(count):
            key = base - (count - 1 - j) * PIECE + lax.broadcasted_iota(jnp.int32, (PIECE, 1), 0)
            fine = jnp.logical_and(key >= begin, key <= query)
            bias_s[j] = jnp.where(fine, 0.0, -1e30).astype(F32)

    def attend(piece, count):
        make_bias(piece, count)
        for t in range(tiles):
            parts = []
            for h, query in enumerate(halves(q_s[piece, t])):
                scores = [
                    mm_back(k_s[piece - (count - 1 - j), t], query) + bias_s[j] for j in range(count)
                ]
                top = functools.reduce(
                    jnp.maximum, [jnp.max(s, axis=0, keepdims=True) for s in scores])
                expo = [jnp.exp(s - top) for s in scores]
                total = functools.reduce(
                    jnp.add, [jnp.sum(e, axis=0, keepdims=True) for e in expo])
                mixed = functools.reduce(jnp.add, [
                    mm(turn_s[piece - (count - 1 - j), t, h * HEAD:(h + 1) * HEAD, :], e.astype(LOW))
                    for j, e in enumerate(expo)
                ])
                parts.append(mixed * (1.0 / total))
                lse_s[piece, 2 * t + h] = top + jnp.log(total)
            o_s[piece, t] = jnp.concatenate(parts, axis=0).T.astype(LOW)

    def attend_back(piece, count):
        make_bias(piece, count)
        for t in range(tiles):
            inner = (do_s[t].astype(F32) * o_s[piece, t].astype(F32)).T
            queries = halves(q_s[piece, t])
            grads = halves(do_s[t])
            dq = [0.0, 0.0]
            inners = [jnp.sum(inner[h * HEAD:(h + 1) * HEAD], axis=0, keepdims=True) for h in range(2)]
            for j in range(count):
                at = piece - (count - 1 - j)
                dk_new, dv_new = 0.0, 0.0
                for h in range(2):
                    probs = jnp.exp(
                        mm_back(k_s[at, t], queries[h]) + bias_s[j] - lse_s[piece, 2 * t + h])
                    dprobs = mm_back(v_s[at, t], grads[h])
                    dscores = (probs * (dprobs - inners[h])).astype(LOW)
                    dv_new = dv_new + mm(probs.astype(LOW), grads[h])
                    dk_new = dk_new + mm(dscores, queries[h])
                    dq[h] = dq[h] + mm(turn_s[at, t, h * HEAD:(h + 1) * HEAD, :], dscores)
                spare[at, t] += dk_new
                spare[at, tiles + t] += dv_new
            dq_t = jnp.concatenate(dq, axis=0) * 0.125
            q_s[piece, t] = dq_t.T.astype(LOW)

    def by_count(piece, run):
        for count in range(1, WINDOW + 1):
            fits = piece >= WINDOW - 1 if count == WINDOW else piece == count - 1

            @pl.when(fits)
            def _(count=count):
                run(piece, count)

    def forward_attention(piece):
        @pl.when(second)
        def _():
            @pl.when(piece < 2)
            def _():
                take_start(piece)

            hand_on(piece).wait()

        rows = jnp.where(first, x_ref[piece], here[piece]).astype(F32)
        plain, factor = normalize(rows)
        plain1[piece] = plain.astype(LOW)
        fac_s[piece, :, 0:1] = factor
        normed = plain * gain1
        a_t[piece] = normed.T.astype(LOW)
        qkv = mm(normed.astype(LOW), wa[:, :qkv_cols])

        @pl.when(second)
        def _():
            take_values(piece)

        for t in range(tiles):
            q_s[piece, t] = (qkv[:, t * LANES:(t + 1) * LANES].astype(LOW) * 0.125).astype(LOW)
            key = qkv[:, (tiles + t) * LANES:(tiles + t + 1) * LANES].astype(LOW)
            value = qkv[:, (2 * tiles + t) * LANES:(2 * tiles + t + 1) * LANES].astype(LOW)
            mask = reused(t)
            if mask is not None:
                value = jnp.where(mask, here_v[piece, t - 1], value)
                there_v[piece, t - 1] = value
            k_s[piece, t] = key
            v_s[piece, t] = value
            turn_s[piece, t] = value.astype(F32).T.astype(LOW)

        @pl.when(first)
        def _():
            hand_values(piece).start()

        by_count(piece, attend)
        put_rows(piece, rows)
        swap_start(first_slots(piece), mm_back(joined(o_s.at[piece]), wa[:, qkv_cols:]).astype(LOW))

    def forward_middle(piece):
        put_rows(piece, get_rows(piece) + swap_end(first_slots(piece)))

    def forward_spread(piece):
        plain, factor = normalize(get_rows(piece))
        plain2[piece] = plain.astype(LOW)
        fac_s[piece, :, 1:2] = factor
        normed = plain * gain2
        m_t[piece] = normed.T.astype(LOW)
        normed = normed.astype(LOW)
        for group in range(2):
            z = mm(normed, w_ref[group, :, hidden:2 * hidden])
            square = z * z
            bent = jnp.tanh(GELU_K * z * (1.0 + GELU_C * square))
            upper = 0.5 * (1.0 + bent)
            slope = upper + 0.5 * z * (1.0 - bent * bent) * (GELU_K * (1.0 + 3.0 * GELU_C * square))
            slope = jnp.where(first, slope, slope * gd_s[piece, group].astype(F32))
            gd_s[piece, group] = slope.astype(LOW)
            e_s[piece, group] = (z * upper).astype(LOW)

    def forward_ahead(piece, carry):
        grad_low = x_ref[piece]
        g_t[piece] = grad_low.astype(F32).T.astype(LOW)
        for group in range(2):
            gd_s[piece, group] = mm(grad_low, w_ref[group, :, 2 * hidden:]).astype(LOW)
        return carry

    def forward_fold(piece):
        total = 0.0
        for group in range(2):
            total = total + mm_back(e_s[piece, group], w_ref[group, :, 2 * hidden:])
        swap_start(second_slots(piece), total.astype(LOW))

    def forward_result(piece):
        result = (get_rows(piece) + swap_end(second_slots(piece))).astype(LOW)

        @pl.when(first)
        def _():
            there[piece] = result
            hand_rows(piece).start()

        @pl.when(second)
        def _():
            here[piece] = result
            for copy in emit(piece, here):
                copy.start()

    def within(step, low_end, high_end):
        return jnp.logical_and(step >= low_end, step < high_end)

    lag = jnp.where(first, 0, 2 * PIECES)

    def forward(step, carry):
        place = step - lag

        @pl.when(within(place, 0, PIECES))
        def _():
            forward_attention(place)

        if inside:
            @pl.when(step == 0)
            def _():
                gather_pass(3, 0, [1])
                gather_start(5)
                gather_cross()

            @pl.when(step == 1)
            def _():
                gather_pass(3, 0, [2])
                gather_pass(4, 0, [0])

            @pl.when(step == 2)
            def _():
                gather_pass(4, 0, [1])
                gather_pass(5, 0, [0])
                gather_pass(5, 1, [0])

            @pl.when(step == 3)
            def _():
                gather_pass(4, 0, [2])
                gather_pass(5, 0, [1])
                gather_pass(5, 1, [1])
                gather_end(2)
                gather_end(3)

            @pl.when(step == 2 * PIECES - 2)
            def _():
                gather_pass(5, 0, [2])
                gather_pass(5, 1, [2])

            @pl.when(step == 2 * PIECES - 1)
            def _():
                gather_end(4)
                gather_end(5)

        @pl.when(jnp.logical_and(second, step == 2 * PIECES - 1))
        def _():
            lax.fori_loop(0, PIECES, forward_ahead, 0)

        @pl.when(jnp.logical_and(second, within(place, 2, PIECES + 1)))
        def _():
            forward_result(place - 2)

        @pl.when(within(place, 1, PIECES + 1))
        def _():
            forward_middle(place - 1)

        spread_place = place - jnp.where(first, PIECES, 1)

        @pl.when(within(spread_place, 0, PIECES))
        def _():
            forward_spread(spread_place)

        fold_place = place - jnp.where(first, 2 * PIECES, 1)

        @pl.when(within(fold_place, 0, PIECES))
        def _():
            @pl.when(jnp.logical_and(second, fold_place < PIECES - 2))
            def _():
                take_start(fold_place + 2)

            forward_fold(fold_place)

            @pl.when(first)
            def _():
                forward_result(fold_place)

        return carry

    lax.fori_loop(0, 3 * PIECES + 1, forward, 0)

    @pl.when(first)
    def _():
        for piece in range(PIECES):
            hand_rows(piece).wait_send()
            hand_values(piece).wait_send()

    gain_grad_ref[...] = jnp.zeros_like(gain_grad_ref)

    def hidden_grads(left, right, base, low_end, high_end):
        def one(index, carry):
            group, column = lax.rem(index, 2), index // 2
            spot = pl.multiple_of(column * block, block)
            total = 0.0
            for piece in range(PIECES):
                total = total + mm(left[piece], right[piece, group, :, pl.ds(spot, block)])
            sums[group, :, pl.ds(pl.multiple_of(base + spot, block), block)] = total.astype(LOW)
            return carry

        lax.fori_loop(2 * low_end, 2 * high_end, one, 0)

    def head_grads():
        pairs = []
        for kind in range(4):
            total = 0.0
            for piece in range(PIECES):
                if kind < 3:
                    total = total + mm(a_t[piece], joined((q_s, k_s, v_s)[kind].at[piece]))
                else:
                    total = total + mm(h_t[piece], joined(o_s.at[piece]))
            for group in range(2):
                part = total[:, group * LANES:(group + 1) * LANES].astype(LOW)
                sums[group, :, kind * LANES:(kind + 1) * LANES] = part
            pairs.append(total[:, 2 * LANES:])
        for pair in range(2):
            one, two = pairs[2 * pair:2 * pair + 2]
            spot = (4 + pair) * LANES
            sums[0, :, spot:spot + LANES] = jnp.where(low_half, one, flip(two)).astype(LOW)
            sums[1, :, spot:spot + LANES] = jnp.where(low_half, flip(one), two).astype(LOW)

    columns_in = hidden // block

    def down_grads():
        hidden_grads(g_t, e_s, 2 * hidden, 0, 1)
        if inside:
            reduce_y(0).start()
        hidden_grads(g_t, e_s, 2 * hidden, 1, columns_in)
        if inside:
            mixed_start()

    def up_grads():
        hidden_grads(m_t, gd_s, hidden, 0, columns_in)
        if inside:
            reduce_y(1).start()
            reduce_y(2).start()

    def grad_rows(piece):
        return jnp.where(first, here[piece], x_ref[piece])

    def backward_hidden(piece):
        @pl.when(first)
        def _():
            @pl.when(jnp.logical_or(piece == PIECES - 1, piece == 0))
            def _():
                take_start(piece)

            hand_on(piece).wait()

            grad_low = here[piece]
            g_t[piece] = grad_low.astype(F32).T.astype(LOW)

            @pl.when(piece == 0)
            def _():
                down_grads()

            for group in range(2):
                dz = mm(grad_low, w_ref[group, :, 2 * hidden:]) * gd_s[piece, group].astype(F32)
                gd_s[piece, group] = dz.astype(LOW)

        total = 0.0
        for group in range(2):
            total = total + mm_back(gd_s[piece, group], w_ref[group, :, hidden:2 * hidden])
        swap_start(turned_slots(piece), total.astype(LOW))

        @pl.when(jnp.logical_and(first, piece == 0))
        def _():
            up_grads()

    def backward_attention(piece):
        dm = swap_end(turned_slots(piece))
        plain = plain2[piece].astype(F32)
        gain_grad_ref[1:2, :] += jnp.sum(dm * plain, axis=0, keepdims=True)
        middle = grad_rows(piece).astype(F32) + norm_back(dm, plain, fac_s[piece, :, 1:2], gain2)
        h_t[piece] = middle.T.astype(LOW)
        dmixed = mm(middle.astype(LOW), wa[:, qkv_cols:]).astype(LOW)
        for t in range(tiles):
            do_s[t] = dmixed[:, t * LANES:(t + 1) * LANES]
        by_count(piece, attend_back)
        for t in range(1, tiles):
            there_v[piece, t - 1] = spare[piece, tiles + t].astype(LOW)

        @pl.when(first)
        def _():
            hand_values(piece).wait_recv()

        @pl.when(second)
        def _():
            hand_values(piece).start()

        for t in range(tiles):
            dvalue = spare[piece, tiles + t]
            mask = reused(t)
            if mask is not None:
                came = jnp.logical_and(first, jnp.logical_or(t == 1, lane >= HEAD))
                dvalue = jnp.where(came, dvalue + here_v[piece, t - 1].astype(F32), dvalue)
                dvalue = jnp.where(mask, 0.0, dvalue)
            k_s[piece, t] = spare[piece, t].astype(LOW)
            v_s[piece, t] = dvalue.astype(LOW)
        put_rows(piece, middle)
        terms = joined(q_s.at[piece], k_s.at[piece], v_s.at[piece])
        swap_start(last_slots(piece), mm_back(terms, wa[:, :qkv_cols]).astype(LOW))

    def backward_result(piece):
        da = swap_end(last_slots(piece))
        plain = plain1[piece].astype(F32)
        gain_grad_ref[0:1, :] += jnp.sum(da * plain, axis=0, keepdims=True)
        there[piece] = (get_rows(piece) + norm_back(da, plain, fac_s[piece, :, 0:1], gain1)).astype(LOW)

        @pl.when(second)
        def _():
            hand_rows(piece).start()

        @pl.when(first)
        def _():
            emit_here(piece, there).start()

            @pl.when(piece >= 2)
            def _():
                emit_there(piece, there).start()

    last_ahead = 2 * PIECES - 2

    def backward(step, carry):
        turn = step // 2
        even = lax.rem(step, 2) == 0
        hidden_first = jnp.logical_or(
            step == last_ahead, jnp.logical_and(jnp.logical_not(even), step < last_ahead))
        hidden_second = jnp.logical_and(even, turn < PIECES)
        hidden_piece = PIECES - 1 - jnp.where(step == last_ahead, PIECES - 1, turn)

        @pl.when(jnp.where(first, hidden_first, hidden_second))
        def _():
            backward_hidden(hidden_piece)

        @pl.when(step == 0)
        def _():
            @pl.when(second)
            def _():
                forward_result(PIECES - 1)

            spare[...] = jnp.zeros_like(spare)
            for piece in range(PIECES):
                for t in range(tiles):
                    turn_s[piece, t] = k_s[piece, t].astype(F32).T.astype(LOW)

        mixed_first = jnp.logical_or(
            jnp.logical_and(step > last_ahead, step <= 2 * PIECES),
            jnp.logical_and(even, jnp.logical_and(step >= 2, step < last_ahead)))
        mixed_second = jnp.logical_and(jnp.logical_not(even), turn >= 1)
        place = PIECES - jnp.where(
            first, jnp.where(step > last_ahead, step - last_ahead + PIECES - 2, turn), turn)

        @pl.when(jnp.where(first, mixed_first, mixed_second))
        def _():
            @pl.when(place < PIECES - 1)
            def _():
                backward_result(place + 1)

            @pl.when(jnp.logical_and(first, place >= 2))
            def _():
                take_start(place - 1)

            backward_attention(place)

        return carry

    lax.fori_loop(0, 2 * PIECES + 2, backward, 0)
    @pl.when(second)
    def _():
        backward_result(0)
        down_grads()
        up_grads()

    head_grads()

    @pl.when(first)
    def _():
        backward_result(0)


    def emit_stage(run):
        @pl.when(first)
        def _():
            run(there)

        @pl.when(second)
        def _():
            run(here)

    def late_outputs():
        @pl.when(first)
        def _():
            for piece in range(2):
                emit_there(piece, there).start()

    def pass_outputs(pieces):
        def one(stage):
            for piece in pieces:
                emit_there(piece, stage).wait_recv()
                emit_on(piece).start()

        emit_stage(one)

    def finish_outputs(stage):
        for piece in range(PIECES):
            emit_here(piece, stage).wait()
            emit_there(piece, stage).wait_send()
            emit_on(piece).wait()

    if inside:
        gain_copy = send(gain_grad_ref, gain_y, sem_gg, (0,), other_y)
        gain_copy.start()
        reduce_y(3).start()
        mixed_mid()
        reduce_mid(0, 4)
        gain_copy.wait()
        gain_y[...] = gain_y[...] + gain_grad_ref[...]
        gain_sends = [
            send(gain_y, gain_z.at[step - 1], sem_gg, (step,), peer(step)) for step in range(1, depth)]
        for copy in gain_sends:
            copy.start()
        reduce_mid(1)
        reduce_late(0)
        reduce_mid(2, 5)
        mixed_late()
        reduce_late(1)
        reduce_mid(3, 6)
        reduce_end(0)
        reduce_late(2)
        reduce_mid(4, 7)
        reduce_end(1)
        reduce_late(3)
        reduce_end(2)
        total = gain_y[...]
        for step, copy in enumerate(gain_sends):
            copy.wait()
            total = total + gain_z[step]
        gain_out[...] = functools.reduce(jnp.add, [
            jnp.where(deep == index, total[0:2, index * rows_own:(index + 1) * rows_own], 0.0)
            for index in range(depth)])
        reduce_mid(5)
        reduce_late(4)
        reduce_end(3)
        pass_outputs((3, 2))
        reduce_mid(6)
        mixed_cross().start()
        reduce_late(5)
        reduce_end(4)

        def place(sec, row, unit):
            return (sec * 2 + row) * 2 + unit

        mine = place(section, lane_y, core)
        for half_tile, tile_index in enumerate((2, 5)):
            value_ref[mine, :, half_tile * LANES:(half_tile + 1) * LANES] = (
                head_tile(tile_index).astype(LOW))
        value_y = send(value_ref.at[mine], value_ref.at[mine], sem_va, (0,), other_y)
        value_y.start()
        reduce_mid(7)
        late_outputs()
        value_y.wait()
        value_x = []
        for row in range(2):
            at = place(section, row, core)
            value_x.append(send(value_ref.at[at], value_ref.at[at], sem_va, (1 + row,), other_layer))
            value_x[-1].start()
        reduce_late(6)
        reduce_end(5)
        reduce_late(7)
        for copy in value_x:
            copy.wait()
        value_c = []
        for sec in range(2):
            for row in range(2):
                at = place(sec, row, core)
                value_c.append(
                    send(value_ref.at[at], value_ref.at[at], sem_va, (3 + 2 * sec + row,), other_core))
                value_c[-1].start()
        reduce_end(6)
        mixed_end()
        reduce_end(7)
        pass_outputs((1, 0))
        edge = 2 * HEAD

        def columns(kind, pair, upper):
            rest = head_tile(pair)
            return jnp.concatenate(
                [head_tile(kind), rest[:, HEAD:] if upper else rest[:, :HEAD]], axis=1)

        head_out[0] = columns(0, 4, False)
        head_out[1] = columns(1, 4, True)
        head_out[2] = columns(3, 5, True)
        for copy in value_c:
            copy.wait()
        value_out[...] = jnp.concatenate(
            [value_ref[index, :, :edge + HEAD] for index in range(value_out.shape[1] // (edge + HEAD))],
            axis=1).astype(F32)
        reduce_sent()
    else:
        late_outputs()
        pass_outputs(range(PIECES))

    emit_stage(finish_outputs)

    @pl.when(second)
    def _():
        for piece in range(PIECES):
            hand_rows(piece).wait_send()
            hand_values(piece).wait_send()


def run_layers(lengths, x_rows, gains, weights, cols, value_cols, depth, inside):
    width = x_rows.shape[3]
    tiles = width // 2 // LANES
    rows_own = width // depth
    columns = 3 * width
    vmem = pl.BlockSpec(memory_space=pltpu.VMEM)
    anywhere = pl.BlockSpec(memory_space=pl.ANY)
    smem = pl.BlockSpec(memory_space=pltpu.SMEM)
    per_tile = (PIECES, tiles, PIECE, LANES)
    turned = (PIECES, tiles, LANES, PIECE)
    flat = (PIECES, PIECE, width)
    flat_turned = (PIECES, width, PIECE)
    wide = (PIECES, 2, PIECE, width)
    low = lambda shape: pltpu.VMEM(shape, LOW)
    full = lambda shape: pltpu.VMEM(shape, F32)
    dma = lambda *shape: pltpu.SemaphoreType.DMA(shape)
    out_shape = [
        jax.ShapeDtypeStruct((2,) + flat, LOW),
        jax.ShapeDtypeStruct((rows_own, 2 * width), F32) if inside
        else jax.ShapeDtypeStruct(weights[0].shape, LOW),
        jax.ShapeDtypeStruct((8, width), F32),
    ]
    out_specs = [anywhere, vmem, vmem]
    scratch = [
        low((width, 4 * tiles * LANES)),
        low(per_tile), low(per_tile), low(per_tile), low(turned), low(per_tile),
        full((PIECES, 2 * tiles, 1, PIECE)),
        low(flat), low(flat), full((PIECES, PIECE, 2)),
        low(flat_turned), low(flat_turned), low(flat_turned), low(flat_turned),
        low(wide), low(wide), low((tiles, PIECE, LANES)),
        full((PIECES, 2 * tiles, PIECE, LANES)),
        full((WINDOW, PIECE, PIECE)), low(flat), pltpu.VMEM((PIECES, 1, PIECE), jnp.int32),
        low(flat), low((PIECES, 2, PIECE, LANES)), low(flat), low((PIECES, 2, PIECE, LANES)),
        low((3, PIECE, width)), low((PIECES + 2, PIECE, width)),
        dma(2, PIECES), dma(2, PIECES), dma(2, PIECES), dma(2, PIECES + 2), dma(2, PIECES),
        dma(2, PIECES), dma(4 + PIECES),
    ]
    if inside:
        out_shape += [
            jax.ShapeDtypeStruct((3, rows_own, cols), F32),
            jax.ShapeDtypeStruct((2, rows_own), F32),
            jax.ShapeDtypeStruct((rows_own, value_cols), F32)]
        out_specs += [vmem] * 3
        scratch += [
            low((2, width, columns)), full((depth, 8, -(-rows_own // LANES) * LANES)),
            low((2, width, columns)), low((width, columns)), low((depth - 1, rows_own, columns)),
            full((8, width)), full((depth - 1, 8, width)),
            low((8, rows_own, 2 * LANES)),
            dma(2, PARTS + 1, depth - 1, 2), dma(2, PARTS, depth), dma(2, depth), dma(2, 8),
            dma(2, 8, 3), dma(2, 2, 4), dma(2, depth), dma(2, 7),
        ]
    return pl.pallas_call(
        functools.partial(layers_kernel, width, depth, inside),
        out_shape=out_shape,
        in_specs=[smem, anywhere, vmem] + [anywhere if inside else vmem] * len(weights),
        out_specs=out_specs,
        scratch_shapes=scratch,
        compiler_params=pltpu.CompilerParams(
            collective_id=0, has_side_effects=True, vmem_limit_bytes=63 << 20),
        name="layers",
    )(lengths, x_rows, gains, *weights)


def pack(w_qk, w_value, w_out):
    query, key, out_t = w_qk[:, 0], w_qk[:, 1], w_out.T
    edge = 2 * HEAD
    return jnp.concatenate(
        [query[:, :edge], key[:, :edge], w_value[:, :edge], out_t[:, :edge],
         query[:, edge:], key[:, edge:], w_value[:, edge:], out_t[:, edge:]],
        axis=1)


def unpack(packed):
    edge = 2 * HEAD
    cut = lambda spot, size: packed[:, spot:spot + size]
    query = jnp.concatenate([cut(0, edge), cut(4 * edge, HEAD)], axis=1)
    key = jnp.concatenate([cut(edge, edge), cut(4 * edge + HEAD, HEAD)], axis=1)
    value = jnp.concatenate([cut(2 * edge, edge), cut(5 * edge, HEAD)], axis=1)
    out_t = jnp.concatenate([cut(3 * edge, edge), cut(5 * edge + HEAD, HEAD)], axis=1)
    hidden = packed.shape[1] // 3
    return (
        jnp.stack([query, key], axis=1), value, out_t.T,
        cut(hidden, hidden), cut(2 * hidden, hidden).T)


def shards(
    ends_in, seq_lengths, norm_gains, qk_weight, value_weight, out_weight, fc_weight, proj_weight
):
    section = lax.axis_index("section")
    lane_y = lax.axis_index("y")
    group = 2 * lane_y + lax.axis_index("core")
    first = section == 0
    cols = qk_weight.shape[3]
    width = ends_in.shape[2]
    fresh = (value_weight.shape[1] - width) // cols
    offset = jnp.where(first, group, width // cols + jnp.minimum(group, fresh - 1)) * cols
    w_value = lax.dynamic_slice_in_dim(value_weight, offset, cols, 1)
    parts = [pack(qk_weight[0], w_value, out_weight[0]), fc_weight[0], proj_weight[0].T]
    depth = lax.axis_size("dp")
    inside = depth == 4 and width % (16 * depth) == 0
    if inside:
        weights = parts
        gains = norm_gains[0].T
    else:
        weights = lax.all_gather(jnp.concatenate(parts, axis=1), "dp", axis=0, tiled=True)
        weights = [lax.all_gather(weights, "y", axis=0)]
        gains = lax.all_gather(norm_gains[0], "dp", axis=0, tiled=True).astype(F32).T
    x_rows = ends_in[0].reshape(2, PIECES, PIECE, width)
    kept = width // cols + fresh
    results = run_layers(
        seq_lengths, x_rows, gains, weights, cols, value_weight.shape[1], depth, inside)
    both = results[0].reshape(2 * MB_TOK, width)
    if inside:
        _, grads, _, heads, gain_rows, d_value = results
        attn_gain, mlp_gain = gain_rows[0], gain_rows[1]
        d_qk = jnp.stack([heads[0], heads[1]], axis=1)
        d_out = heads[2].T
        d_up, d_down = grads[:, :width], grads[:, width:].T
    else:
        _, grads, gain_grads = results
        grads = lax.psum_scatter(grads, "y", scatter_dimension=0, tiled=False)
        grads = lax.psum_scatter(grads, "dp", scatter_dimension=0, tiled=True)
        gain_rows = lax.psum(gain_grads[:2], "y").T
        gain_rows = lax.psum_scatter(gain_rows, "dp", scatter_dimension=0, tiled=True)
        attn_gain, mlp_gain = gain_rows[:, 0], gain_rows[:, 1]
        d_qk, d_value, d_out, d_up, d_down = unpack(grads.astype(F32))
        values = lax.all_gather(d_value.astype(LOW), ("section", "y", "core"), axis=0)
        d_value = jnp.concatenate([values[index] for index in range(kept)], axis=1).astype(F32)
    return (
        both[None], attn_gain[None], mlp_gain[None], d_qk[None], d_value,
        d_out[None], d_up[None], d_down[None])


def solution(mesh):
    sections, depth, split = (mesh.shape[name] for name in ("section", "dp", "mp"))
    grid = Mesh(mesh.devices.reshape(sections, depth, split // 2, 2), ("section", "dp", "y", "core"))
    mp = ("y", "core")
    in_specs = (
        P("section", "dp", None),
        P("dp", None),
        P("section", "dp", None),
        P("section", "dp", None, mp),
        P("dp", None),
        P("section", mp, "dp"),
        P("section", "dp", mp),
        P("section", mp, "dp"),
    )
    out_specs = (
        P("section", "dp", None),
        P("section", "dp"),
        P("section", "dp"),
        P("section", "dp", None, mp),
        P("dp", None),
        P("section", mp, "dp"),
        P("section", "dp", mp),
        P("section", mp, "dp"),
    )
    return jax.shard_map(shards, mesh=grid, in_specs=in_specs, out_specs=out_specs, check_vma=False)
```
